32 devices in a mesh: dp: 8 (over y, x, core), seq: 4 (over z).
Axes of the slice: x: 2, y: 2, z: 4, core: 2. Of those that a mesh axis runs over, the one named last changes fastest.
Arguments:
- tokens: bfloat16 [8, 1024, 1024], P('dp', 'seq'), may hold values from -6 to 6
- first_values: bfloat16 [8, 1024, 1024], P('dp', 'seq'), may hold values from -6 to 6
- out_grad: bfloat16 [8, 1024, 1024], P('dp', 'seq'), may hold values from -6 to 6
- segments: int32 [8, 1024], P('dp', 'seq'), may hold values from 0 to 3, as said below
- span_order: int32 [4], replicated, may hold values from 0 to 3, as said below
- qkv_weight: float32 [1024, 3072], P('dp'), may hold values from -0.1875 to 0.1875
- out_weight: float32 [1024, 1024], P('dp'), may hold values from -1 to 1
- gate_up_weight: float32 [1024, 5632], P('dp'), may hold values from -0.1875 to 0.1875
- down_weight: float32 [2816, 1024], P('dp'), may hold values from -0.109375 to 0.109375
- norm_gains: float32 [1024, 2], P('dp'), may hold values from 0.5 to 1.5
- first_qkv: float32 [1024, 3072], P('dp'), may hold values from -256 to 256
- first_out: float32 [1024, 1024], P('dp'), may hold values from -56 to 56
- first_gate_up: float32 [1024, 5632], P('dp'), may hold values from -192 to 192
- first_down: float32 [2816, 1024], P('dp'), may hold values from -256 to 256
- first_gains: float32 [1024, 2], P('dp'), may hold values from -512 to 512
- second_qkv: float32 [1024, 3072], P('dp'), may hold values from 2048 to 8192
- second_out: float32 [1024, 1024], P('dp'), may hold values from 81.92 to 327.68
- second_gate_up: float32 [1024, 5632], P('dp'), may hold values from 1003.52 to 4014.08
- second_down: float32 [2816, 1024], P('dp'), may hold values from 2048 to 8192
- second_gains: float32 [1024, 2], P('dp'), may hold values from 8192 to 32768
Outputs:
- layer_out: bfloat16 [8, 1024, 1024], P('dp', 'seq')
- tokens_grad: float32 [8, 1024, 1024], P('dp', 'seq')
- values_grad: float32 [8, 1024, 1024], P('dp', 'seq')
- new_qkv: float32 [1024, 3072], P('dp')
- new_out: float32 [1024, 1024], P('dp')
- new_gate_up: float32 [1024, 5632], P('dp')
- new_down: float32 [2816, 1024], P('dp')
- new_gains: float32 [1024, 2], P('dp')
- next_first_qkv: float32 [1024, 3072], P('dp')
- next_first_out: float32 [1024, 1024], P('dp')
- next_first_gate_up: float32 [1024, 5632], P('dp')
- next_first_down: float32 [2816, 1024], P('dp')
- next_first_gains: float32 [1024, 2], P('dp')
- next_second_qkv: float32 [1024, 3072], P('dp')
- next_second_out: float32 [1024, 1024], P('dp')
- next_second_gate_up: float32 [1024, 5632], P('dp')
- next_second_down: float32 [2816, 1024], P('dp')
- next_second_gains: float32 [1024, 2], P('dp')
The draws below stay inside these ranges and needn't reach their ends.
Inputs may be any that keep to these rules, and one draw needn't show every extreme that they name: `segments`: read in order of positions, a sequence's ids never fall; every sequence has ids 0 to 3, and id 2 begins within the first 256 positions and ends within the last 256. `span_order`: A permutation of the span numbers.
All inputs are finite; a program needn't handle non-finite values.
Results may differ from the reference program's by a relative error of at most 0.015.
The reference program's roundings to bfloat16 on the way count: a program that leaves them out, or rounds other values in their place, can miss the bound.
Values may be sent and summed in bfloat16 or wider, within the bound.
A program may use at most 320 MiB of HBM per device.

```python
import math
from functools import partial
import jax
import jax.numpy as jnp
from jax import lax

D = 1024
HEADS = 16
HEAD_DIM = 64
FF = 2816
TOK_DEV = 256
STEP = 10
SEQ_LEN = 1024
TOKENS = 8192
N_DP = 8
N_SEQ = 4


def shared_layout(key):
    span_perm = jax.random.permutation(jax.random.fold_in(key, 11), N_SEQ).astype(jnp.int32)
    bound_key = jax.random.fold_in(key, 12)
    first_cut = jax.random.randint(jax.random.fold_in(bound_key, 1), (N_DP, 1), 1, TOK_DEV // 2)
    second_cut = jax.random.randint(jax.random.fold_in(bound_key, 2), (N_DP, 1), TOK_DEV // 2, TOK_DEV)
    third_cut = SEQ_LEN - jax.random.randint(jax.random.fold_in(bound_key, 3), (N_DP, 1), 1, TOK_DEV)
    spot_index = jnp.arange(SEQ_LEN, dtype=jnp.int32)[None, :]
    by_position = (spot_index >= first_cut).astype(jnp.int32) + (spot_index >= second_cut).astype(jnp.int32) + (spot_index >= third_cut).astype(jnp.int32)
    in_spans = by_position.reshape(N_DP, N_SEQ, TOK_DEV)
    placed = in_spans[:, span_perm, :]
    return (span_perm, placed.reshape(N_DP, SEQ_LEN).astype(jnp.int32))


def draw_segments(key, part):
    span_perm, segment_ids = shared_layout(key)
    return segment_ids


def draw_span_order(key, part):
    span_perm, segment_ids = shared_layout(key)
    return span_perm


def level_of(key, dims, shards, least, high):
    def one(position, blocks):
        draws = jax.random.uniform(jax.random.fold_in(jax.random.fold_in(key, 6), position), (blocks,), jnp.float32, least / len(shards), high / len(shards))
        return jnp.repeat(jnp.exp(draws), dims[position] // blocks).reshape((-1,) + (1,) * (len(dims) - position - 1))

    loudness = one(*shards[0])
    for cut in shards[1:]:
        loudness = loudness * one(*cut)
    return loudness


def gaussian(key, shape, width, reach, shards=(), kind=jnp.bfloat16):
    entries = width * jax.random.normal(key, shape, jnp.float32)
    if shards:
        entries = entries * level_of(key, shape, shards, -0.22, 0.18)
    return jnp.clip(entries, -reach, reach).astype(kind)


def setup_inputs(seed: int = 0) -> dict:
    splits = jax.random.split(jax.random.key(seed), 21)
    return {
        "tokens": gaussian(splits[0], (N_DP, SEQ_LEN, D), 1.0, 6.0, ((0, 8), (1, 4))),
        "first_values": gaussian(splits[1], (N_DP, SEQ_LEN, D), 1.0, 6.0, ((0, 8), (1, 4))),
        "out_grad": gaussian(splits[2], (N_DP, SEQ_LEN, D), 1.0, 6.0, ((0, 8), (1, 4))),
        "segments": draw_segments(jax.random.fold_in(splits[20], 71), 0),
        "span_order": draw_span_order(jax.random.fold_in(splits[20], 71), 0),
        "qkv_weight": gaussian(splits[5], (D, 3 * D), D ** -0.5, 0.1875, ((0, 8),), jnp.float32),
        "out_weight": gaussian(splits[6], (D, D), (D // 32) ** -0.5, 1.0, ((0, 8),), jnp.float32),
        "gate_up_weight": gaussian(splits[7], (D, 2 * FF), D ** -0.5, 0.1875, ((0, 8),), jnp.float32),
        "down_weight": gaussian(splits[8], (FF, D), FF ** -0.5, 0.109375, ((0, 8),), jnp.float32),
        "norm_gains": jnp.clip(1.0 + 0.1 * jax.random.normal(splits[9], (D, 2), jnp.float32), 0.5, 1.5),
        "first_qkv": gaussian(splits[10], (D, 3 * D), (0.5 * TOKENS ** 0.5), 256.0, ((0, 8),), jnp.float32),
        "first_out": gaussian(splits[11], (D, D), (0.1 * TOKENS ** 0.5), 56.0, ((0, 8),), jnp.float32),
        "first_gate_up": gaussian(splits[12], (D, 2 * FF), (0.35 * TOKENS ** 0.5), 192.0, ((0, 8),), jnp.float32),
        "first_down": gaussian(splits[13], (FF, D), (0.5 * TOKENS ** 0.5), 256.0, ((0, 8),), jnp.float32),
        "first_gains": gaussian(splits[14], (D, 2), (TOKENS ** 0.5), 512.0, ((0, 8),), jnp.float32),
        "second_qkv": jnp.clip(jnp.exp(math.log(8192.0) - 1.3862944 * jax.random.uniform(splits[15], (D, 3 * D), jnp.float32) ** level_of(splits[15], (D, 3 * D), ((0, 8),), -0.2, 0.2)), 2048.0, 8192.0),
        "second_out": jnp.clip(jnp.exp(math.log(327.68) - 1.3862944 * jax.random.uniform(splits[16], (D, D), jnp.float32) ** level_of(splits[16], (D, D), ((0, 8),), -0.2, 0.2)), 81.92, 327.68),
        "second_gate_up": jnp.clip(jnp.exp(math.log(4014.08) - 1.3862944 * jax.random.uniform(splits[17], (D, 2 * FF), jnp.float32) ** level_of(splits[17], (D, 2 * FF), ((0, 8),), -0.2, 0.2)), 1003.52, 4014.08),
        "second_down": jnp.clip(jnp.exp(math.log(8192.0) - 1.3862944 * jax.random.uniform(splits[18], (FF, D), jnp.float32) ** level_of(splits[18], (FF, D), ((0, 8),), -0.2, 0.2)), 2048.0, 8192.0),
        "second_gains": jnp.clip(jnp.exp(math.log(32768.0) - 1.3862944 * jax.random.uniform(splits[19], (D, 2), jnp.float32) ** level_of(splits[19], (D, 2), ((0, 8),), -0.2, 0.2)), 8192.0, 32768.0),
    }


@jax.custom_vjp
def low(v):
    return lax.optimization_barrier(v.astype(jnp.bfloat16)).astype(jnp.float32)

@jax.custom_vjp
def low_back(v):
    return v

def low_keep(v):
    return (low(v), None)

def low_pass(kept, grad):
    return (grad,)

def back_keep(v):
    return (v, None)

def back_low(kept, grad):
    return (low(grad),)
low.defvjp(low_keep, low_pass)
low_back.defvjp(back_keep, back_low)
NORM_EPS = 1e-06
ADAM_EPS = 1e-08
BLEND_MIX = 0.5
BETA_FIRST = 0.5
BETA_SECOND = 0.5
MATRIX_RATE = 0.06
MATRIX_DECAY = 0.1
GAIN_RATE = 0.5
ROPE_BASE = 10000.0
MASK_FILL = -1e+30
PRECISE = lax.Precision.HIGHEST

def normalize(matrix, gain_column):
    return matrix * lax.rsqrt(lax.optimization_barrier(jnp.mean(matrix * matrix, axis=-1, keepdims=True)) + NORM_EPS) * gain_column

def rotary(positions):
    half_width = HEAD_DIM // 2
    frequency = jnp.exp(jnp.arange(half_width, dtype=jnp.float32) * (-math.log(ROPE_BASE) / half_width))
    angles = positions.astype(jnp.float32)[:, None] * frequency[None, :]
    return (jnp.cos(angles)[:, None, :], jnp.sin(angles)[:, None, :])

def rotate(head_rows, cosine, sine_table):
    half_width = head_rows.shape[-1] // 2
    lower_half = head_rows[..., :half_width]
    upper_half = head_rows[..., half_width:]
    return jnp.concatenate([lower_half * cosine - upper_half * sine_table, upper_half * cosine + lower_half * sine_table], axis=-1)

def attend_block(query_block, key_rows, value_rows, key_positions, key_segments):
    queries, query_positions, query_segments = query_block
    scores = jnp.einsum('qhd,khd->hqk', queries, key_rows, precision=PRECISE) * HEAD_DIM ** (-0.5)
    scores = low_back(scores)
    allowed = (query_segments[:, None] == key_segments[None, :]) & (key_positions[None, :] <= query_positions[:, None])
    masked = jnp.where(allowed[None], scores, MASK_FILL)
    highest = lax.optimization_barrier(jnp.max(masked, axis=-1, keepdims=True))
    weights = jnp.where(allowed[None], jnp.exp(masked - highest), 0.0)
    probabilities = low(weights / lax.optimization_barrier(jnp.sum(weights, axis=-1, keepdims=True)))
    return jnp.einsum('hqk,khd->qhd', probabilities, value_rows, precision=PRECISE)

def layer_pass(params, tokens_in, first_in, cosine, sine_table, positions, segment_ids):
    qkv_copy, out_copy, gate_up_copy, down_copy, gains_copy = [low(member) for member in params]
    length = tokens_in.shape[0]
    normed_in = low(normalize(tokens_in, gains_copy[:, 0]))
    mixed_rows = low_back(jnp.dot(normed_in, qkv_copy, precision=PRECISE))
    query_raw = mixed_rows[:, :D].reshape(length, HEADS, HEAD_DIM)
    key_raw = mixed_rows[:, D:2 * D].reshape(length, HEADS, HEAD_DIM)
    queries = low_back(low(rotate(query_raw, cosine, sine_table)))
    key_rows = low_back(low(rotate(key_raw, cosine, sine_table)))
    blended = low_back(low(BLEND_MIX * mixed_rows[:, 2 * D:] + (1.0 - BLEND_MIX) * first_in))
    block_rows = min(512, length)
    block_count = length // block_rows
    attend = jax.checkpoint(partial(attend_block, key_rows=key_rows, value_rows=blended.reshape(length, HEADS, HEAD_DIM), key_positions=positions, key_segments=segment_ids))
    attended_raw = lax.map(attend, (queries.reshape(block_count, block_rows, HEADS, HEAD_DIM), positions.reshape(block_count, block_rows), segment_ids.reshape(block_count, block_rows)))
    attended = low_back(low(attended_raw.reshape(length, D)))
    hidden_mid = tokens_in + low_back(jnp.dot(attended, out_copy, precision=PRECISE))
    normed_mid = low(normalize(hidden_mid, gains_copy[:, 1]))
    gate_up = low_back(jnp.dot(normed_mid, gate_up_copy, precision=PRECISE))
    activation = low(jax.nn.silu(gate_up[:, :FF]) * gate_up[:, FF:])
    return hidden_mid + jnp.dot(activation, down_copy, precision=PRECISE)

def apply_adamw(master, first_state, second_state, gradient, rate, decay):
    next_first = BETA_FIRST * first_state + (1.0 - BETA_FIRST) * gradient
    next_second = BETA_SECOND * second_state + (1.0 - BETA_SECOND) * gradient * gradient
    first_hat = next_first / (1.0 - BETA_FIRST ** STEP)
    second_hat = next_second / (1.0 - BETA_SECOND ** STEP)
    new_master = master - rate * (first_hat / (jnp.sqrt(second_hat) + ADAM_EPS) + decay * master)
    return (new_master, next_first, next_second)

def reference(tokens, first_values, out_grad, segments, span_order, qkv_weight, out_weight, gate_up_weight, down_weight, norm_gains, first_qkv, first_out, first_gate_up, first_down, first_gains, second_qkv, second_out, second_gate_up, second_down, second_gains):
    params = (qkv_weight, out_weight, gate_up_weight, down_weight, norm_gains)
    length = tokens.shape[1]
    row_index = jnp.arange(length, dtype=jnp.int32)
    positions = (span_order[row_index // TOK_DEV] * TOK_DEV + row_index % TOK_DEV).astype(jnp.int32)
    cosine, sine_table = rotary(positions)

    def one_group(totals, inputs):
        group_tokens, group_first, group_back, group_segments = inputs

        def forward(weight_set, tokens_in, first_in):
            return layer_pass(weight_set, tokens_in, first_in, cosine, sine_table, positions, group_segments)
        primal, pullback = jax.vjp(forward, params, group_tokens.astype(jnp.float32), group_first.astype(jnp.float32))
        weight_grads, token_grad, first_grad = pullback(group_back.astype(jnp.float32))
        totals = jax.tree.map(jnp.add, totals, weight_grads)
        return (totals, (primal.astype(jnp.bfloat16), token_grad, first_grad))
    zero_grads = jax.tree.map(jnp.zeros_like, params)
    totals, outputs = lax.scan(one_group, zero_grads, (tokens, first_values, out_grad, segments))
    layer_out, tokens_grad, values_grad = outputs
    qkv_new = apply_adamw(qkv_weight, first_qkv, second_qkv, totals[0], MATRIX_RATE, MATRIX_DECAY)
    out_new = apply_adamw(out_weight, first_out, second_out, totals[1], MATRIX_RATE, MATRIX_DECAY)
    gate_up_new = apply_adamw(gate_up_weight, first_gate_up, second_gate_up, totals[2], MATRIX_RATE, MATRIX_DECAY)
    down_new = apply_adamw(down_weight, first_down, second_down, totals[3], MATRIX_RATE, MATRIX_DECAY)
    gains_new = apply_adamw(norm_gains, first_gains, second_gains, totals[4], GAIN_RATE, 0.0)
    return (layer_out, tokens_grad, values_grad, qkv_new[0], out_new[0], gate_up_new[0], down_new[0], gains_new[0], qkv_new[1], out_new[1], gate_up_new[1], down_new[1], gains_new[1], qkv_new[2], out_new[2], gate_up_new[2], down_new[2], gains_new[2])
```

```python
import math

import jax
import jax.numpy as jnp
from jax import lax
from jax.sharding import PartitionSpec as P

HEAD_DIM = 64
STEP = 10


NORM_EPS = 1e-06
ADAM_EPS = 1e-08
BLEND_MIX = 0.5
BETA_FIRST = 0.5
BETA_SECOND = 0.5
MATRIX_RATE = 0.06
MATRIX_DECAY = 0.1
GAIN_RATE = 0.5
ROPE_BASE = 10000.0
MASK_FILL = -1e30
SCALE = HEAD_DIM ** (-0.5)

BF = jnp.bfloat16
F32 = jnp.float32


def dot_nn(left, right):
    return lax.dot_general(left, right, (((1,), (0,)), ((), ())), preferred_element_type=F32)


def dot_nt(left, right):
    return lax.dot_general(left, right, (((1,), (1,)), ((), ())), preferred_element_type=F32)


def dot_tn(left, right):
    return lax.dot_general(left, right, (((0,), (0,)), ((), ())), preferred_element_type=F32)


def normalize_parts(matrix):
    inverse = lax.rsqrt(jnp.mean(matrix * matrix, axis=-1, keepdims=True) + NORM_EPS)
    return (matrix * inverse, inverse)


def norm_backward(grad_rows, scaled, inverse, gain_column):
    pushed = grad_rows * gain_column
    return inverse * (pushed - scaled * jnp.mean(pushed * scaled, axis=-1, keepdims=True))


def rotary(positions):
    half_width = HEAD_DIM // 2
    frequency = jnp.exp(
        jnp.arange(half_width, dtype=F32) * (-math.log(ROPE_BASE) / half_width)
    )
    angles = positions.astype(F32)[:, None] * frequency[None, :]
    return (jnp.cos(angles)[:, None, :], jnp.sin(angles)[:, None, :])


def rotate(head_rows, cosine, sine_table):
    half_width = head_rows.shape[-1] // 2
    lower_half = head_rows[..., :half_width]
    upper_half = head_rows[..., half_width:]
    return jnp.concatenate(
        [
            lower_half * cosine - upper_half * sine_table,
            upper_half * cosine + lower_half * sine_table,
        ],
        axis=-1,
    )


def apply_adamw(master, first_state, second_state, gradient, rate, decay):
    next_first = BETA_FIRST * first_state + (1.0 - BETA_FIRST) * gradient
    next_second = BETA_SECOND * second_state + (1.0 - BETA_SECOND) * gradient * gradient
    first_hat = next_first / (1.0 - BETA_FIRST**STEP)
    second_hat = next_second / (1.0 - BETA_SECOND**STEP)
    new_master = master - rate * (first_hat / (jnp.sqrt(second_hat) + ADAM_EPS) + decay * master)
    return (new_master, next_first, next_second)


def to_heads(rows, span_count):
    return lax.all_to_all(
        rows.reshape(rows.shape[0], span_count, rows.shape[1] // span_count),
        "seq",
        split_axis=1,
        concat_axis=0,
        tiled=True,
    ).reshape(rows.shape[0] * span_count, rows.shape[1] // span_count)


def to_spans(columns, span_count):
    rows_here = columns.shape[0] // span_count
    got = lax.all_to_all(
        columns.reshape(span_count, rows_here, columns.shape[1]),
        "seq",
        split_axis=0,
        concat_axis=0,
        tiled=True,
    )
    return jnp.transpose(got, (1, 0, 2)).reshape(rows_here, columns.shape[1] * span_count)


def on_device(
    tokens,
    first_values,
    out_grad,
    segments,
    span_order,
    qkv_weight,
    out_weight,
    gate_up_weight,
    down_weight,
    norm_gains,
    first_qkv,
    first_out,
    first_gate_up,
    first_down,
    first_gains,
    second_qkv,
    second_out,
    second_gate_up,
    second_down,
    second_gains,
):
    span_count = lax.axis_size("seq")
    mine = lax.axis_index("seq")
    owned_rows, triple = qkv_weight.shape
    model_width = triple // 3
    group = model_width // span_count
    group_heads = group // HEAD_DIM
    residual = tokens[0].astype(F32)
    rows_here = residual.shape[0]
    length = rows_here * span_count
    hidden_width = gate_up_weight.shape[1] // 2

    qkv_owned = qkv_weight.reshape(owned_rows, 3, model_width).astype(BF)
    qkv_mine = lax.dynamic_slice_in_dim(qkv_owned, mine * group, group, 2).reshape(
        owned_rows, 3 * group
    )
    gains_owned = norm_gains.astype(BF).astype(F32)
    gains_full = lax.all_gather(norm_gains.astype(BF), "dp", axis=0, tiled=True).astype(F32)
    qkv_copy = lax.all_gather(qkv_mine, "dp", axis=0, tiled=True)
    out_copy = lax.all_gather(out_weight.astype(BF), "dp", axis=0, tiled=True)
    gate_up_copy = lax.all_gather(gate_up_weight.astype(BF), "dp", axis=0, tiled=True)
    down_copy = lax.all_gather(down_weight.astype(BF), "dp", axis=0, tiled=True)

    row_index = jnp.arange(length, dtype=jnp.int32)
    owner_table = (row_index // rows_here)[:, None] == jnp.arange(span_count, dtype=jnp.int32)[
        None, :
    ]
    positions = (
        jnp.sum(jnp.where(owner_table, span_order[None, :], 0), axis=1) * rows_here
        + row_index % rows_here
    )
    all_segments = lax.all_gather(segments[0], "seq", axis=0, tiled=True)
    cosine, sine_table = rotary(positions)
    allowed = (all_segments[:, None] == all_segments[None, :]) & (
        positions[None, :] <= positions[:, None]
    )

    scaled_in, inverse_in = normalize_parts(residual)
    normed_in = (scaled_in * gains_full[:, 0]).astype(BF)
    normed_all = lax.all_gather(normed_in, "seq", axis=0, tiled=True)
    first_all = to_heads(first_values[0], span_count)
    mixed = dot_nn(normed_all, qkv_copy)
    queries = rotate(
        mixed[:, :group].reshape(length, group_heads, HEAD_DIM), cosine, sine_table
    ).astype(BF)
    keys = rotate(
        mixed[:, group : 2 * group].reshape(length, group_heads, HEAD_DIM), cosine, sine_table
    ).astype(BF)
    blended = (
        (BLEND_MIX * mixed[:, 2 * group :] + (1.0 - BLEND_MIX) * first_all.astype(F32))
        .astype(BF)
        .reshape(length, group_heads, HEAD_DIM)
    )
    scores = jnp.einsum("qhd,khd->hqk", queries, keys, preferred_element_type=F32) * SCALE
    masked = jnp.where(allowed[None], scores, MASK_FILL)
    highest = jnp.max(masked, axis=-1, keepdims=True)
    raised = jnp.where(allowed[None], jnp.exp(masked - highest), 0.0)
    weights = raised / jnp.sum(raised, axis=-1, keepdims=True)
    weights_low = weights.astype(BF)
    attended_raw = jnp.einsum("hqk,khd->qhd", weights_low, blended, preferred_element_type=F32)
    attended = to_spans(attended_raw.reshape(length, group).astype(BF), span_count)

    hidden_mid = residual + dot_nn(attended, out_copy)
    scaled_mid, inverse_mid = normalize_parts(hidden_mid)
    normed_mid = (scaled_mid * gains_full[:, 1]).astype(BF)
    gate_up = dot_nn(normed_mid, gate_up_copy)
    gate_part = gate_up[:, :hidden_width]
    upward = gate_up[:, hidden_width:]
    sigmoid_gate = jax.nn.sigmoid(gate_part)
    swish_gate = gate_part * sigmoid_gate
    activation = (swish_gate * upward).astype(BF)
    layer_out = (hidden_mid + dot_nn(activation, down_copy)).astype(BF)
    back_rows = out_grad[0]
    activation_grad = dot_nt(back_rows, down_copy)
    gate_up_grad = jnp.concatenate(
        [
            activation_grad * upward * sigmoid_gate * (1.0 + gate_part * (1.0 - sigmoid_gate)),
            activation_grad * swish_gate,
        ],
        axis=1,
    ).astype(BF)
    normed_mid_grad = dot_nt(gate_up_grad, gate_up_copy)
    hidden_mid_grad = back_rows.astype(F32) + norm_backward(
        normed_mid_grad, scaled_mid, inverse_mid, gains_full[:, 1]
    )
    mid_grad_low = hidden_mid_grad.astype(BF)
    attended_grad = to_heads(dot_nt(mid_grad_low, out_copy).astype(BF), span_count)

    heads_grad = attended_grad.reshape(length, group_heads, HEAD_DIM)
    delta = jnp.transpose(jnp.sum(heads_grad.astype(F32) * attended_raw, axis=-1))
    weights_grad = jnp.einsum("qhd,khd->hqk", heads_grad, blended, preferred_element_type=F32)
    scores_grad = (weights * (weights_grad - delta[..., None])).astype(BF)
    queries_grad = (
        jnp.einsum("hqk,khd->qhd", scores_grad, keys, preferred_element_type=F32) * SCALE
    ).astype(BF).astype(F32)
    keys_grad = (
        jnp.einsum("hqk,qhd->khd", scores_grad, queries, preferred_element_type=F32) * SCALE
    ).astype(BF).astype(F32)
    blended_grad = jnp.einsum(
        "hqk,qhd->khd", weights_low, heads_grad, preferred_element_type=F32
    ).astype(BF).reshape(length, group)
    values_grad = (1.0 - BLEND_MIX) * to_spans(blended_grad, span_count).astype(F32)
    mixed_grad = jnp.concatenate(
        [
            rotate(queries_grad, cosine, -sine_table).reshape(length, group),
            rotate(keys_grad, cosine, -sine_table).reshape(length, group),
            BLEND_MIX * blended_grad.astype(F32),
        ],
        axis=1,
    ).astype(BF)
    normed_in_grad = lax.psum_scatter(
        dot_nt(mixed_grad, qkv_copy).astype(BF), "seq", scatter_dimension=0, tiled=True
    ).astype(F32)
    tokens_grad = hidden_mid_grad + norm_backward(
        normed_in_grad, scaled_in, inverse_in, gains_full[:, 0]
    )

    def to_owner(terms):
        return lax.psum_scatter(terms.astype(BF), "dp", scatter_dimension=0, tiled=True)

    qkv_part = lax.all_gather(to_owner(dot_tn(normed_all, mixed_grad)), "seq", axis=0)
    qkv_total = (
        jnp.transpose(qkv_part.reshape(span_count, owned_rows, 3, group), (1, 2, 0, 3))
        .reshape(owned_rows, triple)
        .astype(F32)
    )
    out_total, gate_up_total, down_total = lax.psum(
        (
            to_owner(dot_tn(attended, mid_grad_low)),
            to_owner(dot_tn(normed_mid, gate_up_grad)),
            to_owner(dot_tn(activation, back_rows)),
        ),
        "seq",
    )
    out_total, gate_up_total, down_total = (
        out_total.astype(F32),
        gate_up_total.astype(F32),
        down_total.astype(F32),
    )
    gains_total = jnp.stack(
        [
            jnp.sum(qkv_total * qkv_weight.astype(BF).astype(F32), axis=1),
            jnp.sum(gate_up_total * gate_up_weight.astype(BF).astype(F32), axis=1),
        ],
        axis=1,
    ) / gains_owned
    masters = (qkv_weight, out_weight, gate_up_weight, down_weight, norm_gains)
    firsts = (first_qkv, first_out, first_gate_up, first_down, first_gains)
    seconds = (second_qkv, second_out, second_gate_up, second_down, second_gains)
    totals = (qkv_total, out_total, gate_up_total, down_total, gains_total)
    rate_list = (MATRIX_RATE, MATRIX_RATE, MATRIX_RATE, MATRIX_RATE, GAIN_RATE)
    decays = (MATRIX_DECAY, MATRIX_DECAY, MATRIX_DECAY, MATRIX_DECAY, 0.0)
    updated = [
        apply_adamw(masters[i], firsts[i], seconds[i], totals[i], rate_list[i], decays[i])
        for i in range(5)
    ]
    return (
        (layer_out[None], tokens_grad[None], values_grad[None])
        + tuple(member[0] for member in updated)
        + tuple(member[1] for member in updated)
        + tuple(member[2] for member in updated)
    )


def solution(mesh):
    rows = P("dp", "seq", None)
    owned = P("dp", None)
    return jax.shard_map(
        on_device,
        mesh=mesh,
        in_specs=(rows, rows, rows, P("dp", "seq"), P()) + (owned,) * 15,
        out_specs=(rows,) * 3 + (owned,) * 15,
        check_vma=False,
    )
```

```python
import functools
import math

import jax
import jax.numpy as jnp
from jax import lax
from jax.experimental import pallas as pl
from jax.experimental.pallas import tpu as pltpu
from jax.sharding import PartitionSpec as P

HEAD_DIM = 64
STEP = 10


NORM_EPS = 1e-06
ADAM_EPS = 1e-08
BLEND_MIX = 0.5
BETA_FIRST = 0.5
BETA_SECOND = 0.5
MATRIX_RATE = 0.06
MATRIX_DECAY = 0.1
GAIN_RATE = 0.5
ROPE_BASE = 10000.0
MASK_FILL = -1e30
SCALE = HEAD_DIM ** (-0.5)

BF = jnp.bfloat16
F32 = jnp.float32


def dot_nn(left, right):
    return lax.dot_general(left, right, (((1,), (0,)), ((), ())), preferred_element_type=F32)


def dot_nt(left, right):
    return lax.dot_general(left, right, (((1,), (1,)), ((), ())), preferred_element_type=F32)


def dot_tn(left, right):
    return lax.dot_general(left, right, (((0,), (0,)), ((), ())), preferred_element_type=F32)


def normalize_parts(matrix):
    inverse = lax.rsqrt(jnp.mean(matrix * matrix, axis=-1, keepdims=True) + NORM_EPS)
    return (matrix * inverse, inverse)


def norm_backward(grad_rows, scaled, inverse, gain_column):
    pushed = grad_rows * gain_column
    return inverse * (pushed - scaled * jnp.mean(pushed * scaled, axis=-1, keepdims=True))


def rotary(positions):
    half_width = HEAD_DIM // 2
    frequency = jnp.exp(
        jnp.arange(half_width, dtype=F32) * (-math.log(ROPE_BASE) / half_width)
    )
    angles = positions.astype(F32)[:, None] * frequency[None, :]
    return (jnp.cos(angles)[:, None, :], jnp.sin(angles)[:, None, :])


def rotate(head_rows, cosine, sine_table):
    half_width = head_rows.shape[-1] // 2
    lower_half = head_rows[..., :half_width]
    upper_half = head_rows[..., half_width:]
    return jnp.concatenate(
        [
            lower_half * cosine - upper_half * sine_table,
            upper_half * cosine + lower_half * sine_table,
        ],
        axis=-1,
    )


def apply_adamw(master, first_state, second_state, gradient, rate, decay):
    next_first = BETA_FIRST * first_state + (1.0 - BETA_FIRST) * gradient
    next_second = BETA_SECOND * second_state + (1.0 - BETA_SECOND) * gradient * gradient
    first_hat = next_first / (1.0 - BETA_FIRST**STEP)
    second_hat = next_second / (1.0 - BETA_SECOND**STEP)
    new_master = master - rate * (first_hat / (jnp.sqrt(second_hat) + ADAM_EPS) + decay * master)
    return (new_master, next_first, next_second)


MESH = pl.DeviceIdType.MESH
VMEM_BYTES = 58 << 20


def full_spec():
    return pl.BlockSpec(memory_space=pltpu.VMEM)


def any_spec():
    return pl.BlockSpec(memory_space=pl.ANY)


class Place:
    def __init__(self, dp_count, span_count):
        self.dp_count = dp_count
        self.span_count = span_count
        self.inner_count = dp_count // 4
        self.dp = lax.axis_index("dp")
        self.span = lax.axis_index("seq")
        self.core = lax.rem(self.dp, 2)
        self.inner = lax.rem(self.dp // 2, self.inner_count)
        self.outer = self.dp // (2 * self.inner_count)

    def at(self, outer, inner, core):
        return (outer * self.inner_count + inner) * 2 + core

    def inner_plus(self, offset):
        return lax.rem(self.inner + offset, self.inner_count)

    def greet_all(self):
        barrier = pltpu.get_barrier_semaphore()
        for offset in range(1, self.dp_count):
            pl.semaphore_signal(
                barrier,
                inc=1,
                device_id=(lax.rem(self.dp + offset, self.dp_count), self.span),
                device_id_type=MESH,
            )
        for offset in range(1, self.span_count):
            pl.semaphore_signal(
                barrier,
                inc=1,
                device_id=(self.dp, lax.rem(self.span + offset, self.span_count)),
                device_id_type=MESH,
            )
        pl.semaphore_wait(barrier, self.dp_count + self.span_count - 2)


def remote(source, target, send_sem, recv_sem, device):
    return pltpu.make_async_remote_copy(
        src_ref=source,
        dst_ref=target,
        send_sem=send_sem,
        recv_sem=recv_sem,
        device_id=device,
        device_id_type=MESH,
    )


def half_rows(rows):
    return rows // 2 // 16 * 16


class Gather:
    def __init__(self, place, own, whole, send_sems, recv_sems):
        self.place = place
        self.own = own
        self.whole = whole
        self.rows = own.shape[0]
        self.send_sems = send_sems
        self.recv_sems = recv_sems
        self.sent = []
        count = place.inner_count
        self.near, self.lower, self.upper, self.pair = 0, count, 2 * count, 3 * count

    @staticmethod
    def slots(inner_count):
        return 6 * inner_count + 1

    def block(self, index, part=None):
        first = half_rows(self.rows)
        start, size = {None: (0, self.rows), 0: (0, first), 1: (first, self.rows - first)}[part]
        return self.whole.at[pl.ds(pl.multiple_of(index * self.rows + start, 16), size), :]

    def send(self, source, target, slot, far_slot, device):
        copy = remote(
            source, target, self.send_sems.at[slot], self.recv_sems.at[far_slot], (device, self.place.span)
        )
        copy.start()
        self.sent.append(copy)

    def arrived(self, block, slot):
        remote(
            block, block, self.send_sems.at[slot], self.recv_sems.at[slot], (self.place.dp, self.place.span)
        ).wait_recv()

    def sibling(self, block, slot):
        place = self.place
        self.send(block, block, slot, slot, place.at(place.outer, place.inner, 1 - place.core))

    def begin(self):
        place, count = self.place, self.place.inner_count
        mine = self.block(place.dp)
        self.send(self.own, mine, 0, 0, place.at(1 - place.outer, place.inner, place.core))
        for offset in range(1, count):
            self.send(
                self.own,
                mine,
                offset,
                count - offset,
                place.at(place.outer, place.inner_plus(offset), place.core),
            )
        copy = remote(
            self.own,
            mine,
            self.send_sems.at[self.pair],
            self.recv_sems.at[self.pair],
            (place.at(place.outer, place.inner, 1 - place.core), place.span),
        )
        copy.start()
        self.sent.append(copy)

    def forward(self):
        place, count = self.place, self.place.inner_count
        across = place.at(1 - place.outer, place.inner, place.core)
        self.arrived(self.block(across), 0)
        for offset in range(1, count):
            self.send(
                self.block(across, 0),
                self.block(across, 0),
                self.lower + offset,
                self.lower + count - offset,
                place.at(place.outer, place.inner_plus(offset), place.core),
            )
        for offset in range(1, count):
            beside = place.at(place.outer, place.inner_plus(offset), place.core)
            self.arrived(self.block(beside), offset)
            self.send(
                self.block(beside, 1),
                self.block(beside, 1),
                self.upper + offset,
                self.upper + offset,
                across,
            )
        self.sibling(self.block(across), self.pair + count)
        for offset in range(1, count):
            beside = place.at(place.outer, place.inner_plus(offset), place.core)
            self.sibling(self.block(beside), self.pair + offset)

    def share(self):
        place, count = self.place, self.place.inner_count
        for offset in range(1, count):
            far = place.at(1 - place.outer, place.inner_plus(offset), place.core)
            self.arrived(self.block(far, 0), self.lower + offset)
            self.sibling(self.block(far, 0), self.pair + count + offset)
            self.arrived(self.block(far, 1), self.upper + offset)
            self.sibling(self.block(far, 1), self.pair + 2 * count + offset)

    def end(self):
        place, count = self.place, self.place.inner_count
        other = 1 - place.core
        self.arrived(self.block(place.at(place.outer, place.inner, other)), self.pair)
        self.arrived(self.block(place.at(1 - place.outer, place.inner, other)), self.pair + count)
        for offset in range(1, count):
            inner = place.inner_plus(offset)
            self.arrived(self.block(place.at(place.outer, inner, other)), self.pair + offset)
            far = place.at(1 - place.outer, inner, other)
            self.arrived(self.block(far, 0), self.pair + count + offset)
            self.arrived(self.block(far, 1), self.pair + 2 * count + offset)
        for copy in self.sent:
            copy.wait_send()


class Exchange:
    def __init__(self, place, sources, targets, send_sems, recv_sems):
        self.place = place
        self.sources = sources
        self.targets = targets
        self.send_sems = send_sems
        self.recv_sems = recv_sems

    def copy(self, offset):
        place = self.place
        count = place.span_count
        peer = lax.rem(place.span + offset, count)
        return remote(
            self.sources.at[peer],
            self.targets.at[place.span],
            self.send_sems.at[offset],
            self.recv_sems.at[count - offset],
            (place.dp, peer),
        )

    def start(self):
        for offset in range(1, self.place.span_count):
            self.copy(offset).start()
        self.targets[self.place.span] = self.sources[self.place.span]

    def wait(self):
        place = self.place
        count = place.span_count
        for offset in range(1, count):
            peer = lax.rem(place.span + offset, count)
            remote(
                self.sources.at[peer],
                self.targets.at[peer],
                self.send_sems.at[offset],
                self.recv_sems.at[offset],
                (place.dp, peer),
            ).wait_recv()

    def finish(self):
        for offset in range(1, self.place.span_count):
            self.copy(offset).wait_send()


def cast_rows(source, target):
    rows = source.shape[0]

    def step(index, unused):
        at = pl.ds(pl.multiple_of(index * 16, 16), 16)
        target[at, :] = source[at, :].astype(BF)
        return unused

    lax.fori_loop(0, rows // 16, step, 0)


def swap_halves(rows):
    width = rows.shape[1]
    half = HEAD_DIM // 2
    if width % 128:
        pieces = []
        for start in range(0, width, HEAD_DIM):
            pieces += [rows[:, start + half : start + HEAD_DIM], rows[:, start : start + half]]
        return jnp.concatenate(pieces, axis=1)
    lane = lax.broadcasted_iota(jnp.int32, rows.shape, 1)
    return jnp.where(
        lane % HEAD_DIM < half, pltpu.roll(rows, width - half, 1), pltpu.roll(rows, half, 1)
    )


def widen(table, width):
    return jnp.concatenate([table] * (width // table.shape[1]), axis=1)


def segment_starts(bounds, rows, first):
    position = lax.broadcasted_iota(jnp.int32, (rows, 1), 0) + first
    position = position.astype(F32)
    start = jnp.zeros((rows, 1), F32)
    for cut in bounds:
        start = jnp.where(position >= cut, cut, start)
    return position, start


def head_part(matrix, head):
    if matrix.shape[1] == HEAD_DIM:
        return matrix
    lane = lax.broadcasted_iota(jnp.int32, (1, matrix.shape[1]), 1)
    return jnp.where(lane // HEAD_DIM == head, matrix, jnp.zeros_like(matrix))


def forward_kernel(
    dp_count,
    span_count,
    slot_of,
    order,
    tokens,
    first_values,
    segments,
    gains_mine,
    qkv_mine,
    out_mine,
    gate_up_mine,
    down_mine,
    cosine,
    sine,
    out_whole,
    gate_up_whole,
    down_whole,
    qkv_out,
    normed_out,
    gains_out,
    attended_out,
    query_out,
    key_out,
    value_out,
    raw_out,
    lse_out,
    out_own,
    gate_up_own,
    down_own,
    qkv_whole,
    gains_all,
    counts_send,
    counts_all,
    first_send,
    first_all,
    normed_all,
    scores_kept,
    attended_send,
    attended_all,
    gather_send,
    gather_recv,
    gains_send_sem,
    gains_recv_sem,
    counts_send_sem,
    counts_recv_sem,
    first_send_sem,
    first_recv_sem,
    ring_send,
    ring_recv,
    attended_send_sem,
    attended_recv_sem,
    local_sem,
):
    place = Place(dp_count, span_count)
    rows, width = tokens.shape
    group = width // span_count
    heads = group // HEAD_DIM
    last = span_count - 1
    span = place.span

    place.greet_all()
    gains_all[place.dp] = gains_mine[...]
    gains_copies = []
    for offset in range(1, dp_count):
        peer = lax.rem(place.dp + offset, dp_count)
        copy = remote(
            gains_mine,
            gains_all.at[place.dp],
            gains_send_sem.at[offset],
            gains_recv_sem.at[dp_count - offset],
            (peer, span),
        )
        copy.start()
        gains_copies.append(copy)
    gathers = [
        Gather(place, own, whole, gather_send.at[i], gather_recv.at[i])
        for i, (own, whole) in enumerate(
            (
                (qkv_mine, qkv_whole),
                (out_own, out_whole),
                (gate_up_own, gate_up_whole),
                (down_own, down_whole),
            )
        )
    ]
    qkv_gather, out_gather, gate_up_gather, down_gather = gathers
    qkv_gather.begin()
    qkv_whole[pl.ds(pl.multiple_of(place.dp * qkv_mine.shape[0], 16), qkv_mine.shape[0]), :] = (
        qkv_mine[...]
    )
    for index in range(span_count):
        first_send[index] = first_values[:, index * group : (index + 1) * group]
    first_exchange = Exchange(place, first_send, first_all, first_send_sem, first_recv_sem)
    first_exchange.start()
    ids = segments[...]
    row = lax.broadcasted_iota(jnp.int32, (8, 128), 0)
    counts = jnp.zeros((8, 128), F32)
    for cut in range(3):
        below = jnp.sum(jnp.where(ids <= cut, 1.0, 0.0), axis=1, keepdims=True)
        counts = jnp.where(row == cut, below, counts)
    for index in range(span_count):
        counts_send[index] = counts
    counts_exchange = Exchange(place, counts_send, counts_all, counts_send_sem, counts_recv_sem)
    counts_exchange.start()

    residual = tokens[...].astype(F32)
    scaled = residual * lax.rsqrt(jnp.mean(residual * residual, axis=1, keepdims=True) + NORM_EPS)
    for offset in range(1, dp_count):
        peer = lax.rem(place.dp + offset, dp_count)
        remote(
            gains_mine,
            gains_all.at[peer],
            gains_send_sem.at[offset],
            gains_recv_sem.at[offset],
            (peer, span),
        ).wait_recv()
    gains_row = jnp.concatenate([gains_all[i] for i in range(dp_count)], axis=1)
    gains_out[...] = gains_row
    normed_all[span] = (scaled * gains_row[0:1, :]).astype(BF)

    def pass_on(block, step, way):
        return remote(
            normed_all.at[block],
            normed_all.at[block],
            ring_send.at[way, step],
            ring_recv.at[way, step],
            (place.dp, jnp.where(way == 0, jnp.minimum(span + 1, last), jnp.maximum(span - 1, 0))),
        )

    @pl.when(span < last)
    def up():
        pass_on(span, 0, 0).start()

    @pl.when(span > 0)
    def down():
        pass_on(span, 0, 1).start()

    cast_rows(out_mine, out_own)
    out_gather.begin()
    cast_rows(gate_up_mine, gate_up_own)
    qkv_gather.forward()
    gate_up_gather.begin()
    cast_rows(down_mine, down_own)
    down_gather.begin()
    own_copies = []
    for i, member in enumerate(gathers[1:]):
        copy = pltpu.make_async_copy(member.own, member.block(place.dp), local_sem.at[i])
        copy.start()
        own_copies.append(copy)
    qkv_gather.share()
    out_gather.forward()

    for step in range(1, span_count):

        @pl.when(span - step >= 0)
        def from_below():
            block = jnp.maximum(span - step, 0)
            pass_on(block, step - 1, 0).wait_recv()

            @pl.when(span < last)
            def on():
                pass_on(block, step, 0).start()

        @pl.when(span + step <= last)
        def from_above():
            block = jnp.minimum(span + step, last)
            pass_on(block, step - 1, 1).wait_recv()

            @pl.when(span > 0)
            def on():
                pass_on(block, step, 1).start()

    qkv_gather.end()
    normed_copy = pltpu.make_async_copy(normed_all, normed_out, local_sem.at[3])
    normed_copy.start()
    qkv_copy = pltpu.make_async_copy(qkv_whole, qkv_out, local_sem.at[4])
    qkv_copy.start()
    first_exchange.wait()
    counts_exchange.wait()
    cuts = counts_all[0]
    for index in range(1, span_count):
        cuts = cuts + counts_all[index]
    bounds = [cuts[i : i + 1, 0:1] for i in range(3)]

    def project(position, unused):
        slot = slot_of[position]
        mixed = dot_nn(normed_all[slot], qkv_whole[...])
        cos_here = widen(cosine[position], group)
        sin_here = widen(sine[position], group)
        query = mixed[:, :group]
        key = mixed[:, group : 2 * group]
        query_out[position] = (query * cos_here + swap_halves(query) * sin_here).astype(BF)
        key_out[position] = (key * cos_here + swap_halves(key) * sin_here).astype(BF)
        value_out[position] = (
            BLEND_MIX * mixed[:, 2 * group :]
            + (1.0 - BLEND_MIX) * first_all[slot].astype(F32)
        ).astype(BF)
        return unused

    lax.fori_loop(0, span_count, project, 0)
    out_gather.share()
    gate_up_gather.forward()

    def attend(position, unused):
        query = query_out[position]
        parts = [head_part(query, head) for head in range(heads)]
        query_position, start = segment_starts(bounds, rows, position * rows)

        def score(other, highest):
            key = key_out[other]
            key_position = (
                lax.broadcasted_iota(jnp.int32, (1, rows), 1) + other * rows
            ).astype(F32)
            allowed = (key_position <= query_position) & (key_position >= start)
            found = []
            for head in range(heads):
                masked = jnp.where(allowed, dot_nt(parts[head], key) * SCALE, MASK_FILL)
                scores_kept[head, other] = masked
                found.append(jnp.maximum(highest[head], jnp.max(masked, axis=1, keepdims=True)))
            return tuple(found)

        highest = lax.fori_loop(
            0, position + 1, score, (jnp.full((rows, 1), MASK_FILL, F32),) * heads
        )

        def raise_scores(other, total):
            added = []
            for head in range(heads):
                raised = jnp.exp(scores_kept[head, other] - highest[head])
                scores_kept[head, other] = raised
                added.append(total[head] + jnp.sum(raised, axis=1, keepdims=True))
            return tuple(added)

        total = lax.fori_loop(
            0, position + 1, raise_scores, (jnp.zeros((rows, 1), F32),) * heads
        )
        inverse = [1.0 / member for member in total]

        def gather_values(other, attended):
            value = value_out[other]
            for head in range(heads):
                weights = (scores_kept[head, other] * inverse[head]).astype(BF)
                attended = attended + dot_nn(weights, head_part(value, head))
            return attended

        raw_out[position] = lax.fori_loop(
            0, position + 1, gather_values, jnp.zeros((rows, group), F32)
        )
        lane = lax.broadcasted_iota(jnp.int32, (rows, 128), 1)
        kept = jnp.zeros((rows, 128), F32)
        for head in range(heads):
            kept = jnp.where(lane == head, highest[head] + jnp.log(total[head]), kept)
        lse_out[position] = kept
        return unused

    lax.fori_loop(0, span_count // 2, attend, 0)
    down_gather.forward()
    lax.fori_loop(span_count // 2, span_count, attend, 0)

    for index in range(span_count):
        attended_send[index] = raw_out[order[index]].astype(BF)
    attended_exchange = Exchange(
        place, attended_send, attended_all, attended_send_sem, attended_recv_sem
    )
    attended_exchange.start()
    gate_up_gather.share()
    attended_exchange.wait()
    attended_out[...] = jnp.concatenate([attended_all[i] for i in range(span_count)], axis=1)
    out_gather.end()
    down_gather.share()
    gate_up_gather.end()
    down_gather.end()

    for copy in gains_copies:
        copy.wait_send()
    for exchange in (first_exchange, counts_exchange, attended_exchange):
        exchange.finish()
    for step in range(span_count):

        @pl.when((span - step >= 0) & (span < last))
        def sent_up():
            pass_on(jnp.maximum(span - step, 0), step, 0).wait_send()

        @pl.when((span + step <= last) & (span > 0))
        def sent_down():
            pass_on(jnp.minimum(span + step, last), step, 1).wait_send()

    for copy in own_copies:
        copy.wait()
    normed_copy.wait()
    qkv_copy.wait()


def forward_call(
    dp_count, span_count, slot_of, order, tokens, first_values, segments, gains_mine, qkv_mine,
    out_mine, gate_up_mine, down_mine, cosine, sine,
):
    rows, width = tokens.shape
    group = width // span_count
    heads = group // HEAD_DIM
    owned = qkv_mine.shape[0]
    doubled = gate_up_mine.shape[1]
    slots = Gather.slots(dp_count // 4)
    dma = pltpu.SemaphoreType.DMA
    by_span = (span_count, rows, group)
    return pl.pallas_call(
        functools.partial(forward_kernel, dp_count, span_count),
        out_shape=(
            jax.ShapeDtypeStruct((width, width), BF),
            jax.ShapeDtypeStruct((width, doubled), BF),
            jax.ShapeDtypeStruct((doubled // 2, width), BF),
            jax.ShapeDtypeStruct((width, 3 * group), BF),
            jax.ShapeDtypeStruct((span_count, rows, width), BF),
            jax.ShapeDtypeStruct((8, width), F32),
            jax.ShapeDtypeStruct((rows, width), BF),
            jax.ShapeDtypeStruct(by_span, BF),
            jax.ShapeDtypeStruct(by_span, BF),
            jax.ShapeDtypeStruct(by_span, BF),
            jax.ShapeDtypeStruct(by_span, F32),
            jax.ShapeDtypeStruct((span_count, rows, 128), F32),
        ),
        in_specs=[pl.BlockSpec(memory_space=pltpu.SMEM)] * 2 + [full_spec()] * 10,
        out_specs=(any_spec(),) * 5 + (full_spec(),) * 7,
        scratch_shapes=[
            pltpu.VMEM((owned, width), BF),
            pltpu.VMEM((owned, doubled), BF),
            pltpu.VMEM((down_mine.shape[0], width), BF),
            pltpu.VMEM((width, 3 * group), BF),
            pltpu.VMEM((dp_count, 8, owned), F32),
            pltpu.VMEM((span_count, 8, 128), F32),
            pltpu.VMEM((span_count, 8, 128), F32),
            pltpu.VMEM(by_span, BF),
            pltpu.VMEM(by_span, BF),
            pltpu.VMEM((span_count, rows, width), BF),
            pltpu.VMEM((heads, span_count, rows, rows), F32),
            pltpu.VMEM(by_span, BF),
            pltpu.VMEM(by_span, BF),
            dma((4, slots)),
            dma((4, slots)),
            dma((dp_count,)),
            dma((dp_count,)),
            dma((span_count,)),
            dma((span_count,)),
            dma((span_count,)),
            dma((span_count,)),
            dma((2, span_count)),
            dma((2, span_count)),
            dma((span_count,)),
            dma((span_count,)),
            dma((5,)),
        ],
        compiler_params=pltpu.CompilerParams(
            collective_id=0, has_side_effects=True, vmem_limit_bytes=VMEM_BYTES
        ),
    )(
        slot_of, order, tokens, first_values, segments, gains_mine, qkv_mine, out_mine,
        gate_up_mine, down_mine, cosine, sine,
    )


def to_heads(rows, span_count):
    return lax.all_to_all(
        rows.reshape(rows.shape[0], span_count, rows.shape[1] // span_count),
        "seq",
        split_axis=1,
        concat_axis=0,
        tiled=True,
    ).reshape(rows.shape[0] * span_count, rows.shape[1] // span_count)


def to_spans(columns, span_count):
    rows_here = columns.shape[0] // span_count
    got = lax.all_to_all(
        columns.reshape(span_count, rows_here, columns.shape[1]),
        "seq",
        split_axis=0,
        concat_axis=0,
        tiled=True,
    )
    return jnp.transpose(got, (1, 0, 2)).reshape(rows_here, columns.shape[1] * span_count)


def on_device(
    tokens,
    first_values,
    out_grad,
    segments,
    span_order,
    qkv_weight,
    out_weight,
    gate_up_weight,
    down_weight,
    norm_gains,
    first_qkv,
    first_out,
    first_gate_up,
    first_down,
    first_gains,
    second_qkv,
    second_out,
    second_gate_up,
    second_down,
    second_gains,
):
    span_count = lax.axis_size("seq")
    mine = lax.axis_index("seq")
    owned_rows, triple = qkv_weight.shape
    model_width = triple // 3
    group = model_width // span_count
    group_heads = group // HEAD_DIM
    residual = tokens[0].astype(F32)
    rows_here = residual.shape[0]
    length = rows_here * span_count
    hidden_width = gate_up_weight.shape[1] // 2

    slot_of = jnp.sum(
        jnp.where(
            span_order[None, :] == jnp.arange(span_count, dtype=jnp.int32)[:, None],
            jnp.arange(span_count, dtype=jnp.int32)[None, :],
            0,
        ),
        axis=1,
    ).astype(jnp.int32)
    lanes = min(group, 128)
    lane = jnp.arange(lanes, dtype=jnp.int32) % HEAD_DIM
    frequency = jnp.exp(
        (lane % (HEAD_DIM // 2)).astype(F32) * (-math.log(ROPE_BASE) / (HEAD_DIM // 2))
    )
    angles = jnp.arange(length, dtype=jnp.int32).astype(F32)[:, None] * frequency[None, :]
    cosine = jnp.cos(angles).reshape(span_count, rows_here, lanes)
    sine = (jnp.where(lane < HEAD_DIM // 2, -1.0, 1.0) * jnp.sin(angles)).reshape(
        span_count, rows_here, lanes
    )
    qkv_mine = (
        lax.dynamic_slice_in_dim(
            qkv_weight.reshape(owned_rows, 3, model_width), mine * group, group, 2
        )
        .reshape(owned_rows, 3 * group)
        .astype(BF)
    )
    gains_owned = norm_gains.astype(BF).astype(F32)
    gains_mine = jnp.pad(jnp.transpose(gains_owned), ((0, 6), (0, 0)))
    (
        out_copy, gate_up_copy, down_copy, qkv_copy, normed_all, gains_rows, attended,
        query_pos, key_pos, value_pos, raw_pos, lse_pos,
    ) = forward_call(
        lax.axis_size("dp"), span_count, slot_of, span_order, tokens[0], first_values[0], segments,
        gains_mine, qkv_mine, out_weight, gate_up_weight, down_weight, cosine, sine,
    )
    gains_full = jnp.transpose(gains_rows[:2])
    scaled_in, inverse_in = normalize_parts(residual)
    normed_all = jnp.take(normed_all, slot_of, axis=0).reshape(length, model_width)
    all_segments = jnp.take(
        lax.all_gather(segments[0], "seq", axis=0), slot_of, axis=0
    ).reshape(length)
    position = jnp.arange(length)
    allowed = (all_segments[:, None] == all_segments[None, :]) & (
        position[None, :] <= position[:, None]
    )
    queries, keys, blended, attended_raw = [
        member.reshape(length, group_heads, HEAD_DIM)
        for member in (query_pos, key_pos, value_pos, raw_pos)
    ]
    lse = jnp.transpose(lse_pos.reshape(length, 128)[:, :group_heads])
    scores = jnp.einsum("qhd,khd->hqk", queries, keys, preferred_element_type=F32) * SCALE
    weights = jnp.where(allowed[None], jnp.exp(scores - lse[..., None]), 0.0)
    weights_low = weights.astype(BF)
    cos64 = cosine.reshape(length, lanes)[:, None, :32]
    sin64 = sine.reshape(length, lanes)[:, None, 32:64]
    cosine, sine_table = cos64, sin64

    hidden_mid = residual + dot_nn(attended, out_copy)
    scaled_mid, inverse_mid = normalize_parts(hidden_mid)
    normed_mid = (scaled_mid * gains_full[:, 1]).astype(BF)
    gate_up = dot_nn(normed_mid, gate_up_copy)
    gate_part = gate_up[:, :hidden_width]
    upward = gate_up[:, hidden_width:]
    sigmoid_gate = jax.nn.sigmoid(gate_part)
    swish_gate = gate_part * sigmoid_gate
    activation = (swish_gate * upward).astype(BF)
    layer_out = (hidden_mid + dot_nn(activation, down_copy)).astype(BF)
    back_rows = out_grad[0]
    activation_grad = dot_nt(back_rows, down_copy)
    gate_up_grad = jnp.concatenate(
        [
            activation_grad * upward * sigmoid_gate * (1.0 + gate_part * (1.0 - sigmoid_gate)),
            activation_grad * swish_gate,
        ],
        axis=1,
    ).astype(BF)
    normed_mid_grad = dot_nt(gate_up_grad, gate_up_copy)
    hidden_mid_grad = back_rows.astype(F32) + norm_backward(
        normed_mid_grad, scaled_mid, inverse_mid, gains_full[:, 1]
    )
    mid_grad_low = hidden_mid_grad.astype(BF)
    attended_grad = to_heads(dot_nt(mid_grad_low, out_copy).astype(BF), span_count)

    def to_positions(matrix):
        shape = matrix.shape
        return jnp.take(
            matrix.reshape(span_count, rows_here, shape[1]), slot_of, axis=0
        ).reshape(shape)

    def to_slots(matrix):
        shape = matrix.shape
        return jnp.take(
            matrix.reshape(span_count, rows_here, shape[1]), span_order, axis=0
        ).reshape(shape)

    attended_grad = to_positions(attended_grad)

    heads_grad = attended_grad.reshape(length, group_heads, HEAD_DIM)
    delta = jnp.transpose(jnp.sum(heads_grad.astype(F32) * attended_raw, axis=-1))
    weights_grad = jnp.einsum("qhd,khd->hqk", heads_grad, blended, preferred_element_type=F32)
    scores_grad = (weights * (weights_grad - delta[..., None])).astype(BF)
    queries_grad = (
        jnp.einsum("hqk,khd->qhd", scores_grad, keys, preferred_element_type=F32) * SCALE
    ).astype(BF).astype(F32)
    keys_grad = (
        jnp.einsum("hqk,qhd->khd", scores_grad, queries, preferred_element_type=F32) * SCALE
    ).astype(BF).astype(F32)
    blended_grad = jnp.einsum(
        "hqk,qhd->khd", weights_low, heads_grad, preferred_element_type=F32
    ).astype(BF).reshape(length, group)
    values_grad = (1.0 - BLEND_MIX) * to_spans(to_slots(blended_grad), span_count).astype(F32)
    mixed_grad = jnp.concatenate(
        [
            rotate(queries_grad, cosine, -sine_table).reshape(length, group),
            rotate(keys_grad, cosine, -sine_table).reshape(length, group),
            BLEND_MIX * blended_grad.astype(F32),
        ],
        axis=1,
    ).astype(BF)
    normed_in_grad = lax.psum_scatter(
        to_slots(dot_nt(mixed_grad, qkv_copy).astype(BF)), "seq", scatter_dimension=0, tiled=True
    ).astype(F32)
    tokens_grad = hidden_mid_grad + norm_backward(
        normed_in_grad, scaled_in, inverse_in, gains_full[:, 0]
    )

    def to_owner(terms):
        return lax.psum_scatter(terms.astype(BF), "dp", scatter_dimension=0, tiled=True)

    qkv_part = lax.all_gather(to_owner(dot_tn(normed_all, mixed_grad)), "seq", axis=0)
    qkv_total = (
        jnp.transpose(qkv_part.reshape(span_count, owned_rows, 3, group), (1, 2, 0, 3))
        .reshape(owned_rows, triple)
        .astype(F32)
    )
    out_total, gate_up_total, down_total = lax.psum(
        (
            to_owner(dot_tn(attended, mid_grad_low)),
            to_owner(dot_tn(normed_mid, gate_up_grad)),
            to_owner(dot_tn(activation, back_rows)),
        ),
        "seq",
    )
    out_total, gate_up_total, down_total = (
        out_total.astype(F32),
        gate_up_total.astype(F32),
        down_total.astype(F32),
    )
    gains_total = jnp.stack(
        [
            jnp.sum(qkv_total * qkv_weight.astype(BF).astype(F32), axis=1),
            jnp.sum(gate_up_total * gate_up_weight.astype(BF).astype(F32), axis=1),
        ],
        axis=1,
    ) / gains_owned
    masters = (qkv_weight, out_weight, gate_up_weight, down_weight, norm_gains)
    firsts = (first_qkv, first_out, first_gate_up, first_down, first_gains)
    seconds = (second_qkv, second_out, second_gate_up, second_down, second_gains)
    totals = (qkv_total, out_total, gate_up_total, down_total, gains_total)
    rate_list = (MATRIX_RATE, MATRIX_RATE, MATRIX_RATE, MATRIX_RATE, GAIN_RATE)
    decays = (MATRIX_DECAY, MATRIX_DECAY, MATRIX_DECAY, MATRIX_DECAY, 0.0)
    updated = [
        apply_adamw(masters[i], firsts[i], seconds[i], totals[i], rate_list[i], decays[i])
        for i in range(5)
    ]
    return (
        (layer_out[None], tokens_grad[None], values_grad[None])
        + tuple(member[0] for member in updated)
        + tuple(member[1] for member in updated)
        + tuple(member[2] for member in updated)
    )


def solution(mesh):
    rows = P("dp", "seq", None)
    owned = P("dp", None)
    return jax.shard_map(
        on_device,
        mesh=mesh,
        in_specs=(rows, rows, rows, P("dp", "seq"), P()) + (owned,) * 15,
        out_specs=(rows,) * 3 + (owned,) * 15,
        check_vma=False,
    )
```

```python
import functools
import math

import jax
import jax.numpy as jnp
from jax import lax
from jax.experimental import pallas as pl
from jax.experimental.pallas import tpu as pltpu
from jax.sharding import PartitionSpec as P

HEAD_DIM = 64
STEP = 10


NORM_EPS = 1e-06
ADAM_EPS = 1e-08
BLEND_MIX = 0.5
BETA_FIRST = 0.5
BETA_SECOND = 0.5
MATRIX_RATE = 0.06
MATRIX_DECAY = 0.1
GAIN_RATE = 0.5
ROPE_BASE = 10000.0
MASK_FILL = -1e30
SCALE = HEAD_DIM ** (-0.5)

BF = jnp.bfloat16
F32 = jnp.float32


def dot_nn(left, right):
    return lax.dot_general(left, right, (((1,), (0,)), ((), ())), preferred_element_type=F32)


def dot_nt(left, right):
    return lax.dot_general(left, right, (((1,), (1,)), ((), ())), preferred_element_type=F32)


def dot_tn(left, right):
    return lax.dot_general(left, right, (((0,), (0,)), ((), ())), preferred_element_type=F32)


def normalize_parts(matrix):
    inverse = lax.rsqrt(jnp.mean(matrix * matrix, axis=-1, keepdims=True) + NORM_EPS)
    return (matrix * inverse, inverse)


def norm_backward(grad_rows, scaled, inverse, gain_column):
    pushed = grad_rows * gain_column
    return inverse * (pushed - scaled * jnp.mean(pushed * scaled, axis=-1, keepdims=True))


def rotary(positions):
    half_width = HEAD_DIM // 2
    frequency = jnp.exp(
        jnp.arange(half_width, dtype=F32) * (-math.log(ROPE_BASE) / half_width)
    )
    angles = positions.astype(F32)[:, None] * frequency[None, :]
    return (jnp.cos(angles)[:, None, :], jnp.sin(angles)[:, None, :])


def rotate(head_rows, cosine, sine_table):
    half_width = head_rows.shape[-1] // 2
    lower_half = head_rows[..., :half_width]
    upper_half = head_rows[..., half_width:]
    return jnp.concatenate(
        [
            lower_half * cosine - upper_half * sine_table,
            upper_half * cosine + lower_half * sine_table,
        ],
        axis=-1,
    )


def apply_adamw(master, first_state, second_state, gradient, rate, decay):
    next_first = BETA_FIRST * first_state + (1.0 - BETA_FIRST) * gradient
    next_second = BETA_SECOND * second_state + (1.0 - BETA_SECOND) * gradient * gradient
    first_hat = next_first / (1.0 - BETA_FIRST**STEP)
    second_hat = next_second / (1.0 - BETA_SECOND**STEP)
    new_master = master - rate * (first_hat / (jnp.sqrt(second_hat) + ADAM_EPS) + decay * master)
    return (new_master, next_first, next_second)


MESH = pl.DeviceIdType.MESH
VMEM_BYTES = 58 << 20


def full_spec():
    return pl.BlockSpec(memory_space=pltpu.VMEM)


def any_spec():
    return pl.BlockSpec(memory_space=pl.ANY)


class Place:
    def __init__(self, dp_count, span_count):
        self.dp_count = dp_count
        self.span_count = span_count
        self.inner_count = dp_count // 4
        self.dp = lax.axis_index("dp")
        self.span = lax.axis_index("seq")
        self.core = lax.rem(self.dp, 2)
        self.inner = lax.rem(self.dp // 2, self.inner_count)
        self.outer = self.dp // (2 * self.inner_count)

    def at(self, outer, inner, core):
        return (outer * self.inner_count + inner) * 2 + core

    def inner_plus(self, offset):
        return lax.rem(self.inner + offset, self.inner_count)

    def greet_all(self):
        barrier = pltpu.get_barrier_semaphore()
        for offset in range(1, self.dp_count):
            pl.semaphore_signal(
                barrier,
                inc=1,
                device_id=(lax.rem(self.dp + offset, self.dp_count), self.span),
                device_id_type=MESH,
            )
        for offset in range(1, self.span_count):
            pl.semaphore_signal(
                barrier,
                inc=1,
                device_id=(self.dp, lax.rem(self.span + offset, self.span_count)),
                device_id_type=MESH,
            )
        pl.semaphore_wait(barrier, self.dp_count + self.span_count - 2)


def remote(source, target, send_sem, recv_sem, device):
    return pltpu.make_async_remote_copy(
        src_ref=source,
        dst_ref=target,
        send_sem=send_sem,
        recv_sem=recv_sem,
        device_id=device,
        device_id_type=MESH,
    )


def half_rows(rows):
    return rows // 2 // 16 * 16


class Gather:
    def __init__(self, place, own, whole, send_sems, recv_sems):
        self.place = place
        self.own = own
        self.whole = whole
        self.rows = own.shape[0]
        self.send_sems = send_sems
        self.recv_sems = recv_sems
        self.sent = []
        count = place.inner_count
        self.near, self.lower, self.upper, self.pair = 0, count, 2 * count, 3 * count

    @staticmethod
    def slots(inner_count):
        return 6 * inner_count + 1

    def block(self, index, part=None):
        first = half_rows(self.rows)
        start, size = {None: (0, self.rows), 0: (0, first), 1: (first, self.rows - first)}[part]
        return self.whole.at[pl.ds(pl.multiple_of(index * self.rows + start, 16), size), :]

    def send(self, source, target, slot, far_slot, device):
        copy = remote(
            source, target, self.send_sems.at[slot], self.recv_sems.at[far_slot], (device, self.place.span)
        )
        copy.start()
        self.sent.append(copy)

    def arrived(self, block, slot):
        remote(
            block, block, self.send_sems.at[slot], self.recv_sems.at[slot], (self.place.dp, self.place.span)
        ).wait_recv()

    def sibling(self, block, slot):
        place = self.place
        self.send(block, block, slot, slot, place.at(place.outer, place.inner, 1 - place.core))

    def begin(self):
        place, count = self.place, self.place.inner_count
        mine = self.block(place.dp)
        self.send(self.own, mine, 0, 0, place.at(1 - place.outer, place.inner, place.core))
        for offset in range(1, count):
            self.send(
                self.own,
                mine,
                offset,
                count - offset,
                place.at(place.outer, place.inner_plus(offset), place.core),
            )
        copy = remote(
            self.own,
            mine,
            self.send_sems.at[self.pair],
            self.recv_sems.at[self.pair],
            (place.at(place.outer, place.inner, 1 - place.core), place.span),
        )
        copy.start()
        self.sent.append(copy)

    def forward(self):
        place, count = self.place, self.place.inner_count
        across = place.at(1 - place.outer, place.inner, place.core)
        self.arrived(self.block(across), 0)
        for offset in range(1, count):
            self.send(
                self.block(across, 0),
                self.block(across, 0),
                self.lower + offset,
                self.lower + count - offset,
                place.at(place.outer, place.inner_plus(offset), place.core),
            )
        for offset in range(1, count):
            beside = place.at(place.outer, place.inner_plus(offset), place.core)
            self.arrived(self.block(beside), offset)
            self.send(
                self.block(beside, 1),
                self.block(beside, 1),
                self.upper + offset,
                self.upper + offset,
                across,
            )
        self.sibling(self.block(across), self.pair + count)
        for offset in range(1, count):
            beside = place.at(place.outer, place.inner_plus(offset), place.core)
            self.sibling(self.block(beside), self.pair + offset)

    def share(self):
        place, count = self.place, self.place.inner_count
        for offset in range(1, count):
            far = place.at(1 - place.outer, place.inner_plus(offset), place.core)
            self.arrived(self.block(far, 0), self.lower + offset)
            self.sibling(self.block(far, 0), self.pair + count + offset)
            self.arrived(self.block(far, 1), self.upper + offset)
            self.sibling(self.block(far, 1), self.pair + 2 * count + offset)

    def end(self):
        place, count = self.place, self.place.inner_count
        other = 1 - place.core
        self.arrived(self.block(place.at(place.outer, place.inner, other)), self.pair)
        self.arrived(self.block(place.at(1 - place.outer, place.inner, other)), self.pair + count)
        for offset in range(1, count):
            inner = place.inner_plus(offset)
            self.arrived(self.block(place.at(place.outer, inner, other)), self.pair + offset)
            far = place.at(1 - place.outer, inner, other)
            self.arrived(self.block(far, 0), self.pair + count + offset)
            self.arrived(self.block(far, 1), self.pair + 2 * count + offset)
        for copy in self.sent:
            copy.wait_send()


class Exchange:
    def __init__(self, place, sources, targets, send_sems, recv_sems):
        self.place = place
        self.sources = sources
        self.targets = targets
        self.send_sems = send_sems
        self.recv_sems = recv_sems

    def copy(self, offset):
        place = self.place
        count = place.span_count
        peer = lax.rem(place.span + offset, count)
        return remote(
            self.sources.at[peer],
            self.targets.at[place.span],
            self.send_sems.at[offset],
            self.recv_sems.at[count - offset],
            (place.dp, peer),
        )

    def start(self):
        for offset in range(1, self.place.span_count):
            self.copy(offset).start()
        self.targets[self.place.span] = self.sources[self.place.span]

    def wait(self):
        place = self.place
        count = place.span_count
        for offset in range(1, count):
            peer = lax.rem(place.span + offset, count)
            remote(
                self.sources.at[peer],
                self.targets.at[peer],
                self.send_sems.at[offset],
                self.recv_sems.at[offset],
                (place.dp, peer),
            ).wait_recv()

    def finish(self):
        for offset in range(1, self.place.span_count):
            self.copy(offset).wait_send()


def cast_rows(source, target):
    rows = source.shape[0]

    def step(index, unused):
        at = pl.ds(pl.multiple_of(index * 16, 16), 16)
        target[at, :] = source[at, :].astype(BF)
        return unused

    lax.fori_loop(0, rows // 16, step, 0)


def swap_halves(rows):
    width = rows.shape[1]
    half = HEAD_DIM // 2
    if width % 128:
        pieces = []
        for start in range(0, width, HEAD_DIM):
            pieces += [rows[:, start + half : start + HEAD_DIM], rows[:, start : start + half]]
        return jnp.concatenate(pieces, axis=1)
    lane = lax.broadcasted_iota(jnp.int32, rows.shape, 1)
    return jnp.where(
        lane % HEAD_DIM < half, pltpu.roll(rows, width - half, 1), pltpu.roll(rows, half, 1)
    )


def segment_starts(bounds, rows, first):
    position = lax.broadcasted_iota(jnp.int32, (rows, 1), 0) + first
    position = position.astype(F32)
    start = jnp.zeros((rows, 1), F32)
    for cut in bounds:
        start = jnp.where(position >= cut, cut, start)
    return position, start


def head_part(matrix, head):
    if matrix.shape[1] == HEAD_DIM:
        return matrix
    lane = lax.broadcasted_iota(jnp.int32, (1, matrix.shape[1]), 1)
    return jnp.where(lane // HEAD_DIM == head, matrix, jnp.zeros_like(matrix))


def forward_kernel(
    dp_count,
    span_count,
    slot_of,
    order,
    tokens,
    first_values,
    segments,
    gains_mine,
    qkv_mine,
    out_mine,
    gate_up_mine,
    down_mine,
    cosine,
    sine,
    out_whole,
    gate_up_whole,
    down_whole,
    qkv_out,
    normed_out,
    counts_out,
    gains_out,
    attended_out,
    query_out,
    key_out,
    value_out,
    raw_out,
    lse_out,
    out_own,
    gate_up_own,
    down_own,
    qkv_whole,
    gains_all,
    counts_send,
    counts_all,
    first_send,
    first_all,
    normed_all,
    scores_kept,
    attended_send,
    attended_all,
    gather_send,
    gather_recv,
    gains_send_sem,
    gains_recv_sem,
    counts_send_sem,
    counts_recv_sem,
    first_send_sem,
    first_recv_sem,
    ring_send,
    ring_recv,
    attended_send_sem,
    attended_recv_sem,
    local_sem,
):
    place = Place(dp_count, span_count)
    rows, width = tokens.shape
    group = width // span_count
    heads = group // HEAD_DIM
    last = span_count - 1
    span = place.span

    place.greet_all()
    gains_all[place.dp] = gains_mine[...]
    gains_copies = []
    for offset in range(1, dp_count):
        peer = lax.rem(place.dp + offset, dp_count)
        copy = remote(
            gains_mine,
            gains_all.at[place.dp],
            gains_send_sem.at[offset],
            gains_recv_sem.at[dp_count - offset],
            (peer, span),
        )
        copy.start()
        gains_copies.append(copy)
    gathers = [
        Gather(place, own, whole, gather_send.at[i], gather_recv.at[i])
        for i, (own, whole) in enumerate(
            (
                (qkv_mine, qkv_whole),
                (out_own, out_whole),
                (gate_up_own, gate_up_whole),
                (down_own, down_whole),
            )
        )
    ]
    qkv_gather, out_gather, gate_up_gather, down_gather = gathers
    qkv_gather.begin()
    qkv_whole[pl.ds(pl.multiple_of(place.dp * qkv_mine.shape[0], 16), qkv_mine.shape[0]), :] = (
        qkv_mine[...]
    )
    for index in range(span_count):
        first_send[index] = first_values[:, index * group : (index + 1) * group]
    first_exchange = Exchange(place, first_send, first_all, first_send_sem, first_recv_sem)
    first_exchange.start()
    ids = segments[...]
    row = lax.broadcasted_iota(jnp.int32, (8, 128), 0)
    counts = jnp.zeros((8, 128), F32)
    for cut in range(3):
        below = jnp.sum(jnp.where(ids <= cut, 1.0, 0.0), axis=1, keepdims=True)
        counts = jnp.where(row == cut, below, counts)
    for index in range(span_count):
        counts_send[index] = counts
    counts_exchange = Exchange(place, counts_send, counts_all, counts_send_sem, counts_recv_sem)
    counts_exchange.start()

    residual = tokens[...].astype(F32)
    scaled = residual * lax.rsqrt(jnp.mean(residual * residual, axis=1, keepdims=True) + NORM_EPS)
    for offset in range(1, dp_count):
        peer = lax.rem(place.dp + offset, dp_count)
        remote(
            gains_mine,
            gains_all.at[peer],
            gains_send_sem.at[offset],
            gains_recv_sem.at[offset],
            (peer, span),
        ).wait_recv()
    gains_row = jnp.concatenate([gains_all[i] for i in range(dp_count)], axis=1)
    gains_out[...] = gains_row
    normed_all[span] = (scaled * gains_row[0:1, :]).astype(BF)

    def pass_on(block, step, way):
        return remote(
            normed_all.at[block],
            normed_all.at[block],
            ring_send.at[way, step],
            ring_recv.at[way, step],
            (place.dp, jnp.where(way == 0, jnp.minimum(span + 1, last), jnp.maximum(span - 1, 0))),
        )

    @pl.when(span < last)
    def up():
        pass_on(span, 0, 0).start()

    @pl.when(span > 0)
    def down():
        pass_on(span, 0, 1).start()

    cast_rows(out_mine, out_own)
    out_gather.begin()
    cast_rows(gate_up_mine, gate_up_own)
    qkv_gather.forward()
    gate_up_gather.begin()
    cast_rows(down_mine, down_own)
    down_gather.begin()
    own_copies = []
    for i, member in enumerate(gathers[1:]):
        copy = pltpu.make_async_copy(member.own, member.block(place.dp), local_sem.at[i])
        copy.start()
        own_copies.append(copy)
    qkv_gather.share()
    out_gather.forward()

    for step in range(1, span_count):

        @pl.when(span - step >= 0)
        def from_below():
            block = jnp.maximum(span - step, 0)
            pass_on(block, step - 1, 0).wait_recv()

            @pl.when(span < last)
            def on():
                pass_on(block, step, 0).start()

        @pl.when(span + step <= last)
        def from_above():
            block = jnp.minimum(span + step, last)
            pass_on(block, step - 1, 1).wait_recv()

            @pl.when(span > 0)
            def on():
                pass_on(block, step, 1).start()

    qkv_gather.end()
    qkv_copy = pltpu.make_async_copy(qkv_whole, qkv_out, local_sem.at[4])
    qkv_copy.start()
    first_exchange.wait()
    counts_exchange.wait()
    cuts = counts_all[0]
    for index in range(1, span_count):
        cuts = cuts + counts_all[index]
    counts_out[...] = cuts
    bounds = [cuts[i : i + 1, 0:1] for i in range(3)]

    def project(position, unused):
        slot = slot_of[position]
        normed_here = normed_all[slot]
        normed_out[:, pl.ds(pl.multiple_of(position * rows, rows), rows)] = jnp.transpose(normed_here)
        mixed = dot_nn(normed_here, qkv_whole[...])
        cos_here = jnp.concatenate([cosine[position]] * (2 * heads), axis=1)
        sin_here = jnp.concatenate([-sine[position], sine[position]] * heads, axis=1)
        query = mixed[:, :group]
        key = mixed[:, group : 2 * group]
        query_out[position] = (query * cos_here + swap_halves(query) * sin_here).astype(BF)
        key_out[position] = (key * cos_here + swap_halves(key) * sin_here).astype(BF)
        value_out[position] = (
            BLEND_MIX * mixed[:, 2 * group :]
            + (1.0 - BLEND_MIX) * first_all[slot].astype(F32)
        ).astype(BF)
        return unused

    lax.fori_loop(0, span_count, project, 0)
    out_gather.share()
    gate_up_gather.forward()

    def attend(position, unused):
        query = query_out[position]
        parts = [head_part(query, head) for head in range(heads)]
        query_position, start = segment_starts(bounds, rows, position * rows)

        def score(other, highest):
            key = key_out[other]
            key_position = (
                lax.broadcasted_iota(jnp.int32, (1, rows), 1) + other * rows
            ).astype(F32)
            allowed = (key_position <= query_position) & (key_position >= start)
            found = []
            for head in range(heads):
                masked = jnp.where(allowed, dot_nt(parts[head], key) * SCALE, MASK_FILL)
                scores_kept[head, other] = masked
                found.append(jnp.maximum(highest[head], jnp.max(masked, axis=1, keepdims=True)))
            return tuple(found)

        highest = lax.fori_loop(
            0, position + 1, score, (jnp.full((rows, 1), MASK_FILL, F32),) * heads
        )

        def raise_scores(other, total):
            added = []
            for head in range(heads):
                raised = jnp.exp(scores_kept[head, other] - highest[head])
                scores_kept[head, other] = raised
                added.append(total[head] + jnp.sum(raised, axis=1, keepdims=True))
            return tuple(added)

        total = lax.fori_loop(
            0, position + 1, raise_scores, (jnp.zeros((rows, 1), F32),) * heads
        )
        inverse = [1.0 / member for member in total]

        def gather_values(other, attended):
            value = value_out[other]
            for head in range(heads):
                weights = (scores_kept[head, other] * inverse[head]).astype(BF)
                attended = attended + dot_nn(weights, head_part(value, head))
            return attended

        raw_out[position] = lax.fori_loop(
            0, position + 1, gather_values, jnp.zeros((rows, group), F32)
        )
        lane = lax.broadcasted_iota(jnp.int32, (rows, 128), 1)
        kept = jnp.zeros((rows, 128), F32)
        for head in range(heads):
            kept = jnp.where(lane == head, highest[head] + jnp.log(total[head]), kept)
        lse_out[position] = kept
        return unused

    lax.fori_loop(0, span_count // 2, attend, 0)
    down_gather.forward()
    lax.fori_loop(span_count // 2, span_count, attend, 0)

    for index in range(span_count):
        attended_send[index] = raw_out[order[index]].astype(BF)
    attended_exchange = Exchange(
        place, attended_send, attended_all, attended_send_sem, attended_recv_sem
    )
    attended_exchange.start()
    gate_up_gather.share()
    attended_exchange.wait()
    attended_out[...] = jnp.concatenate([attended_all[i] for i in range(span_count)], axis=1)
    out_gather.end()
    down_gather.share()
    gate_up_gather.end()
    down_gather.end()

    for copy in gains_copies:
        copy.wait_send()
    for exchange in (first_exchange, counts_exchange, attended_exchange):
        exchange.finish()
    for step in range(span_count):

        @pl.when((span - step >= 0) & (span < last))
        def sent_up():
            pass_on(jnp.maximum(span - step, 0), step, 0).wait_send()

        @pl.when((span + step <= last) & (span > 0))
        def sent_down():
            pass_on(jnp.minimum(span + step, last), step, 1).wait_send()

    for copy in own_copies:
        copy.wait()
    qkv_copy.wait()


def forward_call(
    dp_count, span_count, slot_of, order, tokens, first_values, segments, gains_mine, qkv_mine,
    out_mine, gate_up_mine, down_mine, cosine, sine,
):
    rows, width = tokens.shape
    group = width // span_count
    heads = group // HEAD_DIM
    owned = qkv_mine.shape[0]
    doubled = gate_up_mine.shape[1]
    slots = Gather.slots(dp_count // 4)
    dma = pltpu.SemaphoreType.DMA
    by_span = (span_count, rows, group)
    return pl.pallas_call(
        functools.partial(forward_kernel, dp_count, span_count),
        out_shape=(
            jax.ShapeDtypeStruct((width, width), BF),
            jax.ShapeDtypeStruct((width, doubled), BF),
            jax.ShapeDtypeStruct((doubled // 2, width), BF),
            jax.ShapeDtypeStruct((width, 3 * group), BF),
            jax.ShapeDtypeStruct((width, span_count * rows), BF),
            jax.ShapeDtypeStruct((8, 128), F32),
            jax.ShapeDtypeStruct((8, width), F32),
            jax.ShapeDtypeStruct((rows, width), BF),
            jax.ShapeDtypeStruct(by_span, BF),
            jax.ShapeDtypeStruct(by_span, BF),
            jax.ShapeDtypeStruct(by_span, BF),
            jax.ShapeDtypeStruct(by_span, F32),
            jax.ShapeDtypeStruct((span_count, rows, 128), F32),
        ),
        in_specs=[pl.BlockSpec(memory_space=pltpu.SMEM)] * 2 + [full_spec()] * 10,
        out_specs=(any_spec(),) * 4 + (full_spec(),) * 9,
        scratch_shapes=[
            pltpu.VMEM((owned, width), BF),
            pltpu.VMEM((owned, doubled), BF),
            pltpu.VMEM((down_mine.shape[0], width), BF),
            pltpu.VMEM((width, 3 * group), BF),
            pltpu.VMEM((dp_count, 8, owned), F32),
            pltpu.VMEM((span_count, 8, 128), F32),
            pltpu.VMEM((span_count, 8, 128), F32),
            pltpu.VMEM(by_span, BF),
            pltpu.VMEM(by_span, BF),
            pltpu.VMEM((span_count, rows, width), BF),
            pltpu.VMEM((heads, span_count, rows, rows), F32),
            pltpu.VMEM(by_span, BF),
            pltpu.VMEM(by_span, BF),
            dma((4, slots)),
            dma((4, slots)),
            dma((dp_count,)),
            dma((dp_count,)),
            dma((span_count,)),
            dma((span_count,)),
            dma((span_count,)),
            dma((span_count,)),
            dma((2, span_count)),
            dma((2, span_count)),
            dma((span_count,)),
            dma((span_count,)),
            dma((5,)),
        ],
        compiler_params=pltpu.CompilerParams(
            collective_id=0, has_side_effects=True, vmem_limit_bytes=VMEM_BYTES
        ),
    )(
        slot_of, order, tokens, first_values, segments, gains_mine, qkv_mine, out_mine,
        gate_up_mine, down_mine, cosine, sine,
    )


class Pair:
    def __init__(
        self, place, left_whole, left, left_other, right, right_other, send_sems, recv_sems
    ):
        self.place = place
        self.left = left
        self.left_other = left_other
        self.right = right
        self.right_other = right_other
        other = (place.at(place.outer, place.inner, 1 - place.core), place.span)
        self.left_copy = remote(
            left_whole.at[:, 1 - place.core], left_other, send_sems.at[0], recv_sems.at[0], other
        )
        self.own_copy = pltpu.make_async_copy(
            left_whole.at[:, place.core], left, send_sems.at[2]
        )
        self.right_copy = remote(right, right_other, send_sems.at[1], recv_sems.at[1], other)

    def lend_left(self):
        self.own_copy.start()
        self.left_copy.start()

    def wait(self):
        self.own_copy.wait()
        self.left_copy.wait_recv()
        self.right_copy.wait_recv()

    def finish(self):
        self.left_copy.wait_send()
        self.right_copy.wait_send()

    def product(self, outer, inner, columns):
        chip = outer * self.place.inner_count + inner
        depth = self.right.shape[1]
        found = None
        for block in range(self.right.shape[0]):
            at = slice(block * depth, (block + 1) * depth)
            mine = dot_nn(self.left[chip, :, at], self.right[block, :, columns])
            theirs = dot_nn(self.left_other[chip, :, at], self.right_other[block, :, columns])
            found = mine + theirs if found is None else found + mine + theirs
        return found


class Piece:
    def __init__(self, pair, columns, kind, buffers, sems, result):
        self.pair = pair
        self.place = pair.place
        self.columns = columns
        self.kind = kind
        self.send1, self.recv1, self.send2, self.recv2 = buffers[:4]
        mine = self.recv1.at[0, pair.place.inner if kind == 0 else pair.place.outer]
        self.line = [mine] + list(buffers[4:])
        self.send_sems, self.recv_sems = sems
        self.result = result
        self.sent = []

    def send(self, source, target, slot, far_slot, dp, span=None):
        copy = remote(
            source,
            target,
            self.send_sems.at[slot],
            self.recv_sems.at[far_slot],
            (dp, self.place.span if span is None else span),
        )
        copy.start()
        self.sent.append(copy)

    def arrived(self, target, slot):
        remote(
            target, target, self.send_sems.at[slot], self.recv_sems.at[slot], (self.place.dp, self.place.span)
        ).wait_recv()

    def across(self):
        place = self.place
        return place.at(1 - place.outer, place.inner, place.core)

    def beside(self, offset):
        place = self.place
        return place.at(place.outer, place.inner_plus(offset), place.core)

    def product(self, outer, inner):
        return self.pair.product(outer, inner, self.columns)

    def first(self):
        place, count = self.place, self.place.inner_count
        if self.kind == 0:
            for inner in range(count):
                self.send1[0, inner] = self.product(1 - place.outer, inner).astype(BF)
            self.send(self.send1.at[0], self.recv1.at[0], 0, 0, self.across())
            return
        for offset in range(1, count):
            for outer in range(2):
                self.send1[offset - 1, outer] = self.product(
                    outer, place.inner_plus(offset)
                ).astype(BF)
            self.send(
                self.send1.at[offset - 1],
                self.recv1.at[count - offset - 1],
                offset - 1,
                count - offset - 1,
                self.beside(offset),
            )

    def second(self):
        place, count = self.place, self.place.inner_count
        base = count
        if self.kind == 0:
            self.arrived(self.recv1.at[0], 0)
            for offset in range(1, count):
                inner = place.inner_plus(offset)
                total = self.product(place.outer, inner) + self.recv1[0, inner].astype(F32)
                self.send2[offset - 1] = total.astype(BF)
                self.send(
                    self.send2.at[offset - 1],
                    self.recv2.at[count - offset - 1],
                    base + offset - 1,
                    base + count - offset - 1,
                    self.beside(offset),
                )
            return
        total = self.product(1 - place.outer, place.inner)
        for offset in range(1, count):
            self.arrived(self.recv1.at[offset - 1], offset - 1)
            total = total + self.recv1[offset - 1, 1 - place.outer].astype(F32)
        self.send2[0] = total.astype(BF)
        self.send(self.send2.at[0], self.recv2.at[0], base, base, self.across())

    def total(self):
        place, count = self.place, self.place.inner_count
        base = count
        total = self.product(place.outer, place.inner)
        if self.kind == 0:
            total = total + self.recv1[0, place.inner].astype(F32)
            for offset in range(1, count):
                self.arrived(self.recv2.at[offset - 1], base + offset - 1)
                total = total + self.recv2[offset - 1].astype(F32)
            return total
        for offset in range(1, count):
            total = total + self.recv1[offset - 1, place.outer].astype(F32)
        self.arrived(self.recv2.at[0], base)
        return total + self.recv2[0].astype(F32)


    def shape_of_line(self):
        place = self.place
        half = place.span_count // 2
        low = place.span < half
        depth = jnp.where(low, place.span, place.span_count - 1 - place.span)
        inward = jnp.where(low, place.span + 1, place.span - 1)
        outward = jnp.where(low, place.span - 1, place.span + 1)
        outward = jnp.clip(outward, 0, place.span_count - 1)
        return half, depth, inward, outward

    def line_copy(self, source, target, slot, span):
        base = 2 * self.place.inner_count
        return remote(
            source,
            target,
            self.send_sems.at[base + slot],
            self.recv_sems.at[base + slot],
            (self.place.dp, span),
        )

    def send_inward(self):
        half, depth, inward, outward = self.shape_of_line()
        sum_here, from_out, from_mid = self.line

        @pl.when(depth == half - 1)
        def cross():
            self.line_copy(sum_here, from_mid, 1, inward).start()

        @pl.when(depth < half - 1)
        def in_():
            self.line_copy(sum_here, from_out, 0, inward).start()

    def line_start(self):
        half, depth, inward, outward = self.shape_of_line()
        sum_here, from_out, from_mid = self.line
        sum_here[...] = self.total().astype(BF)

        @pl.when(depth == 0)
        def go():
            self.send_inward()

    def line_in(self):
        half, depth, inward, outward = self.shape_of_line()
        sum_here, from_out, from_mid = self.line

        @pl.when(depth > 0)
        def go():
            self.line_copy(from_out, from_out, 0, outward).wait_recv()
            sum_here[...] = (sum_here[...].astype(F32) + from_out[...].astype(F32)).astype(BF)
            self.send_inward()

    def line_mid(self):
        half, depth, inward, outward = self.shape_of_line()
        sum_here, from_out, from_mid = self.line

        @pl.when(depth == half - 1)
        def go():
            self.line_copy(from_mid, from_mid, 1, inward).wait_recv()
            self.result[...] = (
                sum_here[...].astype(F32) + from_mid[...].astype(F32)
            ).astype(BF)

            @pl.when(depth > 0)
            def out():
                self.line_copy(self.result, self.result, 2, outward).start()

    def line_out(self):
        half, depth, inward, outward = self.shape_of_line()

        @pl.when(depth < half - 1)
        def go():
            self.line_copy(self.result, self.result, 2, inward).wait_recv()

            @pl.when(depth > 0)
            def out():
                self.line_copy(self.result, self.result, 2, outward).start()

    def line_finish(self):
        half, depth, inward, outward = self.shape_of_line()
        sum_here, from_out, from_mid = self.line

        @pl.when(depth == half - 1)
        def cross():
            self.line_copy(sum_here, from_mid, 1, inward).wait_send()

        @pl.when(depth < half - 1)
        def in_():
            self.line_copy(sum_here, from_out, 0, inward).wait_send()

        @pl.when(depth > 0)
        def out():
            self.line_copy(self.result, self.result, 2, outward).wait_send()


    def spread_start(self, results):
        place = self.place
        base = 2 * place.inner_count
        self.results = results
        results[place.span, :, self.columns] = self.total().astype(BF)
        for offset in range(1, place.span_count):
            peer = lax.rem(place.span + offset, place.span_count)
            block = results.at[place.span, :, self.columns]
            self.send(
                block, block, base + offset, base + place.span_count - offset, place.dp, peer
            )

    def spread_wait(self):
        place = self.place
        base = 2 * place.inner_count
        for offset in range(1, place.span_count):
            peer = lax.rem(place.span + offset, place.span_count)
            self.arrived(self.results.at[peer, :, self.columns], base + offset)

    def finish(self):
        for copy in self.sent:
            copy.wait_send()


def cut_columns(width):
    if width > 4096:
        quarter = width // 4 // 128 * 128
        return [slice(i * quarter, (i + 1) * quarter if i < 3 else width) for i in range(4)]
    half = width // 2 // 128 * 128
    return [slice(0, half), slice(half, width)]


def piece_scratch(inner_count, rows, columns, kind, on_line):
    width = columns.stop - columns.start
    if kind == 0:
        shapes = [(1, inner_count, rows, width)] * 2 + [(inner_count - 1, rows, width)] * 2
    else:
        shapes = [(inner_count - 1, 2, rows, width)] * 2 + [(1, rows, width)] * 2
    if on_line:
        shapes += [(rows, width)] * 2
    return shapes


def backward_kernel(
    dp_count,
    span_count,
    slot_of,
    order,
    gate_up_left,
    gate_up_right,
    down_left,
    down_right,
    out_left,
    out_right,
    qkv_left,
    attended_grad,
    query,
    key,
    value,
    raw,
    lse,
    counts,
    cosine,
    sine,
    qkv_copy,
    gate_up_result,
    down_result,
    out_result,
    qkv_result,
    blended_result,
    normed_result,
    gate_up_own,
    gate_up_other,
    gate_up_right_other,
    down_own,
    down_other,
    down_right_other,
    out_own,
    out_other,
    out_right_other,
    qkv_own,
    qkv_other,
    mixed_other,
    mixed,
    grad_send,
    grad_all,
    key_sum,
    value_sum,
    blended_all,
    chain,
    pair_send,
    pair_recv,
    piece_send,
    piece_recv,
    grad_send_sem,
    grad_recv_sem,
    blended_send_sem,
    blended_recv_sem,
    chain_send,
    chain_recv,
    *piece_buffers,
):
    place = Place(dp_count, span_count)
    span, last = place.span, span_count - 1
    rows, width = attended_grad.shape
    group = width // span_count
    heads = group // HEAD_DIM

    place.greet_all()
    for index in range(span_count):
        grad_send[index] = attended_grad[:, index * group : (index + 1) * group]
    grad_exchange = Exchange(place, grad_send, grad_all, grad_send_sem, grad_recv_sem)
    grad_exchange.start()
    pairs = [
        Pair(place, *members, pair_send.at[i], pair_recv.at[i])
        for i, members in enumerate(
            (
                (gate_up_left, gate_up_own, gate_up_other, gate_up_right, gate_up_right_other),
                (down_left, down_own, down_other, down_right, down_right_other),
                (out_left, out_own, out_other, out_right, out_right_other),
                (qkv_left, qkv_own, qkv_other, mixed, mixed_other),
            )
        )
    ]
    for pair in pairs[:3]:
        pair.lend_left()
        pair.right_copy.start()
    pairs[3].lend_left()

    free = list(piece_buffers)
    pieces = []
    for pair, result, on_line in zip(
        pairs, (gate_up_result, down_result, out_result, qkv_result), (True, True, True, False)
    ):
        members = []
        for i, columns in enumerate(cut_columns(pair.right.shape[2])):
            number = 6 if on_line else 4
            buffers, free = free[:number], free[number:]
            at = len(pieces) * 4 + i
            members.append(
                Piece(
                    pair,
                    columns,
                    i % 2,
                    buffers,
                    (piece_send.at[at], piece_recv.at[at]),
                    result.at[:, columns] if on_line else None,
                )
            )
        pieces.append(members)
    (gate_up_a, gate_up_b), down, out, qkv = (
        (pieces[0][:2], pieces[0][2:]),
        pieces[1],
        pieces[2],
        pieces[3],
    )

    def each(members, name):
        for member in members:
            getattr(member, name)()

    pairs[0].wait()
    each(gate_up_a, "first")
    pairs[1].wait()
    each(down, "first")

    def clear(index, unused):
        key_sum[index] = jnp.zeros((rows, group), F32)
        value_sum[index] = jnp.zeros((rows, group), F32)
        return unused

    lax.fori_loop(0, span_count, clear, 0)

    def clear_chain(index, unused):
        chain[index] = jnp.zeros(chain.shape[1:], BF)
        return unused

    @pl.when(span == 0)
    def nothing_from_below():
        lax.fori_loop(1, span_count + 1, clear_chain, 0)

    @pl.when(span == last)
    def nothing_from_above():
        lax.fori_loop(0, span_count, clear_chain, 0)

    cuts = counts[...]
    bounds = [cuts[i : i + 1, 0:1] for i in range(3)]
    pairs[2].wait()
    grad_exchange.wait()

    def turned_back(rows_in, position):
        cos_here = jnp.concatenate([cosine[position]] * (2 * heads), axis=1)
        sin_here = jnp.concatenate([-sine[position], sine[position]] * heads, axis=1)
        low = rows_in.astype(BF).astype(F32)
        return (low * cos_here - swap_halves(low) * sin_here).astype(BF)

    def attend_back(position, unused):
        query_here = query[position]
        grad_here = grad_all[slot_of[position]]
        query_parts = [head_part(query_here, head) for head in range(heads)]
        grad_parts = [head_part(grad_here, head) for head in range(heads)]
        agreed = grad_here.astype(F32) * raw[position]
        deltas = [
            jnp.sum(head_part(agreed, head), axis=1, keepdims=True) for head in range(heads)
        ]
        logs = lse[position]
        query_position, start = segment_starts(bounds, rows, position * rows)

        def block(other, query_sum):
            key_here, value_here = key[other], value[other]
            key_position = (
                lax.broadcasted_iota(jnp.int32, (1, rows), 1) + other * rows
            ).astype(F32)
            allowed = (key_position <= query_position) & (key_position >= start)
            key_add, value_add = key_sum[other], value_sum[other]
            for head in range(heads):
                scores = dot_nt(query_parts[head], key_here) * SCALE
                weights = jnp.where(allowed, jnp.exp(scores - logs[:, head : head + 1]), 0.0)
                weights_grad = dot_nt(grad_parts[head], value_here)
                scores_grad = (weights * (weights_grad - deltas[head])).astype(BF)
                query_sum = query_sum + dot_nn(scores_grad, head_part(key_here, head))
                key_add = key_add + dot_tn(scores_grad, query_parts[head])
                value_add = value_add + dot_tn(weights.astype(BF), grad_parts[head])
            key_sum[other] = key_add
            value_sum[other] = value_add
            return query_sum

        query_sum = lax.fori_loop(0, position + 1, block, jnp.zeros((rows, group), F32))
        mixed[position, :, :group] = turned_back(query_sum * SCALE, position)
        return unused

    half = span_count // 2
    lax.fori_loop(0, half, attend_back, 0)
    each(gate_up_a, "second")
    each(gate_up_b, "first")
    lax.fori_loop(half, last, attend_back, 0)
    each(gate_up_a, "line_start")
    lax.fori_loop(last, span_count, attend_back, 0)

    def close(position, unused):
        mixed[position, :, group : 2 * group] = turned_back(key_sum[position] * SCALE, position)
        mixed[position, :, 2 * group :] = (
            BLEND_MIX * value_sum[position].astype(BF).astype(F32)
        ).astype(BF)
        return unused

    lax.fori_loop(0, span_count, close, 0)
    pairs[3].right_copy.start()
    grad_exchange.finish()
    blended_send = grad_send
    for index in range(span_count):
        blended_send[index] = value_sum[order[index]].astype(BF)
    blended_exchange = Exchange(
        place, blended_send, blended_all, blended_send_sem, blended_recv_sem
    )

    def normed_grad(block):
        return dot_nt(mixed[order[block]], qkv_copy[...])

    def pass_on(block, way):
        return remote(
            chain.at[block + 1 - way],
            chain.at[block + 1 - way],
            chain_send.at[way, block],
            chain_recv.at[way, block],
            (place.dp, jnp.minimum(span + 1, last) if way == 0 else jnp.maximum(span - 1, 0)),
        )

    def chain_step(step):
        up = last + span - step
        down = step - (last - span)

        @pl.when((span <= step) & (up > span))
        def going_up():
            block = jnp.clip(up, 0, last)

            @pl.when(span > 0)
            def more():
                pass_on(block, 0).wait_recv()

            chain[block + 1] = (normed_grad(block) + chain[block + 1].astype(F32)).astype(BF)
            pass_on(block, 0).start()

        @pl.when((down >= 0) & (down < span))
        def going_down():
            block = jnp.clip(down, 0, last)

            @pl.when(span < last)
            def more():
                pass_on(block, 1).wait_recv()

            chain[block] = (normed_grad(block) + chain[block].astype(F32)).astype(BF)
            pass_on(block, 1).start()

    def chain_end():
        @pl.when(span > 0)
        def from_below():
            pass_on(span, 0).wait_recv()

        @pl.when(span < last)
        def from_above():
            pass_on(span, 1).wait_recv()

        normed_result[...] = (
            normed_grad(span) + chain[span + 1].astype(F32) + chain[span].astype(F32)
        )

    chain_step(0)
    blended_exchange.start()
    each(gate_up_a, "line_in")
    pairs[3].wait()
    each(qkv, "first")
    each(down, "second")
    each(out, "first")
    for step in range(1, last):
        chain_step(step)
        if step == 1:
            each(gate_up_a, "line_mid")
    each(qkv, "second")
    each(down, "line_start")
    each(gate_up_a, "line_out")
    chain_end()
    blended_exchange.wait()
    blended_result[...] = jnp.concatenate([blended_all[i] for i in range(span_count)], axis=1)
    for member in qkv:
        member.spread_start(qkv_result)
    each(down, "line_in")
    each(gate_up_b, "second")
    each(out, "second")
    each(down, "line_mid")
    each(gate_up_b, "line_start")
    each(down, "line_out")
    each(gate_up_b, "line_in")
    each(out, "line_start")
    each(gate_up_b, "line_mid")
    each(out, "line_in")
    each(gate_up_b, "line_out")
    each(out, "line_mid")
    each(out, "line_out")
    each(qkv, "spread_wait")

    for pair in pairs:
        pair.finish()
    blended_exchange.finish()
    for members in (gate_up_a, gate_up_b, down, out):
        each(members, "line_finish")
        each(members, "finish")
    each(qkv, "finish")
    for step in range(last):
        up = last + span - step
        down_block = step - (last - span)

        @pl.when((span <= step) & (up > span))
        def sent_up():
            pass_on(jnp.clip(up, 0, last), 0).wait_send()

        @pl.when((down_block >= 0) & (down_block < span))
        def sent_down():
            pass_on(jnp.clip(down_block, 0, last), 1).wait_send()


def backward_call(dp_count, span_count, slot_of, order, factors, others):
    (gate_up_left, gate_up_right, down_left, down_right, out_left, out_right, qkv_left) = factors
    rows, width = others[0].shape
    group = width // span_count
    inner_count = dp_count // 4
    dma = pltpu.SemaphoreType.DMA
    by_span = (span_count, rows, group)
    mixed_shape = (span_count, rows, 3 * group)

    def less(left):
        return (left.shape[0],) + left.shape[2:]

    scratch = []
    for left, columns_in, on_line in (
        (gate_up_left, gate_up_right.shape[2], True),
        (down_left, down_right.shape[2], True),
        (out_left, out_right.shape[2], True),
        (qkv_left, 3 * group, False),
    ):
        for i, columns in enumerate(cut_columns(columns_in)):
            scratch += [
                pltpu.VMEM(shape, BF)
                for shape in piece_scratch(inner_count, left.shape[2], columns, i % 2, on_line)
            ]
    slots = 2 * inner_count + max(3, span_count)
    return pl.pallas_call(
        functools.partial(backward_kernel, dp_count, span_count),
        out_shape=(
            jax.ShapeDtypeStruct((gate_up_left.shape[2], gate_up_right.shape[2]), BF),
            jax.ShapeDtypeStruct((down_left.shape[2], down_right.shape[2]), BF),
            jax.ShapeDtypeStruct((out_left.shape[2], out_right.shape[2]), BF),
            jax.ShapeDtypeStruct((span_count, qkv_left.shape[2], 3 * group), BF),
            jax.ShapeDtypeStruct((rows, width), BF),
            jax.ShapeDtypeStruct((rows, width), F32),
        ),
        in_specs=[pl.BlockSpec(memory_space=pltpu.SMEM)] * 2
        + [any_spec(), full_spec()] * 3
        + [any_spec()]
        + [full_spec()] * len(others),
        out_specs=(full_spec(),) * 6,
        scratch_shapes=[
            pltpu.VMEM(less(gate_up_left), BF),
            pltpu.VMEM(less(gate_up_left), BF),
            pltpu.VMEM(gate_up_right.shape, BF),
            pltpu.VMEM(less(down_left), BF),
            pltpu.VMEM(less(down_left), BF),
            pltpu.VMEM(down_right.shape, BF),
            pltpu.VMEM(less(out_left), BF),
            pltpu.VMEM(less(out_left), BF),
            pltpu.VMEM(out_right.shape, BF),
            pltpu.VMEM(less(qkv_left), BF),
            pltpu.VMEM(less(qkv_left), BF),
            pltpu.VMEM(mixed_shape, BF),
            pltpu.VMEM(mixed_shape, BF),
            pltpu.VMEM(by_span, BF),
            pltpu.VMEM(by_span, BF),
            pltpu.VMEM(by_span, F32),
            pltpu.VMEM(by_span, F32),
            pltpu.VMEM(by_span, BF),
            pltpu.VMEM((span_count + 1, rows, width), BF),
            dma((4, 3)),
            dma((4, 3)),
            dma((16, slots)),
            dma((16, slots)),
            dma((span_count,)),
            dma((span_count,)),
            dma((span_count,)),
            dma((span_count,)),
            dma((2, span_count)),
            dma((2, span_count)),
        ]
        + scratch,
        compiler_params=pltpu.CompilerParams(
            collective_id=1, has_side_effects=True, vmem_limit_bytes=61 << 20
        ),
    )(slot_of, order, *factors, *others)


def to_heads(rows, span_count):
    return lax.all_to_all(
        rows.reshape(rows.shape[0], span_count, rows.shape[1] // span_count),
        "seq",
        split_axis=1,
        concat_axis=0,
        tiled=True,
    ).reshape(rows.shape[0] * span_count, rows.shape[1] // span_count)


def to_spans(columns, span_count):
    rows_here = columns.shape[0] // span_count
    got = lax.all_to_all(
        columns.reshape(span_count, rows_here, columns.shape[1]),
        "seq",
        split_axis=0,
        concat_axis=0,
        tiled=True,
    )
    return jnp.transpose(got, (1, 0, 2)).reshape(rows_here, columns.shape[1] * span_count)


def on_device(
    tokens,
    first_values,
    out_grad,
    segments,
    span_order,
    qkv_weight,
    out_weight,
    gate_up_weight,
    down_weight,
    norm_gains,
    first_qkv,
    first_out,
    first_gate_up,
    first_down,
    first_gains,
    second_qkv,
    second_out,
    second_gate_up,
    second_down,
    second_gains,
):
    span_count = lax.axis_size("seq")
    mine = lax.axis_index("seq")
    owned_rows, triple = qkv_weight.shape
    model_width = triple // 3
    group = model_width // span_count
    group_heads = group // HEAD_DIM
    residual = tokens[0].astype(F32)
    rows_here = residual.shape[0]
    length = rows_here * span_count
    hidden_width = gate_up_weight.shape[1] // 2

    dp_count = lax.axis_size("dp")
    gains_owned = norm_gains.astype(BF).astype(F32)
    in_kernels = (
        length * model_width <= 1 << 20
        and dp_count % 4 == 0
        and dp_count >= 8
        and span_count % 2 == 0
        and group % 128 == 0
    )
    if in_kernels:
        slot_of = jnp.sum(
            jnp.where(
                span_order[None, :] == jnp.arange(span_count, dtype=jnp.int32)[:, None],
                jnp.arange(span_count, dtype=jnp.int32)[None, :],
                0,
            ),
            axis=1,
        ).astype(jnp.int32)
        ordered = lax.optimization_barrier(jnp.arange(length, dtype=jnp.int32))
        cosine, sine = rotary(ordered)
        cosine = cosine.reshape(span_count, rows_here, HEAD_DIM // 2)
        sine = sine.reshape(span_count, rows_here, HEAD_DIM // 2)
        qkv_mine = (
            lax.dynamic_slice_in_dim(
                qkv_weight.reshape(owned_rows, 3, model_width), mine * group, group, 2
            )
            .reshape(owned_rows, 3 * group)
            .astype(BF)
        )
        gains_mine = jnp.pad(jnp.transpose(gains_owned), ((0, 6), (0, 0)))
        (
            out_copy, gate_up_copy, down_copy, qkv_copy, normed_left, counts, gains_rows, attended,
            query_pos, key_pos, value_pos, raw_pos, lse_pos,
        ) = forward_call(
            dp_count, span_count, slot_of, span_order, tokens[0], first_values[0], segments,
            gains_mine, qkv_mine, out_weight, gate_up_weight, down_weight, cosine, sine,
        )
        gains_full = jnp.transpose(gains_rows[:2])
        scaled_in, inverse_in = normalize_parts(residual)
    else:
        qkv_owned = qkv_weight.reshape(owned_rows, 3, model_width).astype(BF)
        qkv_mine = lax.dynamic_slice_in_dim(qkv_owned, mine * group, group, 2).reshape(
            owned_rows, 3 * group
        )
        gains_full = lax.all_gather(norm_gains.astype(BF), "dp", axis=0, tiled=True).astype(F32)
        qkv_copy = lax.all_gather(qkv_mine, "dp", axis=0, tiled=True)
        out_copy = lax.all_gather(out_weight.astype(BF), "dp", axis=0, tiled=True)
        gate_up_copy = lax.all_gather(gate_up_weight.astype(BF), "dp", axis=0, tiled=True)
        down_copy = lax.all_gather(down_weight.astype(BF), "dp", axis=0, tiled=True)

        row_index = jnp.arange(length, dtype=jnp.int32)
        owner_table = (row_index // rows_here)[:, None] == jnp.arange(span_count, dtype=jnp.int32)[
            None, :
        ]
        positions = (
            jnp.sum(jnp.where(owner_table, span_order[None, :], 0), axis=1) * rows_here
            + row_index % rows_here
        )
        all_segments = lax.all_gather(segments[0], "seq", axis=0, tiled=True)
        cosine, sine_table = rotary(positions)
        allowed = (all_segments[:, None] == all_segments[None, :]) & (
            positions[None, :] <= positions[:, None]
        )

        scaled_in, inverse_in = normalize_parts(residual)
        normed_in = (scaled_in * gains_full[:, 0]).astype(BF)
        normed_all = lax.all_gather(normed_in, "seq", axis=0, tiled=True)
        first_all = to_heads(first_values[0], span_count)
        mixed = dot_nn(normed_all, qkv_copy)
        queries = rotate(
            mixed[:, :group].reshape(length, group_heads, HEAD_DIM), cosine, sine_table
        ).astype(BF)
        keys = rotate(
            mixed[:, group : 2 * group].reshape(length, group_heads, HEAD_DIM), cosine, sine_table
        ).astype(BF)
        blended = (
            (BLEND_MIX * mixed[:, 2 * group :] + (1.0 - BLEND_MIX) * first_all.astype(F32))
            .astype(BF)
            .reshape(length, group_heads, HEAD_DIM)
        )
        scores = jnp.einsum("qhd,khd->hqk", queries, keys, preferred_element_type=F32) * SCALE
        masked = jnp.where(allowed[None], scores, MASK_FILL)
        highest = jnp.max(masked, axis=-1, keepdims=True)
        raised = jnp.where(allowed[None], jnp.exp(masked - highest), 0.0)
        weights = raised / jnp.sum(raised, axis=-1, keepdims=True)
        weights_low = weights.astype(BF)
        attended_raw = jnp.einsum("hqk,khd->qhd", weights_low, blended, preferred_element_type=F32)
        attended = to_spans(attended_raw.reshape(length, group).astype(BF), span_count)

    hidden_mid = residual + dot_nn(attended, out_copy)
    scaled_mid, inverse_mid = normalize_parts(hidden_mid)
    normed_mid = (scaled_mid * gains_full[:, 1]).astype(BF)
    gate_up = dot_nn(normed_mid, gate_up_copy)
    gate_part = gate_up[:, :hidden_width]
    upward = gate_up[:, hidden_width:]
    sigmoid_gate = jax.nn.sigmoid(gate_part)
    swish_gate = gate_part * sigmoid_gate
    activation = (swish_gate * upward).astype(BF)
    layer_out = (hidden_mid + dot_nn(activation, down_copy)).astype(BF)
    back_rows = out_grad[0]
    activation_grad = dot_nt(back_rows, down_copy)
    gate_up_grad = jnp.concatenate(
        [
            activation_grad * upward * sigmoid_gate * (1.0 + gate_part * (1.0 - sigmoid_gate)),
            activation_grad * swish_gate,
        ],
        axis=1,
    ).astype(BF)
    normed_mid_grad = dot_nt(gate_up_grad, gate_up_copy)
    hidden_mid_grad = back_rows.astype(F32) + norm_backward(
        normed_mid_grad, scaled_mid, inverse_mid, gains_full[:, 1]
    )
    mid_grad_low = hidden_mid_grad.astype(BF)
    if in_kernels:
        def left_factor(rows_in):
            columns = rows_in.shape[1]
            return jnp.transpose(rows_in).reshape(
                dp_count // 2, 2, columns // dp_count, rows_in.shape[0]
            )

        factors = (
            left_factor(normed_mid),
            gate_up_grad[None],
            left_factor(activation),
            back_rows[None],
            left_factor(attended),
            mid_grad_low[None],
            normed_left.reshape(dp_count // 2, 2, owned_rows, length),
        )
        others = (
            dot_nt(mid_grad_low, out_copy).astype(BF),
            query_pos, key_pos, value_pos, raw_pos, lse_pos, counts, cosine, sine, qkv_copy,
        )
        gate_up_total, down_total, out_total, qkv_part, blended_grad, normed_in_grad = backward_call(
            dp_count, span_count, slot_of, span_order, factors, others
        )
        values_grad = (1.0 - BLEND_MIX) * blended_grad.astype(F32)
        tokens_grad = hidden_mid_grad + norm_backward(
            normed_in_grad, scaled_in, inverse_in, gains_full[:, 0]
        )
        qkv_total = (
            jnp.transpose(qkv_part.reshape(span_count, owned_rows, 3, group), (1, 2, 0, 3))
            .reshape(owned_rows, triple)
            .astype(F32)
        )
        out_total, gate_up_total, down_total = (
            out_total.astype(F32),
            gate_up_total.astype(F32),
            down_total.astype(F32),
        )
    else:
        attended_grad = to_heads(dot_nt(mid_grad_low, out_copy).astype(BF), span_count)

        heads_grad = attended_grad.reshape(length, group_heads, HEAD_DIM)
        delta = jnp.transpose(jnp.sum(heads_grad.astype(F32) * attended_raw, axis=-1))
        weights_grad = jnp.einsum("qhd,khd->hqk", heads_grad, blended, preferred_element_type=F32)
        scores_grad = (weights * (weights_grad - delta[..., None])).astype(BF)
        queries_grad = (
            jnp.einsum("hqk,khd->qhd", scores_grad, keys, preferred_element_type=F32) * SCALE
        ).astype(BF).astype(F32)
        keys_grad = (
            jnp.einsum("hqk,qhd->khd", scores_grad, queries, preferred_element_type=F32) * SCALE
        ).astype(BF).astype(F32)
        blended_grad = jnp.einsum(
            "hqk,qhd->khd", weights_low, heads_grad, preferred_element_type=F32
        ).astype(BF).reshape(length, group)
        values_grad = (1.0 - BLEND_MIX) * to_spans(blended_grad, span_count).astype(F32)
        mixed_grad = jnp.concatenate(
            [
                rotate(queries_grad, cosine, -sine_table).reshape(length, group),
                rotate(keys_grad, cosine, -sine_table).reshape(length, group),
                BLEND_MIX * blended_grad.astype(F32),
            ],
            axis=1,
        ).astype(BF)
        normed_in_grad = lax.psum_scatter(
            dot_nt(mixed_grad, qkv_copy).astype(BF), "seq", scatter_dimension=0, tiled=True
        ).astype(F32)
        tokens_grad = hidden_mid_grad + norm_backward(
            normed_in_grad, scaled_in, inverse_in, gains_full[:, 0]
        )

        def to_owner(terms):
            return lax.psum_scatter(terms.astype(BF), "dp", scatter_dimension=0, tiled=True)

        qkv_part = lax.all_gather(to_owner(dot_tn(normed_all, mixed_grad)), "seq", axis=0)
        qkv_total = (
            jnp.transpose(qkv_part.reshape(span_count, owned_rows, 3, group), (1, 2, 0, 3))
            .reshape(owned_rows, triple)
            .astype(F32)
        )
        out_total, gate_up_total, down_total = lax.psum(
            (
                to_owner(dot_tn(attended, mid_grad_low)),
                to_owner(dot_tn(normed_mid, gate_up_grad)),
                to_owner(dot_tn(activation, back_rows)),
            ),
            "seq",
        )
        out_total, gate_up_total, down_total = (
            out_total.astype(F32),
            gate_up_total.astype(F32),
            down_total.astype(F32),
        )

    gains_total = jnp.stack(
        [
            jnp.sum(qkv_total * qkv_weight.astype(BF).astype(F32), axis=1),
            jnp.sum(gate_up_total * gate_up_weight.astype(BF).astype(F32), axis=1),
        ],
        axis=1,
    ) / gains_owned
    masters = (qkv_weight, out_weight, gate_up_weight, down_weight, norm_gains)
    firsts = (first_qkv, first_out, first_gate_up, first_down, first_gains)
    seconds = (second_qkv, second_out, second_gate_up, second_down, second_gains)
    totals = (qkv_total, out_total, gate_up_total, down_total, gains_total)
    rate_list = (MATRIX_RATE, MATRIX_RATE, MATRIX_RATE, MATRIX_RATE, GAIN_RATE)
    decays = (MATRIX_DECAY, MATRIX_DECAY, MATRIX_DECAY, MATRIX_DECAY, 0.0)
    updated = [
        apply_adamw(masters[i], firsts[i], seconds[i], totals[i], rate_list[i], decays[i])
        for i in range(5)
    ]
    return (
        (layer_out[None], tokens_grad[None], values_grad[None])
        + tuple(member[0] for member in updated)
        + tuple(member[1] for member in updated)
        + tuple(member[2] for member in updated)
    )


def solution(mesh):
    rows = P("dp", "seq", None)
    owned = P("dp", None)
    return jax.shard_map(
        on_device,
        mesh=mesh,
        in_specs=(rows, rows, rows, P("dp", "seq"), P()) + (owned,) * 15,
        out_specs=(rows,) * 3 + (owned,) * 15,
        check_vma=False,
    )
```

```python
import functools
import math

import jax
import jax.numpy as jnp
from jax import lax
from jax.experimental import pallas as pl
from jax.experimental.pallas import tpu as pltpu
from jax.sharding import PartitionSpec as P

HEAD_DIM = 64
STEP = 10


NORM_EPS = 1e-06
ADAM_EPS = 1e-08
BLEND_MIX = 0.5
BETA_FIRST = 0.5
BETA_SECOND = 0.5
MATRIX_RATE = 0.06
MATRIX_DECAY = 0.1
GAIN_RATE = 0.5
ROPE_BASE = 10000.0
MASK_FILL = -1e30
SCALE = HEAD_DIM ** (-0.5)

BF = jnp.bfloat16
F32 = jnp.float32


def dot_nn(left, right):
    return lax.dot_general(left, right, (((1,), (0,)), ((), ())), preferred_element_type=F32)


def dot_nt(left, right):
    return lax.dot_general(left, right, (((1,), (1,)), ((), ())), preferred_element_type=F32)


def dot_tn(left, right):
    return lax.dot_general(left, right, (((0,), (0,)), ((), ())), preferred_element_type=F32)


def normalize_parts(matrix):
    inverse = lax.rsqrt(jnp.mean(matrix * matrix, axis=-1, keepdims=True) + NORM_EPS)
    return (matrix * inverse, inverse)


def norm_backward(grad_rows, scaled, inverse, gain_column):
    pushed = grad_rows * gain_column
    return inverse * (pushed - scaled * jnp.mean(pushed * scaled, axis=-1, keepdims=True))


def rotary(positions):
    half_width = HEAD_DIM // 2
    frequency = jnp.exp(
        jnp.arange(half_width, dtype=F32) * (-math.log(ROPE_BASE) / half_width)
    )
    angles = positions.astype(F32)[:, None] * frequency[None, :]
    return (jnp.cos(angles)[:, None, :], jnp.sin(angles)[:, None, :])


def rotate(head_rows, cosine, sine_table):
    half_width = head_rows.shape[-1] // 2
    lower_half = head_rows[..., :half_width]
    upper_half = head_rows[..., half_width:]
    return jnp.concatenate(
        [
            lower_half * cosine - upper_half * sine_table,
            upper_half * cosine + lower_half * sine_table,
        ],
        axis=-1,
    )


def apply_adamw(master, first_state, second_state, gradient, rate, decay):
    next_first = BETA_FIRST * first_state + (1.0 - BETA_FIRST) * gradient
    next_second = BETA_SECOND * second_state + (1.0 - BETA_SECOND) * gradient * gradient
    first_hat = next_first / (1.0 - BETA_FIRST**STEP)
    second_hat = next_second / (1.0 - BETA_SECOND**STEP)
    new_master = master - rate * (first_hat / (jnp.sqrt(second_hat) + ADAM_EPS) + decay * master)
    return (new_master, next_first, next_second)


MESH = pl.DeviceIdType.MESH
VMEM_BYTES = 58 << 20


def full_spec():
    return pl.BlockSpec(memory_space=pltpu.VMEM)


def any_spec():
    return pl.BlockSpec(memory_space=pl.ANY)


class Place:
    def __init__(self, dp_count, span_count):
        self.dp_count = dp_count
        self.span_count = span_count
        self.inner_count = dp_count // 4
        self.dp = lax.axis_index("dp")
        self.span = lax.axis_index("seq")
        self.core = lax.rem(self.dp, 2)
        self.inner = lax.rem(self.dp // 2, self.inner_count)
        self.outer = self.dp // (2 * self.inner_count)

    def at(self, outer, inner, core):
        return (outer * self.inner_count + inner) * 2 + core

    def inner_plus(self, offset):
        return lax.rem(self.inner + offset, self.inner_count)

    def greet_all(self):
        barrier = pltpu.get_barrier_semaphore()
        for offset in range(1, self.dp_count):
            pl.semaphore_signal(
                barrier,
                inc=1,
                device_id=(lax.rem(self.dp + offset, self.dp_count), self.span),
                device_id_type=MESH,
            )
        for offset in range(1, self.span_count):
            pl.semaphore_signal(
                barrier,
                inc=1,
                device_id=(self.dp, lax.rem(self.span + offset, self.span_count)),
                device_id_type=MESH,
            )
        pl.semaphore_wait(barrier, self.dp_count + self.span_count - 2)


def remote(source, target, send_sem, recv_sem, device):
    return pltpu.make_async_remote_copy(
        src_ref=source,
        dst_ref=target,
        send_sem=send_sem,
        recv_sem=recv_sem,
        device_id=device,
        device_id_type=MESH,
    )


def half_rows(rows):
    return rows // 2 // 16 * 16


class Gather:
    def __init__(self, place, own, whole, send_sems, recv_sems):
        self.place = place
        self.own = own
        self.whole = whole
        self.rows = own.shape[0]
        self.send_sems = send_sems
        self.recv_sems = recv_sems
        self.sent = []
        count = place.inner_count
        self.near, self.lower, self.upper, self.pair = 0, count, 2 * count, 3 * count

    @staticmethod
    def slots(inner_count):
        return 6 * inner_count + 1

    def block(self, index, part=None):
        first = half_rows(self.rows)
        start, size = {None: (0, self.rows), 0: (0, first), 1: (first, self.rows - first)}[part]
        return self.whole.at[pl.ds(pl.multiple_of(index * self.rows + start, 16), size), :]

    def send(self, source, target, slot, far_slot, device):
        copy = remote(
            source, target, self.send_sems.at[slot], self.recv_sems.at[far_slot], (device, self.place.span)
        )
        copy.start()
        self.sent.append(copy)

    def arrived(self, block, slot):
        remote(
            block, block, self.send_sems.at[slot], self.recv_sems.at[slot], (self.place.dp, self.place.span)
        ).wait_recv()

    def sibling(self, block, slot):
        place = self.place
        self.send(block, block, slot, slot, place.at(place.outer, place.inner, 1 - place.core))

    def begin(self):
        place, count = self.place, self.place.inner_count
        mine = self.block(place.dp)
        self.send(self.own, mine, 0, 0, place.at(1 - place.outer, place.inner, place.core))
        for offset in range(1, count):
            self.send(
                self.own,
                mine,
                offset,
                count - offset,
                place.at(place.outer, place.inner_plus(offset), place.core),
            )
        copy = remote(
            self.own,
            mine,
            self.send_sems.at[self.pair],
            self.recv_sems.at[self.pair],
            (place.at(place.outer, place.inner, 1 - place.core), place.span),
        )
        copy.start()
        self.sent.append(copy)

    def forward(self):
        place, count = self.place, self.place.inner_count
        across = place.at(1 - place.outer, place.inner, place.core)
        self.arrived(self.block(across), 0)
        for offset in range(1, count):
            self.send(
                self.block(across, 0),
                self.block(across, 0),
                self.lower + offset,
                self.lower + count - offset,
                place.at(place.outer, place.inner_plus(offset), place.core),
            )
        for offset in range(1, count):
            beside = place.at(place.outer, place.inner_plus(offset), place.core)
            self.arrived(self.block(beside), offset)
            self.send(
                self.block(beside, 1),
                self.block(beside, 1),
                self.upper + offset,
                self.upper + offset,
                across,
            )
        self.sibling(self.block(across), self.pair + count)
        for offset in range(1, count):
            beside = place.at(place.outer, place.inner_plus(offset), place.core)
            self.sibling(self.block(beside), self.pair + offset)

    def share(self):
        place, count = self.place, self.place.inner_count
        for offset in range(1, count):
            far = place.at(1 - place.outer, place.inner_plus(offset), place.core)
            self.arrived(self.block(far, 0), self.lower + offset)
            self.sibling(self.block(far, 0), self.pair + count + offset)
            self.arrived(self.block(far, 1), self.upper + offset)
            self.sibling(self.block(far, 1), self.pair + 2 * count + offset)

    def end(self):
        place, count = self.place, self.place.inner_count
        other = 1 - place.core
        self.arrived(self.block(place.at(place.outer, place.inner, other)), self.pair)
        self.arrived(self.block(place.at(1 - place.outer, place.inner, other)), self.pair + count)
        for offset in range(1, count):
            inner = place.inner_plus(offset)
            self.arrived(self.block(place.at(place.outer, inner, other)), self.pair + offset)
            far = place.at(1 - place.outer, inner, other)
            self.arrived(self.block(far, 0), self.pair + count + offset)
            self.arrived(self.block(far, 1), self.pair + 2 * count + offset)
        for copy in self.sent:
            copy.wait_send()


class Exchange:
    def __init__(self, place, sources, targets, send_sems, recv_sems):
        self.place = place
        self.sources = sources
        self.targets = targets
        self.send_sems = send_sems
        self.recv_sems = recv_sems

    def copy(self, offset):
        place = self.place
        count = place.span_count
        peer = lax.rem(place.span + offset, count)
        return remote(
            self.sources.at[peer],
            self.targets.at[place.span],
            self.send_sems.at[offset],
            self.recv_sems.at[count - offset],
            (place.dp, peer),
        )

    def start(self):
        for offset in range(1, self.place.span_count):
            self.copy(offset).start()
        self.targets[self.place.span] = self.sources[self.place.span]

    def wait(self):
        place = self.place
        count = place.span_count
        for offset in range(1, count):
            peer = lax.rem(place.span + offset, count)
            remote(
                self.sources.at[peer],
                self.targets.at[peer],
                self.send_sems.at[offset],
                self.recv_sems.at[offset],
                (place.dp, peer),
            ).wait_recv()

    def finish(self):
        for offset in range(1, self.place.span_count):
            self.copy(offset).wait_send()


def cast_rows(source, target):
    rows = source.shape[0]

    def step(index, unused):
        at = pl.ds(pl.multiple_of(index * 16, 16), 16)
        target[at, :] = source[at, :].astype(BF)
        return unused

    lax.fori_loop(0, rows // 16, step, 0)


def swap_halves(rows):
    width = rows.shape[1]
    half = HEAD_DIM // 2
    if width % 128:
        pieces = []
        for start in range(0, width, HEAD_DIM):
            pieces += [rows[:, start + half : start + HEAD_DIM], rows[:, start : start + half]]
        return jnp.concatenate(pieces, axis=1)
    lane = lax.broadcasted_iota(jnp.int32, rows.shape, 1)
    return jnp.where(
        lane % HEAD_DIM < half, pltpu.roll(rows, width - half, 1), pltpu.roll(rows, half, 1)
    )


def segment_starts(bounds, rows, first):
    position = lax.broadcasted_iota(jnp.int32, (rows, 1), 0) + first
    position = position.astype(F32)
    start = jnp.zeros((rows, 1), F32)
    for cut in bounds:
        start = jnp.where(position >= cut, cut, start)
    return position, start


def head_part(matrix, head):
    if matrix.shape[1] == HEAD_DIM:
        return matrix
    lane = lax.broadcasted_iota(jnp.int32, (1, matrix.shape[1]), 1)
    return jnp.where(lane // HEAD_DIM == head, matrix, jnp.zeros_like(matrix))


def forward_kernel(
    dp_count,
    span_count,
    slot_of,
    order,
    tokens,
    first_values,
    segments,
    gains_mine,
    qkv_mine,
    out_mine,
    gate_up_mine,
    down_mine,
    cosine,
    sine,
    out_whole,
    gate_up_whole,
    down_whole,
    qkv_out,
    normed_out,
    counts_out,
    gains_out,
    attended_out,
    query_out,
    key_out,
    value_out,
    raw_out,
    lse_out,
    out_own,
    gate_up_own,
    down_own,
    qkv_whole,
    gains_all,
    counts_send,
    counts_all,
    first_send,
    first_all,
    normed_all,
    scores_kept,
    attended_send,
    attended_all,
    gather_send,
    gather_recv,
    gains_send_sem,
    gains_recv_sem,
    counts_send_sem,
    counts_recv_sem,
    first_send_sem,
    first_recv_sem,
    ring_send,
    ring_recv,
    attended_send_sem,
    attended_recv_sem,
    local_sem,
):
    place = Place(dp_count, span_count)
    rows, width = tokens.shape
    group = width // span_count
    heads = group // HEAD_DIM
    last = span_count - 1
    span = place.span

    place.greet_all()
    gains_all[place.dp] = gains_mine[...]
    gains_copies = []
    for offset in range(1, dp_count):
        peer = lax.rem(place.dp + offset, dp_count)
        copy = remote(
            gains_mine,
            gains_all.at[place.dp],
            gains_send_sem.at[offset],
            gains_recv_sem.at[dp_count - offset],
            (peer, span),
        )
        copy.start()
        gains_copies.append(copy)
    gathers = [
        Gather(place, own, whole, gather_send.at[i], gather_recv.at[i])
        for i, (own, whole) in enumerate(
            (
                (qkv_mine, qkv_whole),
                (out_own, out_whole),
                (gate_up_own, gate_up_whole),
                (down_own, down_whole),
            )
        )
    ]
    qkv_gather, out_gather, gate_up_gather, down_gather = gathers
    qkv_gather.begin()
    qkv_whole[pl.ds(pl.multiple_of(place.dp * qkv_mine.shape[0], 16), qkv_mine.shape[0]), :] = (
        qkv_mine[...]
    )
    for index in range(span_count):
        first_send[index] = first_values[:, index * group : (index + 1) * group]
    first_exchange = Exchange(place, first_send, first_all, first_send_sem, first_recv_sem)
    first_exchange.start()
    ids = segments[...]
    row = lax.broadcasted_iota(jnp.int32, (8, 128), 0)
    counts = jnp.zeros((8, 128), F32)
    for cut in range(3):
        below = jnp.sum(jnp.where(ids <= cut, 1.0, 0.0), axis=1, keepdims=True)
        counts = jnp.where(row == cut, below, counts)
    for index in range(span_count):
        counts_send[index] = counts
    counts_exchange = Exchange(place, counts_send, counts_all, counts_send_sem, counts_recv_sem)
    counts_exchange.start()

    residual = tokens[...].astype(F32)
    scaled = residual * lax.rsqrt(jnp.mean(residual * residual, axis=1, keepdims=True) + NORM_EPS)
    for offset in range(1, dp_count):
        peer = lax.rem(place.dp + offset, dp_count)
        remote(
            gains_mine,
            gains_all.at[peer],
            gains_send_sem.at[offset],
            gains_recv_sem.at[offset],
            (peer, span),
        ).wait_recv()
    gains_row = jnp.concatenate([gains_all[i] for i in range(dp_count)], axis=1)
    gains_out[...] = gains_row
    normed_all[span] = (scaled * gains_row[0:1, :]).astype(BF)

    def pass_on(block, step, way):
        return remote(
            normed_all.at[block],
            normed_all.at[block],
            ring_send.at[way, step],
            ring_recv.at[way, step],
            (place.dp, jnp.where(way == 0, jnp.minimum(span + 1, last), jnp.maximum(span - 1, 0))),
        )

    @pl.when(span < last)
    def up():
        pass_on(span, 0, 0).start()

    @pl.when(span > 0)
    def down():
        pass_on(span, 0, 1).start()

    cast_rows(out_mine, out_own)
    out_gather.begin()
    cast_rows(gate_up_mine, gate_up_own)
    qkv_gather.forward()
    gate_up_gather.begin()
    cast_rows(down_mine, down_own)
    down_gather.begin()
    own_copies = []
    for i, member in enumerate(gathers[1:]):
        copy = pltpu.make_async_copy(member.own, member.block(place.dp), local_sem.at[i])
        copy.start()
        own_copies.append(copy)
    qkv_gather.share()
    out_gather.forward()

    for step in range(1, span_count):

        @pl.when(span - step >= 0)
        def from_below():
            block = jnp.maximum(span - step, 0)
            pass_on(block, step - 1, 0).wait_recv()

            @pl.when(span < last)
            def on():
                pass_on(block, step, 0).start()

        @pl.when(span + step <= last)
        def from_above():
            block = jnp.minimum(span + step, last)
            pass_on(block, step - 1, 1).wait_recv()

            @pl.when(span > 0)
            def on():
                pass_on(block, step, 1).start()

    qkv_gather.end()
    qkv_copy = pltpu.make_async_copy(qkv_whole, qkv_out, local_sem.at[4])
    qkv_copy.start()
    first_exchange.wait()
    counts_exchange.wait()
    cuts = counts_all[0]
    for index in range(1, span_count):
        cuts = cuts + counts_all[index]
    counts_out[...] = cuts
    bounds = [cuts[i : i + 1, 0:1] for i in range(3)]

    def project(position, unused):
        slot = slot_of[position]
        normed_here = normed_all[slot]
        normed_out[:, pl.ds(pl.multiple_of(position * rows, rows), rows)] = jnp.transpose(normed_here)
        mixed = dot_nn(normed_here, qkv_whole[...])
        cos_here = jnp.concatenate([cosine[position]] * (2 * heads), axis=1)
        sin_here = jnp.concatenate([-sine[position], sine[position]] * heads, axis=1)
        query = mixed[:, :group]
        key = mixed[:, group : 2 * group]
        query_out[position] = (query * cos_here + swap_halves(query) * sin_here).astype(BF)
        key_out[position] = (key * cos_here + swap_halves(key) * sin_here).astype(BF)
        value_out[position] = (
            BLEND_MIX * mixed[:, 2 * group :]
            + (1.0 - BLEND_MIX) * first_all[slot].astype(F32)
        ).astype(BF)
        return unused

    lax.fori_loop(0, span_count, project, 0)
    out_gather.share()
    gate_up_gather.forward()

    def attend(position, unused):
        query = query_out[position]
        parts = [head_part(query, head) for head in range(heads)]
        query_position, start = segment_starts(bounds, rows, position * rows)

        def score(other, highest):
            key = key_out[other]
            key_position = (
                lax.broadcasted_iota(jnp.int32, (1, rows), 1) + other * rows
            ).astype(F32)
            allowed = (key_position <= query_position) & (key_position >= start)
            found = []
            for head in range(heads):
                masked = jnp.where(allowed, dot_nt(parts[head], key) * SCALE, MASK_FILL)
                scores_kept[head, other] = masked
                found.append(jnp.maximum(highest[head], jnp.max(masked, axis=1, keepdims=True)))
            return tuple(found)

        highest = lax.fori_loop(
            0, position + 1, score, (jnp.full((rows, 1), MASK_FILL, F32),) * heads
        )

        def raise_scores(other, total):
            added = []
            for head in range(heads):
                raised = jnp.exp(scores_kept[head, other] - highest[head])
                scores_kept[head, other] = raised
                added.append(total[head] + jnp.sum(raised, axis=1, keepdims=True))
            return tuple(added)

        total = lax.fori_loop(
            0, position + 1, raise_scores, (jnp.zeros((rows, 1), F32),) * heads
        )
        inverse = [1.0 / member for member in total]

        def gather_values(other, attended):
            value = value_out[other]
            for head in range(heads):
                weights = (scores_kept[head, other] * inverse[head]).astype(BF)
                attended = attended + dot_nn(weights, head_part(value, head))
            return attended

        raw_out[position] = lax.fori_loop(
            0, position + 1, gather_values, jnp.zeros((rows, group), F32)
        )
        lane = lax.broadcasted_iota(jnp.int32, (rows, 128), 1)
        kept = jnp.zeros((rows, 128), F32)
        for head in range(heads):
            kept = jnp.where(lane == head, highest[head] + jnp.log(total[head]), kept)
        lse_out[position] = kept
        return unused

    lax.fori_loop(0, span_count // 2, attend, 0)
    down_gather.forward()
    lax.fori_loop(span_count // 2, span_count, attend, 0)

    for index in range(span_count):
        attended_send[index] = raw_out[order[index]].astype(BF)
    attended_exchange = Exchange(
        place, attended_send, attended_all, attended_send_sem, attended_recv_sem
    )
    attended_exchange.start()
    gate_up_gather.share()
    attended_exchange.wait()
    attended_out[...] = jnp.concatenate([attended_all[i] for i in range(span_count)], axis=1)
    out_gather.end()
    down_gather.share()
    gate_up_gather.end()
    down_gather.end()

    for copy in gains_copies:
        copy.wait_send()
    for exchange in (first_exchange, counts_exchange, attended_exchange):
        exchange.finish()
    for step in range(span_count):

        @pl.when((span - step >= 0) & (span < last))
        def sent_up():
            pass_on(jnp.maximum(span - step, 0), step, 0).wait_send()

        @pl.when((span + step <= last) & (span > 0))
        def sent_down():
            pass_on(jnp.minimum(span + step, last), step, 1).wait_send()

    for copy in own_copies:
        copy.wait()
    qkv_copy.wait()


def forward_call(
    dp_count, span_count, slot_of, order, tokens, first_values, segments, gains_mine, qkv_mine,
    out_mine, gate_up_mine, down_mine, cosine, sine,
):
    rows, width = tokens.shape
    group = width // span_count
    heads = group // HEAD_DIM
    owned = qkv_mine.shape[0]
    doubled = gate_up_mine.shape[1]
    slots = Gather.slots(dp_count // 4)
    dma = pltpu.SemaphoreType.DMA
    by_span = (span_count, rows, group)
    return pl.pallas_call(
        functools.partial(forward_kernel, dp_count, span_count),
        out_shape=(
            jax.ShapeDtypeStruct((width, width), BF),
            jax.ShapeDtypeStruct((width, doubled), BF),
            jax.ShapeDtypeStruct((doubled // 2, width), BF),
            jax.ShapeDtypeStruct((width, 3 * group), BF),
            jax.ShapeDtypeStruct((width, span_count * rows), BF),
            jax.ShapeDtypeStruct((8, 128), F32),
            jax.ShapeDtypeStruct((8, width), F32),
            jax.ShapeDtypeStruct((rows, width), BF),
            jax.ShapeDtypeStruct(by_span, BF),
            jax.ShapeDtypeStruct(by_span, BF),
            jax.ShapeDtypeStruct(by_span, BF),
            jax.ShapeDtypeStruct(by_span, F32),
            jax.ShapeDtypeStruct((span_count, rows, 128), F32),
        ),
        in_specs=[pl.BlockSpec(memory_space=pltpu.SMEM)] * 2 + [full_spec()] * 10,
        out_specs=(any_spec(),) * 4 + (full_spec(),) * 9,
        scratch_shapes=[
            pltpu.VMEM((owned, width), BF),
            pltpu.VMEM((owned, doubled), BF),
            pltpu.VMEM((down_mine.shape[0], width), BF),
            pltpu.VMEM((width, 3 * group), BF),
            pltpu.VMEM((dp_count, 8, owned), F32),
            pltpu.VMEM((span_count, 8, 128), F32),
            pltpu.VMEM((span_count, 8, 128), F32),
            pltpu.VMEM(by_span, BF),
            pltpu.VMEM(by_span, BF),
            pltpu.VMEM((span_count, rows, width), BF),
            pltpu.VMEM((heads, span_count, rows, rows), F32),
            pltpu.VMEM(by_span, BF),
            pltpu.VMEM(by_span, BF),
            dma((4, slots)),
            dma((4, slots)),
            dma((dp_count,)),
            dma((dp_count,)),
            dma((span_count,)),
            dma((span_count,)),
            dma((span_count,)),
            dma((span_count,)),
            dma((2, span_count)),
            dma((2, span_count)),
            dma((span_count,)),
            dma((span_count,)),
            dma((5,)),
        ],
        compiler_params=pltpu.CompilerParams(
            collective_id=0, has_side_effects=True, vmem_limit_bytes=VMEM_BYTES
        ),
    )(
        slot_of, order, tokens, first_values, segments, gains_mine, qkv_mine, out_mine,
        gate_up_mine, down_mine, cosine, sine,
    )


class Pair:
    def __init__(
        self, place, left_whole, left, left_other, right, right_other, send_sems, recv_sems
    ):
        self.place = place
        self.left = left
        self.left_other = left_other
        self.right = right
        self.right_other = right_other
        other = (place.at(place.outer, place.inner, 1 - place.core), place.span)
        self.left_copy = remote(
            left_whole.at[:, 1 - place.core], left_other, send_sems.at[0], recv_sems.at[0], other
        )
        self.own_copy = pltpu.make_async_copy(
            left_whole.at[:, place.core], left, send_sems.at[2]
        )
        self.right_copy = remote(right, right_other, send_sems.at[1], recv_sems.at[1], other)

    def lend_left(self):
        self.own_copy.start()
        self.left_copy.start()

    def wait(self):
        self.own_copy.wait()
        self.left_copy.wait_recv()
        self.right_copy.wait_recv()

    def finish(self):
        self.left_copy.wait_send()
        self.right_copy.wait_send()

    def product(self, outer, inner, columns):
        chip = outer * self.place.inner_count + inner
        depth = self.right.shape[1]
        found = None
        for block in range(self.right.shape[0]):
            at = slice(block * depth, (block + 1) * depth)
            mine = dot_nn(self.left[chip, :, at], self.right[block, :, columns])
            theirs = dot_nn(self.left_other[chip, :, at], self.right_other[block, :, columns])
            found = mine + theirs if found is None else found + mine + theirs
        return found


class Piece:
    def __init__(self, pair, columns, kind, buffers, sems, result):
        self.pair = pair
        self.place = pair.place
        self.columns = columns
        self.kind = kind
        self.send1, self.recv1, self.send2, self.recv2 = buffers[:4]
        mine = self.recv1.at[0, pair.place.inner if kind == 0 else pair.place.outer]
        self.line = [mine] + list(buffers[4:])
        self.send_sems, self.recv_sems = sems
        self.result = result
        self.sent = []

    def send(self, source, target, slot, far_slot, dp, span=None):
        copy = remote(
            source,
            target,
            self.send_sems.at[slot],
            self.recv_sems.at[far_slot],
            (dp, self.place.span if span is None else span),
        )
        copy.start()
        self.sent.append(copy)

    def arrived(self, target, slot):
        remote(
            target, target, self.send_sems.at[slot], self.recv_sems.at[slot], (self.place.dp, self.place.span)
        ).wait_recv()

    def across(self):
        place = self.place
        return place.at(1 - place.outer, place.inner, place.core)

    def beside(self, offset):
        place = self.place
        return place.at(place.outer, place.inner_plus(offset), place.core)

    def product(self, outer, inner):
        return self.pair.product(outer, inner, self.columns)

    def first(self):
        place, count = self.place, self.place.inner_count
        if self.kind == 0:
            for inner in range(count):
                self.send1[0, inner] = self.product(1 - place.outer, inner).astype(BF)
            self.send(self.send1.at[0], self.recv1.at[0], 0, 0, self.across())
            return
        for offset in range(1, count):
            for outer in range(2):
                self.send1[offset - 1, outer] = self.product(
                    outer, place.inner_plus(offset)
                ).astype(BF)
            self.send(
                self.send1.at[offset - 1],
                self.recv1.at[count - offset - 1],
                offset - 1,
                count - offset - 1,
                self.beside(offset),
            )

    def second(self):
        place, count = self.place, self.place.inner_count
        base = count
        if self.kind == 0:
            self.arrived(self.recv1.at[0], 0)
            for offset in range(1, count):
                inner = place.inner_plus(offset)
                total = self.product(place.outer, inner) + self.recv1[0, inner].astype(F32)
                self.send2[offset - 1] = total.astype(BF)
                self.send(
                    self.send2.at[offset - 1],
                    self.recv2.at[count - offset - 1],
                    base + offset - 1,
                    base + count - offset - 1,
                    self.beside(offset),
                )
            return
        total = self.product(1 - place.outer, place.inner)
        for offset in range(1, count):
            self.arrived(self.recv1.at[offset - 1], offset - 1)
            total = total + self.recv1[offset - 1, 1 - place.outer].astype(F32)
        self.send2[0] = total.astype(BF)
        self.send(self.send2.at[0], self.recv2.at[0], base, base, self.across())

    def total(self):
        place, count = self.place, self.place.inner_count
        base = count
        total = self.product(place.outer, place.inner)
        if self.kind == 0:
            total = total + self.recv1[0, place.inner].astype(F32)
            for offset in range(1, count):
                self.arrived(self.recv2.at[offset - 1], base + offset - 1)
                total = total + self.recv2[offset - 1].astype(F32)
            return total
        for offset in range(1, count):
            total = total + self.recv1[offset - 1, place.outer].astype(F32)
        self.arrived(self.recv2.at[0], base)
        return total + self.recv2[0].astype(F32)


    def shape_of_line(self):
        place = self.place
        half = place.span_count // 2
        low = place.span < half
        depth = jnp.where(low, place.span, place.span_count - 1 - place.span)
        inward = jnp.where(low, place.span + 1, place.span - 1)
        outward = jnp.where(low, place.span - 1, place.span + 1)
        outward = jnp.clip(outward, 0, place.span_count - 1)
        return half, depth, inward, outward

    def line_copy(self, source, target, slot, span):
        base = 2 * self.place.inner_count
        return remote(
            source,
            target,
            self.send_sems.at[base + slot],
            self.recv_sems.at[base + slot],
            (self.place.dp, span),
        )

    def send_inward(self):
        half, depth, inward, outward = self.shape_of_line()
        sum_here, from_out, from_mid = self.line

        @pl.when(depth == half - 1)
        def cross():
            self.line_copy(sum_here, from_mid, 1, inward).start()

        @pl.when(depth < half - 1)
        def in_():
            self.line_copy(sum_here, from_out, 0, inward).start()

    def line_start(self):
        half, depth, inward, outward = self.shape_of_line()
        sum_here, from_out, from_mid = self.line
        sum_here[...] = self.total().astype(BF)

        @pl.when(depth == 0)
        def go():
            self.send_inward()

    def line_in(self):
        half, depth, inward, outward = self.shape_of_line()
        sum_here, from_out, from_mid = self.line

        @pl.when(depth > 0)
        def go():
            self.line_copy(from_out, from_out, 0, outward).wait_recv()
            sum_here[...] = (sum_here[...].astype(F32) + from_out[...].astype(F32)).astype(BF)
            self.send_inward()

    def line_mid(self):
        half, depth, inward, outward = self.shape_of_line()
        sum_here, from_out, from_mid = self.line

        @pl.when(depth == half - 1)
        def go():
            self.line_copy(from_mid, from_mid, 1, inward).wait_recv()
            self.result[...] = (
                sum_here[...].astype(F32) + from_mid[...].astype(F32)
            ).astype(BF)

            @pl.when(depth > 0)
            def out():
                self.line_copy(self.result, self.result, 2, outward).start()

    def line_out(self):
        half, depth, inward, outward = self.shape_of_line()

        @pl.when(depth < half - 1)
        def go():
            self.line_copy(self.result, self.result, 2, inward).wait_recv()

            @pl.when(depth > 0)
            def out():
                self.line_copy(self.result, self.result, 2, outward).start()

    def line_finish(self):
        half, depth, inward, outward = self.shape_of_line()
        sum_here, from_out, from_mid = self.line

        @pl.when(depth == half - 1)
        def cross():
            self.line_copy(sum_here, from_mid, 1, inward).wait_send()

        @pl.when(depth < half - 1)
        def in_():
            self.line_copy(sum_here, from_out, 0, inward).wait_send()

        @pl.when(depth > 0)
        def out():
            self.line_copy(self.result, self.result, 2, outward).wait_send()


    def spread_start(self, results):
        place = self.place
        base = 2 * place.inner_count
        self.results = results
        results[place.span, :, self.columns] = self.total().astype(BF)
        for offset in range(1, place.span_count):
            peer = lax.rem(place.span + offset, place.span_count)
            block = results.at[place.span, :, self.columns]
            self.send(
                block, block, base + offset, base + place.span_count - offset, place.dp, peer
            )

    def spread_wait(self):
        place = self.place
        base = 2 * place.inner_count
        for offset in range(1, place.span_count):
            peer = lax.rem(place.span + offset, place.span_count)
            self.arrived(self.results.at[peer, :, self.columns], base + offset)

    def finish(self):
        for copy in self.sent:
            copy.wait_send()


def cut_columns(width):
    if width > 4096:
        quarter = width // 4 // 128 * 128
        return [slice(i * quarter, (i + 1) * quarter if i < 3 else width) for i in range(4)]
    half = width // 2 // 128 * 128
    return [slice(0, half), slice(half, width)]


def piece_scratch(inner_count, rows, columns, kind, on_line):
    width = columns.stop - columns.start
    if kind == 0:
        shapes = [(1, inner_count, rows, width)] * 2 + [(inner_count - 1, rows, width)] * 2
    else:
        shapes = [(inner_count - 1, 2, rows, width)] * 2 + [(1, rows, width)] * 2
    if on_line:
        shapes += [(rows, width)] * 2
    return shapes


def backward_kernel(
    dp_count,
    span_count,
    slot_of,
    order,
    gate_up_left,
    gate_up_right,
    down_left,
    down_right,
    out_left,
    out_right,
    qkv_left,
    attended_grad,
    query,
    key,
    value,
    raw,
    lse,
    counts,
    cosine,
    sine,
    qkv_copy,
    gate_up_result,
    down_result,
    out_result,
    qkv_result,
    blended_result,
    normed_result,
    gate_up_own,
    gate_up_other,
    gate_up_right_other,
    down_own,
    down_other,
    down_right_other,
    out_own,
    out_other,
    out_right_other,
    qkv_own,
    qkv_other,
    mixed_other,
    mixed,
    grad_send,
    grad_all,
    key_sum,
    value_sum,
    blended_all,
    chain,
    pair_send,
    pair_recv,
    piece_send,
    piece_recv,
    grad_send_sem,
    grad_recv_sem,
    blended_send_sem,
    blended_recv_sem,
    chain_send,
    chain_recv,
    *piece_buffers,
):
    place = Place(dp_count, span_count)
    span, last = place.span, span_count - 1
    rows, width = attended_grad.shape
    group = width // span_count
    heads = group // HEAD_DIM

    place.greet_all()
    for index in range(span_count):
        grad_send[index] = attended_grad[:, index * group : (index + 1) * group]
    grad_exchange = Exchange(place, grad_send, grad_all, grad_send_sem, grad_recv_sem)
    grad_exchange.start()
    pairs = [
        Pair(place, *members, pair_send.at[i], pair_recv.at[i])
        for i, members in enumerate(
            (
                (gate_up_left, gate_up_own, gate_up_other, gate_up_right, gate_up_right_other),
                (down_left, down_own, down_other, down_right, down_right_other),
                (out_left, out_own, out_other, out_right, out_right_other),
                (qkv_left, qkv_own, qkv_other, mixed, mixed_other),
            )
        )
    ]
    for pair in pairs[:3]:
        pair.lend_left()
        pair.right_copy.start()
    pairs[3].lend_left()

    free = list(piece_buffers)
    pieces = []
    for pair, result, on_line in zip(
        pairs, (gate_up_result, down_result, out_result, qkv_result), (True, True, True, False)
    ):
        members = []
        for i, columns in enumerate(cut_columns(pair.right.shape[2])):
            number = 6 if on_line else 4
            buffers, free = free[:number], free[number:]
            at = len(pieces) * 4 + i
            members.append(
                Piece(
                    pair,
                    columns,
                    i % 2,
                    buffers,
                    (piece_send.at[at], piece_recv.at[at]),
                    result.at[:, columns] if on_line else None,
                )
            )
        pieces.append(members)
    (gate_up_a, gate_up_b), down, out, qkv = (
        (pieces[0][:2], pieces[0][2:]),
        pieces[1],
        pieces[2],
        pieces[3],
    )

    def each(members, name):
        for member in members:
            getattr(member, name)()

    pairs[0].wait()
    each(gate_up_a, "first")
    pairs[1].wait()
    each(down, "first")

    def clear(index, unused):
        key_sum[index] = jnp.zeros((rows, group), F32)
        value_sum[index] = jnp.zeros((rows, group), F32)
        return unused

    lax.fori_loop(0, span_count, clear, 0)

    def clear_chain(index, unused):
        chain[index] = jnp.zeros(chain.shape[1:], BF)
        return unused

    @pl.when(span == 0)
    def nothing_from_below():
        lax.fori_loop(1, span_count + 1, clear_chain, 0)

    @pl.when(span == last)
    def nothing_from_above():
        lax.fori_loop(0, span_count, clear_chain, 0)

    cuts = counts[...]
    bounds = [cuts[i : i + 1, 0:1] for i in range(3)]
    pairs[2].wait()
    grad_exchange.wait()

    def turned_back(rows_in, position):
        cos_here = jnp.concatenate([cosine[position]] * (2 * heads), axis=1)
        sin_here = jnp.concatenate([-sine[position], sine[position]] * heads, axis=1)
        low = rows_in.astype(BF).astype(F32)
        return (low * cos_here - swap_halves(low) * sin_here).astype(BF)

    def attend_back(position, unused):
        query_here = query[position]
        grad_here = grad_all[slot_of[position]]
        query_parts = [head_part(query_here, head) for head in range(heads)]
        grad_parts = [head_part(grad_here, head) for head in range(heads)]
        agreed = grad_here.astype(F32) * raw[position]
        deltas = [
            jnp.sum(head_part(agreed, head), axis=1, keepdims=True) for head in range(heads)
        ]
        logs = lse[position]
        query_position, start = segment_starts(bounds, rows, position * rows)

        def block(other, query_sum):
            key_here, value_here = key[other], value[other]
            key_position = (
                lax.broadcasted_iota(jnp.int32, (1, rows), 1) + other * rows
            ).astype(F32)
            allowed = (key_position <= query_position) & (key_position >= start)
            key_add, value_add = key_sum[other], value_sum[other]
            for head in range(heads):
                scores = dot_nt(query_parts[head], key_here) * SCALE
                weights = jnp.where(allowed, jnp.exp(scores - logs[:, head : head + 1]), 0.0)
                weights_grad = dot_nt(grad_parts[head], value_here)
                scores_grad = (weights * (weights_grad - deltas[head])).astype(BF)
                query_sum = query_sum + dot_nn(scores_grad, head_part(key_here, head))
                key_add = key_add + dot_tn(scores_grad, query_parts[head])
                value_add = value_add + dot_tn(weights.astype(BF), grad_parts[head])
            key_sum[other] = key_add
            value_sum[other] = value_add
            return query_sum

        query_sum = lax.fori_loop(0, position + 1, block, jnp.zeros((rows, group), F32))
        mixed[position, :, :group] = turned_back(query_sum * SCALE, position)
        return unused

    half = span_count // 2
    lax.fori_loop(0, half, attend_back, 0)
    each(gate_up_a, "second")
    each(gate_up_b, "first")
    lax.fori_loop(half, last, attend_back, 0)
    each(gate_up_a, "line_start")
    lax.fori_loop(last, span_count, attend_back, 0)

    def close(position, unused):
        mixed[position, :, group : 2 * group] = turned_back(key_sum[position] * SCALE, position)
        mixed[position, :, 2 * group :] = (
            BLEND_MIX * value_sum[position].astype(BF).astype(F32)
        ).astype(BF)
        return unused

    lax.fori_loop(0, span_count, close, 0)
    pairs[3].right_copy.start()
    grad_exchange.finish()
    blended_send = grad_send
    for index in range(span_count):
        blended_send[index] = value_sum[order[index]].astype(BF)
    blended_exchange = Exchange(
        place, blended_send, blended_all, blended_send_sem, blended_recv_sem
    )

    def normed_grad(block):
        return dot_nt(mixed[order[block]], qkv_copy[...])

    def pass_on(block, way):
        return remote(
            chain.at[block + 1 - way],
            chain.at[block + 1 - way],
            chain_send.at[way, block],
            chain_recv.at[way, block],
            (place.dp, jnp.minimum(span + 1, last) if way == 0 else jnp.maximum(span - 1, 0)),
        )

    def chain_step(step):
        up = last + span - step
        down = step - (last - span)

        @pl.when((span <= step) & (up > span))
        def going_up():
            block = jnp.clip(up, 0, last)

            @pl.when(span > 0)
            def more():
                pass_on(block, 0).wait_recv()

            chain[block + 1] = (normed_grad(block) + chain[block + 1].astype(F32)).astype(BF)
            pass_on(block, 0).start()

        @pl.when((down >= 0) & (down < span))
        def going_down():
            block = jnp.clip(down, 0, last)

            @pl.when(span < last)
            def more():
                pass_on(block, 1).wait_recv()

            chain[block] = (normed_grad(block) + chain[block].astype(F32)).astype(BF)
            pass_on(block, 1).start()

    def chain_end():
        @pl.when(span > 0)
        def from_below():
            pass_on(span, 0).wait_recv()

        @pl.when(span < last)
        def from_above():
            pass_on(span, 1).wait_recv()

        normed_result[...] = (
            normed_grad(span) + chain[span + 1].astype(F32) + chain[span].astype(F32)
        )

    chain_step(0)
    blended_exchange.start()
    each(gate_up_a, "line_in")
    pairs[3].wait()
    each(qkv, "first")
    each(down, "second")
    each(out, "first")
    for step in range(1, last):
        chain_step(step)
        if step == 1:
            each(gate_up_a, "line_mid")
    each(qkv, "second")
    each(down, "line_start")
    each(gate_up_a, "line_out")
    chain_end()
    blended_exchange.wait()
    blended_result[...] = jnp.concatenate([blended_all[i] for i in range(span_count)], axis=1)
    for member in qkv:
        member.spread_start(qkv_result)
    each(down, "line_in")
    each(gate_up_b, "second")
    each(out, "second")
    each(down, "line_mid")
    each(gate_up_b, "line_start")
    each(down, "line_out")
    each(gate_up_b, "line_in")
    each(out, "line_start")
    each(gate_up_b, "line_mid")
    each(out, "line_in")
    each(gate_up_b, "line_out")
    each(out, "line_mid")
    each(out, "line_out")
    each(qkv, "spread_wait")

    for pair in pairs:
        pair.finish()
    blended_exchange.finish()
    for members in (gate_up_a, gate_up_b, down, out):
        each(members, "line_finish")
        each(members, "finish")
    each(qkv, "finish")
    for step in range(last):
        up = last + span - step
        down_block = step - (last - span)

        @pl.when((span <= step) & (up > span))
        def sent_up():
            pass_on(jnp.clip(up, 0, last), 0).wait_send()

        @pl.when((down_block >= 0) & (down_block < span))
        def sent_down():
            pass_on(jnp.clip(down_block, 0, last), 1).wait_send()


def backward_call(dp_count, span_count, slot_of, order, factors, others):
    (gate_up_left, gate_up_right, down_left, down_right, out_left, out_right, qkv_left) = factors
    rows, width = others[0].shape
    group = width // span_count
    inner_count = dp_count // 4
    dma = pltpu.SemaphoreType.DMA
    by_span = (span_count, rows, group)
    mixed_shape = (span_count, rows, 3 * group)

    def less(left):
        return (left.shape[0],) + left.shape[2:]

    scratch = []
    for left, columns_in, on_line in (
        (gate_up_left, gate_up_right.shape[2], True),
        (down_left, down_right.shape[2], True),
        (out_left, out_right.shape[2], True),
        (qkv_left, 3 * group, False),
    ):
        for i, columns in enumerate(cut_columns(columns_in)):
            scratch += [
                pltpu.VMEM(shape, BF)
                for shape in piece_scratch(inner_count, left.shape[2], columns, i % 2, on_line)
            ]
    slots = 2 * inner_count + max(3, span_count)
    return pl.pallas_call(
        functools.partial(backward_kernel, dp_count, span_count),
        out_shape=(
            jax.ShapeDtypeStruct((gate_up_left.shape[2], gate_up_right.shape[2]), BF),
            jax.ShapeDtypeStruct((down_left.shape[2], down_right.shape[2]), BF),
            jax.ShapeDtypeStruct((out_left.shape[2], out_right.shape[2]), BF),
            jax.ShapeDtypeStruct((span_count, qkv_left.shape[2], 3 * group), BF),
            jax.ShapeDtypeStruct((rows, width), BF),
            jax.ShapeDtypeStruct((rows, width), F32),
        ),
        in_specs=[pl.BlockSpec(memory_space=pltpu.SMEM)] * 2
        + [any_spec(), full_spec()] * 3
        + [any_spec()]
        + [full_spec()] * len(others),
        out_specs=(full_spec(),) * 6,
        scratch_shapes=[
            pltpu.VMEM(less(gate_up_left), BF),
            pltpu.VMEM(less(gate_up_left), BF),
            pltpu.VMEM(gate_up_right.shape, BF),
            pltpu.VMEM(less(down_left), BF),
            pltpu.VMEM(less(down_left), BF),
            pltpu.VMEM(down_right.shape, BF),
            pltpu.VMEM(less(out_left), BF),
            pltpu.VMEM(less(out_left), BF),
            pltpu.VMEM(out_right.shape, BF),
            pltpu.VMEM(less(qkv_left), BF),
            pltpu.VMEM(less(qkv_left), BF),
            pltpu.VMEM(mixed_shape, BF),
            pltpu.VMEM(mixed_shape, BF),
            pltpu.VMEM(by_span, BF),
            pltpu.VMEM(by_span, BF),
            pltpu.VMEM(by_span, F32),
            pltpu.VMEM(by_span, F32),
            pltpu.VMEM(by_span, BF),
            pltpu.VMEM((span_count + 1, rows, width), BF),
            dma((4, 3)),
            dma((4, 3)),
            dma((16, slots)),
            dma((16, slots)),
            dma((span_count,)),
            dma((span_count,)),
            dma((span_count,)),
            dma((span_count,)),
            dma((2, span_count)),
            dma((2, span_count)),
        ]
        + scratch,
        compiler_params=pltpu.CompilerParams(
            collective_id=1, has_side_effects=True, vmem_limit_bytes=61 << 20
        ),
    )(slot_of, order, *factors, *others)


def update_rows(master, first_state, second_state, gradient, rate, decay):
    next_first = BETA_FIRST * first_state + (1.0 - BETA_FIRST) * gradient
    next_second = BETA_SECOND * second_state + (1.0 - BETA_SECOND) * gradient * gradient
    first_hat = next_first * (1.0 / (1.0 - BETA_FIRST**STEP))
    second_hat = next_second * (1.0 / (1.0 - BETA_SECOND**STEP))
    new_master = master - rate * (first_hat / (jnp.sqrt(second_hat) + ADAM_EPS) + decay * master)
    return (new_master, next_first, next_second)


def finish_kernel(
    qkv_total,
    out_total,
    gate_up_total,
    down_total,
    gains,
    gains_first,
    gains_second,
    tokens,
    mid_grad,
    normed_grad,
    gains_rows,
    blended_grad,
    qkv,
    qkv_first,
    qkv_second,
    out,
    out_first,
    out_second,
    gate_up,
    gate_up_first,
    gate_up_second,
    down,
    down_first,
    down_second,
    tokens_grad,
    values_grad,
    new_gains,
    new_gains_first,
    new_gains_second,
    *rest,
):
    results, held, in_sem, out_sem = rest[:12], rest[12:24], rest[24], rest[25]
    states = (
        (qkv, qkv_first, qkv_second),
        (out, out_first, out_second),
        (gate_up, gate_up_first, gate_up_second),
        (down, down_first, down_second),
    )
    width = tokens.shape[1]
    span_count = qkv_total.shape[0]
    group = width // span_count

    def qkv_rows(part):
        def rows(at):
            return jnp.concatenate(
                [
                    qkv_total[i, at, part * group : (part + 1) * group].astype(F32)
                    for i in range(span_count)
                ],
                axis=1,
            )

        return rows

    def rows_of(total, columns):
        return lambda at: total[at, columns].astype(F32)

    parts = []
    for columns in cut_columns(gate_up_total.shape[1]):
        parts.append((2, columns, rows_of(gate_up_total, columns)))
    for part in range(3):
        parts.append((0, slice(part * width, (part + 1) * width), qkv_rows(part)))
    for columns in cut_columns(width):
        parts.append((3, columns, rows_of(down_total, columns)))
    parts.append((1, slice(0, width), rows_of(out_total, slice(0, width))))

    def moves(number, source, target, sems):
        weight, columns, _ = parts[number]
        return [
            pltpu.make_async_copy(
                source[i].at[:, columns], target[i].at[:, columns], sems.at[number, i]
            )
            for i in range(3)
        ]

    loads, stores = [], []
    for number, (weight, _, _) in enumerate(parts):
        here = held[3 * weight : 3 * weight + 3]
        loads.append(moves(number, states[weight], here, in_sem))
        stores.append(moves(number, here, results[3 * weight : 3 * weight + 3], out_sem))
        for copy in loads[-1]:
            copy.start()

    residual = tokens[...].astype(F32)
    scaled, inverse = normalize_parts(residual)
    tokens_grad[...] = mid_grad[...] + norm_backward(
        normed_grad[...], scaled, inverse, gains_rows[0:1, :]
    )
    values_grad[...] = (1.0 - BLEND_MIX) * blended_grad[...].astype(F32)

    sums = {}
    for number, (weight, columns, total) in enumerate(parts):
        here = held[3 * weight : 3 * weight + 3]
        for copy in loads[number]:
            copy.wait()
        owned = here[0].shape[0]
        wants_sum = weight in (0, 2)

        def step(index, unused):
            at = pl.ds(pl.multiple_of(index * 16, 16), 16)
            gradient = total(at)
            master = here[0][at, columns]
            if wants_sum:
                partial = jnp.sum(
                    gradient * master.astype(BF).astype(F32), axis=1, keepdims=True
                )
                lane = 0 if weight == 0 else 1
                slot = lax.broadcasted_iota(jnp.int32, (16, 2), 1) == lane
                sums_ref[at, :] = sums_ref[at, :] + jnp.where(slot, partial, 0.0)
            updated = update_rows(
                master,
                here[1][at, columns],
                here[2][at, columns],
                gradient,
                MATRIX_RATE,
                MATRIX_DECAY,
            )
            for i in range(3):
                here[i][at, columns] = updated[i]
            return unused

        sums_ref = new_gains_first
        if not sums:
            sums_ref[...] = jnp.zeros_like(sums_ref)
            sums["begun"] = True
        lax.fori_loop(0, owned // 16, step, 0)
        for copy in stores[number]:
            copy.start()

    gain = gains[...]
    gains_total = new_gains_first[...] / gain.astype(BF).astype(F32)
    updated = update_rows(gain, gains_first[...], gains_second[...], gains_total, GAIN_RATE, 0.0)
    new_gains[...], new_gains_first[...], new_gains_second[...] = updated
    for group_of_copies in stores:
        for copy in group_of_copies:
            copy.wait()


def finish_call(totals, gains_states, token_parts, states):
    flat = [member for weight in states for member in weight]
    rows, width = token_parts[0].shape
    gains_shape = jax.ShapeDtypeStruct(gains_states[0].shape, F32)
    dma = pltpu.SemaphoreType.DMA
    count = len(cut_columns(totals[2].shape[1])) + 3 + 2 + 1
    return pl.pallas_call(
        finish_kernel,
        out_shape=(
            jax.ShapeDtypeStruct((rows, width), F32),
            jax.ShapeDtypeStruct((rows, width), F32),
            gains_shape,
            gains_shape,
            gains_shape,
        )
        + tuple(jax.ShapeDtypeStruct(member.shape, F32) for member in flat),
        in_specs=[full_spec()] * 12 + [any_spec()] * 12,
        out_specs=(full_spec(),) * 5 + (any_spec(),) * 12,
        scratch_shapes=[pltpu.VMEM(member.shape, F32) for member in flat]
        + [dma((count, 3)), dma((count, 3))],
        compiler_params=pltpu.CompilerParams(vmem_limit_bytes=VMEM_BYTES),
    )(*totals, *gains_states, *token_parts, *flat)


def to_heads(rows, span_count):
    return lax.all_to_all(
        rows.reshape(rows.shape[0], span_count, rows.shape[1] // span_count),
        "seq",
        split_axis=1,
        concat_axis=0,
        tiled=True,
    ).reshape(rows.shape[0] * span_count, rows.shape[1] // span_count)


def to_spans(columns, span_count):
    rows_here = columns.shape[0] // span_count
    got = lax.all_to_all(
        columns.reshape(span_count, rows_here, columns.shape[1]),
        "seq",
        split_axis=0,
        concat_axis=0,
        tiled=True,
    )
    return jnp.transpose(got, (1, 0, 2)).reshape(rows_here, columns.shape[1] * span_count)


def on_device(
    tokens,
    first_values,
    out_grad,
    segments,
    span_order,
    qkv_weight,
    out_weight,
    gate_up_weight,
    down_weight,
    norm_gains,
    first_qkv,
    first_out,
    first_gate_up,
    first_down,
    first_gains,
    second_qkv,
    second_out,
    second_gate_up,
    second_down,
    second_gains,
):
    span_count = lax.axis_size("seq")
    mine = lax.axis_index("seq")
    owned_rows, triple = qkv_weight.shape
    model_width = triple // 3
    group = model_width // span_count
    group_heads = group // HEAD_DIM
    residual = tokens[0].astype(F32)
    rows_here = residual.shape[0]
    length = rows_here * span_count
    hidden_width = gate_up_weight.shape[1] // 2

    dp_count = lax.axis_size("dp")
    gains_owned = norm_gains.astype(BF).astype(F32)
    in_kernels = (
        length * model_width <= 1 << 20
        and dp_count % 4 == 0
        and dp_count >= 8
        and span_count % 2 == 0
        and group % 128 == 0
    )
    if in_kernels:
        slot_of = jnp.sum(
            jnp.where(
                span_order[None, :] == jnp.arange(span_count, dtype=jnp.int32)[:, None],
                jnp.arange(span_count, dtype=jnp.int32)[None, :],
                0,
            ),
            axis=1,
        ).astype(jnp.int32)
        ordered = lax.optimization_barrier(jnp.arange(length, dtype=jnp.int32))
        cosine, sine = rotary(ordered)
        cosine = cosine.reshape(span_count, rows_here, HEAD_DIM // 2)
        sine = sine.reshape(span_count, rows_here, HEAD_DIM // 2)
        qkv_mine = (
            lax.dynamic_slice_in_dim(
                qkv_weight.reshape(owned_rows, 3, model_width), mine * group, group, 2
            )
            .reshape(owned_rows, 3 * group)
            .astype(BF)
        )
        gains_mine = jnp.pad(jnp.transpose(gains_owned), ((0, 6), (0, 0)))
        (
            out_copy, gate_up_copy, down_copy, qkv_copy, normed_left, counts, gains_rows, attended,
            query_pos, key_pos, value_pos, raw_pos, lse_pos,
        ) = forward_call(
            dp_count, span_count, slot_of, span_order, tokens[0], first_values[0], segments,
            gains_mine, qkv_mine, out_weight, gate_up_weight, down_weight, cosine, sine,
        )
        gains_full = jnp.transpose(gains_rows[:2])
    else:
        qkv_owned = qkv_weight.reshape(owned_rows, 3, model_width).astype(BF)
        qkv_mine = lax.dynamic_slice_in_dim(qkv_owned, mine * group, group, 2).reshape(
            owned_rows, 3 * group
        )
        gains_full = lax.all_gather(norm_gains.astype(BF), "dp", axis=0, tiled=True).astype(F32)
        qkv_copy = lax.all_gather(qkv_mine, "dp", axis=0, tiled=True)
        out_copy = lax.all_gather(out_weight.astype(BF), "dp", axis=0, tiled=True)
        gate_up_copy = lax.all_gather(gate_up_weight.astype(BF), "dp", axis=0, tiled=True)
        down_copy = lax.all_gather(down_weight.astype(BF), "dp", axis=0, tiled=True)

        row_index = jnp.arange(length, dtype=jnp.int32)
        owner_table = (row_index // rows_here)[:, None] == jnp.arange(span_count, dtype=jnp.int32)[
            None, :
        ]
        positions = (
            jnp.sum(jnp.where(owner_table, span_order[None, :], 0), axis=1) * rows_here
            + row_index % rows_here
        )
        all_segments = lax.all_gather(segments[0], "seq", axis=0, tiled=True)
        cosine, sine_table = rotary(positions)
        allowed = (all_segments[:, None] == all_segments[None, :]) & (
            positions[None, :] <= positions[:, None]
        )

        scaled_in, inverse_in = normalize_parts(residual)
        normed_in = (scaled_in * gains_full[:, 0]).astype(BF)
        normed_all = lax.all_gather(normed_in, "seq", axis=0, tiled=True)
        first_all = to_heads(first_values[0], span_count)
        mixed = dot_nn(normed_all, qkv_copy)
        queries = rotate(
            mixed[:, :group].reshape(length, group_heads, HEAD_DIM), cosine, sine_table
        ).astype(BF)
        keys = rotate(
            mixed[:, group : 2 * group].reshape(length, group_heads, HEAD_DIM), cosine, sine_table
        ).astype(BF)
        blended = (
            (BLEND_MIX * mixed[:, 2 * group :] + (1.0 - BLEND_MIX) * first_all.astype(F32))
            .astype(BF)
            .reshape(length, group_heads, HEAD_DIM)
        )
        scores = jnp.einsum("qhd,khd->hqk", queries, keys, preferred_element_type=F32) * SCALE
        masked = jnp.where(allowed[None], scores, MASK_FILL)
        highest = jnp.max(masked, axis=-1, keepdims=True)
        raised = jnp.where(allowed[None], jnp.exp(masked - highest), 0.0)
        weights = raised / jnp.sum(raised, axis=-1, keepdims=True)
        weights_low = weights.astype(BF)
        attended_raw = jnp.einsum("hqk,khd->qhd", weights_low, blended, preferred_element_type=F32)
        attended = to_spans(attended_raw.reshape(length, group).astype(BF), span_count)

    hidden_mid = residual + dot_nn(attended, out_copy)
    scaled_mid, inverse_mid = normalize_parts(hidden_mid)
    normed_mid = (scaled_mid * gains_full[:, 1]).astype(BF)
    gate_up = dot_nn(normed_mid, gate_up_copy)
    gate_part = gate_up[:, :hidden_width]
    upward = gate_up[:, hidden_width:]
    sigmoid_gate = jax.nn.sigmoid(gate_part)
    swish_gate = gate_part * sigmoid_gate
    activation = (swish_gate * upward).astype(BF)
    layer_out = (hidden_mid + dot_nn(activation, down_copy)).astype(BF)
    back_rows = out_grad[0]
    activation_grad = dot_nt(back_rows, down_copy)
    gate_up_grad = jnp.concatenate(
        [
            activation_grad * upward * sigmoid_gate * (1.0 + gate_part * (1.0 - sigmoid_gate)),
            activation_grad * swish_gate,
        ],
        axis=1,
    ).astype(BF)
    normed_mid_grad = dot_nt(gate_up_grad, gate_up_copy)
    hidden_mid_grad = back_rows.astype(F32) + norm_backward(
        normed_mid_grad, scaled_mid, inverse_mid, gains_full[:, 1]
    )
    mid_grad_low = hidden_mid_grad.astype(BF)
    if in_kernels:
        def left_factor(rows_in):
            columns = rows_in.shape[1]
            return jnp.transpose(rows_in).reshape(
                dp_count // 2, 2, columns // dp_count, rows_in.shape[0]
            )

        factors = (
            left_factor(normed_mid),
            gate_up_grad[None],
            left_factor(activation),
            back_rows[None],
            left_factor(attended),
            mid_grad_low[None],
            normed_left.reshape(dp_count // 2, 2, owned_rows, length),
        )
        others = (
            dot_nt(mid_grad_low, out_copy).astype(BF),
            query_pos, key_pos, value_pos, raw_pos, lse_pos, counts, cosine, sine, qkv_copy,
        )
        gate_up_total, down_total, out_total, qkv_part, blended_grad, normed_in_grad = backward_call(
            dp_count, span_count, slot_of, span_order, factors, others
        )
        finished = finish_call(
            (qkv_part, out_total, gate_up_total, down_total),
            (norm_gains, first_gains, second_gains),
            (tokens[0], hidden_mid_grad, normed_in_grad, gains_rows, blended_grad),
            (
                (qkv_weight, first_qkv, second_qkv),
                (out_weight, first_out, second_out),
                (gate_up_weight, first_gate_up, second_gate_up),
                (down_weight, first_down, second_down),
            ),
        )
        tokens_grad, values_grad = finished[:2]
        return (
            (layer_out[None], tokens_grad[None], values_grad[None])
            + finished[5::3]
            + finished[2:3]
            + finished[6::3]
            + finished[3:4]
            + finished[7::3]
            + finished[4:5]
        )
    attended_grad = to_heads(dot_nt(mid_grad_low, out_copy).astype(BF), span_count)

    heads_grad = attended_grad.reshape(length, group_heads, HEAD_DIM)
    delta = jnp.transpose(jnp.sum(heads_grad.astype(F32) * attended_raw, axis=-1))
    weights_grad = jnp.einsum("qhd,khd->hqk", heads_grad, blended, preferred_element_type=F32)
    scores_grad = (weights * (weights_grad - delta[..., None])).astype(BF)
    queries_grad = (
        jnp.einsum("hqk,khd->qhd", scores_grad, keys, preferred_element_type=F32) * SCALE
    ).astype(BF).astype(F32)
    keys_grad = (
        jnp.einsum("hqk,qhd->khd", scores_grad, queries, preferred_element_type=F32) * SCALE
    ).astype(BF).astype(F32)
    blended_grad = jnp.einsum(
        "hqk,qhd->khd", weights_low, heads_grad, preferred_element_type=F32
    ).astype(BF).reshape(length, group)
    values_grad = (1.0 - BLEND_MIX) * to_spans(blended_grad, span_count).astype(F32)
    mixed_grad = jnp.concatenate(
        [
            rotate(queries_grad, cosine, -sine_table).reshape(length, group),
            rotate(keys_grad, cosine, -sine_table).reshape(length, group),
            BLEND_MIX * blended_grad.astype(F32),
        ],
        axis=1,
    ).astype(BF)
    normed_in_grad = lax.psum_scatter(
        dot_nt(mixed_grad, qkv_copy).astype(BF), "seq", scatter_dimension=0, tiled=True
    ).astype(F32)
    tokens_grad = hidden_mid_grad + norm_backward(
        normed_in_grad, scaled_in, inverse_in, gains_full[:, 0]
    )

    def to_owner(terms):
        return lax.psum_scatter(terms.astype(BF), "dp", scatter_dimension=0, tiled=True)

    qkv_part = lax.all_gather(to_owner(dot_tn(normed_all, mixed_grad)), "seq", axis=0)
    qkv_total = (
        jnp.transpose(qkv_part.reshape(span_count, owned_rows, 3, group), (1, 2, 0, 3))
        .reshape(owned_rows, triple)
        .astype(F32)
    )
    out_total, gate_up_total, down_total = lax.psum(
        (
            to_owner(dot_tn(attended, mid_grad_low)),
            to_owner(dot_tn(normed_mid, gate_up_grad)),
            to_owner(dot_tn(activation, back_rows)),
        ),
        "seq",
    )
    out_total, gate_up_total, down_total = (
        out_total.astype(F32),
        gate_up_total.astype(F32),
        down_total.astype(F32),
    )

    gains_total = jnp.stack(
        [
            jnp.sum(qkv_total * qkv_weight.astype(BF).astype(F32), axis=1),
            jnp.sum(gate_up_total * gate_up_weight.astype(BF).astype(F32), axis=1),
        ],
        axis=1,
    ) / gains_owned
    masters = (qkv_weight, out_weight, gate_up_weight, down_weight, norm_gains)
    firsts = (first_qkv, first_out, first_gate_up, first_down, first_gains)
    seconds = (second_qkv, second_out, second_gate_up, second_down, second_gains)
    totals = (qkv_total, out_total, gate_up_total, down_total, gains_total)
    rate_list = (MATRIX_RATE, MATRIX_RATE, MATRIX_RATE, MATRIX_RATE, GAIN_RATE)
    decays = (MATRIX_DECAY, MATRIX_DECAY, MATRIX_DECAY, MATRIX_DECAY, 0.0)
    updated = [
        apply_adamw(masters[i], firsts[i], seconds[i], totals[i], rate_list[i], decays[i])
        for i in range(5)
    ]
    return (
        (layer_out[None], tokens_grad[None], values_grad[None])
        + tuple(member[0] for member in updated)
        + tuple(member[1] for member in updated)
        + tuple(member[2] for member in updated)
    )


def solution(mesh):
    rows = P("dp", "seq", None)
    owned = P("dp", None)
    return jax.shard_map(
        on_device,
        mesh=mesh,
        in_specs=(rows, rows, rows, P("dp", "seq"), P()) + (owned,) * 15,
        out_specs=(rows,) * 3 + (owned,) * 15,
        check_vma=False,
    )
```

```python
import functools
import math

import jax
import jax.numpy as jnp
from jax import lax
from jax.experimental import pallas as pl
from jax.experimental.pallas import tpu as pltpu
from jax.sharding import PartitionSpec as P

HEAD_DIM = 64
STEP = 10


NORM_EPS = 1e-06
ADAM_EPS = 1e-08
BLEND_MIX = 0.5
BETA_FIRST = 0.5
BETA_SECOND = 0.5
MATRIX_RATE = 0.06
MATRIX_DECAY = 0.1
GAIN_RATE = 0.5
ROPE_BASE = 10000.0
MASK_FILL = -1e30
SCALE = HEAD_DIM ** (-0.5)

BF = jnp.bfloat16
F32 = jnp.float32


def dot_nn(left, right):
    return lax.dot_general(left, right, (((1,), (0,)), ((), ())), preferred_element_type=F32)


def dot_nt(left, right):
    return lax.dot_general(left, right, (((1,), (1,)), ((), ())), preferred_element_type=F32)


def dot_tn(left, right):
    return lax.dot_general(left, right, (((0,), (0,)), ((), ())), preferred_element_type=F32)


def normalize_parts(matrix):
    inverse = lax.rsqrt(jnp.mean(matrix * matrix, axis=-1, keepdims=True) + NORM_EPS)
    return (matrix * inverse, inverse)


def norm_backward(grad_rows, scaled, inverse, gain_column):
    pushed = grad_rows * gain_column
    return inverse * (pushed - scaled * jnp.mean(pushed * scaled, axis=-1, keepdims=True))


def rotary(positions):
    half_width = HEAD_DIM // 2
    frequency = jnp.exp(
        jnp.arange(half_width, dtype=F32) * (-math.log(ROPE_BASE) / half_width)
    )
    angles = positions.astype(F32)[:, None] * frequency[None, :]
    return (jnp.cos(angles)[:, None, :], jnp.sin(angles)[:, None, :])


def rotate(head_rows, cosine, sine_table):
    half_width = head_rows.shape[-1] // 2
    lower_half = head_rows[..., :half_width]
    upper_half = head_rows[..., half_width:]
    return jnp.concatenate(
        [
            lower_half * cosine - upper_half * sine_table,
            upper_half * cosine + lower_half * sine_table,
        ],
        axis=-1,
    )


def apply_adamw(master, first_state, second_state, gradient, rate, decay):
    next_first = BETA_FIRST * first_state + (1.0 - BETA_FIRST) * gradient
    next_second = BETA_SECOND * second_state + (1.0 - BETA_SECOND) * gradient * gradient
    first_hat = next_first / (1.0 - BETA_FIRST**STEP)
    second_hat = next_second / (1.0 - BETA_SECOND**STEP)
    new_master = master - rate * (first_hat / (jnp.sqrt(second_hat) + ADAM_EPS) + decay * master)
    return (new_master, next_first, next_second)


MESH = pl.DeviceIdType.MESH
VMEM_BYTES = 58 << 20


def full_spec():
    return pl.BlockSpec(memory_space=pltpu.VMEM)


def any_spec():
    return pl.BlockSpec(memory_space=pl.ANY)


class Place:
    def __init__(self, dp_count, span_count):
        self.dp_count = dp_count
        self.span_count = span_count
        self.inner_count = dp_count // 4
        self.dp = lax.axis_index("dp")
        self.span = lax.axis_index("seq")
        self.core = lax.rem(self.dp, 2)
        self.inner = lax.rem(self.dp // 2, self.inner_count)
        self.outer = self.dp // (2 * self.inner_count)

    def at(self, outer, inner, core):
        return (outer * self.inner_count + inner) * 2 + core

    def inner_plus(self, offset):
        return lax.rem(self.inner + offset, self.inner_count)

    def greet_all(self):
        barrier = pltpu.get_barrier_semaphore()
        for offset in range(1, self.dp_count):
            pl.semaphore_signal(
                barrier,
                inc=1,
                device_id=(lax.rem(self.dp + offset, self.dp_count), self.span),
                device_id_type=MESH,
            )
        for offset in range(1, self.span_count):
            pl.semaphore_signal(
                barrier,
                inc=1,
                device_id=(self.dp, lax.rem(self.span + offset, self.span_count)),
                device_id_type=MESH,
            )
        pl.semaphore_wait(barrier, self.dp_count + self.span_count - 2)


def remote(source, target, send_sem, recv_sem, device):
    return pltpu.make_async_remote_copy(
        src_ref=source,
        dst_ref=target,
        send_sem=send_sem,
        recv_sem=recv_sem,
        device_id=device,
        device_id_type=MESH,
    )


def half_rows(rows):
    return rows // 2 // 16 * 16


class Gather:
    def __init__(self, place, whole, columns, send_sems, recv_sems):
        self.place = place
        self.whole = whole
        self.columns = columns
        self.rows = whole.shape[0] // place.dp_count
        self.send_sems = send_sems
        self.recv_sems = recv_sems
        self.sent = []
        count = place.inner_count
        self.near, self.lower, self.upper, self.pair = 0, count, 2 * count, 3 * count

    @staticmethod
    def slots(inner_count):
        return 6 * inner_count + 1

    def block(self, index, part=None):
        first = half_rows(self.rows)
        start, size = {None: (0, self.rows), 0: (0, first), 1: (first, self.rows - first)}[part]
        return self.whole.at[
            pl.ds(pl.multiple_of(index * self.rows + start, 16), size), self.columns
        ]

    def send(self, source, target, slot, far_slot, device):
        copy = remote(
            source, target, self.send_sems.at[slot], self.recv_sems.at[far_slot], (device, self.place.span)
        )
        copy.start()
        self.sent.append(copy)

    def arrived(self, block, slot):
        remote(
            block, block, self.send_sems.at[slot], self.recv_sems.at[slot], (self.place.dp, self.place.span)
        ).wait_recv()

    def sibling(self, block, slot):
        place = self.place
        self.send(block, block, slot, slot, place.at(place.outer, place.inner, 1 - place.core))

    def begin(self):
        place, count = self.place, self.place.inner_count
        mine = self.block(place.dp)
        self.send(mine, mine, 0, 0, place.at(1 - place.outer, place.inner, place.core))
        for offset in range(1, count):
            self.send(
                mine,
                mine,
                offset,
                count - offset,
                place.at(place.outer, place.inner_plus(offset), place.core),
            )
        copy = remote(
            mine,
            mine,
            self.send_sems.at[self.pair],
            self.recv_sems.at[self.pair],
            (place.at(place.outer, place.inner, 1 - place.core), place.span),
        )
        copy.start()
        self.sent.append(copy)

    def forward(self):
        place, count = self.place, self.place.inner_count
        across = place.at(1 - place.outer, place.inner, place.core)
        self.arrived(self.block(across), 0)
        for offset in range(1, count):
            self.send(
                self.block(across, 0),
                self.block(across, 0),
                self.lower + offset,
                self.lower + count - offset,
                place.at(place.outer, place.inner_plus(offset), place.core),
            )
        for offset in range(1, count):
            beside = place.at(place.outer, place.inner_plus(offset), place.core)
            self.arrived(self.block(beside), offset)
            self.send(
                self.block(beside, 1),
                self.block(beside, 1),
                self.upper + offset,
                self.upper + offset,
                across,
            )
        self.sibling(self.block(across), self.pair + count)
        for offset in range(1, count):
            beside = place.at(place.outer, place.inner_plus(offset), place.core)
            self.sibling(self.block(beside), self.pair + offset)

    def share(self):
        place, count = self.place, self.place.inner_count
        for offset in range(1, count):
            far = place.at(1 - place.outer, place.inner_plus(offset), place.core)
            self.arrived(self.block(far, 0), self.lower + offset)
            self.sibling(self.block(far, 0), self.pair + count + offset)
            self.arrived(self.block(far, 1), self.upper + offset)
            self.sibling(self.block(far, 1), self.pair + 2 * count + offset)

    def end(self):
        place, count = self.place, self.place.inner_count
        other = 1 - place.core
        self.arrived(self.block(place.at(place.outer, place.inner, other)), self.pair)
        self.arrived(self.block(place.at(1 - place.outer, place.inner, other)), self.pair + count)
        for offset in range(1, count):
            inner = place.inner_plus(offset)
            self.arrived(self.block(place.at(place.outer, inner, other)), self.pair + offset)
            far = place.at(1 - place.outer, inner, other)
            self.arrived(self.block(far, 0), self.pair + count + offset)
            self.arrived(self.block(far, 1), self.pair + 2 * count + offset)
        for copy in self.sent:
            copy.wait_send()


class Exchange:
    def __init__(self, place, sources, targets, send_sems, recv_sems):
        self.place = place
        self.sources = sources
        self.targets = targets
        self.send_sems = send_sems
        self.recv_sems = recv_sems

    def copy(self, offset):
        place = self.place
        count = place.span_count
        peer = lax.rem(place.span + offset, count)
        return remote(
            self.sources.at[peer],
            self.targets.at[place.span],
            self.send_sems.at[offset],
            self.recv_sems.at[count - offset],
            (place.dp, peer),
        )

    def start(self):
        for offset in range(1, self.place.span_count):
            self.copy(offset).start()
        self.targets[self.place.span] = self.sources[self.place.span]

    def wait(self):
        place = self.place
        count = place.span_count
        for offset in range(1, count):
            peer = lax.rem(place.span + offset, count)
            remote(
                self.sources.at[peer],
                self.targets.at[peer],
                self.send_sems.at[offset],
                self.recv_sems.at[offset],
                (place.dp, peer),
            ).wait_recv()

    def finish(self):
        for offset in range(1, self.place.span_count):
            self.copy(offset).wait_send()


def cast_rows(source, target, first, moves=None):
    rows = source.shape[0]

    def step(index, unused):
        at = pl.ds(pl.multiple_of(index * 16, 16), 16)
        there = pl.ds(pl.multiple_of(first + index * 16, 16), 16)
        for from_columns, to_columns in moves or ((slice(None), slice(None)),):
            target[there, to_columns] = source[at, from_columns].astype(BF)
        return unused

    lax.fori_loop(0, rows // 16, step, 0)


def swap_halves(rows):
    width = rows.shape[1]
    half = HEAD_DIM // 2
    if width % 128:
        pieces = []
        for start in range(0, width, HEAD_DIM):
            pieces += [rows[:, start + half : start + HEAD_DIM], rows[:, start : start + half]]
        return jnp.concatenate(pieces, axis=1)
    lane = lax.broadcasted_iota(jnp.int32, rows.shape, 1)
    return jnp.where(
        lane % HEAD_DIM < half, pltpu.roll(rows, width - half, 1), pltpu.roll(rows, half, 1)
    )


def angles_of(cosine, sine, position, heads):
    half = HEAD_DIM // 2
    back = lax.rem(cosine.shape[1] - half * position, cosine.shape[1])
    cos_half = pltpu.roll(cosine[...], back, 1)[:, :half]
    sin_half = pltpu.roll(sine[...], back, 1)[:, :half]
    return (
        jnp.concatenate([cos_half] * (2 * heads), axis=1),
        jnp.concatenate([-sin_half, sin_half] * heads, axis=1),
    )


def segment_starts(bounds, rows, first):
    position = lax.broadcasted_iota(jnp.int32, (rows, 1), 0) + first
    position = position.astype(F32)
    start = jnp.zeros((rows, 1), F32)
    for cut in bounds:
        start = jnp.where(position >= cut, cut, start)
    return position, start


def head_part(matrix, head):
    if matrix.shape[1] == HEAD_DIM:
        return matrix
    lane = lax.broadcasted_iota(jnp.int32, (1, matrix.shape[1]), 1)
    return jnp.where(lane // HEAD_DIM == head, matrix, jnp.zeros_like(matrix))


def forward_kernel(
    dp_count,
    span_count,
    slot_of,
    order,
    tokens,
    first_values,
    segments,
    gains_mine,
    qkv_mine,
    out_mine,
    gate_up_mine,
    down_mine,
    cosine,
    sine,
    out_grad,
    qkv_out,
    normed_out,
    counts_out,
    gains_out,
    query_out,
    key_out,
    value_out,
    raw_out,
    lse_out,
    layer_low,
    mid_grad,
    mid_grad_low,
    gate_up_grad,
    normed_left,
    activation_left,
    attended_left,
    attended_grad,
    qkv_held,
    out_whole,
    gate_up_whole,
    down_whole,
    qkv_whole,
    attended,
    normed,
    outward,
    normed_grad,
    gains_all,
    counts_send,
    counts_all,
    first_send,
    first_all,
    normed_all,
    scores_kept,
    attended_send,
    attended_all,
    gather_send,
    gather_recv,
    gains_send_sem,
    gains_recv_sem,
    counts_send_sem,
    counts_recv_sem,
    first_send_sem,
    first_recv_sem,
    ring_send,
    ring_recv,
    attended_send_sem,
    attended_recv_sem,
    local_sem,
):
    place = Place(dp_count, span_count)
    rows, width = tokens.shape
    group = width // span_count
    hidden = down_whole.shape[0]
    owned = out_mine.shape[0]
    heads = group // HEAD_DIM
    last = span_count - 1
    span = place.span

    qkv_loads = []
    for part in range(3):
        first = pl.multiple_of(part * width + span * group, 128)
        copy = pltpu.make_async_copy(
            qkv_mine.at[:, pl.ds(first, group)],
            qkv_held.at[:, part * group : (part + 1) * group],
            local_sem.at[part],
        )
        copy.start()
        qkv_loads.append(copy)

    place.greet_all()
    gains_all[place.dp] = gains_mine[...]
    gains_copies = []
    for offset in range(1, dp_count):
        peer = lax.rem(place.dp + offset, dp_count)
        copy = remote(
            gains_mine,
            gains_all.at[place.dp],
            gains_send_sem.at[offset],
            gains_recv_sem.at[dp_count - offset],
            (peer, span),
        )
        copy.start()
        gains_copies.append(copy)
    parts = hidden_parts(hidden)
    moves = []
    gate_up_columns = []
    for start, size in parts:
        moves.append((slice(start, start + size), slice(2 * start, 2 * start + size)))
        moves.append(
            (
                slice(hidden + start, hidden + start + size),
                slice(2 * start + size, 2 * start + 2 * size),
            )
        )
        gate_up_columns.append(slice(2 * start, 2 * (start + size)))
    every = slice(None)
    sources = [(qkv_whole, every), (out_whole, every), (down_whole, every)]
    sources += [(gate_up_whole, columns) for columns in gate_up_columns]
    gathers = [
        Gather(place, whole, columns, gather_send.at[i], gather_recv.at[i])
        for i, (whole, columns) in enumerate(sources)
    ]
    qkv_gather, out_gather, down_gather = gathers[:3]
    gate_up_gathers = gathers[3:]
    for copy in qkv_loads:
        copy.wait()
    cast_rows(qkv_held, qkv_whole, place.dp * owned)
    qkv_gather.begin()
    for index in range(span_count):
        first_send[index] = first_values[:, index * group : (index + 1) * group]
    first_exchange = Exchange(place, first_send, first_all, first_send_sem, first_recv_sem)
    first_exchange.start()
    ids = segments[...]
    row = lax.broadcasted_iota(jnp.int32, (8, 128), 0)
    counts = jnp.zeros((8, 128), F32)
    for cut in range(3):
        below = jnp.sum(jnp.where(ids <= cut, 1.0, 0.0), axis=1, keepdims=True)
        counts = jnp.where(row == cut, below, counts)
    for index in range(span_count):
        counts_send[index] = counts
    counts_exchange = Exchange(place, counts_send, counts_all, counts_send_sem, counts_recv_sem)
    counts_exchange.start()

    residual = tokens[...].astype(F32)
    scaled = residual * lax.rsqrt(jnp.mean(residual * residual, axis=1, keepdims=True) + NORM_EPS)
    for offset in range(1, dp_count):
        peer = lax.rem(place.dp + offset, dp_count)
        remote(
            gains_mine,
            gains_all.at[peer],
            gains_send_sem.at[offset],
            gains_recv_sem.at[offset],
            (peer, span),
        ).wait_recv()
    gains_row = jnp.concatenate([gains_all[i] for i in range(dp_count)], axis=1)
    gains_out[...] = gains_row
    normed_all[span] = (scaled * gains_row[0:1, :]).astype(BF)

    def pass_on(block, step, way):
        return remote(
            normed_all.at[block],
            normed_all.at[block],
            ring_send.at[way, step],
            ring_recv.at[way, step],
            (place.dp, jnp.where(way == 0, jnp.minimum(span + 1, last), jnp.maximum(span - 1, 0))),
        )

    @pl.when(span < last)
    def up():
        pass_on(span, 0, 0).start()

    @pl.when(span > 0)
    def down():
        pass_on(span, 0, 1).start()

    cast_rows(out_mine, out_whole, place.dp * owned)
    out_gather.begin()
    cast_rows(down_mine, down_whole, place.dp * down_mine.shape[0])
    qkv_gather.forward()
    down_gather.begin()
    cast_rows(gate_up_mine, gate_up_whole, place.dp * owned, moves)
    for member in gate_up_gathers:
        member.begin()
    qkv_gather.share()
    out_gather.forward()

    for step in range(1, span_count):

        @pl.when(span - step >= 0)
        def from_below():
            block = jnp.maximum(span - step, 0)
            pass_on(block, step - 1, 0).wait_recv()

            @pl.when(span < last)
            def on():
                pass_on(block, step, 0).start()

        @pl.when(span + step <= last)
        def from_above():
            block = jnp.minimum(span + step, last)
            pass_on(block, step - 1, 1).wait_recv()

            @pl.when(span > 0)
            def on():
                pass_on(block, step, 1).start()

    qkv_gather.end()
    qkv_copy = pltpu.make_async_copy(qkv_whole, qkv_out, local_sem.at[3])
    qkv_copy.start()
    first_exchange.wait()
    counts_exchange.wait()
    cuts = counts_all[0]
    for index in range(1, span_count):
        cuts = cuts + counts_all[index]
    counts_out[...] = cuts
    bounds = [cuts[i : i + 1, 0:1] for i in range(3)]

    def project(position, unused):
        slot = slot_of[position]
        normed_here = normed_all[slot]
        normed_out[:, pl.ds(pl.multiple_of(position * rows, rows), rows)] = jnp.transpose(normed_here)
        mixed = dot_nn(normed_here, qkv_whole[...])
        cos_here, sin_here = angles_of(cosine, sine, position, heads)
        query = mixed[:, :group]
        key = mixed[:, group : 2 * group]
        query_out[position] = (query * cos_here + swap_halves(query) * sin_here).astype(BF)
        key_out[position] = (key * cos_here + swap_halves(key) * sin_here).astype(BF)
        value_out[position] = (
            BLEND_MIX * mixed[:, 2 * group :]
            + (1.0 - BLEND_MIX) * first_all[slot].astype(F32)
        ).astype(BF)
        return unused

    lax.fori_loop(0, span_count, project, 0)
    out_gather.share()
    down_gather.forward()

    def attend(position, unused):
        query = query_out[position]
        parts = [head_part(query, head) for head in range(heads)]
        query_position, start = segment_starts(bounds, rows, position * rows)

        def score(other, highest):
            key = key_out[other]
            key_position = (
                lax.broadcasted_iota(jnp.int32, (1, rows), 1) + other * rows
            ).astype(F32)
            allowed = (key_position <= query_position) & (key_position >= start)
            found = []
            for head in range(heads):
                masked = jnp.where(allowed, dot_nt(parts[head], key) * SCALE, MASK_FILL)
                scores_kept[head, other] = masked
                found.append(jnp.maximum(highest[head], jnp.max(masked, axis=1, keepdims=True)))
            return tuple(found)

        highest = lax.fori_loop(
            0, position + 1, score, (jnp.full((rows, 1), MASK_FILL, F32),) * heads
        )

        def raise_scores(other, total):
            added = []
            for head in range(heads):
                raised = jnp.exp(scores_kept[head, other] - highest[head])
                scores_kept[head, other] = raised
                added.append(total[head] + jnp.sum(raised, axis=1, keepdims=True))
            return tuple(added)

        total = lax.fori_loop(
            0, position + 1, raise_scores, (jnp.zeros((rows, 1), F32),) * heads
        )
        inverse = [1.0 / member for member in total]

        def gather_values(other, attended):
            value = value_out[other]
            for head in range(heads):
                weights = (scores_kept[head, other] * inverse[head]).astype(BF)
                attended = attended + dot_nn(weights, head_part(value, head))
            return attended

        raw_out[position] = lax.fori_loop(
            0, position + 1, gather_values, jnp.zeros((rows, group), F32)
        )
        lane = lax.broadcasted_iota(jnp.int32, (rows, 128), 1)
        kept = jnp.zeros((rows, 128), F32)
        for head in range(heads):
            kept = jnp.where(lane == head, highest[head] + jnp.log(total[head]), kept)
        lse_out[position] = kept
        return unused

    gate_up_gathers[0].forward()
    lax.fori_loop(0, span_count // 2, attend, 0)
    for member in gate_up_gathers[1:-1]:
        member.forward()
    lax.fori_loop(span_count // 2, span_count - 1, attend, 0)
    gate_up_gathers[-1].forward()
    down_gather.share()
    lax.fori_loop(span_count - 1, span_count, attend, 0)

    for index in range(span_count):
        attended_send[index] = raw_out[order[index]].astype(BF)
    attended_exchange = Exchange(
        place, attended_send, attended_all, attended_send_sem, attended_recv_sem
    )
    attended_exchange.start()
    gate_up_gathers[0].share()
    out_gather.end()
    attended_exchange.wait()
    attended[...] = jnp.concatenate([attended_all[i] for i in range(span_count)], axis=1)

    hidden_mid = tokens[...].astype(F32) + dot_nn(attended[...], out_whole[...])
    outward[...] = hidden_mid
    scaled, inverse = normalize_parts(hidden_mid)
    normed[...] = (scaled * gains_out[1:2, :]).astype(BF)
    normed_left[...] = jnp.transpose(normed[...])
    attended_left[...] = jnp.transpose(attended[...])
    normed_grad[...] = jnp.zeros_like(normed_grad)
    down_gather.end()
    block = 256

    for number, (start, size) in enumerate(parts):
        if number + 1 < len(parts):
            gate_up_gathers[number + 1].share()
        gate_up_gathers[number].end()

        def step(index, unused):
            offset = index * block
            gate_at = pl.ds(pl.multiple_of(2 * start + offset, block), block)
            up_at = pl.ds(pl.multiple_of(2 * start + size + offset, block), block)
            here = pl.ds(pl.multiple_of(start + offset, block), block)
            there = pl.ds(pl.multiple_of(hidden + start + offset, block), block)
            gate = dot_nn(normed[...], gate_up_whole[:, gate_at])
            upward = dot_nn(normed[...], gate_up_whole[:, up_at])
            activation_grad = dot_nt(out_grad[...], down_whole[here, :])
            sigmoid = jax.nn.sigmoid(gate)
            swish = gate * sigmoid
            activation = (swish * upward).astype(BF)
            activation_left[here, :] = jnp.transpose(activation)
            gate_grad = (
                activation_grad * upward * sigmoid * (1.0 + gate * (1.0 - sigmoid))
            ).astype(BF)
            up_grad = (activation_grad * swish).astype(BF)
            gate_up_grad[:, here] = gate_grad
            gate_up_grad[:, there] = up_grad
            outward[...] += dot_nn(activation, down_whole[here, :])
            normed_grad[...] += dot_nt(gate_grad, gate_up_whole[:, gate_at]) + dot_nt(
                up_grad, gate_up_whole[:, up_at]
            )
            return unused

        lax.fori_loop(0, size // block, step, 0)
    layer_low[...] = outward[...].astype(BF)
    hidden_mid = tokens[...].astype(F32) + dot_nn(attended[...], out_whole[...])
    scaled, inverse = normalize_parts(hidden_mid)
    grad = out_grad[...].astype(F32) + norm_backward(
        normed_grad[...], scaled, inverse, gains_out[1:2, :]
    )
    mid_grad[...] = grad
    mid_grad_low[...] = grad.astype(BF)
    attended_grad[...] = dot_nt(mid_grad_low[...], out_whole[...]).astype(BF)

    for copy in gains_copies:
        copy.wait_send()
    for exchange in (first_exchange, counts_exchange, attended_exchange):
        exchange.finish()
    for step in range(span_count):

        @pl.when((span - step >= 0) & (span < last))
        def sent_up():
            pass_on(jnp.maximum(span - step, 0), step, 0).wait_send()

        @pl.when((span + step <= last) & (span > 0))
        def sent_down():
            pass_on(jnp.minimum(span + step, last), step, 1).wait_send()

    qkv_copy.wait()


def hidden_parts(hidden):
    count = hidden // 256
    sizes = [256 * ((count + 3 - i) // 4) for i in range(4)]
    return [(sum(sizes[:i]), size) for i, size in enumerate(sizes) if size]


def forward_call(
    dp_count, span_count, slot_of, order, tokens, first_values, segments, gains_mine, qkv_mine,
    out_mine, gate_up_mine, down_mine, cosine, sine, out_grad,
):
    rows, width = tokens.shape
    group = width // span_count
    heads = group // HEAD_DIM
    owned = qkv_mine.shape[0]
    doubled = gate_up_mine.shape[1]
    hidden = doubled // 2
    gathers = 3 + len(hidden_parts(hidden))
    slots = Gather.slots(dp_count // 4)
    dma = pltpu.SemaphoreType.DMA
    by_span = (span_count, rows, group)
    return pl.pallas_call(
        functools.partial(forward_kernel, dp_count, span_count),
        out_shape=(
            jax.ShapeDtypeStruct((width, 3 * group), BF),
            jax.ShapeDtypeStruct((width, span_count * rows), BF),
            jax.ShapeDtypeStruct((8, 128), F32),
            jax.ShapeDtypeStruct((8, width), F32),
            jax.ShapeDtypeStruct(by_span, BF),
            jax.ShapeDtypeStruct(by_span, BF),
            jax.ShapeDtypeStruct(by_span, BF),
            jax.ShapeDtypeStruct(by_span, F32),
            jax.ShapeDtypeStruct((span_count, rows, 128), F32),
            jax.ShapeDtypeStruct((rows, width), BF),
            jax.ShapeDtypeStruct((rows, width), F32),
            jax.ShapeDtypeStruct((rows, width), BF),
            jax.ShapeDtypeStruct((rows, doubled), BF),
            jax.ShapeDtypeStruct((width, rows), BF),
            jax.ShapeDtypeStruct((hidden, rows), BF),
            jax.ShapeDtypeStruct((width, rows), BF),
            jax.ShapeDtypeStruct((rows, width), BF),
        ),
        in_specs=[pl.BlockSpec(memory_space=pltpu.SMEM)] * 2
        + [full_spec()] * 4
        + [any_spec()]
        + [full_spec()] * 6,
        out_specs=(any_spec(),) + (full_spec(),) * 16,
        scratch_shapes=[
            pltpu.VMEM((owned, 3 * group), F32),
            pltpu.VMEM((width, width), BF),
            pltpu.VMEM((width, doubled), BF),
            pltpu.VMEM((hidden, width), BF),
            pltpu.VMEM((width, 3 * group), BF),
            pltpu.VMEM((rows, width), BF),
            pltpu.VMEM((rows, width), BF),
            pltpu.VMEM((rows, width), F32),
            pltpu.VMEM((rows, width), F32),
            pltpu.VMEM((dp_count, 8, owned), F32),
            pltpu.VMEM((span_count, 8, 128), F32),
            pltpu.VMEM((span_count, 8, 128), F32),
            pltpu.VMEM(by_span, BF),
            pltpu.VMEM(by_span, BF),
            pltpu.VMEM((span_count, rows, width), BF),
            pltpu.VMEM((heads, span_count, rows, rows), F32),
            pltpu.VMEM(by_span, BF),
            pltpu.VMEM(by_span, BF),
            dma((gathers, slots)),
            dma((gathers, slots)),
            dma((dp_count,)),
            dma((dp_count,)),
            dma((span_count,)),
            dma((span_count,)),
            dma((span_count,)),
            dma((span_count,)),
            dma((2, span_count)),
            dma((2, span_count)),
            dma((span_count,)),
            dma((span_count,)),
            dma((5,)),
        ],
        compiler_params=pltpu.CompilerParams(
            collective_id=0, has_side_effects=True, vmem_limit_bytes=61 << 20
        ),
    )(
        slot_of, order, tokens, first_values, segments, gains_mine, qkv_mine, out_mine,
        gate_up_mine, down_mine, cosine, sine, out_grad,
    )


class Pair:
    def __init__(
        self, place, left_whole, left, left_other, right, right_other, send_sems, recv_sems
    ):
        self.place = place
        self.left = left
        self.left_other = left_other
        self.right = right
        self.right_other = right_other
        other = (place.at(place.outer, place.inner, 1 - place.core), place.span)
        self.left_copy = remote(
            left_whole.at[:, 1 - place.core], left_other, send_sems.at[0], recv_sems.at[0], other
        )
        self.own_copy = pltpu.make_async_copy(
            left_whole.at[:, place.core], left, send_sems.at[2]
        )
        self.right_copy = remote(right, right_other, send_sems.at[1], recv_sems.at[1], other)

    def lend_left(self):
        self.own_copy.start()
        self.left_copy.start()

    def wait(self):
        self.own_copy.wait()
        self.left_copy.wait_recv()
        self.right_copy.wait_recv()

    def finish(self):
        self.left_copy.wait_send()
        self.right_copy.wait_send()

    def product(self, outer, inner, columns):
        chip = outer * self.place.inner_count + inner
        depth = self.right.shape[1]
        found = None
        for block in range(self.right.shape[0]):
            at = slice(block * depth, (block + 1) * depth)
            mine = dot_nn(self.left[chip, :, at], self.right[block, :, columns])
            theirs = dot_nn(self.left_other[chip, :, at], self.right_other[block, :, columns])
            found = mine + theirs if found is None else found + mine + theirs
        return found


class Piece:
    def __init__(self, pair, columns, kind, buffers, sems, result):
        self.pair = pair
        self.place = pair.place
        self.columns = columns
        self.kind = kind
        self.send1, self.recv1, self.send2, self.recv2 = buffers[:4]
        mine = self.recv1.at[0, pair.place.inner if kind == 0 else pair.place.outer]
        self.line = [mine] + list(buffers[4:])
        self.send_sems, self.recv_sems = sems
        self.result = result
        self.sent = []

    def send(self, source, target, slot, far_slot, dp, span=None):
        copy = remote(
            source,
            target,
            self.send_sems.at[slot],
            self.recv_sems.at[far_slot],
            (dp, self.place.span if span is None else span),
        )
        copy.start()
        self.sent.append(copy)

    def arrived(self, target, slot):
        remote(
            target, target, self.send_sems.at[slot], self.recv_sems.at[slot], (self.place.dp, self.place.span)
        ).wait_recv()

    def across(self):
        place = self.place
        return place.at(1 - place.outer, place.inner, place.core)

    def beside(self, offset):
        place = self.place
        return place.at(place.outer, place.inner_plus(offset), place.core)

    def product(self, outer, inner):
        return self.pair.product(outer, inner, self.columns)

    def first(self):
        place, count = self.place, self.place.inner_count
        if self.kind == 0:
            for inner in range(count):
                self.send1[0, inner] = self.product(1 - place.outer, inner).astype(BF)
            self.send(self.send1.at[0], self.recv1.at[0], 0, 0, self.across())
            return
        for offset in range(1, count):
            for outer in range(2):
                self.send1[offset - 1, outer] = self.product(
                    outer, place.inner_plus(offset)
                ).astype(BF)
            self.send(
                self.send1.at[offset - 1],
                self.recv1.at[count - offset - 1],
                offset - 1,
                count - offset - 1,
                self.beside(offset),
            )

    def second(self):
        place, count = self.place, self.place.inner_count
        base = count
        if self.kind == 0:
            self.arrived(self.recv1.at[0], 0)
            for offset in range(1, count):
                inner = place.inner_plus(offset)
                total = self.product(place.outer, inner) + self.recv1[0, inner].astype(F32)
                self.send2[offset - 1] = total.astype(BF)
                self.send(
                    self.send2.at[offset - 1],
                    self.recv2.at[count - offset - 1],
                    base + offset - 1,
                    base + count - offset - 1,
                    self.beside(offset),
                )
            return
        total = self.product(1 - place.outer, place.inner)
        for offset in range(1, count):
            self.arrived(self.recv1.at[offset - 1], offset - 1)
            total = total + self.recv1[offset - 1, 1 - place.outer].astype(F32)
        self.send2[0] = total.astype(BF)
        self.send(self.send2.at[0], self.recv2.at[0], base, base, self.across())

    def total(self):
        place, count = self.place, self.place.inner_count
        base = count
        total = self.product(place.outer, place.inner)
        if self.kind == 0:
            total = total + self.recv1[0, place.inner].astype(F32)
            for offset in range(1, count):
                self.arrived(self.recv2.at[offset - 1], base + offset - 1)
                total = total + self.recv2[offset - 1].astype(F32)
            return total
        for offset in range(1, count):
            total = total + self.recv1[offset - 1, place.outer].astype(F32)
        self.arrived(self.recv2.at[0], base)
        return total + self.recv2[0].astype(F32)


    def shape_of_line(self):
        place = self.place
        half = place.span_count // 2
        low = place.span < half
        depth = jnp.where(low, place.span, place.span_count - 1 - place.span)
        inward = jnp.where(low, place.span + 1, place.span - 1)
        outward = jnp.where(low, place.span - 1, place.span + 1)
        outward = jnp.clip(outward, 0, place.span_count - 1)
        return half, depth, inward, outward

    def line_copy(self, source, target, slot, span):
        base = 2 * self.place.inner_count
        return remote(
            source,
            target,
            self.send_sems.at[base + slot],
            self.recv_sems.at[base + slot],
            (self.place.dp, span),
        )

    def send_inward(self):
        half, depth, inward, outward = self.shape_of_line()
        sum_here, from_out, from_mid = self.line

        @pl.when(depth == half - 1)
        def cross():
            self.line_copy(sum_here, from_mid, 1, inward).start()

        @pl.when(depth < half - 1)
        def in_():
            self.line_copy(sum_here, from_out, 0, inward).start()

    def line_start(self):
        half, depth, inward, outward = self.shape_of_line()
        sum_here, from_out, from_mid = self.line
        sum_here[...] = self.total().astype(BF)

        @pl.when(depth == 0)
        def go():
            self.send_inward()

    def line_in(self):
        half, depth, inward, outward = self.shape_of_line()
        sum_here, from_out, from_mid = self.line

        @pl.when(depth > 0)
        def go():
            self.line_copy(from_out, from_out, 0, outward).wait_recv()
            sum_here[...] = (sum_here[...].astype(F32) + from_out[...].astype(F32)).astype(BF)
            self.send_inward()

    def line_mid(self):
        half, depth, inward, outward = self.shape_of_line()
        sum_here, from_out, from_mid = self.line

        @pl.when(depth == half - 1)
        def go():
            self.line_copy(from_mid, from_mid, 1, inward).wait_recv()
            self.result[...] = (
                sum_here[...].astype(F32) + from_mid[...].astype(F32)
            ).astype(BF)

            @pl.when(depth > 0)
            def out():
                self.line_copy(self.result, self.result, 2, outward).start()

    def line_out(self):
        half, depth, inward, outward = self.shape_of_line()

        @pl.when(depth < half - 1)
        def go():
            self.line_copy(self.result, self.result, 2, inward).wait_recv()

            @pl.when(depth > 0)
            def out():
                self.line_copy(self.result, self.result, 2, outward).start()

    def line_finish(self):
        half, depth, inward, outward = self.shape_of_line()
        sum_here, from_out, from_mid = self.line

        @pl.when(depth == half - 1)
        def cross():
            self.line_copy(sum_here, from_mid, 1, inward).wait_send()

        @pl.when(depth < half - 1)
        def in_():
            self.line_copy(sum_here, from_out, 0, inward).wait_send()

        @pl.when(depth > 0)
        def out():
            self.line_copy(self.result, self.result, 2, outward).wait_send()


    def spread_start(self, results):
        place = self.place
        base = 2 * place.inner_count
        self.results = results
        results[place.span, :, self.columns] = self.total().astype(BF)
        for offset in range(1, place.span_count):
            peer = lax.rem(place.span + offset, place.span_count)
            block = results.at[place.span, :, self.columns]
            self.send(
                block, block, base + offset, base + place.span_count - offset, place.dp, peer
            )

    def spread_wait(self):
        place = self.place
        base = 2 * place.inner_count
        for offset in range(1, place.span_count):
            peer = lax.rem(place.span + offset, place.span_count)
            self.arrived(self.results.at[peer, :, self.columns], base + offset)

    def finish(self):
        for copy in self.sent:
            copy.wait_send()


def cut_columns(width):
    if width > 4096:
        quarter = width // 4 // 128 * 128
        return [slice(i * quarter, (i + 1) * quarter if i < 3 else width) for i in range(4)]
    half = width // 2 // 128 * 128
    return [slice(0, half), slice(half, width)]


def piece_scratch(inner_count, rows, columns, kind, on_line):
    width = columns.stop - columns.start
    if kind == 0:
        shapes = [(1, inner_count, rows, width)] * 2 + [(inner_count - 1, rows, width)] * 2
    else:
        shapes = [(inner_count - 1, 2, rows, width)] * 2 + [(1, rows, width)] * 2
    if on_line:
        shapes += [(rows, width)] * 2
    return shapes


ORDER = (
    ("wait_pair", "down", 0),
    ("first", "down", 0),
    ("first", "down", 1),
    ("wait_pair", "gate_up", 0),
    ("first", "gate_up", 2),
    ("first", "gate_up", 3),
    ("wait_grad", "", 0),
    ("wait_pair", "out", 0),
    ("attend", "", 0),
    ("attend", "", 1),
    ("first", "gate_up", 0),
    ("attend", "", 2),
    ("close", "", 0),
    ("send_blended", "", 0),
    ("second", "down", 0),
    ("second", "gate_up", 2),
    ("line_start", "down", 0),
    ("lend_mixed", "", 0),
    ("second", "down", 1),
    ("second", "gate_up", 0),
    ("line_start", "gate_up", 2),
    ("first", "out", 0),
    ("first", "out", 1),
    ("line_in", "down", 0),
    ("second", "gate_up", 3),
    ("line_in", "gate_up", 2),
    ("wait_pair", "qkv", 0),
    ("first", "gate_up", 1),
    ("line_start", "gate_up", 0),
    ("line_mid", "down", 0),
    ("second", "out", 1),
    ("line_start", "down", 1),
    ("second", "out", 0),
    ("line_in", "gate_up", 0),
    ("line_start", "gate_up", 3),
    ("first", "qkv", 0),
    ("line_start", "out", 1),
    ("wait_blended", "", 0),
    ("line_in", "down", 1),
    ("line_mid", "gate_up", 2),
    ("second", "gate_up", 1),
    ("second", "qkv", 0),
    ("line_start", "out", 0),
    ("line_out", "down", 0),
    ("first", "qkv", 1),
    ("line_in", "gate_up", 3),
    ("line_mid", "gate_up", 0),
    ("chain", "", 0),
    ("line_out", "gate_up", 2),
    ("spread_start", "qkv", 0),
    ("second", "qkv", 1),
    ("line_mid", "down", 1),
    ("line_in", "out", 0),
    ("line_mid", "gate_up", 3),
    ("line_start", "gate_up", 1),
    ("chain", "", 1),
    ("line_in", "out", 1),
    ("spread_start", "qkv", 1),
    ("spread_wait", "qkv", 0),
    ("line_mid", "out", 0),
    ("line_mid", "out", 1),
    ("line_out", "out", 1),
    ("line_out", "down", 1),
    ("line_in", "gate_up", 1),
    ("line_out", "gate_up", 0),
    ("line_out", "gate_up", 3),
    ("chain", "", 2),
    ("line_mid", "gate_up", 1),
    ("chain_end", "", 0),
    ("line_out", "gate_up", 1),
    ("line_out", "out", 0),
    ("spread_wait", "qkv", 1),
)


def backward_kernel(
    dp_count,
    span_count,
    slot_of,
    order,
    gate_up_left,
    gate_up_right,
    down_left,
    down_right,
    out_left,
    out_right,
    qkv_left,
    attended_grad,
    query,
    key,
    value,
    raw,
    lse,
    counts,
    cosine,
    sine,
    qkv_copy,
    gate_up_result,
    down_result,
    out_result,
    qkv_result,
    blended_result,
    normed_result,
    gate_up_own,
    gate_up_other,
    gate_up_right_other,
    down_own,
    down_other,
    down_right_other,
    out_own,
    out_other,
    out_right_other,
    qkv_own,
    qkv_other,
    mixed_other,
    mixed,
    grad_send,
    grad_all,
    key_sum,
    value_sum,
    key_turned,
    query_sum,
    blended_all,
    chain,
    pair_send,
    pair_recv,
    piece_send,
    piece_recv,
    grad_send_sem,
    grad_recv_sem,
    blended_send_sem,
    blended_recv_sem,
    chain_send,
    chain_recv,
    *piece_buffers,
):
    place = Place(dp_count, span_count)
    span, last = place.span, span_count - 1
    rows, width = attended_grad.shape
    group = width // span_count
    heads = group // HEAD_DIM

    place.greet_all()
    for index in range(span_count):
        grad_send[index] = attended_grad[:, index * group : (index + 1) * group]
    grad_exchange = Exchange(place, grad_send, grad_all, grad_send_sem, grad_recv_sem)
    grad_exchange.start()
    pairs = [
        Pair(place, *members, pair_send.at[i], pair_recv.at[i])
        for i, members in enumerate(
            (
                (gate_up_left, gate_up_own, gate_up_other, gate_up_right, gate_up_right_other),
                (down_left, down_own, down_other, down_right, down_right_other),
                (out_left, out_own, out_other, out_right, out_right_other),
                (qkv_left, qkv_own, qkv_other, mixed, mixed_other),
            )
        )
    ]
    named = dict(zip(("gate_up", "down", "out", "qkv"), pairs))
    for name in ("out", "down", "gate_up"):
        named[name].lend_left()
        named[name].right_copy.start()
    named["qkv"].lend_left()

    free = list(piece_buffers)
    pieces = []
    for pair, result, on_line in zip(
        pairs, (gate_up_result, down_result, out_result, qkv_result), (True, True, True, False)
    ):
        members = []
        for i, columns in enumerate(cut_columns(pair.right.shape[2])):
            number = 6 if on_line else 4
            buffers, free = free[:number], free[number:]
            at = len(pieces) * 4 + i
            members.append(
                Piece(
                    pair,
                    columns,
                    i % 2,
                    buffers,
                    (piece_send.at[at], piece_recv.at[at]),
                    result.at[:, columns] if on_line else None,
                )
            )
        pieces.append(members)
    pieces = dict(zip(("gate_up", "down", "out", "qkv"), pieces))

    def clear(index, unused):
        key_sum[index] = jnp.zeros((rows, group), F32)
        value_sum[index] = jnp.zeros((rows, group), F32)
        return unused

    lax.fori_loop(0, span_count, clear, 0)

    def clear_chain(index, unused):
        chain[index] = jnp.zeros(chain.shape[1:], BF)
        return unused

    @pl.when(span == 0)
    def nothing_from_below():
        lax.fori_loop(1, span_count + 1, clear_chain, 0)

    @pl.when(span == last)
    def nothing_from_above():
        lax.fori_loop(0, span_count, clear_chain, 0)

    cuts = counts[...]
    bounds = [cuts[i : i + 1, 0:1] for i in range(3)]

    def turned_back(rows_in, position):
        cos_here, sin_here = angles_of(cosine, sine, position, heads)
        low = rows_in.astype(BF).astype(F32)
        return (low * cos_here - swap_halves(low) * sin_here).astype(BF)

    def turn_keys(position, unused):
        key_turned[position] = jnp.transpose(key[position])
        return unused

    lax.fori_loop(0, span_count, turn_keys, 0)

    def attend_back(position, unused):
        query_here = (query[position].astype(F32) * SCALE).astype(BF)
        grad_here = grad_all[slot_of[position]]
        query_parts = [head_part(query_here, head) for head in range(heads)]
        grad_parts = [head_part(grad_here, head) for head in range(heads)]
        query_stack = jnp.concatenate(query_parts, axis=0)
        grad_stack = jnp.concatenate(grad_parts, axis=0)
        agreed = jnp.transpose(grad_here.astype(F32) * raw[position])
        logs = jnp.transpose(lse[position])
        query_position = (
            lax.broadcasted_iota(jnp.int32, (1, rows), 1) + position * rows
        ).astype(F32)
        start = jnp.zeros((1, rows), F32)
        for cut in bounds:
            start = jnp.where(query_position >= cut, cut, start)
        query_sum[...] = jnp.zeros((group, rows), F32)

        def block(other, unused):
            key_here, value_here, key_back = key[other], value[other], key_turned[other]
            key_position = (
                lax.broadcasted_iota(jnp.int32, (rows, 1), 0) + other * rows
            ).astype(F32)
            allowed = (key_position <= query_position) & (key_position >= start)
            lows, grads = [], []
            for head in range(heads):
                at = slice(head * HEAD_DIM, (head + 1) * HEAD_DIM)
                scores = dot_nt(key_here, query_parts[head])
                weights = jnp.where(allowed, jnp.exp(scores - logs[head : head + 1]), 0.0)
                weights_grad = dot_nt(value_here, grad_parts[head])
                delta = jnp.sum(agreed[at], axis=0, keepdims=True)
                scores_grad = (weights * (weights_grad - delta)).astype(BF)
                lows.append(weights.astype(BF))
                grads.append(scores_grad)
                query_sum[at, :] += dot_nn(key_back[at], scores_grad)
            key_sum[other] += dot_nn(jnp.concatenate(grads, axis=1), query_stack)
            value_sum[other] += dot_nn(jnp.concatenate(lows, axis=1), grad_stack)
            return unused

        lax.fori_loop(0, position + 1, block, 0)
        mixed[position, :, :group] = turned_back(
            jnp.transpose(query_sum[...]) * SCALE, position
        )
        return unused

    def close(position, unused):
        mixed[position, :, group : 2 * group] = turned_back(key_sum[position], position)
        mixed[position, :, 2 * group :] = (
            BLEND_MIX * value_sum[position].astype(BF).astype(F32)
        ).astype(BF)
        return unused

    blended_send = grad_send
    blended_exchange = Exchange(
        place, blended_send, blended_all, blended_send_sem, blended_recv_sem
    )

    def normed_grad(block):
        return dot_nt(mixed[order[block]], qkv_copy[...])

    def pass_on(block, way):
        return remote(
            chain.at[block + 1 - way],
            chain.at[block + 1 - way],
            chain_send.at[way, block],
            chain_recv.at[way, block],
            (place.dp, jnp.minimum(span + 1, last) if way == 0 else jnp.maximum(span - 1, 0)),
        )

    def chain_step(step):
        up = last + span - step
        down = step - (last - span)

        @pl.when((span <= step) & (up > span))
        def going_up():
            block = jnp.clip(up, 0, last)

            @pl.when(span > 0)
            def more():
                pass_on(block, 0).wait_recv()

            chain[block + 1] = (normed_grad(block) + chain[block + 1].astype(F32)).astype(BF)
            pass_on(block, 0).start()

        @pl.when((down >= 0) & (down < span))
        def going_down():
            block = jnp.clip(down, 0, last)

            @pl.when(span < last)
            def more():
                pass_on(block, 1).wait_recv()

            chain[block] = (normed_grad(block) + chain[block].astype(F32)).astype(BF)
            pass_on(block, 1).start()

    def chain_end():
        @pl.when(span > 0)
        def from_below():
            pass_on(span, 0).wait_recv()

        @pl.when(span < last)
        def from_above():
            pass_on(span, 1).wait_recv()

        normed_result[...] = (
            normed_grad(span) + chain[span + 1].astype(F32) + chain[span].astype(F32)
        )

    half = span_count // 2
    ranges = ((0, half), (half, last), (last, span_count))

    def send_blended():
        grad_exchange.finish()
        for index in range(span_count):
            blended_send[index] = value_sum[order[index]].astype(BF)
        blended_exchange.start()

    def keep_blended():
        blended_exchange.wait()
        blended_result[...] = jnp.concatenate(
            [blended_all[i] for i in range(span_count)], axis=1
        )

    single = {
        "wait_grad": grad_exchange.wait,
        "close": lambda: lax.fori_loop(0, span_count, close, 0),
        "lend_mixed": named["qkv"].right_copy.start,
        "send_blended": send_blended,
        "wait_blended": keep_blended,
        "chain_end": chain_end,
    }
    for action, name, number in ORDER:
        if action in single:
            single[action]()
        elif action == "wait_pair":
            named[name].wait()
        elif action == "attend":
            lax.fori_loop(*ranges[number], attend_back, 0)
        elif action == "chain":
            for step in [number] if number < 2 else range(2, last):
                chain_step(step)
        elif action == "spread_start":
            pieces[name][number].spread_start(qkv_result)
        else:
            getattr(pieces[name][number], action)()

    for pair in pairs:
        pair.finish()
    blended_exchange.finish()
    for name, members in pieces.items():
        for member in members:
            if name != "qkv":
                member.line_finish()
            member.finish()
    for step in range(last):
        up = last + span - step
        down_block = step - (last - span)

        @pl.when((span <= step) & (up > span))
        def sent_up():
            pass_on(jnp.clip(up, 0, last), 0).wait_send()

        @pl.when((down_block >= 0) & (down_block < span))
        def sent_down():
            pass_on(jnp.clip(down_block, 0, last), 1).wait_send()


def backward_call(dp_count, span_count, slot_of, order, factors, others):
    (gate_up_left, gate_up_right, down_left, down_right, out_left, out_right, qkv_left) = factors
    rows, width = others[0].shape
    group = width // span_count
    inner_count = dp_count // 4
    dma = pltpu.SemaphoreType.DMA
    by_span = (span_count, rows, group)
    mixed_shape = (span_count, rows, 3 * group)

    def less(left):
        return (left.shape[0],) + left.shape[2:]

    scratch = []
    for left, columns_in, on_line in (
        (gate_up_left, gate_up_right.shape[2], True),
        (down_left, down_right.shape[2], True),
        (out_left, out_right.shape[2], True),
        (qkv_left, 3 * group, False),
    ):
        for i, columns in enumerate(cut_columns(columns_in)):
            scratch += [
                pltpu.VMEM(shape, BF)
                for shape in piece_scratch(inner_count, left.shape[2], columns, i % 2, on_line)
            ]
    slots = 2 * inner_count + max(3, span_count)
    return pl.pallas_call(
        functools.partial(backward_kernel, dp_count, span_count),
        out_shape=(
            jax.ShapeDtypeStruct((gate_up_left.shape[2], gate_up_right.shape[2]), BF),
            jax.ShapeDtypeStruct((down_left.shape[2], down_right.shape[2]), BF),
            jax.ShapeDtypeStruct((out_left.shape[2], out_right.shape[2]), BF),
            jax.ShapeDtypeStruct((span_count, qkv_left.shape[2], 3 * group), BF),
            jax.ShapeDtypeStruct((rows, width), BF),
            jax.ShapeDtypeStruct((rows, width), F32),
        ),
        in_specs=[pl.BlockSpec(memory_space=pltpu.SMEM)] * 2
        + [any_spec(), full_spec()] * 3
        + [any_spec()]
        + [full_spec()] * len(others),
        out_specs=(full_spec(),) * 6,
        scratch_shapes=[
            pltpu.VMEM(less(gate_up_left), BF),
            pltpu.VMEM(less(gate_up_left), BF),
            pltpu.VMEM(gate_up_right.shape, BF),
            pltpu.VMEM(less(down_left), BF),
            pltpu.VMEM(less(down_left), BF),
            pltpu.VMEM(down_right.shape, BF),
            pltpu.VMEM(less(out_left), BF),
            pltpu.VMEM(less(out_left), BF),
            pltpu.VMEM(out_right.shape, BF),
            pltpu.VMEM(less(qkv_left), BF),
            pltpu.VMEM(less(qkv_left), BF),
            pltpu.VMEM(mixed_shape, BF),
            pltpu.VMEM(mixed_shape, BF),
            pltpu.VMEM(by_span, BF),
            pltpu.VMEM(by_span, BF),
            pltpu.VMEM(by_span, F32),
            pltpu.VMEM(by_span, F32),
            pltpu.VMEM((span_count, group, rows), BF),
            pltpu.VMEM((group, rows), F32),
            pltpu.VMEM(by_span, BF),
            pltpu.VMEM((span_count + 1, rows, width), BF),
            dma((4, 3)),
            dma((4, 3)),
            dma((16, slots)),
            dma((16, slots)),
            dma((span_count,)),
            dma((span_count,)),
            dma((span_count,)),
            dma((span_count,)),
            dma((2, span_count)),
            dma((2, span_count)),
        ]
        + scratch,
        compiler_params=pltpu.CompilerParams(
            collective_id=1, has_side_effects=True, vmem_limit_bytes=61 << 20
        ),
    )(slot_of, order, *factors, *others)


def update_rows(master, first_state, second_state, gradient, rate, decay):
    next_first = BETA_FIRST * first_state + (1.0 - BETA_FIRST) * gradient
    next_second = BETA_SECOND * second_state + (1.0 - BETA_SECOND) * gradient * gradient
    first_hat = next_first * (1.0 / (1.0 - BETA_FIRST**STEP))
    second_hat = next_second * (1.0 / (1.0 - BETA_SECOND**STEP))
    new_master = master - rate * (first_hat / (jnp.sqrt(second_hat) + ADAM_EPS) + decay * master)
    return (new_master, next_first, next_second)


def finish_kernel(
    qkv_total,
    out_total,
    gate_up_total,
    down_total,
    gains,
    gains_first,
    gains_second,
    tokens,
    mid_grad,
    normed_grad,
    gains_rows,
    blended_grad,
    layer_low,
    qkv,
    qkv_first,
    qkv_second,
    out,
    out_first,
    out_second,
    gate_up,
    gate_up_first,
    gate_up_second,
    down,
    down_first,
    down_second,
    layer_out,
    tokens_grad,
    values_grad,
    new_gains,
    new_gains_first,
    new_gains_second,
    *rest,
):
    results, held, sums, in_sem, out_sem = rest[:12], rest[12:24], rest[24], rest[25], rest[26]
    states = (
        (qkv, qkv_first, qkv_second),
        (out, out_first, out_second),
        (gate_up, gate_up_first, gate_up_second),
        (down, down_first, down_second),
    )
    width = tokens.shape[1]
    span_count = qkv_total.shape[0]
    group = width // span_count

    def qkv_rows(part):
        def rows(at):
            return jnp.concatenate(
                [
                    qkv_total[i, at, part * group : (part + 1) * group].astype(F32)
                    for i in range(span_count)
                ],
                axis=1,
            )

        return rows

    def rows_of(total, columns):
        return lambda at: total[at, columns].astype(F32)

    parts = []
    for columns in cut_columns(gate_up_total.shape[1]):
        parts.append((2, columns, rows_of(gate_up_total, columns)))
    for part in range(3):
        parts.append((0, slice(part * width, (part + 1) * width), qkv_rows(part)))
    for columns in cut_columns(width):
        parts.append((3, columns, rows_of(down_total, columns)))
    parts.append((1, slice(0, width), rows_of(out_total, slice(0, width))))

    def moves(number, source, target, sems):
        weight, columns, _ = parts[number]
        return [
            pltpu.make_async_copy(
                source[i].at[:, columns], target[i].at[:, columns], sems.at[number, i]
            )
            for i in range(3)
        ]

    loads, stores = [], []
    for number, (weight, _, _) in enumerate(parts):
        here = held[3 * weight : 3 * weight + 3]
        loads.append(moves(number, states[weight], here, in_sem))
        stores.append(moves(number, here, results[3 * weight : 3 * weight + 3], out_sem))
        for copy in loads[-1]:
            copy.start()

    residual = tokens[...].astype(F32)
    scaled, inverse = normalize_parts(residual)
    tokens_grad[...] = mid_grad[...] + norm_backward(
        normed_grad[...], scaled, inverse, gains_rows[0:1, :]
    )
    layer_out[...] = layer_low[...]
    sums[...] = jnp.zeros_like(sums)
    values_grad[...] = (1.0 - BLEND_MIX) * blended_grad[...].astype(F32)

    for number, (weight, columns, total) in enumerate(parts):
        here = held[3 * weight : 3 * weight + 3]
        for copy in loads[number]:
            copy.wait()
        owned = here[0].shape[0]
        wants_sum = weight in (0, 2)

        def step(index, unused):
            at = pl.ds(pl.multiple_of(index * 16, 16), 16)
            gradient = total(at)
            master = here[0][at, columns]
            if wants_sum:
                partial = jnp.sum(
                    gradient * master.astype(BF).astype(F32), axis=1, keepdims=True
                )
                lane = 0 if weight == 0 else 1
                slot = lax.broadcasted_iota(jnp.int32, (16, 128), 1) == lane
                sums[at, :] += jnp.where(slot, partial, 0.0)
            updated = update_rows(
                master,
                here[1][at, columns],
                here[2][at, columns],
                gradient,
                MATRIX_RATE,
                MATRIX_DECAY,
            )
            for i in range(3):
                here[i][at, columns] = updated[i]
            return unused

        lax.fori_loop(0, owned // 16, step, 0)
        for copy in stores[number]:
            copy.start()

    gain = gains[...]
    gains_total = jnp.transpose(sums[...])[:2, :] / gain.astype(BF).astype(F32)
    updated = update_rows(gain, gains_first[...], gains_second[...], gains_total, GAIN_RATE, 0.0)
    new_gains[...], new_gains_first[...], new_gains_second[...] = updated
    for group_of_copies in stores:
        for copy in group_of_copies:
            copy.wait()


def finish_call(totals, gains_states, token_parts, states):
    flat = [member for weight in states for member in weight]
    rows, width = token_parts[0].shape
    gains_shape = jax.ShapeDtypeStruct(gains_states[0].shape, F32)
    dma = pltpu.SemaphoreType.DMA
    count = len(cut_columns(totals[2].shape[1])) + 3 + 2 + 1
    return pl.pallas_call(
        finish_kernel,
        out_shape=(
            jax.ShapeDtypeStruct((rows, width), BF),
            jax.ShapeDtypeStruct((rows, width), F32),
            jax.ShapeDtypeStruct((rows, width), F32),
            gains_shape,
            gains_shape,
            gains_shape,
        )
        + tuple(jax.ShapeDtypeStruct(member.shape, F32) for member in flat),
        in_specs=[full_spec()] * 13 + [any_spec()] * 12,
        out_specs=(full_spec(),) * 6 + (any_spec(),) * 12,
        scratch_shapes=[pltpu.VMEM(member.shape, F32) for member in flat]
        + [
            pltpu.VMEM((gains_states[0].shape[1], 128), F32),
            dma((count, 3)),
            dma((count, 3)),
        ],
        compiler_params=pltpu.CompilerParams(vmem_limit_bytes=VMEM_BYTES),
    )(*totals, *gains_states, *token_parts, *flat)


def to_heads(rows, span_count):
    return lax.all_to_all(
        rows.reshape(rows.shape[0], span_count, rows.shape[1] // span_count),
        "seq",
        split_axis=1,
        concat_axis=0,
        tiled=True,
    ).reshape(rows.shape[0] * span_count, rows.shape[1] // span_count)


def to_spans(columns, span_count):
    rows_here = columns.shape[0] // span_count
    got = lax.all_to_all(
        columns.reshape(span_count, rows_here, columns.shape[1]),
        "seq",
        split_axis=0,
        concat_axis=0,
        tiled=True,
    )
    return jnp.transpose(got, (1, 0, 2)).reshape(rows_here, columns.shape[1] * span_count)


def on_device(
    tokens,
    first_values,
    out_grad,
    segments,
    span_order,
    qkv_weight,
    out_weight,
    gate_up_weight,
    down_weight,
    norm_gains,
    first_qkv,
    first_out,
    first_gate_up,
    first_down,
    first_gains,
    second_qkv,
    second_out,
    second_gate_up,
    second_down,
    second_gains,
):
    span_count = lax.axis_size("seq")
    mine = lax.axis_index("seq")
    owned_rows, triple = qkv_weight.shape
    model_width = triple // 3
    group = model_width // span_count
    group_heads = group // HEAD_DIM
    residual = tokens[0].astype(F32)
    rows_here = residual.shape[0]
    length = rows_here * span_count
    hidden_width = gate_up_weight.shape[1] // 2

    dp_count = lax.axis_size("dp")
    gains_owned = norm_gains.astype(BF).astype(F32)
    in_kernels = (
        length * model_width <= 1 << 20
        and dp_count % 4 == 0
        and dp_count >= 8
        and span_count % 2 == 0
        and group % 128 == 0
        and span_count * HEAD_DIM // 2 <= 128
        and hidden_width % 256 == 0
    )
    if in_kernels:
        slot_of = jnp.sum(
            jnp.where(
                span_order[None, :] == jnp.arange(span_count, dtype=jnp.int32)[:, None],
                jnp.arange(span_count, dtype=jnp.int32)[None, :],
                0,
            ),
            axis=1,
        ).astype(jnp.int32)
        half_width = HEAD_DIM // 2
        lane = lax.broadcasted_iota(jnp.int32, (rows_here, 128), 1)
        position = lax.broadcasted_iota(jnp.int32, (rows_here, 128), 0) + lane // half_width * rows_here
        frequency = jnp.exp(
            (jnp.arange(128, dtype=jnp.int32) % half_width).astype(F32)
            * (-math.log(ROPE_BASE) / half_width)
        )
        angles = lax.optimization_barrier(position).astype(F32) * frequency[None, :]
        cosine, sine = jnp.cos(angles), jnp.sin(angles)
        gains_mine = jnp.pad(jnp.transpose(gains_owned), ((0, 6), (0, 0)))
        (
            qkv_copy, normed_left, counts, gains_rows, query_pos, key_pos, value_pos, raw_pos, lse_pos,
            layer_low, hidden_mid_grad, mid_grad_low, gate_up_grad, normed_mid_left, activation_left,
            attended_left, attended_grad,
        ) = forward_call(
            dp_count, span_count, slot_of, span_order, tokens[0], first_values[0], segments,
            gains_mine, qkv_weight, out_weight, gate_up_weight, down_weight, cosine, sine, out_grad[0],
        )
        def in_blocks(left):
            return left.reshape(dp_count // 2, 2, left.shape[0] // dp_count, left.shape[1])

        factors = (
            in_blocks(normed_mid_left),
            gate_up_grad[None],
            in_blocks(activation_left),
            out_grad,
            in_blocks(attended_left),
            mid_grad_low[None],
            in_blocks(normed_left),
        )
        others = (
            attended_grad,
            query_pos, key_pos, value_pos, raw_pos, lse_pos, counts, cosine, sine, qkv_copy,
        )
        gate_up_total, down_total, out_total, qkv_part, blended_grad, normed_in_grad = backward_call(
            dp_count, span_count, slot_of, span_order, factors, others
        )
        finished = finish_call(
            (qkv_part, out_total, gate_up_total, down_total),
            tuple(jnp.transpose(member) for member in (norm_gains, first_gains, second_gains)),
            (tokens[0], hidden_mid_grad, normed_in_grad, gains_rows, blended_grad, layer_low),
            (
                (qkv_weight, first_qkv, second_qkv),
                (out_weight, first_out, second_out),
                (gate_up_weight, first_gate_up, second_gate_up),
                (down_weight, first_down, second_down),
            ),
        )
        new_gains = tuple(jnp.transpose(member) for member in finished[3:6])
        return (
            tuple(member[None] for member in finished[:3])
            + finished[6::3]
            + new_gains[:1]
            + finished[7::3]
            + new_gains[1:2]
            + finished[8::3]
            + new_gains[2:]
        )

    qkv_owned = qkv_weight.reshape(owned_rows, 3, model_width).astype(BF)
    qkv_mine = lax.dynamic_slice_in_dim(qkv_owned, mine * group, group, 2).reshape(
        owned_rows, 3 * group
    )
    gains_full = lax.all_gather(norm_gains.astype(BF), "dp", axis=0, tiled=True).astype(F32)
    qkv_copy = lax.all_gather(qkv_mine, "dp", axis=0, tiled=True)
    out_copy = lax.all_gather(out_weight.astype(BF), "dp", axis=0, tiled=True)
    gate_up_copy = lax.all_gather(gate_up_weight.astype(BF), "dp", axis=0, tiled=True)
    down_copy = lax.all_gather(down_weight.astype(BF), "dp", axis=0, tiled=True)

    row_index = jnp.arange(length, dtype=jnp.int32)
    owner_table = (row_index // rows_here)[:, None] == jnp.arange(span_count, dtype=jnp.int32)[
        None, :
    ]
    positions = (
        jnp.sum(jnp.where(owner_table, span_order[None, :], 0), axis=1) * rows_here
        + row_index % rows_here
    )
    all_segments = lax.all_gather(segments[0], "seq", axis=0, tiled=True)
    cosine, sine_table = rotary(positions)
    allowed = (all_segments[:, None] == all_segments[None, :]) & (
        positions[None, :] <= positions[:, None]
    )

    scaled_in, inverse_in = normalize_parts(residual)
    normed_in = (scaled_in * gains_full[:, 0]).astype(BF)
    normed_all = lax.all_gather(normed_in, "seq", axis=0, tiled=True)
    first_all = to_heads(first_values[0], span_count)
    mixed = dot_nn(normed_all, qkv_copy)
    queries = rotate(
        mixed[:, :group].reshape(length, group_heads, HEAD_DIM), cosine, sine_table
    ).astype(BF)
    keys = rotate(
        mixed[:, group : 2 * group].reshape(length, group_heads, HEAD_DIM), cosine, sine_table
    ).astype(BF)
    blended = (
        (BLEND_MIX * mixed[:, 2 * group :] + (1.0 - BLEND_MIX) * first_all.astype(F32))
        .astype(BF)
        .reshape(length, group_heads, HEAD_DIM)
    )
    scores = jnp.einsum("qhd,khd->hqk", queries, keys, preferred_element_type=F32) * SCALE
    masked = jnp.where(allowed[None], scores, MASK_FILL)
    highest = jnp.max(masked, axis=-1, keepdims=True)
    raised = jnp.where(allowed[None], jnp.exp(masked - highest), 0.0)
    weights = raised / jnp.sum(raised, axis=-1, keepdims=True)
    weights_low = weights.astype(BF)
    attended_raw = jnp.einsum("hqk,khd->qhd", weights_low, blended, preferred_element_type=F32)
    attended = to_spans(attended_raw.reshape(length, group).astype(BF), span_count)

    hidden_mid = residual + dot_nn(attended, out_copy)
    scaled_mid, inverse_mid = normalize_parts(hidden_mid)
    normed_mid = (scaled_mid * gains_full[:, 1]).astype(BF)
    gate_up = dot_nn(normed_mid, gate_up_copy)
    gate_part = gate_up[:, :hidden_width]
    upward = gate_up[:, hidden_width:]
    sigmoid_gate = jax.nn.sigmoid(gate_part)
    swish_gate = gate_part * sigmoid_gate
    activation = (swish_gate * upward).astype(BF)
    layer_out = (hidden_mid + dot_nn(activation, down_copy)).astype(BF)
    back_rows = out_grad[0]
    activation_grad = dot_nt(back_rows, down_copy)
    gate_up_grad = jnp.concatenate(
        [
            activation_grad * upward * sigmoid_gate * (1.0 + gate_part * (1.0 - sigmoid_gate)),
            activation_grad * swish_gate,
        ],
        axis=1,
    ).astype(BF)
    normed_mid_grad = dot_nt(gate_up_grad, gate_up_copy)
    hidden_mid_grad = back_rows.astype(F32) + norm_backward(
        normed_mid_grad, scaled_mid, inverse_mid, gains_full[:, 1]
    )
    mid_grad_low = hidden_mid_grad.astype(BF)
    attended_grad = to_heads(dot_nt(mid_grad_low, out_copy).astype(BF), span_count)

    heads_grad = attended_grad.reshape(length, group_heads, HEAD_DIM)
    delta = jnp.transpose(jnp.sum(heads_grad.astype(F32) * attended_raw, axis=-1))
    weights_grad = jnp.einsum("qhd,khd->hqk", heads_grad, blended, preferred_element_type=F32)
    scores_grad = (weights * (weights_grad - delta[..., None])).astype(BF)
    queries_grad = (
        jnp.einsum("hqk,khd->qhd", scores_grad, keys, preferred_element_type=F32) * SCALE
    ).astype(BF).astype(F32)
    keys_grad = (
        jnp.einsum("hqk,qhd->khd", scores_grad, queries, preferred_element_type=F32) * SCALE
    ).astype(BF).astype(F32)
    blended_grad = jnp.einsum(
        "hqk,qhd->khd", weights_low, heads_grad, preferred_element_type=F32
    ).astype(BF).reshape(length, group)
    values_grad = (1.0 - BLEND_MIX) * to_spans(blended_grad, span_count).astype(F32)
    mixed_grad = jnp.concatenate(
        [
            rotate(queries_grad, cosine, -sine_table).reshape(length, group),
            rotate(keys_grad, cosine, -sine_table).reshape(length, group),
            BLEND_MIX * blended_grad.astype(F32),
        ],
        axis=1,
    ).astype(BF)
    normed_in_grad = lax.psum_scatter(
        dot_nt(mixed_grad, qkv_copy).astype(BF), "seq", scatter_dimension=0, tiled=True
    ).astype(F32)
    tokens_grad = hidden_mid_grad + norm_backward(
        normed_in_grad, scaled_in, inverse_in, gains_full[:, 0]
    )

    def to_owner(terms):
        return lax.psum_scatter(terms.astype(BF), "dp", scatter_dimension=0, tiled=True)

    qkv_part = lax.all_gather(to_owner(dot_tn(normed_all, mixed_grad)), "seq", axis=0)
    qkv_total = (
        jnp.transpose(qkv_part.reshape(span_count, owned_rows, 3, group), (1, 2, 0, 3))
        .reshape(owned_rows, triple)
        .astype(F32)
    )
    out_total, gate_up_total, down_total = lax.psum(
        (
            to_owner(dot_tn(attended, mid_grad_low)),
            to_owner(dot_tn(normed_mid, gate_up_grad)),
            to_owner(dot_tn(activation, back_rows)),
        ),
        "seq",
    )
    out_total, gate_up_total, down_total = (
        out_total.astype(F32),
        gate_up_total.astype(F32),
        down_total.astype(F32),
    )

    gains_total = jnp.stack(
        [
            jnp.sum(qkv_total * qkv_weight.astype(BF).astype(F32), axis=1),
            jnp.sum(gate_up_total * gate_up_weight.astype(BF).astype(F32), axis=1),
        ],
        axis=1,
    ) / gains_owned
    masters = (qkv_weight, out_weight, gate_up_weight, down_weight, norm_gains)
    firsts = (first_qkv, first_out, first_gate_up, first_down, first_gains)
    seconds = (second_qkv, second_out, second_gate_up, second_down, second_gains)
    totals = (qkv_total, out_total, gate_up_total, down_total, gains_total)
    rate_list = (MATRIX_RATE, MATRIX_RATE, MATRIX_RATE, MATRIX_RATE, GAIN_RATE)
    decays = (MATRIX_DECAY, MATRIX_DECAY, MATRIX_DECAY, MATRIX_DECAY, 0.0)
    updated = [
        apply_adamw(masters[i], firsts[i], seconds[i], totals[i], rate_list[i], decays[i])
        for i in range(5)
    ]
    return (
        (layer_out[None], tokens_grad[None], values_grad[None])
        + tuple(member[0] for member in updated)
        + tuple(member[1] for member in updated)
        + tuple(member[2] for member in updated)
    )


def solution(mesh):
    rows = P("dp", "seq", None)
    owned = P("dp", None)
    return jax.shard_map(
        on_device,
        mesh=mesh,
        in_specs=(rows, rows, rows, P("dp", "seq"), P()) + (owned,) * 15,
        out_specs=(rows,) * 3 + (owned,) * 15,
        check_vma=False,
    )
```

```python
import functools
import math

import jax
import jax.numpy as jnp
from jax import lax
from jax.experimental import pallas as pl
from jax.experimental.pallas import tpu as pltpu
from jax.sharding import PartitionSpec as P

HEAD_DIM = 64
STEP = 10


NORM_EPS = 1e-06
ADAM_EPS = 1e-08
BLEND_MIX = 0.5
BETA_FIRST = 0.5
BETA_SECOND = 0.5
MATRIX_RATE = 0.06
MATRIX_DECAY = 0.1
GAIN_RATE = 0.5
ROPE_BASE = 10000.0
MASK_FILL = -1e30
SCALE = HEAD_DIM ** (-0.5)

BF = jnp.bfloat16
F32 = jnp.float32


def dot_nn(left, right):
    return lax.dot_general(left, right, (((1,), (0,)), ((), ())), preferred_element_type=F32)


def dot_nt(left, right):
    return lax.dot_general(left, right, (((1,), (1,)), ((), ())), preferred_element_type=F32)


def dot_tn(left, right):
    return lax.dot_general(left, right, (((0,), (0,)), ((), ())), preferred_element_type=F32)


def normalize_parts(matrix):
    inverse = lax.rsqrt(jnp.mean(matrix * matrix, axis=-1, keepdims=True) + NORM_EPS)
    return (matrix * inverse, inverse)


def norm_backward(grad_rows, scaled, inverse, gain_column):
    pushed = grad_rows * gain_column
    return inverse * (pushed - scaled * jnp.mean(pushed * scaled, axis=-1, keepdims=True))


def rotary(positions):
    half_width = HEAD_DIM // 2
    frequency = jnp.exp(
        jnp.arange(half_width, dtype=F32) * (-math.log(ROPE_BASE) / half_width)
    )
    angles = positions.astype(F32)[:, None] * frequency[None, :]
    return (jnp.cos(angles)[:, None, :], jnp.sin(angles)[:, None, :])


def rotate(head_rows, cosine, sine_table):
    half_width = head_rows.shape[-1] // 2
    lower_half = head_rows[..., :half_width]
    upper_half = head_rows[..., half_width:]
    return jnp.concatenate(
        [
            lower_half * cosine - upper_half * sine_table,
            upper_half * cosine + lower_half * sine_table,
        ],
        axis=-1,
    )


def apply_adamw(master, first_state, second_state, gradient, rate, decay):
    next_first = BETA_FIRST * first_state + (1.0 - BETA_FIRST) * gradient
    next_second = BETA_SECOND * second_state + (1.0 - BETA_SECOND) * gradient * gradient
    first_hat = next_first / (1.0 - BETA_FIRST**STEP)
    second_hat = next_second / (1.0 - BETA_SECOND**STEP)
    new_master = master - rate * (first_hat / (jnp.sqrt(second_hat) + ADAM_EPS) + decay * master)
    return (new_master, next_first, next_second)


MESH = pl.DeviceIdType.MESH
VMEM_BYTES = 58 << 20


def full_spec():
    return pl.BlockSpec(memory_space=pltpu.VMEM)


def any_spec():
    return pl.BlockSpec(memory_space=pl.ANY)


class Place:
    def __init__(self, dp_count, span_count):
        self.dp_count = dp_count
        self.span_count = span_count
        self.inner_count = dp_count // 4
        self.dp = lax.axis_index("dp")
        self.span = lax.axis_index("seq")
        self.core = lax.rem(self.dp, 2)
        self.inner = lax.rem(self.dp // 2, self.inner_count)
        self.outer = self.dp // (2 * self.inner_count)

    def at(self, outer, inner, core):
        return (outer * self.inner_count + inner) * 2 + core

    def inner_plus(self, offset):
        return lax.rem(self.inner + offset, self.inner_count)

    def greet_all(self):
        barrier = pltpu.get_barrier_semaphore()
        for offset in range(1, self.dp_count):
            pl.semaphore_signal(
                barrier,
                inc=1,
                device_id=(lax.rem(self.dp + offset, self.dp_count), self.span),
                device_id_type=MESH,
            )
        for offset in range(1, self.span_count):
            pl.semaphore_signal(
                barrier,
                inc=1,
                device_id=(self.dp, lax.rem(self.span + offset, self.span_count)),
                device_id_type=MESH,
            )
        pl.semaphore_wait(barrier, self.dp_count + self.span_count - 2)


def remote(source, target, send_sem, recv_sem, device):
    return pltpu.make_async_remote_copy(
        src_ref=source,
        dst_ref=target,
        send_sem=send_sem,
        recv_sem=recv_sem,
        device_id=device,
        device_id_type=MESH,
    )


def half_rows(rows):
    return rows // 2 // 16 * 16


class Gather:
    def __init__(self, place, whole, columns, send_sems, recv_sems):
        self.place = place
        self.whole = whole
        self.columns = columns
        self.rows = whole.shape[0] // place.dp_count
        self.send_sems = send_sems
        self.recv_sems = recv_sems
        self.sent = []
        count = place.inner_count
        self.near, self.lower, self.upper, self.pair = 0, count, 2 * count, 3 * count

    @staticmethod
    def slots(inner_count):
        return 6 * inner_count + 1

    def block(self, index, part=None):
        first = half_rows(self.rows)
        start, size = {None: (0, self.rows), 0: (0, first), 1: (first, self.rows - first)}[part]
        return self.whole.at[
            pl.ds(pl.multiple_of(index * self.rows + start, 16), size), self.columns
        ]

    def send(self, source, target, slot, far_slot, device):
        copy = remote(
            source, target, self.send_sems.at[slot], self.recv_sems.at[far_slot], (device, self.place.span)
        )
        copy.start()
        self.sent.append(copy)

    def arrived(self, block, slot):
        remote(
            block, block, self.send_sems.at[slot], self.recv_sems.at[slot], (self.place.dp, self.place.span)
        ).wait_recv()

    def sibling(self, block, slot):
        place = self.place
        self.send(block, block, slot, slot, place.at(place.outer, place.inner, 1 - place.core))

    def begin(self):
        place, count = self.place, self.place.inner_count
        mine = self.block(place.dp)
        self.send(mine, mine, 0, 0, place.at(1 - place.outer, place.inner, place.core))
        for offset in range(1, count):
            self.send(
                mine,
                mine,
                offset,
                count - offset,
                place.at(place.outer, place.inner_plus(offset), place.core),
            )
        copy = remote(
            mine,
            mine,
            self.send_sems.at[self.pair],
            self.recv_sems.at[self.pair],
            (place.at(place.outer, place.inner, 1 - place.core), place.span),
        )
        copy.start()
        self.sent.append(copy)

    def forward(self):
        place, count = self.place, self.place.inner_count
        across = place.at(1 - place.outer, place.inner, place.core)
        self.arrived(self.block(across), 0)
        for offset in range(1, count):
            self.send(
                self.block(across, 0),
                self.block(across, 0),
                self.lower + offset,
                self.lower + count - offset,
                place.at(place.outer, place.inner_plus(offset), place.core),
            )
        for offset in range(1, count):
            beside = place.at(place.outer, place.inner_plus(offset), place.core)
            self.arrived(self.block(beside), offset)
            self.send(
                self.block(beside, 1),
                self.block(beside, 1),
                self.upper + offset,
                self.upper + offset,
                across,
            )
        self.sibling(self.block(across), self.pair + count)
        for offset in range(1, count):
            beside = place.at(place.outer, place.inner_plus(offset), place.core)
            self.sibling(self.block(beside), self.pair + offset)

    def share(self):
        place, count = self.place, self.place.inner_count
        for offset in range(1, count):
            far = place.at(1 - place.outer, place.inner_plus(offset), place.core)
            self.arrived(self.block(far, 0), self.lower + offset)
            self.sibling(self.block(far, 0), self.pair + count + offset)
            self.arrived(self.block(far, 1), self.upper + offset)
            self.sibling(self.block(far, 1), self.pair + 2 * count + offset)

    def end(self):
        place, count = self.place, self.place.inner_count
        other = 1 - place.core
        self.arrived(self.block(place.at(place.outer, place.inner, other)), self.pair)
        self.arrived(self.block(place.at(1 - place.outer, place.inner, other)), self.pair + count)
        for offset in range(1, count):
            inner = place.inner_plus(offset)
            self.arrived(self.block(place.at(place.outer, inner, other)), self.pair + offset)
            far = place.at(1 - place.outer, inner, other)
            self.arrived(self.block(far, 0), self.pair + count + offset)
            self.arrived(self.block(far, 1), self.pair + 2 * count + offset)
        for copy in self.sent:
            copy.wait_send()


class Exchange:
    def __init__(self, place, sources, targets, send_sems, recv_sems):
        self.place = place
        self.sources = sources
        self.targets = targets
        self.send_sems = send_sems
        self.recv_sems = recv_sems

    def copy(self, offset):
        place = self.place
        count = place.span_count
        peer = lax.rem(place.span + offset, count)
        return remote(
            self.sources.at[peer],
            self.targets.at[place.span],
            self.send_sems.at[offset],
            self.recv_sems.at[count - offset],
            (place.dp, peer),
        )

    def start(self):
        for offset in range(1, self.place.span_count):
            self.copy(offset).start()
        self.targets[self.place.span] = self.sources[self.place.span]

    def wait(self):
        place = self.place
        count = place.span_count
        for offset in range(1, count):
            peer = lax.rem(place.span + offset, count)
            remote(
                self.sources.at[peer],
                self.targets.at[peer],
                self.send_sems.at[offset],
                self.recv_sems.at[offset],
                (place.dp, peer),
            ).wait_recv()

    def finish(self):
        for offset in range(1, self.place.span_count):
            self.copy(offset).wait_send()


def cast_rows(source, target, first, moves=None):
    rows = source.shape[0]

    def step(index, unused):
        at = pl.ds(pl.multiple_of(index * 16, 16), 16)
        there = pl.ds(pl.multiple_of(first + index * 16, 16), 16)
        for from_columns, to_columns in moves or ((slice(None), slice(None)),):
            target[there, to_columns] = source[at, from_columns].astype(BF)
        return unused

    lax.fori_loop(0, rows // 16, step, 0)


def swap_halves(rows):
    width = rows.shape[1]
    half = HEAD_DIM // 2
    if width % 128:
        pieces = []
        for start in range(0, width, HEAD_DIM):
            pieces += [rows[:, start + half : start + HEAD_DIM], rows[:, start : start + half]]
        return jnp.concatenate(pieces, axis=1)
    lane = lax.broadcasted_iota(jnp.int32, rows.shape, 1)
    return jnp.where(
        lane % HEAD_DIM < half, pltpu.roll(rows, width - half, 1), pltpu.roll(rows, half, 1)
    )


def angles_of(cosine, sine, position, heads):
    half = HEAD_DIM // 2
    back = lax.rem(cosine.shape[1] - half * position, cosine.shape[1])
    cos_half = pltpu.roll(cosine[...], back, 1)[:, :half]
    sin_half = pltpu.roll(sine[...], back, 1)[:, :half]
    return (
        jnp.concatenate([cos_half] * (2 * heads), axis=1),
        jnp.concatenate([-sin_half, sin_half] * heads, axis=1),
    )


def slot_with(order, position):
    slot = 0
    for index in range(order.shape[0]):
        slot = jnp.where(order[index] == position, index, slot)
    return slot


def segment_starts(bounds, rows, first):
    position = lax.broadcasted_iota(jnp.int32, (rows, 1), 0) + first
    position = position.astype(F32)
    start = jnp.zeros((rows, 1), F32)
    for cut in bounds:
        start = jnp.where(position >= cut, cut, start)
    return position, start


def head_part(matrix, head):
    if matrix.shape[1] == HEAD_DIM:
        return matrix
    lane = lax.broadcasted_iota(jnp.int32, (1, matrix.shape[1]), 1)
    return jnp.where(lane // HEAD_DIM == head, matrix, jnp.zeros_like(matrix))


def forward_kernel(
    dp_count,
    span_count,
    order,
    tokens,
    first_values,
    segments,
    gains_mine,
    qkv_mine,
    out_mine,
    gate_up_mine,
    down_mine,
    cosine,
    sine,
    out_grad,
    counts_out,
    gains_out,
    layer_low,
    mid_grad,
    mid_grad_low,
    normed_left,
    attended_left,
    attended_grad,
    qkv_result,
    normed_result,
    query_result,
    key_result,
    value_result,
    raw_result,
    lse_result,
    gate_up_grad_result,
    activation_result,
    normed_out,
    query_out,
    key_out,
    value_out,
    raw_out,
    lse_out,
    gate_up_grad,
    activation_left,
    gains_send,
    qkv_held,
    out_whole,
    gate_up_whole,
    down_whole,
    qkv_whole,
    attended,
    normed,
    outward,
    normed_grad,
    gains_all,
    counts_send,
    counts_all,
    first_send,
    first_all,
    normed_all,
    scores_kept,
    attended_send,
    attended_all,
    gather_send,
    gather_recv,
    gains_send_sem,
    gains_recv_sem,
    counts_send_sem,
    counts_recv_sem,
    first_send_sem,
    first_recv_sem,
    ring_send,
    ring_recv,
    attended_send_sem,
    attended_recv_sem,
    local_sem,
    result_sem,
):
    place = Place(dp_count, span_count)
    rows, width = tokens.shape
    group = width // span_count
    hidden = down_whole.shape[0]
    owned = out_mine.shape[0]
    heads = group // HEAD_DIM
    last = span_count - 1
    span = place.span

    qkv_loads = []
    for part in range(3):
        first = pl.multiple_of(part * width + span * group, 128)
        copy = pltpu.make_async_copy(
            qkv_mine.at[:, pl.ds(first, group)],
            qkv_held.at[:, part * group : (part + 1) * group],
            local_sem.at[part],
        )
        copy.start()
        qkv_loads.append(copy)

    place.greet_all()
    gains_send[...] = jnp.zeros_like(gains_send)
    gains_send[0:2, :] = gains_mine[...].astype(BF).astype(F32)
    gains_all[place.dp] = gains_send[...]
    gains_copies = []
    for offset in range(1, dp_count):
        peer = lax.rem(place.dp + offset, dp_count)
        copy = remote(
            gains_send,
            gains_all.at[place.dp],
            gains_send_sem.at[offset],
            gains_recv_sem.at[dp_count - offset],
            (peer, span),
        )
        copy.start()
        gains_copies.append(copy)
    parts = hidden_parts(hidden)
    moves = []
    gate_up_columns = []
    for start, size in parts:
        moves.append((slice(start, start + size), slice(2 * start, 2 * start + size)))
        moves.append(
            (
                slice(hidden + start, hidden + start + size),
                slice(2 * start + size, 2 * start + 2 * size),
            )
        )
        gate_up_columns.append(slice(2 * start, 2 * (start + size)))
    every = slice(None)
    sources = [(qkv_whole, every), (out_whole, every), (down_whole, every)]
    sources += [(gate_up_whole, columns) for columns in gate_up_columns]
    gathers = [
        Gather(place, whole, columns, gather_send.at[i], gather_recv.at[i])
        for i, (whole, columns) in enumerate(sources)
    ]
    qkv_gather, out_gather, down_gather = gathers[:3]
    gate_up_gathers = gathers[3:]
    for copy in qkv_loads:
        copy.wait()
    cast_rows(qkv_held, qkv_whole, place.dp * owned)
    qkv_gather.begin()
    for index in range(span_count):
        first_send[index] = first_values[:, index * group : (index + 1) * group]
    first_exchange = Exchange(place, first_send, first_all, first_send_sem, first_recv_sem)
    first_exchange.start()
    ids = segments[...]
    row = lax.broadcasted_iota(jnp.int32, (8, 128), 0)
    counts = jnp.zeros((8, 128), F32)
    for cut in range(3):
        below = jnp.sum(jnp.where(ids <= cut, 1.0, 0.0), axis=1, keepdims=True)
        counts = jnp.where(row == cut, below, counts)
    for index in range(span_count):
        counts_send[index] = counts
    counts_exchange = Exchange(place, counts_send, counts_all, counts_send_sem, counts_recv_sem)
    counts_exchange.start()

    residual = tokens[...].astype(F32)
    scaled = residual * lax.rsqrt(jnp.mean(residual * residual, axis=1, keepdims=True) + NORM_EPS)
    for offset in range(1, dp_count):
        peer = lax.rem(place.dp + offset, dp_count)
        remote(
            gains_send,
            gains_all.at[peer],
            gains_send_sem.at[offset],
            gains_recv_sem.at[offset],
            (peer, span),
        ).wait_recv()
    gains_row = jnp.concatenate([gains_all[i] for i in range(dp_count)], axis=1)
    gains_out[...] = gains_row
    normed_all[span] = (scaled * gains_row[0:1, :]).astype(BF)

    def pass_on(block, step, way):
        return remote(
            normed_all.at[block],
            normed_all.at[block],
            ring_send.at[way, step],
            ring_recv.at[way, step],
            (place.dp, jnp.where(way == 0, jnp.minimum(span + 1, last), jnp.maximum(span - 1, 0))),
        )

    @pl.when(span < last)
    def up():
        pass_on(span, 0, 0).start()

    @pl.when(span > 0)
    def down():
        pass_on(span, 0, 1).start()

    cast_rows(out_mine, out_whole, place.dp * owned)
    out_gather.begin()
    cast_rows(down_mine, down_whole, place.dp * down_mine.shape[0])
    qkv_gather.forward()
    down_gather.begin()
    cast_rows(gate_up_mine, gate_up_whole, place.dp * owned, moves)
    for member in gate_up_gathers:
        member.begin()
    qkv_gather.share()
    out_gather.forward()

    for step in range(1, span_count):

        @pl.when(span - step >= 0)
        def from_below():
            block = jnp.maximum(span - step, 0)
            pass_on(block, step - 1, 0).wait_recv()

            @pl.when(span < last)
            def on():
                pass_on(block, step, 0).start()

        @pl.when(span + step <= last)
        def from_above():
            block = jnp.minimum(span + step, last)
            pass_on(block, step - 1, 1).wait_recv()

            @pl.when(span > 0)
            def on():
                pass_on(block, step, 1).start()

    qkv_gather.end()
    results = []

    def keep(source, target):
        copy = pltpu.make_async_copy(source, target, result_sem.at[len(results)])
        copy.start()
        results.append(copy)

    keep(qkv_whole, qkv_result)
    first_exchange.wait()
    counts_exchange.wait()
    cuts = counts_all[0]
    for index in range(1, span_count):
        cuts = cuts + counts_all[index]
    counts_out[...] = cuts
    bounds = [cuts[i : i + 1, 0:1] for i in range(3)]

    def project(position, unused):
        slot = slot_with(order, position)
        normed_here = normed_all[slot]
        normed_out[:, pl.ds(pl.multiple_of(position * rows, rows), rows)] = jnp.transpose(normed_here)
        mixed = dot_nn(normed_here, qkv_whole[...])
        cos_here, sin_here = angles_of(cosine, sine, position, heads)
        query = mixed[:, :group]
        key = mixed[:, group : 2 * group]
        query_out[position] = (query * cos_here + swap_halves(query) * sin_here).astype(BF)
        key_out[position] = (key * cos_here + swap_halves(key) * sin_here).astype(BF)
        value_out[position] = (
            BLEND_MIX * mixed[:, 2 * group :]
            + (1.0 - BLEND_MIX) * first_all[slot].astype(F32)
        ).astype(BF)
        return unused

    lax.fori_loop(0, span_count, project, 0)
    for source, target in (
        (normed_out, normed_result),
        (query_out, query_result),
        (key_out, key_result),
        (value_out, value_result),
    ):
        keep(source, target)
    out_gather.share()
    down_gather.forward()

    def attend(position, unused):
        query = query_out[position]
        parts = [head_part(query, head) for head in range(heads)]
        query_position, start = segment_starts(bounds, rows, position * rows)

        def score(other, highest):
            key = key_out[other]
            key_position = (
                lax.broadcasted_iota(jnp.int32, (1, rows), 1) + other * rows
            ).astype(F32)
            allowed = (key_position <= query_position) & (key_position >= start)
            found = []
            for head in range(heads):
                masked = jnp.where(allowed, dot_nt(parts[head], key) * SCALE, MASK_FILL)
                scores_kept[head, other] = masked
                found.append(jnp.maximum(highest[head], jnp.max(masked, axis=1, keepdims=True)))
            return tuple(found)

        highest = lax.fori_loop(
            0, position + 1, score, (jnp.full((rows, 1), MASK_FILL, F32),) * heads
        )

        def raise_scores(other, total):
            added = []
            for head in range(heads):
                raised = jnp.exp(scores_kept[head, other] - highest[head])
                scores_kept[head, other] = raised
                added.append(total[head] + jnp.sum(raised, axis=1, keepdims=True))
            return tuple(added)

        total = lax.fori_loop(
            0, position + 1, raise_scores, (jnp.zeros((rows, 1), F32),) * heads
        )
        inverse = [1.0 / member for member in total]

        def gather_values(other, attended):
            value = value_out[other]
            for head in range(heads):
                weights = (scores_kept[head, other] * inverse[head]).astype(BF)
                attended = attended + dot_nn(weights, head_part(value, head))
            return attended

        raw_out[position] = lax.fori_loop(
            0, position + 1, gather_values, jnp.zeros((rows, group), F32)
        )
        lane = lax.broadcasted_iota(jnp.int32, (rows, 128), 1)
        kept = jnp.zeros((rows, 128), F32)
        for head in range(heads):
            kept = jnp.where(lane == head, highest[head] + jnp.log(total[head]), kept)
        lse_out[position] = kept
        return unused

    gate_up_gathers[0].forward()
    lax.fori_loop(0, span_count // 2, attend, 0)
    for member in gate_up_gathers[1:-1]:
        member.forward()
    lax.fori_loop(span_count // 2, span_count - 1, attend, 0)
    gate_up_gathers[-1].forward()
    down_gather.share()
    lax.fori_loop(span_count - 1, span_count, attend, 0)

    for index in range(span_count):
        attended_send[index] = raw_out[order[index]].astype(BF)
    attended_exchange = Exchange(
        place, attended_send, attended_all, attended_send_sem, attended_recv_sem
    )
    attended_exchange.start()
    keep(raw_out, raw_result)
    keep(lse_out, lse_result)
    gate_up_gathers[0].share()
    out_gather.end()
    attended_exchange.wait()
    attended[...] = jnp.concatenate([attended_all[i] for i in range(span_count)], axis=1)

    hidden_mid = tokens[...].astype(F32) + dot_nn(attended[...], out_whole[...])
    outward[...] = hidden_mid
    scaled, inverse = normalize_parts(hidden_mid)
    normed[...] = (scaled * gains_out[1:2, :]).astype(BF)
    normed_left[...] = jnp.transpose(normed[...])
    attended_left[...] = jnp.transpose(attended[...])
    normed_grad[...] = jnp.zeros_like(normed_grad)
    down_gather.end()
    block = 256

    for number, (start, size) in enumerate(parts):
        if number + 1 < len(parts):
            gate_up_gathers[number + 1].share()
        gate_up_gathers[number].end()

        def step(index, unused):
            offset = index * block
            gate_at = pl.ds(pl.multiple_of(2 * start + offset, block), block)
            up_at = pl.ds(pl.multiple_of(2 * start + size + offset, block), block)
            here = pl.ds(pl.multiple_of(start + offset, block), block)
            there = pl.ds(pl.multiple_of(hidden + start + offset, block), block)
            gate = dot_nn(normed[...], gate_up_whole[:, gate_at])
            upward = dot_nn(normed[...], gate_up_whole[:, up_at])
            activation_grad = dot_nt(out_grad[...], down_whole[here, :])
            sigmoid = jax.nn.sigmoid(gate)
            swish = gate * sigmoid
            activation = (swish * upward).astype(BF)
            activation_left[here, :] = jnp.transpose(activation)
            gate_grad = (
                activation_grad * upward * sigmoid * (1.0 + gate * (1.0 - sigmoid))
            ).astype(BF)
            up_grad = (activation_grad * swish).astype(BF)
            gate_up_grad[:, here] = gate_grad
            gate_up_grad[:, there] = up_grad
            outward[...] += dot_nn(activation, down_whole[here, :])
            normed_grad[...] += dot_nt(gate_grad, gate_up_whole[:, gate_at]) + dot_nt(
                up_grad, gate_up_whole[:, up_at]
            )
            return unused

        lax.fori_loop(0, size // block, step, 0)
        for first in (start, hidden + start):
            columns = slice(first, first + size)
            keep(gate_up_grad.at[:, columns], gate_up_grad_result.at[:, columns])
        here = slice(start, start + size)
        keep(activation_left.at[here, :], activation_result.at[here, :])
    layer_low[...] = outward[...].astype(BF)
    hidden_mid = tokens[...].astype(F32) + dot_nn(attended[...], out_whole[...])
    scaled, inverse = normalize_parts(hidden_mid)
    grad = out_grad[...].astype(F32) + norm_backward(
        normed_grad[...], scaled, inverse, gains_out[1:2, :]
    )
    mid_grad[...] = grad
    mid_grad_low[...] = grad.astype(BF)
    attended_grad[...] = dot_nt(mid_grad_low[...], out_whole[...]).astype(BF)

    for copy in gains_copies:
        copy.wait_send()
    for exchange in (first_exchange, counts_exchange, attended_exchange):
        exchange.finish()
    for step in range(span_count):

        @pl.when((span - step >= 0) & (span < last))
        def sent_up():
            pass_on(jnp.maximum(span - step, 0), step, 0).wait_send()

        @pl.when((span + step <= last) & (span > 0))
        def sent_down():
            pass_on(jnp.minimum(span + step, last), step, 1).wait_send()

    for copy in results:
        copy.wait()


def hidden_parts(hidden):
    count = hidden // 256
    sizes = [256 * ((count + 3 - i) // 4) for i in range(4)]
    return [(sum(sizes[:i]), size) for i, size in enumerate(sizes) if size]


def forward_call(
    dp_count, span_count, order, tokens, first_values, segments, gains_mine, qkv_mine,
    out_mine, gate_up_mine, down_mine, cosine, sine, out_grad,
):
    rows, width = tokens.shape
    group = width // span_count
    heads = group // HEAD_DIM
    owned = qkv_mine.shape[0]
    doubled = gate_up_mine.shape[1]
    hidden = doubled // 2
    gathers = 3 + len(hidden_parts(hidden))
    slots = Gather.slots(dp_count // 4)
    dma = pltpu.SemaphoreType.DMA
    by_span = (span_count, rows, group)
    kept = (
        ((width, span_count * rows), BF),
        (by_span, BF),
        (by_span, BF),
        (by_span, BF),
        (by_span, F32),
        ((span_count, rows, 128), F32),
        ((rows, doubled), BF),
        ((hidden, rows), BF),
    )
    return pl.pallas_call(
        functools.partial(forward_kernel, dp_count, span_count),
        out_shape=(
            jax.ShapeDtypeStruct((8, 128), F32),
            jax.ShapeDtypeStruct((8, width), F32),
            jax.ShapeDtypeStruct((rows, width), BF),
            jax.ShapeDtypeStruct((rows, width), F32),
            jax.ShapeDtypeStruct((rows, width), BF),
            jax.ShapeDtypeStruct((width, rows), BF),
            jax.ShapeDtypeStruct((width, rows), BF),
            jax.ShapeDtypeStruct((rows, width), BF),
            jax.ShapeDtypeStruct((width, 3 * group), BF),
        )
        + tuple(jax.ShapeDtypeStruct(shape, kind) for shape, kind in kept),
        in_specs=[pl.BlockSpec(memory_space=pltpu.SMEM)]
        + [full_spec()] * 4
        + [any_spec()]
        + [full_spec()] * 6,
        out_specs=(full_spec(),) * 8 + (any_spec(),) * 9,
        scratch_shapes=[pltpu.VMEM(shape, kind) for shape, kind in kept]
        + [
            pltpu.VMEM((8, owned), F32),
            pltpu.VMEM((owned, 3 * group), F32),
            pltpu.VMEM((width, width), BF),
            pltpu.VMEM((width, doubled), BF),
            pltpu.VMEM((hidden, width), BF),
            pltpu.VMEM((width, 3 * group), BF),
            pltpu.VMEM((rows, width), BF),
            pltpu.VMEM((rows, width), BF),
            pltpu.VMEM((rows, width), F32),
            pltpu.VMEM((rows, width), F32),
            pltpu.VMEM((dp_count, 8, owned), F32),
            pltpu.VMEM((span_count, 8, 128), F32),
            pltpu.VMEM((span_count, 8, 128), F32),
            pltpu.VMEM(by_span, BF),
            pltpu.VMEM(by_span, BF),
            pltpu.VMEM((span_count, rows, width), BF),
            pltpu.VMEM((heads, span_count, rows, rows), F32),
            pltpu.VMEM(by_span, BF),
            pltpu.VMEM(by_span, BF),
            dma((gathers, slots)),
            dma((gathers, slots)),
            dma((dp_count,)),
            dma((dp_count,)),
            dma((span_count,)),
            dma((span_count,)),
            dma((span_count,)),
            dma((span_count,)),
            dma((2, span_count)),
            dma((2, span_count)),
            dma((span_count,)),
            dma((span_count,)),
            dma((3,)),
            dma((7 + 3 * len(hidden_parts(hidden)),)),
        ],
        compiler_params=pltpu.CompilerParams(
            collective_id=0, has_side_effects=True, vmem_limit_bytes=61 << 20
        ),
    )(
        order, tokens, first_values, segments, gains_mine, qkv_mine, out_mine,
        gate_up_mine, down_mine, cosine, sine, out_grad,
    )


class Pair:
    def __init__(
        self,
        place,
        left_whole,
        left,
        left_other,
        right_whole,
        right,
        right_other,
        send_sems,
        recv_sems,
    ):
        self.place = place
        self.left = left
        self.left_other = left_other
        self.right = right
        self.right_other = right_other
        other = (place.at(place.outer, place.inner, 1 - place.core), place.span)
        self.left_copy = remote(
            left_whole.at[:, 1 - place.core], left_other, send_sems.at[0], recv_sems.at[0], other
        )
        self.own_copy = pltpu.make_async_copy(
            left_whole.at[:, place.core], left, send_sems.at[2]
        )
        self.right_copy = remote(
            right_whole, right_other, send_sems.at[1], recv_sems.at[1], other
        )
        self.own_right = None
        if right_whole is not right:
            self.own_right = pltpu.make_async_copy(right_whole, right, send_sems.at[3])

    def lend_left(self):
        self.left_copy.start()
        self.own_copy.start()

    def lend_right(self):
        self.right_copy.start()
        self.own_right.start()

    def wait(self):
        self.own_copy.wait()
        if self.own_right is not None:
            self.own_right.wait()
        self.left_copy.wait_recv()
        self.right_copy.wait_recv()

    def finish(self):
        self.left_copy.wait_send()
        self.right_copy.wait_send()

    def product(self, outer, inner, columns):
        chip = outer * self.place.inner_count + inner
        depth = self.right.shape[1]
        found = None
        for block in range(self.right.shape[0]):
            at = slice(block * depth, (block + 1) * depth)
            mine = dot_nn(self.left[chip, :, at], self.right[block, :, columns])
            theirs = dot_nn(self.left_other[chip, :, at], self.right_other[block, :, columns])
            found = mine + theirs if found is None else found + mine + theirs
        return found


class Piece:
    def __init__(self, pair, columns, kind, buffers, sems, result):
        self.pair = pair
        self.place = pair.place
        self.columns = columns
        self.kind = kind
        self.send1, self.recv1, self.send2, self.recv2 = buffers[:4]
        mine = self.recv1.at[0, pair.place.inner if kind == 0 else pair.place.outer]
        self.line = [mine] + list(buffers[4:])
        self.send_sems, self.recv_sems = sems
        self.result = result
        self.sent = []

    def send(self, source, target, slot, far_slot, dp, span=None):
        copy = remote(
            source,
            target,
            self.send_sems.at[slot],
            self.recv_sems.at[far_slot],
            (dp, self.place.span if span is None else span),
        )
        copy.start()
        self.sent.append(copy)

    def arrived(self, target, slot):
        remote(
            target, target, self.send_sems.at[slot], self.recv_sems.at[slot], (self.place.dp, self.place.span)
        ).wait_recv()

    def across(self):
        place = self.place
        return place.at(1 - place.outer, place.inner, place.core)

    def beside(self, offset):
        place = self.place
        return place.at(place.outer, place.inner_plus(offset), place.core)

    def product(self, outer, inner):
        return self.pair.product(outer, inner, self.columns)

    def first(self):
        place, count = self.place, self.place.inner_count
        if self.kind == 0:
            for inner in range(count):
                self.send1[0, inner] = self.product(1 - place.outer, inner).astype(BF)
            self.send(self.send1.at[0], self.recv1.at[0], 0, 0, self.across())
            return
        for offset in range(1, count):
            for outer in range(2):
                self.send1[offset - 1, outer] = self.product(
                    outer, place.inner_plus(offset)
                ).astype(BF)
            self.send(
                self.send1.at[offset - 1],
                self.recv1.at[count - offset - 1],
                offset - 1,
                count - offset - 1,
                self.beside(offset),
            )

    def second(self):
        place, count = self.place, self.place.inner_count
        base = count
        if self.kind == 0:
            self.arrived(self.recv1.at[0], 0)
            for offset in range(1, count):
                inner = place.inner_plus(offset)
                total = self.product(place.outer, inner) + self.recv1[0, inner].astype(F32)
                self.send2[offset - 1] = total.astype(BF)
                self.send(
                    self.send2.at[offset - 1],
                    self.recv2.at[count - offset - 1],
                    base + offset - 1,
                    base + count - offset - 1,
                    self.beside(offset),
                )
            return
        total = self.product(1 - place.outer, place.inner)
        for offset in range(1, count):
            self.arrived(self.recv1.at[offset - 1], offset - 1)
            total = total + self.recv1[offset - 1, 1 - place.outer].astype(F32)
        self.send2[0] = total.astype(BF)
        self.send(self.send2.at[0], self.recv2.at[0], base, base, self.across())

    def total(self):
        place, count = self.place, self.place.inner_count
        base = count
        total = self.product(place.outer, place.inner)
        if self.kind == 0:
            total = total + self.recv1[0, place.inner].astype(F32)
            for offset in range(1, count):
                self.arrived(self.recv2.at[offset - 1], base + offset - 1)
                total = total + self.recv2[offset - 1].astype(F32)
            return total
        for offset in range(1, count):
            total = total + self.recv1[offset - 1, place.outer].astype(F32)
        self.arrived(self.recv2.at[0], base)
        return total + self.recv2[0].astype(F32)


    def shape_of_line(self):
        place = self.place
        half = place.span_count // 2
        low = place.span < half
        depth = jnp.where(low, place.span, place.span_count - 1 - place.span)
        inward = jnp.where(low, place.span + 1, place.span - 1)
        outward = jnp.where(low, place.span - 1, place.span + 1)
        outward = jnp.clip(outward, 0, place.span_count - 1)
        return half, depth, inward, outward

    def line_copy(self, source, target, slot, span):
        base = 2 * self.place.inner_count
        return remote(
            source,
            target,
            self.send_sems.at[base + slot],
            self.recv_sems.at[base + slot],
            (self.place.dp, span),
        )

    def send_inward(self):
        half, depth, inward, outward = self.shape_of_line()
        sum_here, from_out, from_mid = self.line

        @pl.when(depth == half - 1)
        def cross():
            self.line_copy(sum_here, from_mid, 1, inward).start()

        @pl.when(depth < half - 1)
        def in_():
            self.line_copy(sum_here, from_out, 0, inward).start()

    def line_start(self):
        half, depth, inward, outward = self.shape_of_line()
        sum_here, from_out, from_mid = self.line
        sum_here[...] = self.total().astype(BF)

        @pl.when(depth == 0)
        def go():
            self.send_inward()

    def line_in(self):
        half, depth, inward, outward = self.shape_of_line()
        sum_here, from_out, from_mid = self.line

        @pl.when(depth > 0)
        def go():
            self.line_copy(from_out, from_out, 0, outward).wait_recv()
            sum_here[...] = (sum_here[...].astype(F32) + from_out[...].astype(F32)).astype(BF)
            self.send_inward()

    def line_mid(self):
        half, depth, inward, outward = self.shape_of_line()
        sum_here, from_out, from_mid = self.line

        @pl.when(depth == half - 1)
        def go():
            self.line_copy(from_mid, from_mid, 1, inward).wait_recv()
            self.result[...] = (
                sum_here[...].astype(F32) + from_mid[...].astype(F32)
            ).astype(BF)

            @pl.when(depth > 0)
            def out():
                self.line_copy(self.result, self.result, 2, outward).start()

    def line_out(self):
        half, depth, inward, outward = self.shape_of_line()

        @pl.when(depth < half - 1)
        def go():
            self.line_copy(self.result, self.result, 2, inward).wait_recv()

            @pl.when(depth > 0)
            def out():
                self.line_copy(self.result, self.result, 2, outward).start()

    def line_finish(self):
        half, depth, inward, outward = self.shape_of_line()
        sum_here, from_out, from_mid = self.line

        @pl.when(depth == half - 1)
        def cross():
            self.line_copy(sum_here, from_mid, 1, inward).wait_send()

        @pl.when(depth < half - 1)
        def in_():
            self.line_copy(sum_here, from_out, 0, inward).wait_send()

        @pl.when(depth > 0)
        def out():
            self.line_copy(self.result, self.result, 2, outward).wait_send()


    def spread_start(self, results):
        place = self.place
        base = 2 * place.inner_count
        self.results = results
        results[place.span, :, self.columns] = self.total().astype(BF)
        for offset in range(1, place.span_count):
            peer = lax.rem(place.span + offset, place.span_count)
            block = results.at[place.span, :, self.columns]
            self.send(
                block, block, base + offset, base + place.span_count - offset, place.dp, peer
            )

    def spread_wait(self):
        place = self.place
        base = 2 * place.inner_count
        for offset in range(1, place.span_count):
            peer = lax.rem(place.span + offset, place.span_count)
            self.arrived(self.results.at[peer, :, self.columns], base + offset)

    def finish(self):
        for copy in self.sent:
            copy.wait_send()


def cut_columns(width):
    if width > 4096:
        quarter = width // 4 // 128 * 128
        return [slice(i * quarter, (i + 1) * quarter if i < 3 else width) for i in range(4)]
    half = width // 2 // 128 * 128
    return [slice(0, half), slice(half, width)]


def piece_scratch(inner_count, rows, columns, kind, on_line):
    width = columns.stop - columns.start
    if kind == 0:
        shapes = [(1, inner_count, rows, width)] * 2 + [(inner_count - 1, rows, width)] * 2
    else:
        shapes = [(inner_count - 1, 2, rows, width)] * 2 + [(1, rows, width)] * 2
    if on_line:
        shapes += [(rows, width)] * 2
    return shapes


GATE_UP, DOWN, OUT, QKV = range(4)
WAIT_PAIR, ATTEND, CLOSE, WAIT_GRAD, LEND_MIXED, SEND_BLENDED, WAIT_BLENDED, CHAIN, CHAIN_END = range(9)
ORDER = (
    (WAIT_PAIR, DOWN, 0),
    (Piece.first, DOWN, 0),
    (Piece.first, DOWN, 1),
    (WAIT_PAIR, GATE_UP, 0),
    (Piece.first, GATE_UP, 2),
    (Piece.first, GATE_UP, 3),
    (WAIT_GRAD, None, 0),
    (WAIT_PAIR, OUT, 0),
    (ATTEND, None, 0),
    (ATTEND, None, 1),
    (Piece.first, GATE_UP, 0),
    (ATTEND, None, 2),
    (CLOSE, None, 0),
    (SEND_BLENDED, None, 0),
    (Piece.second, DOWN, 0),
    (Piece.second, GATE_UP, 2),
    (Piece.line_start, DOWN, 0),
    (LEND_MIXED, None, 0),
    (Piece.second, DOWN, 1),
    (Piece.second, GATE_UP, 0),
    (Piece.line_start, GATE_UP, 2),
    (Piece.first, OUT, 0),
    (Piece.first, OUT, 1),
    (Piece.line_in, DOWN, 0),
    (Piece.second, GATE_UP, 3),
    (Piece.line_in, GATE_UP, 2),
    (WAIT_PAIR, QKV, 0),
    (Piece.first, GATE_UP, 1),
    (Piece.line_start, GATE_UP, 0),
    (Piece.line_mid, DOWN, 0),
    (Piece.second, OUT, 1),
    (Piece.line_start, DOWN, 1),
    (Piece.second, OUT, 0),
    (Piece.line_in, GATE_UP, 0),
    (Piece.line_start, GATE_UP, 3),
    (Piece.first, QKV, 0),
    (Piece.line_start, OUT, 1),
    (WAIT_BLENDED, None, 0),
    (Piece.line_in, DOWN, 1),
    (Piece.line_mid, GATE_UP, 2),
    (Piece.second, GATE_UP, 1),
    (Piece.second, QKV, 0),
    (Piece.line_start, OUT, 0),
    (Piece.line_out, DOWN, 0),
    (Piece.first, QKV, 1),
    (Piece.line_in, GATE_UP, 3),
    (Piece.line_mid, GATE_UP, 0),
    (CHAIN, None, 0),
    (Piece.line_out, GATE_UP, 2),
    (Piece.spread_start, QKV, 0),
    (Piece.second, QKV, 1),
    (Piece.line_mid, DOWN, 1),
    (Piece.line_in, OUT, 0),
    (Piece.line_mid, GATE_UP, 3),
    (Piece.line_start, GATE_UP, 1),
    (CHAIN, None, 1),
    (Piece.line_in, OUT, 1),
    (Piece.spread_start, QKV, 1),
    (Piece.spread_wait, QKV, 0),
    (Piece.line_mid, OUT, 0),
    (Piece.line_mid, OUT, 1),
    (Piece.line_out, OUT, 1),
    (Piece.line_out, DOWN, 1),
    (Piece.line_in, GATE_UP, 1),
    (Piece.line_out, GATE_UP, 0),
    (Piece.line_out, GATE_UP, 3),
    (CHAIN, None, 2),
    (Piece.line_mid, GATE_UP, 1),
    (CHAIN_END, None, 0),
    (Piece.line_out, GATE_UP, 1),
    (Piece.line_out, OUT, 0),
    (Piece.spread_wait, QKV, 1),
)


def backward_kernel(
    dp_count,
    span_count,
    order,
    gate_up_left,
    gate_up_right,
    down_left,
    down_right,
    out_left,
    out_right,
    qkv_left,
    attended_grad_whole,
    query_whole,
    key_whole,
    value_whole,
    raw_whole,
    lse_whole,
    qkv_whole,
    counts,
    cosine,
    sine,
    gate_up_result,
    down_result,
    out_result,
    qkv_result,
    blended_result,
    normed_result,
    attended_grad,
    query,
    key,
    value,
    raw,
    lse,
    qkv_copy,
    load_sem,
    gate_up_own,
    gate_up_other,
    gate_up_right_own,
    gate_up_right_other,
    down_own,
    down_other,
    down_right_own,
    down_right_other,
    out_own,
    out_other,
    out_right_own,
    out_right_other,
    qkv_own,
    qkv_other,
    mixed_other,
    mixed,
    grad_send,
    grad_all,
    key_sum,
    value_sum,
    key_turned,
    query_sum,
    blended_all,
    chain,
    pair_send,
    pair_recv,
    piece_send,
    piece_recv,
    grad_send_sem,
    grad_recv_sem,
    blended_send_sem,
    blended_recv_sem,
    chain_send,
    chain_recv,
    *piece_buffers,
):
    place = Place(dp_count, span_count)
    span, last = place.span, span_count - 1
    rows, width = attended_grad.shape
    group = width // span_count
    heads = group // HEAD_DIM

    loads = []
    for source, target in (
        (attended_grad_whole, attended_grad),
        (key_whole, key),
        (query_whole, query),
        (value_whole, value),
        (raw_whole, raw),
        (lse_whole, lse),
        (qkv_whole, qkv_copy),
    ):
        loads.append(pltpu.make_async_copy(source, target, load_sem.at[len(loads)]))
        loads[-1].start()
    place.greet_all()
    loads[0].wait()
    for index in range(span_count):
        grad_send[index] = attended_grad[:, index * group : (index + 1) * group]
    grad_exchange = Exchange(place, grad_send, grad_all, grad_send_sem, grad_recv_sem)
    grad_exchange.start()
    pairs = [
        Pair(place, *members, pair_send.at[i], pair_recv.at[i])
        for i, members in enumerate(
            (
                (
                    gate_up_left, gate_up_own, gate_up_other,
                    gate_up_right, gate_up_right_own, gate_up_right_other,
                ),
                (down_left, down_own, down_other, down_right, down_right_own, down_right_other),
                (out_left, out_own, out_other, out_right, out_right_own, out_right_other),
                (qkv_left, qkv_own, qkv_other, mixed, mixed, mixed_other),
            )
        )
    ]
    for which in (OUT, DOWN, GATE_UP):
        pairs[which].lend_left()
        pairs[which].lend_right()
    pairs[QKV].lend_left()

    free = list(piece_buffers)
    pieces = []
    for pair, result, on_line in zip(
        pairs, (gate_up_result, down_result, out_result, qkv_result), (True, True, True, False)
    ):
        members = []
        for i, columns in enumerate(cut_columns(pair.right.shape[2])):
            number = 6 if on_line else 4
            buffers, free = free[:number], free[number:]
            at = len(pieces) * 4 + i
            members.append(
                Piece(
                    pair,
                    columns,
                    i % 2,
                    buffers,
                    (piece_send.at[at], piece_recv.at[at]),
                    result.at[:, columns] if on_line else None,
                )
            )
        pieces.append(members)
    def clear(index, unused):
        key_sum[index] = jnp.zeros((rows, group), F32)
        value_sum[index] = jnp.zeros((rows, group), F32)
        return unused

    lax.fori_loop(0, span_count, clear, 0)

    def clear_chain(index, unused):
        chain[index] = jnp.zeros(chain.shape[1:], BF)
        return unused

    @pl.when(span == 0)
    def nothing_from_below():
        lax.fori_loop(1, span_count + 1, clear_chain, 0)

    @pl.when(span == last)
    def nothing_from_above():
        lax.fori_loop(0, span_count, clear_chain, 0)

    cuts = counts[...]
    bounds = [cuts[i : i + 1, 0:1] for i in range(3)]

    def turned_back(rows_in, position):
        cos_here, sin_here = angles_of(cosine, sine, position, heads)
        low = rows_in.astype(BF).astype(F32)
        return (low * cos_here - swap_halves(low) * sin_here).astype(BF)

    for copy in loads[1:]:
        copy.wait()

    def turn_keys(position, unused):
        key_turned[position] = jnp.transpose(key[position])
        return unused

    lax.fori_loop(0, span_count, turn_keys, 0)

    def attend_back(position, unused):
        query_here = (query[position].astype(F32) * SCALE).astype(BF)
        grad_here = grad_all[slot_with(order, position)]
        query_parts = [head_part(query_here, head) for head in range(heads)]
        grad_parts = [head_part(grad_here, head) for head in range(heads)]
        query_stack = jnp.concatenate(query_parts, axis=0)
        grad_stack = jnp.concatenate(grad_parts, axis=0)
        agreed = jnp.transpose(grad_here.astype(F32) * raw[position])
        logs = jnp.transpose(lse[position])
        query_position = (
            lax.broadcasted_iota(jnp.int32, (1, rows), 1) + position * rows
        ).astype(F32)
        start = jnp.zeros((1, rows), F32)
        for cut in bounds:
            start = jnp.where(query_position >= cut, cut, start)
        query_sum[...] = jnp.zeros((group, rows), F32)

        def block(other, unused):
            key_here, value_here, key_back = key[other], value[other], key_turned[other]
            key_position = (
                lax.broadcasted_iota(jnp.int32, (rows, 1), 0) + other * rows
            ).astype(F32)
            allowed = (key_position <= query_position) & (key_position >= start)
            lows, grads = [], []
            for head in range(heads):
                at = slice(head * HEAD_DIM, (head + 1) * HEAD_DIM)
                scores = dot_nt(key_here, query_parts[head])
                weights = jnp.where(allowed, jnp.exp(scores - logs[head : head + 1]), 0.0)
                weights_grad = dot_nt(value_here, grad_parts[head])
                delta = jnp.sum(agreed[at], axis=0, keepdims=True)
                scores_grad = (weights * (weights_grad - delta)).astype(BF)
                lows.append(weights.astype(BF))
                grads.append(scores_grad)
                query_sum[at, :] += dot_nn(key_back[at], scores_grad)
            key_sum[other] += dot_nn(jnp.concatenate(grads, axis=1), query_stack)
            value_sum[other] += dot_nn(jnp.concatenate(lows, axis=1), grad_stack)
            return unused

        lax.fori_loop(0, position + 1, block, 0)
        mixed[position, :, :group] = turned_back(
            jnp.transpose(query_sum[...]) * SCALE, position
        )
        return unused

    def close(position, unused):
        mixed[position, :, group : 2 * group] = turned_back(key_sum[position], position)
        mixed[position, :, 2 * group :] = (
            BLEND_MIX * value_sum[position].astype(BF).astype(F32)
        ).astype(BF)
        return unused

    blended_send = grad_send
    blended_exchange = Exchange(
        place, blended_send, blended_all, blended_send_sem, blended_recv_sem
    )

    def normed_grad(block):
        return dot_nt(mixed[order[block]], qkv_copy[...])

    def pass_on(block, way):
        return remote(
            chain.at[block + 1 - way],
            chain.at[block + 1 - way],
            chain_send.at[way, block],
            chain_recv.at[way, block],
            (place.dp, jnp.minimum(span + 1, last) if way == 0 else jnp.maximum(span - 1, 0)),
        )

    def chain_step(step):
        up = last + span - step
        down = step - (last - span)

        @pl.when((span <= step) & (up > span))
        def going_up():
            block = jnp.clip(up, 0, last)

            @pl.when(span > 0)
            def more():
                pass_on(block, 0).wait_recv()

            chain[block + 1] = (normed_grad(block) + chain[block + 1].astype(F32)).astype(BF)
            pass_on(block, 0).start()

        @pl.when((down >= 0) & (down < span))
        def going_down():
            block = jnp.clip(down, 0, last)

            @pl.when(span < last)
            def more():
                pass_on(block, 1).wait_recv()

            chain[block] = (normed_grad(block) + chain[block].astype(F32)).astype(BF)
            pass_on(block, 1).start()

    def chain_end():
        @pl.when(span > 0)
        def from_below():
            pass_on(span, 0).wait_recv()

        @pl.when(span < last)
        def from_above():
            pass_on(span, 1).wait_recv()

        normed_result[...] = (
            normed_grad(span) + chain[span + 1].astype(F32) + chain[span].astype(F32)
        )

    half = span_count // 2
    ranges = ((0, half), (half, last), (last, span_count))

    def send_blended():
        grad_exchange.finish()
        for index in range(span_count):
            blended_send[index] = value_sum[order[index]].astype(BF)
        blended_exchange.start()

    def keep_blended():
        blended_exchange.wait()
        blended_result[...] = jnp.concatenate(
            [blended_all[i] for i in range(span_count)], axis=1
        )

    single = {
        WAIT_GRAD: grad_exchange.wait,
        CLOSE: lambda: lax.fori_loop(0, span_count, close, 0),
        LEND_MIXED: pairs[3].right_copy.start,
        SEND_BLENDED: send_blended,
        WAIT_BLENDED: keep_blended,
        CHAIN_END: chain_end,
    }
    for action, which, number in ORDER:
        if action in single:
            single[action]()
        elif action == WAIT_PAIR:
            pairs[which].wait()
        elif action == ATTEND:
            lax.fori_loop(*ranges[number], attend_back, 0)
        elif action == CHAIN:
            for step in [number] if number < 2 else range(2, last):
                chain_step(step)
        elif action == Piece.spread_start:
            pieces[which][number].spread_start(qkv_result)
        else:
            action(pieces[which][number])

    for pair in pairs:
        pair.finish()
    blended_exchange.finish()
    for which, members in enumerate(pieces):
        for member in members:
            if which != QKV:
                member.line_finish()
            member.finish()
    for step in range(last):
        up = last + span - step
        down_block = step - (last - span)

        @pl.when((span <= step) & (up > span))
        def sent_up():
            pass_on(jnp.clip(up, 0, last), 0).wait_send()

        @pl.when((down_block >= 0) & (down_block < span))
        def sent_down():
            pass_on(jnp.clip(down_block, 0, last), 1).wait_send()


def backward_call(dp_count, span_count, order, factors, others, tables):
    (gate_up_left, gate_up_right, down_left, down_right, out_left, out_right, qkv_left) = factors
    rows, width = others[0].shape
    kept = [pltpu.VMEM(member.shape, member.dtype) for member in others]
    group = width // span_count
    inner_count = dp_count // 4
    dma = pltpu.SemaphoreType.DMA
    by_span = (span_count, rows, group)
    mixed_shape = (span_count, rows, 3 * group)

    def less(left):
        return (left.shape[0],) + left.shape[2:]

    scratch = []
    for left, columns_in, on_line in (
        (gate_up_left, gate_up_right.shape[2], True),
        (down_left, down_right.shape[2], True),
        (out_left, out_right.shape[2], True),
        (qkv_left, 3 * group, False),
    ):
        for i, columns in enumerate(cut_columns(columns_in)):
            scratch += [
                pltpu.VMEM(shape, BF)
                for shape in piece_scratch(inner_count, left.shape[2], columns, i % 2, on_line)
            ]
    slots = 2 * inner_count + max(3, span_count)
    return pl.pallas_call(
        functools.partial(backward_kernel, dp_count, span_count),
        out_shape=(
            jax.ShapeDtypeStruct((gate_up_left.shape[2], gate_up_right.shape[2]), BF),
            jax.ShapeDtypeStruct((down_left.shape[2], down_right.shape[2]), BF),
            jax.ShapeDtypeStruct((out_left.shape[2], out_right.shape[2]), BF),
            jax.ShapeDtypeStruct((span_count, qkv_left.shape[2], 3 * group), BF),
            jax.ShapeDtypeStruct((rows, width), BF),
            jax.ShapeDtypeStruct((rows, width), F32),
        ),
        in_specs=[pl.BlockSpec(memory_space=pltpu.SMEM)]
        + [any_spec()] * (len(factors) + len(others))
        + [full_spec()] * len(tables),
        out_specs=(full_spec(),) * 6,
        scratch_shapes=kept
        + [
            dma((len(others),)),
            pltpu.VMEM(less(gate_up_left), BF),
            pltpu.VMEM(less(gate_up_left), BF),
            pltpu.VMEM(gate_up_right.shape, BF),
            pltpu.VMEM(gate_up_right.shape, BF),
            pltpu.VMEM(less(down_left), BF),
            pltpu.VMEM(less(down_left), BF),
            pltpu.VMEM(down_right.shape, BF),
            pltpu.VMEM(down_right.shape, BF),
            pltpu.VMEM(less(out_left), BF),
            pltpu.VMEM(less(out_left), BF),
            pltpu.VMEM(out_right.shape, BF),
            pltpu.VMEM(out_right.shape, BF),
            pltpu.VMEM(less(qkv_left), BF),
            pltpu.VMEM(less(qkv_left), BF),
            pltpu.VMEM(mixed_shape, BF),
            pltpu.VMEM(mixed_shape, BF),
            pltpu.VMEM(by_span, BF),
            pltpu.VMEM(by_span, BF),
            pltpu.VMEM(by_span, F32),
            pltpu.VMEM(by_span, F32),
            pltpu.VMEM((span_count, group, rows), BF),
            pltpu.VMEM((group, rows), F32),
            pltpu.VMEM(by_span, BF),
            pltpu.VMEM((span_count + 1, rows, width), BF),
            dma((4, 4)),
            dma((4, 4)),
            dma((16, slots)),
            dma((16, slots)),
            dma((span_count,)),
            dma((span_count,)),
            dma((span_count,)),
            dma((span_count,)),
            dma((2, span_count)),
            dma((2, span_count)),
        ]
        + scratch,
        compiler_params=pltpu.CompilerParams(
            collective_id=1, has_side_effects=True, vmem_limit_bytes=61 << 20
        ),
    )(order, *factors, *others, *tables)


def update_rows(master, first_state, second_state, gradient, rate, decay):
    next_first = BETA_FIRST * first_state + (1.0 - BETA_FIRST) * gradient
    next_second = BETA_SECOND * second_state + (1.0 - BETA_SECOND) * gradient * gradient
    first_hat = next_first * (1.0 / (1.0 - BETA_FIRST**STEP))
    second_hat = next_second * (1.0 / (1.0 - BETA_SECOND**STEP))
    new_master = master - rate * (first_hat / (jnp.sqrt(second_hat) + ADAM_EPS) + decay * master)
    return (new_master, next_first, next_second)


def finish_kernel(
    qkv_total,
    out_total,
    gate_up_total,
    down_total,
    gains,
    gains_first,
    gains_second,
    tokens,
    mid_grad,
    normed_grad,
    gains_rows,
    blended_grad,
    layer_low,
    qkv,
    qkv_first,
    qkv_second,
    out,
    out_first,
    out_second,
    gate_up,
    gate_up_first,
    gate_up_second,
    down,
    down_first,
    down_second,
    layer_out,
    tokens_grad,
    values_grad,
    new_gains,
    new_gains_first,
    new_gains_second,
    *rest,
):
    results, held, sums, in_sem, out_sem = rest[:12], rest[12:24], rest[24], rest[25], rest[26]
    states = (
        (qkv, qkv_first, qkv_second),
        (out, out_first, out_second),
        (gate_up, gate_up_first, gate_up_second),
        (down, down_first, down_second),
    )
    width = tokens.shape[1]
    span_count = qkv_total.shape[0]
    group = width // span_count

    def qkv_rows(part):
        def rows(at):
            return jnp.concatenate(
                [
                    qkv_total[i, at, part * group : (part + 1) * group].astype(F32)
                    for i in range(span_count)
                ],
                axis=1,
            )

        return rows

    def rows_of(total, columns):
        return lambda at: total[at, columns].astype(F32)

    parts = []
    for columns in cut_columns(gate_up_total.shape[1]):
        parts.append((2, columns, rows_of(gate_up_total, columns)))
    for part in range(3):
        parts.append((0, slice(part * width, (part + 1) * width), qkv_rows(part)))
    for columns in cut_columns(width):
        parts.append((3, columns, rows_of(down_total, columns)))
    parts.append((1, slice(0, width), rows_of(out_total, slice(0, width))))

    def moves(number, source, target, sems):
        weight, columns, _ = parts[number]
        return [
            pltpu.make_async_copy(
                source[i].at[:, columns], target[i].at[:, columns], sems.at[number, i]
            )
            for i in range(3)
        ]

    loads, stores = [], []
    for number, (weight, _, _) in enumerate(parts):
        here = held[3 * weight : 3 * weight + 3]
        loads.append(moves(number, states[weight], here, in_sem))
        stores.append(moves(number, here, results[3 * weight : 3 * weight + 3], out_sem))
        for copy in loads[-1]:
            copy.start()

    residual = tokens[...].astype(F32)
    scaled, inverse = normalize_parts(residual)
    tokens_grad[...] = mid_grad[...] + norm_backward(
        normed_grad[...], scaled, inverse, gains_rows[0:1, :]
    )
    layer_out[...] = layer_low[...]
    sums[...] = jnp.zeros_like(sums)
    values_grad[...] = (1.0 - BLEND_MIX) * blended_grad[...].astype(F32)

    for number, (weight, columns, total) in enumerate(parts):
        here = held[3 * weight : 3 * weight + 3]
        for copy in loads[number]:
            copy.wait()
        owned = here[0].shape[0]
        wants_sum = weight in (0, 2)

        def step(index, unused):
            at = pl.ds(pl.multiple_of(index * 16, 16), 16)
            gradient = total(at)
            master = here[0][at, columns]
            if wants_sum:
                partial = jnp.sum(
                    gradient * master.astype(BF).astype(F32), axis=1, keepdims=True
                )
                lane = 0 if weight == 0 else 1
                slot = lax.broadcasted_iota(jnp.int32, (16, 128), 1) == lane
                sums[at, :] += jnp.where(slot, partial, 0.0)
            updated = update_rows(
                master,
                here[1][at, columns],
                here[2][at, columns],
                gradient,
                MATRIX_RATE,
                MATRIX_DECAY,
            )
            for i in range(3):
                here[i][at, columns] = updated[i]
            return unused

        lax.fori_loop(0, owned // 16, step, 0)
        for copy in stores[number]:
            copy.start()

    gain = gains[...]
    gains_total = jnp.transpose(sums[...])[:2, :] / gain.astype(BF).astype(F32)
    updated = update_rows(gain, gains_first[...], gains_second[...], gains_total, GAIN_RATE, 0.0)
    new_gains[...], new_gains_first[...], new_gains_second[...] = updated
    for group_of_copies in stores:
        for copy in group_of_copies:
            copy.wait()


def finish_call(totals, gains_states, token_parts, states):
    flat = [member for weight in states for member in weight]
    rows, width = token_parts[0].shape
    gains_shape = jax.ShapeDtypeStruct(gains_states[0].shape, F32)
    dma = pltpu.SemaphoreType.DMA
    count = len(cut_columns(totals[2].shape[1])) + 3 + 2 + 1
    return pl.pallas_call(
        finish_kernel,
        out_shape=(
            jax.ShapeDtypeStruct((rows, width), BF),
            jax.ShapeDtypeStruct((rows, width), F32),
            jax.ShapeDtypeStruct((rows, width), F32),
            gains_shape,
            gains_shape,
            gains_shape,
        )
        + tuple(jax.ShapeDtypeStruct(member.shape, F32) for member in flat),
        in_specs=[full_spec()] * 13 + [any_spec()] * 12,
        out_specs=(full_spec(),) * 6 + (any_spec(),) * 12,
        scratch_shapes=[pltpu.VMEM(member.shape, F32) for member in flat]
        + [
            pltpu.VMEM((gains_states[0].shape[1], 128), F32),
            dma((count, 3)),
            dma((count, 3)),
        ],
        compiler_params=pltpu.CompilerParams(vmem_limit_bytes=VMEM_BYTES),
    )(*totals, *gains_states, *token_parts, *flat)


def to_heads(rows, span_count):
    return lax.all_to_all(
        rows.reshape(rows.shape[0], span_count, rows.shape[1] // span_count),
        "seq",
        split_axis=1,
        concat_axis=0,
        tiled=True,
    ).reshape(rows.shape[0] * span_count, rows.shape[1] // span_count)


def to_spans(columns, span_count):
    rows_here = columns.shape[0] // span_count
    got = lax.all_to_all(
        columns.reshape(span_count, rows_here, columns.shape[1]),
        "seq",
        split_axis=0,
        concat_axis=0,
        tiled=True,
    )
    return jnp.transpose(got, (1, 0, 2)).reshape(rows_here, columns.shape[1] * span_count)


def on_device(
    tokens,
    first_values,
    out_grad,
    segments,
    span_order,
    qkv_weight,
    out_weight,
    gate_up_weight,
    down_weight,
    norm_gains,
    first_qkv,
    first_out,
    first_gate_up,
    first_down,
    first_gains,
    second_qkv,
    second_out,
    second_gate_up,
    second_down,
    second_gains,
):
    span_count = lax.axis_size("seq")
    mine = lax.axis_index("seq")
    owned_rows, triple = qkv_weight.shape
    model_width = triple // 3
    group = model_width // span_count
    group_heads = group // HEAD_DIM
    residual = tokens[0].astype(F32)
    rows_here = residual.shape[0]
    length = rows_here * span_count
    hidden_width = gate_up_weight.shape[1] // 2

    dp_count = lax.axis_size("dp")
    gains_owned = norm_gains.astype(BF).astype(F32)
    in_kernels = (
        length * model_width <= 1 << 20
        and dp_count % 4 == 0
        and dp_count >= 8
        and span_count % 2 == 0
        and group % 128 == 0
        and span_count * HEAD_DIM // 2 <= 128
        and hidden_width % 256 == 0
    )
    if in_kernels:
        half_width = HEAD_DIM // 2
        lane = lax.broadcasted_iota(jnp.int32, (rows_here, 128), 1)
        position = lax.broadcasted_iota(jnp.int32, (rows_here, 128), 0) + lane // half_width * rows_here
        frequency = jnp.exp(
            (jnp.arange(128, dtype=jnp.int32) % half_width).astype(F32)
            * (-math.log(ROPE_BASE) / half_width)
        )
        angles = lax.optimization_barrier(position).astype(F32) * frequency[None, :]
        cosine, sine = jnp.cos(angles), jnp.sin(angles)
        gains_states = tuple(
            jnp.transpose(member) for member in (norm_gains, first_gains, second_gains)
        )
        (
            counts, gains_rows, layer_low, hidden_mid_grad, mid_grad_low, normed_mid_left,
            attended_left, attended_grad, qkv_copy, normed_left, query_pos, key_pos, value_pos,
            raw_pos, lse_pos, gate_up_grad, activation_left,
        ) = forward_call(
            dp_count, span_count, span_order, tokens[0], first_values[0], segments,
            gains_states[0], qkv_weight, out_weight, gate_up_weight, down_weight, cosine, sine, out_grad[0],
        )
        def in_blocks(left):
            return left.reshape(dp_count // 2, 2, left.shape[0] // dp_count, left.shape[1])

        factors = (
            in_blocks(normed_mid_left),
            gate_up_grad[None],
            in_blocks(activation_left),
            out_grad,
            in_blocks(attended_left),
            mid_grad_low[None],
            in_blocks(normed_left),
        )
        others = (
            attended_grad,
            query_pos, key_pos, value_pos, raw_pos, lse_pos, qkv_copy,
        )
        gate_up_total, down_total, out_total, qkv_part, blended_grad, normed_in_grad = backward_call(
            dp_count, span_count, span_order, factors, others, (counts, cosine, sine)
        )
        finished = finish_call(
            (qkv_part, out_total, gate_up_total, down_total),
            gains_states,
            (tokens[0], hidden_mid_grad, normed_in_grad, gains_rows, blended_grad, layer_low),
            (
                (qkv_weight, first_qkv, second_qkv),
                (out_weight, first_out, second_out),
                (gate_up_weight, first_gate_up, second_gate_up),
                (down_weight, first_down, second_down),
            ),
        )
        new_gains = tuple(jnp.transpose(member) for member in finished[3:6])
        return (
            tuple(member[None] for member in finished[:3])
            + finished[6::3]
            + new_gains[:1]
            + finished[7::3]
            + new_gains[1:2]
            + finished[8::3]
            + new_gains[2:]
        )

    qkv_owned = qkv_weight.reshape(owned_rows, 3, model_width).astype(BF)
    qkv_mine = lax.dynamic_slice_in_dim(qkv_owned, mine * group, group, 2).reshape(
        owned_rows, 3 * group
    )
    gains_full = lax.all_gather(norm_gains.astype(BF), "dp", axis=0, tiled=True).astype(F32)
    qkv_copy = lax.all_gather(qkv_mine, "dp", axis=0, tiled=True)
    out_copy = lax.all_gather(out_weight.astype(BF), "dp", axis=0, tiled=True)
    gate_up_copy = lax.all_gather(gate_up_weight.astype(BF), "dp", axis=0, tiled=True)
    down_copy = lax.all_gather(down_weight.astype(BF), "dp", axis=0, tiled=True)

    row_index = jnp.arange(length, dtype=jnp.int32)
    owner_table = (row_index // rows_here)[:, None] == jnp.arange(span_count, dtype=jnp.int32)[
        None, :
    ]
    positions = (
        jnp.sum(jnp.where(owner_table, span_order[None, :], 0), axis=1) * rows_here
        + row_index % rows_here
    )
    all_segments = lax.all_gather(segments[0], "seq", axis=0, tiled=True)
    cosine, sine_table = rotary(positions)
    allowed = (all_segments[:, None] == all_segments[None, :]) & (
        positions[None, :] <= positions[:, None]
    )

    scaled_in, inverse_in = normalize_parts(residual)
    normed_in = (scaled_in * gains_full[:, 0]).astype(BF)
    normed_all = lax.all_gather(normed_in, "seq", axis=0, tiled=True)
    first_all = to_heads(first_values[0], span_count)
    mixed = dot_nn(normed_all, qkv_copy)
    queries = rotate(
        mixed[:, :group].reshape(length, group_heads, HEAD_DIM), cosine, sine_table
    ).astype(BF)
    keys = rotate(
        mixed[:, group : 2 * group].reshape(length, group_heads, HEAD_DIM), cosine, sine_table
    ).astype(BF)
    blended = (
        (BLEND_MIX * mixed[:, 2 * group :] + (1.0 - BLEND_MIX) * first_all.astype(F32))
        .astype(BF)
        .reshape(length, group_heads, HEAD_DIM)
    )
    scores = jnp.einsum("qhd,khd->hqk", queries, keys, preferred_element_type=F32) * SCALE
    masked = jnp.where(allowed[None], scores, MASK_FILL)
    highest = jnp.max(masked, axis=-1, keepdims=True)
    raised = jnp.where(allowed[None], jnp.exp(masked - highest), 0.0)
    weights = raised / jnp.sum(raised, axis=-1, keepdims=True)
    weights_low = weights.astype(BF)
    attended_raw = jnp.einsum("hqk,khd->qhd", weights_low, blended, preferred_element_type=F32)
    attended = to_spans(attended_raw.reshape(length, group).astype(BF), span_count)

    hidden_mid = residual + dot_nn(attended, out_copy)
    scaled_mid, inverse_mid = normalize_parts(hidden_mid)
    normed_mid = (scaled_mid * gains_full[:, 1]).astype(BF)
    gate_up = dot_nn(normed_mid, gate_up_copy)
    gate_part = gate_up[:, :hidden_width]
    upward = gate_up[:, hidden_width:]
    sigmoid_gate = jax.nn.sigmoid(gate_part)
    swish_gate = gate_part * sigmoid_gate
    activation = (swish_gate * upward).astype(BF)
    layer_out = (hidden_mid + dot_nn(activation, down_copy)).astype(BF)
    back_rows = out_grad[0]
    activation_grad = dot_nt(back_rows, down_copy)
    gate_up_grad = jnp.concatenate(
        [
            activation_grad * upward * sigmoid_gate * (1.0 + gate_part * (1.0 - sigmoid_gate)),
            activation_grad * swish_gate,
        ],
        axis=1,
    ).astype(BF)
    normed_mid_grad = dot_nt(gate_up_grad, gate_up_copy)
    hidden_mid_grad = back_rows.astype(F32) + norm_backward(
        normed_mid_grad, scaled_mid, inverse_mid, gains_full[:, 1]
    )
    mid_grad_low = hidden_mid_grad.astype(BF)
    attended_grad = to_heads(dot_nt(mid_grad_low, out_copy).astype(BF), span_count)

    heads_grad = attended_grad.reshape(length, group_heads, HEAD_DIM)
    delta = jnp.transpose(jnp.sum(heads_grad.astype(F32) * attended_raw, axis=-1))
    weights_grad = jnp.einsum("qhd,khd->hqk", heads_grad, blended, preferred_element_type=F32)
    scores_grad = (weights * (weights_grad - delta[..., None])).astype(BF)
    queries_grad = (
        jnp.einsum("hqk,khd->qhd", scores_grad, keys, preferred_element_type=F32) * SCALE
    ).astype(BF).astype(F32)
    keys_grad = (
        jnp.einsum("hqk,qhd->khd", scores_grad, queries, preferred_element_type=F32) * SCALE
    ).astype(BF).astype(F32)
    blended_grad = jnp.einsum(
        "hqk,qhd->khd", weights_low, heads_grad, preferred_element_type=F32
    ).astype(BF).reshape(length, group)
    values_grad = (1.0 - BLEND_MIX) * to_spans(blended_grad, span_count).astype(F32)
    mixed_grad = jnp.concatenate(
        [
            rotate(queries_grad, cosine, -sine_table).reshape(length, group),
            rotate(keys_grad, cosine, -sine_table).reshape(length, group),
            BLEND_MIX * blended_grad.astype(F32),
        ],
        axis=1,
    ).astype(BF)
    normed_in_grad = lax.psum_scatter(
        dot_nt(mixed_grad, qkv_copy).astype(BF), "seq", scatter_dimension=0, tiled=True
    ).astype(F32)
    tokens_grad = hidden_mid_grad + norm_backward(
        normed_in_grad, scaled_in, inverse_in, gains_full[:, 0]
    )

    def to_owner(terms):
        return lax.psum_scatter(terms.astype(BF), "dp", scatter_dimension=0, tiled=True)

    qkv_part = lax.all_gather(to_owner(dot_tn(normed_all, mixed_grad)), "seq", axis=0)
    qkv_total = (
        jnp.transpose(qkv_part.reshape(span_count, owned_rows, 3, group), (1, 2, 0, 3))
        .reshape(owned_rows, triple)
        .astype(F32)
    )
    out_total, gate_up_total, down_total = lax.psum(
        (
            to_owner(dot_tn(attended, mid_grad_low)),
            to_owner(dot_tn(normed_mid, gate_up_grad)),
            to_owner(dot_tn(activation, back_rows)),
        ),
        "seq",
    )
    out_total, gate_up_total, down_total = (
        out_total.astype(F32),
        gate_up_total.astype(F32),
        down_total.astype(F32),
    )

    gains_total = jnp.stack(
        [
            jnp.sum(qkv_total * qkv_weight.astype(BF).astype(F32), axis=1),
            jnp.sum(gate_up_total * gate_up_weight.astype(BF).astype(F32), axis=1),
        ],
        axis=1,
    ) / gains_owned
    masters = (qkv_weight, out_weight, gate_up_weight, down_weight, norm_gains)
    firsts = (first_qkv, first_out, first_gate_up, first_down, first_gains)
    seconds = (second_qkv, second_out, second_gate_up, second_down, second_gains)
    totals = (qkv_total, out_total, gate_up_total, down_total, gains_total)
    rate_list = (MATRIX_RATE, MATRIX_RATE, MATRIX_RATE, MATRIX_RATE, GAIN_RATE)
    decays = (MATRIX_DECAY, MATRIX_DECAY, MATRIX_DECAY, MATRIX_DECAY, 0.0)
    updated = [
        apply_adamw(masters[i], firsts[i], seconds[i], totals[i], rate_list[i], decays[i])
        for i in range(5)
    ]
    return (
        (layer_out[None], tokens_grad[None], values_grad[None])
        + tuple(member[0] for member in updated)
        + tuple(member[1] for member in updated)
        + tuple(member[2] for member in updated)
    )


def solution(mesh):
    rows = P("dp", "seq", None)
    owned = P("dp", None)
    return jax.shard_map(
        on_device,
        mesh=mesh,
        in_specs=(rows, rows, rows, P("dp", "seq"), P()) + (owned,) * 15,
        out_specs=(rows,) * 3 + (owned,) * 15,
        check_vma=False,
    )
```

```python
import functools
import math

import jax
import jax.numpy as jnp
from jax import lax
from jax.experimental import pallas as pl
from jax.experimental.pallas import tpu as pltpu
from jax.sharding import PartitionSpec as P

HEAD_DIM = 64
STEP = 10


NORM_EPS = 1e-06
ADAM_EPS = 1e-08
BLEND_MIX = 0.5
BETA_FIRST = 0.5
BETA_SECOND = 0.5
MATRIX_RATE = 0.06
MATRIX_DECAY = 0.1
GAIN_RATE = 0.5
ROPE_BASE = 10000.0
MASK_FILL = -1e30
SCALE = HEAD_DIM ** (-0.5)

BF = jnp.bfloat16
F32 = jnp.float32


def dot_nn(left, right):
    return lax.dot_general(left, right, (((1,), (0,)), ((), ())), preferred_element_type=F32)


def dot_nt(left, right):
    return lax.dot_general(left, right, (((1,), (1,)), ((), ())), preferred_element_type=F32)


def dot_tn(left, right):
    return lax.dot_general(left, right, (((0,), (0,)), ((), ())), preferred_element_type=F32)


def normalize_parts(matrix):
    inverse = lax.rsqrt(jnp.mean(matrix * matrix, axis=-1, keepdims=True) + NORM_EPS)
    return (matrix * inverse, inverse)


def norm_backward(grad_rows, scaled, inverse, gain_column):
    pushed = grad_rows * gain_column
    return inverse * (pushed - scaled * jnp.mean(pushed * scaled, axis=-1, keepdims=True))


def rotary(positions):
    half_width = HEAD_DIM // 2
    frequency = jnp.exp(
        jnp.arange(half_width, dtype=F32) * (-math.log(ROPE_BASE) / half_width)
    )
    angles = positions.astype(F32)[:, None] * frequency[None, :]
    return (jnp.cos(angles)[:, None, :], jnp.sin(angles)[:, None, :])


def rotate(head_rows, cosine, sine_table):
    half_width = head_rows.shape[-1] // 2
    lower_half = head_rows[..., :half_width]
    upper_half = head_rows[..., half_width:]
    return jnp.concatenate(
        [
            lower_half * cosine - upper_half * sine_table,
            upper_half * cosine + lower_half * sine_table,
        ],
        axis=-1,
    )


def apply_adamw(master, first_state, second_state, gradient, rate, decay):
    next_first = BETA_FIRST * first_state + (1.0 - BETA_FIRST) * gradient
    next_second = BETA_SECOND * second_state + (1.0 - BETA_SECOND) * gradient * gradient
    first_hat = next_first / (1.0 - BETA_FIRST**STEP)
    second_hat = next_second / (1.0 - BETA_SECOND**STEP)
    new_master = master - rate * (first_hat / (jnp.sqrt(second_hat) + ADAM_EPS) + decay * master)
    return (new_master, next_first, next_second)


MESH = pl.DeviceIdType.MESH
VMEM_BYTES = 58 << 20


def full_spec():
    return pl.BlockSpec(memory_space=pltpu.VMEM)


def any_spec():
    return pl.BlockSpec(memory_space=pl.ANY)


class Place:
    def __init__(self, dp_count, span_count):
        self.dp_count = dp_count
        self.span_count = span_count
        self.inner_count = dp_count // 4
        self.dp = lax.axis_index("dp")
        self.span = lax.axis_index("seq")
        self.core = lax.rem(self.dp, 2)
        self.inner = lax.rem(self.dp // 2, self.inner_count)
        self.outer = self.dp // (2 * self.inner_count)

    def at(self, outer, inner, core):
        return (outer * self.inner_count + inner) * 2 + core

    def inner_plus(self, offset):
        return lax.rem(self.inner + offset, self.inner_count)

    def greet_all(self):
        barrier = pltpu.get_barrier_semaphore()
        for offset in range(1, self.dp_count):
            pl.semaphore_signal(
                barrier,
                inc=1,
                device_id=(lax.rem(self.dp + offset, self.dp_count), self.span),
                device_id_type=MESH,
            )
        for offset in range(1, self.span_count):
            pl.semaphore_signal(
                barrier,
                inc=1,
                device_id=(self.dp, lax.rem(self.span + offset, self.span_count)),
                device_id_type=MESH,
            )
        pl.semaphore_wait(barrier, self.dp_count + self.span_count - 2)


def remote(source, target, send_sem, recv_sem, device):
    return pltpu.make_async_remote_copy(
        src_ref=source,
        dst_ref=target,
        send_sem=send_sem,
        recv_sem=recv_sem,
        device_id=device,
        device_id_type=MESH,
    )


def half_rows(rows):
    return rows // 2 // 16 * 16


class Gather:
    def __init__(self, place, whole, columns, send_sems, recv_sems):
        self.place = place
        self.whole = whole
        self.columns = columns
        self.rows = whole.shape[0] // place.dp_count
        self.send_sems = send_sems
        self.recv_sems = recv_sems
        count = place.inner_count
        self.near, self.lower, self.upper, self.pair = 0, count, 2 * count, 3 * count

    @staticmethod
    def slots(inner_count):
        return 6 * inner_count + 1

    def block(self, index, part=None):
        first = half_rows(self.rows)
        start, size = {None: (0, self.rows), 0: (0, first), 1: (first, self.rows - first)}[part]
        return self.whole.at[
            pl.ds(pl.multiple_of(index * self.rows + start, 16), size), self.columns
        ]

    def send(self, source, target, slot, far_slot, device):
        remote(
            source, target, self.send_sems.at[slot], self.recv_sems.at[far_slot], (device, self.place.span)
        ).start()

    def left(self, block, slot):
        remote(
            block, block, self.send_sems.at[slot], self.recv_sems.at[slot], (self.place.dp, self.place.span)
        ).wait_send()

    def arrived(self, block, slot):
        remote(
            block, block, self.send_sems.at[slot], self.recv_sems.at[slot], (self.place.dp, self.place.span)
        ).wait_recv()

    def sibling(self, block, slot):
        place = self.place
        self.send(block, block, slot, slot, place.at(place.outer, place.inner, 1 - place.core))

    def begin(self):
        place, count = self.place, self.place.inner_count
        mine = self.block(place.dp)
        self.send(mine, mine, 0, 0, place.at(1 - place.outer, place.inner, place.core))
        for offset in range(1, count):
            self.send(
                mine,
                mine,
                offset,
                count - offset,
                place.at(place.outer, place.inner_plus(offset), place.core),
            )
        self.sibling(mine, self.pair)

    def forward(self):
        place, count = self.place, self.place.inner_count
        across = place.at(1 - place.outer, place.inner, place.core)
        self.arrived(self.block(across), 0)
        for offset in range(1, count):
            self.send(
                self.block(across, 0),
                self.block(across, 0),
                self.lower + offset,
                self.lower + count - offset,
                place.at(place.outer, place.inner_plus(offset), place.core),
            )
        for offset in range(1, count):
            beside = place.at(place.outer, place.inner_plus(offset), place.core)
            self.arrived(self.block(beside), offset)
            self.send(
                self.block(beside, 1),
                self.block(beside, 1),
                self.upper + offset,
                self.upper + offset,
                across,
            )
        self.sibling(self.block(across), self.pair + count)
        for offset in range(1, count):
            beside = place.at(place.outer, place.inner_plus(offset), place.core)
            self.sibling(self.block(beside), self.pair + offset)

    def share(self):
        place, count = self.place, self.place.inner_count
        for offset in range(1, count):
            far = place.at(1 - place.outer, place.inner_plus(offset), place.core)
            self.arrived(self.block(far, 0), self.lower + offset)
            self.sibling(self.block(far, 0), self.pair + count + offset)
            self.arrived(self.block(far, 1), self.upper + offset)
            self.sibling(self.block(far, 1), self.pair + 2 * count + offset)

    def end(self):
        place, count = self.place, self.place.inner_count
        other = 1 - place.core
        self.arrived(self.block(place.at(place.outer, place.inner, other)), self.pair)
        self.arrived(self.block(place.at(1 - place.outer, place.inner, other)), self.pair + count)
        for offset in range(1, count):
            inner = place.inner_plus(offset)
            self.arrived(self.block(place.at(place.outer, inner, other)), self.pair + offset)
            far = place.at(1 - place.outer, inner, other)
            self.arrived(self.block(far, 0), self.pair + count + offset)
            self.arrived(self.block(far, 1), self.pair + 2 * count + offset)
        mine = self.block(place.dp)
        across = self.block(place.at(1 - place.outer, place.inner, place.core))
        self.left(mine, 0)
        self.left(mine, self.pair)
        self.left(across, self.pair + count)
        for offset in range(1, count):
            inner = place.inner_plus(offset)
            beside = place.at(place.outer, inner, place.core)
            far = place.at(1 - place.outer, inner, place.core)
            self.left(mine, offset)
            self.left(self.block(beside), self.pair + offset)
            self.left(
                self.block(place.at(1 - place.outer, place.inner, place.core), 0),
                self.lower + offset,
            )
            self.left(self.block(beside, 1), self.upper + offset)
            self.left(self.block(far, 0), self.pair + count + offset)
            self.left(self.block(far, 1), self.pair + 2 * count + offset)


class Exchange:
    def __init__(self, place, sources, targets, send_sems, recv_sems):
        self.place = place
        self.sources = sources
        self.targets = targets
        self.send_sems = send_sems
        self.recv_sems = recv_sems

    def copy(self, offset):
        place = self.place
        count = place.span_count
        peer = lax.rem(place.span + offset, count)
        return remote(
            self.sources.at[peer],
            self.targets.at[place.span],
            self.send_sems.at[offset],
            self.recv_sems.at[count - offset],
            (place.dp, peer),
        )

    def start(self):
        for offset in range(1, self.place.span_count):
            self.copy(offset).start()
        self.targets[self.place.span] = self.sources[self.place.span]

    def wait(self):
        place = self.place
        count = place.span_count
        for offset in range(1, count):
            peer = lax.rem(place.span + offset, count)
            remote(
                self.sources.at[peer],
                self.targets.at[peer],
                self.send_sems.at[offset],
                self.recv_sems.at[offset],
                (place.dp, peer),
            ).wait_recv()

    def finish(self):
        for offset in range(1, self.place.span_count):
            self.copy(offset).wait_send()


def cast_rows(source, target, first, moves=None):
    rows = source.shape[0]

    def step(index, unused):
        at = pl.ds(pl.multiple_of(index * 16, 16), 16)
        there = pl.ds(pl.multiple_of(first + index * 16, 16), 16)
        for from_columns, to_columns in moves or ((slice(None), slice(None)),):
            target[there, to_columns] = source[at, from_columns].astype(BF)
        return unused

    lax.fori_loop(0, rows // 16, step, 0)


def swap_halves(rows):
    width = rows.shape[1]
    half = HEAD_DIM // 2
    if width % 128:
        pieces = []
        for start in range(0, width, HEAD_DIM):
            pieces += [rows[:, start + half : start + HEAD_DIM], rows[:, start : start + half]]
        return jnp.concatenate(pieces, axis=1)
    lane = lax.broadcasted_iota(jnp.int32, rows.shape, 1)
    return jnp.where(
        lane % HEAD_DIM < half, pltpu.roll(rows, width - half, 1), pltpu.roll(rows, half, 1)
    )


def angles_of(cosine, sine, position, heads):
    half = HEAD_DIM // 2
    back = lax.rem(cosine.shape[1] - half * position, cosine.shape[1])
    cos_half = pltpu.roll(cosine[...], back, 1)[:, :half]
    sin_half = pltpu.roll(sine[...], back, 1)[:, :half]
    return (
        jnp.concatenate([cos_half] * (2 * heads), axis=1),
        jnp.concatenate([-sin_half, sin_half] * heads, axis=1),
    )


def slot_with(order, position):
    slot = 0
    for index in range(order.shape[0]):
        slot = jnp.where(order[index] == position, index, slot)
    return slot


def segment_starts(bounds, rows, first):
    position = lax.broadcasted_iota(jnp.int32, (rows, 1), 0) + first
    position = position.astype(F32)
    start = jnp.zeros((rows, 1), F32)
    for cut in bounds:
        start = jnp.where(position >= cut, cut, start)
    return position, start


def head_part(matrix, head):
    if matrix.shape[1] == HEAD_DIM:
        return matrix
    lane = lax.broadcasted_iota(jnp.int32, (1, matrix.shape[1]), 1)
    return jnp.where(lane // HEAD_DIM == head, matrix, jnp.zeros_like(matrix))


def forward_kernel(
    dp_count,
    span_count,
    order,
    tokens,
    first_values,
    segments,
    gains_mine,
    qkv_mine,
    out_mine,
    gate_up_mine,
    down_mine,
    cosine,
    sine,
    out_grad,
    counts_out,
    gains_out,
    layer_low,
    mid_grad,
    mid_grad_low,
    normed_left,
    attended_left,
    attended_grad,
    qkv_result,
    normed_result,
    query_result,
    key_result,
    value_result,
    raw_result,
    lse_result,
    gate_up_grad_result,
    activation_result,
    normed_out,
    query_out,
    key_out,
    value_out,
    raw_out,
    lse_out,
    gate_up_grad,
    activation_left,
    gains_send,
    qkv_held,
    out_whole,
    gate_up_whole,
    down_whole,
    qkv_whole,
    attended,
    normed,
    outward,
    normed_grad,
    gains_all,
    counts_send,
    counts_all,
    first_send,
    first_all,
    normed_all,
    scores_kept,
    attended_send,
    attended_all,
    gather_send,
    gather_recv,
    gains_send_sem,
    gains_recv_sem,
    counts_send_sem,
    counts_recv_sem,
    first_send_sem,
    first_recv_sem,
    ring_send,
    ring_recv,
    attended_send_sem,
    attended_recv_sem,
    local_sem,
    result_sem,
):
    place = Place(dp_count, span_count)
    rows, width = tokens.shape
    group = width // span_count
    hidden = down_whole.shape[0]
    owned = out_mine.shape[0]
    heads = group // HEAD_DIM
    last = span_count - 1
    span = place.span

    qkv_loads = []
    for part in range(3):
        first = pl.multiple_of(part * width + span * group, 128)
        copy = pltpu.make_async_copy(
            qkv_mine.at[:, pl.ds(first, group)],
            qkv_held.at[:, part * group : (part + 1) * group],
            local_sem.at[part],
        )
        copy.start()
        qkv_loads.append(copy)

    place.greet_all()
    gains_send[...] = jnp.zeros_like(gains_send)
    gains_send[0:2, :] = gains_mine[...].astype(BF).astype(F32)
    gains_all[place.dp] = gains_send[...]
    gains_copies = []
    for offset in range(1, dp_count):
        peer = lax.rem(place.dp + offset, dp_count)
        copy = remote(
            gains_send,
            gains_all.at[place.dp],
            gains_send_sem.at[offset],
            gains_recv_sem.at[dp_count - offset],
            (peer, span),
        )
        copy.start()
        gains_copies.append(copy)
    parts = hidden_parts(hidden)
    moves = []
    gate_up_columns = []
    for start, size in parts:
        moves.append((slice(start, start + size), slice(2 * start, 2 * start + size)))
        moves.append(
            (
                slice(hidden + start, hidden + start + size),
                slice(2 * start + size, 2 * start + 2 * size),
            )
        )
        gate_up_columns.append(slice(2 * start, 2 * (start + size)))
    every = slice(None)
    sources = [(qkv_whole, every), (out_whole, every), (down_whole, every)]
    sources += [(gate_up_whole, columns) for columns in gate_up_columns]
    gathers = [
        Gather(place, whole, columns, gather_send.at[i], gather_recv.at[i])
        for i, (whole, columns) in enumerate(sources)
    ]
    qkv_gather, out_gather, down_gather = gathers[:3]
    gate_up_gathers = gathers[3:]
    for copy in qkv_loads:
        copy.wait()
    cast_rows(qkv_held, qkv_whole, place.dp * owned)
    qkv_gather.begin()
    for index in range(span_count):
        first_send[index] = first_values[:, index * group : (index + 1) * group]
    first_exchange = Exchange(place, first_send, first_all, first_send_sem, first_recv_sem)
    ids = segments[...]
    row = lax.broadcasted_iota(jnp.int32, (8, 128), 0)
    counts = jnp.zeros((8, 128), F32)
    for cut in range(3):
        below = jnp.sum(jnp.where(ids <= cut, 1.0, 0.0), axis=1, keepdims=True)
        counts = jnp.where(row == cut, below, counts)
    for index in range(span_count):
        counts_send[index] = counts
    counts_exchange = Exchange(place, counts_send, counts_all, counts_send_sem, counts_recv_sem)
    counts_exchange.start()

    residual = tokens[...].astype(F32)
    scaled = residual * lax.rsqrt(jnp.mean(residual * residual, axis=1, keepdims=True) + NORM_EPS)
    for offset in range(1, dp_count):
        peer = lax.rem(place.dp + offset, dp_count)
        remote(
            gains_send,
            gains_all.at[peer],
            gains_send_sem.at[offset],
            gains_recv_sem.at[offset],
            (peer, span),
        ).wait_recv()
    gains_row = jnp.concatenate([gains_all[i] for i in range(dp_count)], axis=1)
    gains_out[...] = gains_row
    normed_all[span] = (scaled * gains_row[0:1, :]).astype(BF)

    def pass_on(block, step, way):
        return remote(
            normed_all.at[block],
            normed_all.at[block],
            ring_send.at[way, step],
            ring_recv.at[way, step],
            (place.dp, jnp.where(way == 0, jnp.minimum(span + 1, last), jnp.maximum(span - 1, 0))),
        )

    @pl.when(span < last)
    def up():
        pass_on(span, 0, 0).start()

    @pl.when(span > 0)
    def down():
        pass_on(span, 0, 1).start()

    cast_rows(out_mine, out_whole, place.dp * owned)
    out_gather.begin()
    cast_rows(down_mine, down_whole, place.dp * down_mine.shape[0])
    qkv_gather.forward()
    down_gather.begin()
    cast_rows(gate_up_mine, gate_up_whole, place.dp * owned, moves)
    for member in gate_up_gathers:
        member.begin()
    qkv_gather.share()
    out_gather.forward()

    for step in range(1, span_count):

        @pl.when(span - step >= 0)
        def from_below():
            block = jnp.maximum(span - step, 0)
            pass_on(block, step - 1, 0).wait_recv()

            @pl.when(span < last)
            def on():
                pass_on(block, step, 0).start()

        @pl.when(span + step <= last)
        def from_above():
            block = jnp.minimum(span + step, last)
            pass_on(block, step - 1, 1).wait_recv()

            @pl.when(span > 0)
            def on():
                pass_on(block, step, 1).start()

        if step == last - 1:
            first_exchange.start()

    qkv_gather.end()
    results = []

    def keep(source, target):
        copy = pltpu.make_async_copy(source, target, result_sem.at[len(results)])
        copy.start()
        results.append(copy)

    keep(qkv_whole, qkv_result)
    counts_exchange.wait()
    cuts = counts_all[0]
    for index in range(1, span_count):
        cuts = cuts + counts_all[index]
    counts_out[...] = cuts
    bounds = [cuts[i : i + 1, 0:1] for i in range(3)]

    def project(position, unused):
        slot = slot_with(order, position)
        normed_here = normed_all[slot]
        normed_out[:, pl.ds(pl.multiple_of(position * rows, rows), rows)] = jnp.transpose(normed_here)
        mixed = dot_nn(normed_here, qkv_whole[...])
        cos_here, sin_here = angles_of(cosine, sine, position, heads)
        query = mixed[:, :group]
        key = mixed[:, group : 2 * group]
        query_out[position] = (query * cos_here + swap_halves(query) * sin_here).astype(BF)
        key_out[position] = (key * cos_here + swap_halves(key) * sin_here).astype(BF)
        raw_out[position] = BLEND_MIX * mixed[:, 2 * group :]
        return unused

    def blend(position, unused):
        slot = slot_with(order, position)
        value_out[position] = (
            raw_out[position] + (1.0 - BLEND_MIX) * first_all[slot].astype(F32)
        ).astype(BF)
        return unused

    lax.fori_loop(0, span_count, project, 0)
    first_exchange.wait()
    lax.fori_loop(0, span_count, blend, 0)
    for source, target in (
        (normed_out, normed_result),
        (query_out, query_result),
        (key_out, key_result),
        (value_out, value_result),
    ):
        keep(source, target)
    out_gather.share()
    down_gather.forward()

    def attend(position, unused):
        query = query_out[position]
        parts = [head_part(query, head) for head in range(heads)]
        query_position, start = segment_starts(bounds, rows, position * rows)

        def score(other, highest):
            key = key_out[other]
            key_position = (
                lax.broadcasted_iota(jnp.int32, (1, rows), 1) + other * rows
            ).astype(F32)
            allowed = (key_position <= query_position) & (key_position >= start)
            found = []
            for head in range(heads):
                masked = jnp.where(allowed, dot_nt(parts[head], key) * SCALE, MASK_FILL)
                scores_kept[head, other] = masked
                found.append(jnp.maximum(highest[head], jnp.max(masked, axis=1, keepdims=True)))
            return tuple(found)

        highest = lax.fori_loop(
            0, position + 1, score, (jnp.full((rows, 1), MASK_FILL, F32),) * heads
        )

        def raise_scores(other, total):
            added = []
            for head in range(heads):
                raised = jnp.exp(scores_kept[head, other] - highest[head])
                scores_kept[head, other] = raised
                added.append(total[head] + jnp.sum(raised, axis=1, keepdims=True))
            return tuple(added)

        total = lax.fori_loop(
            0, position + 1, raise_scores, (jnp.zeros((rows, 1), F32),) * heads
        )
        inverse = [1.0 / member for member in total]

        def gather_values(other, attended):
            value = value_out[other]
            for head in range(heads):
                weights = (scores_kept[head, other] * inverse[head]).astype(BF)
                attended = attended + dot_nn(weights, head_part(value, head))
            return attended

        raw_out[position] = lax.fori_loop(
            0, position + 1, gather_values, jnp.zeros((rows, group), F32)
        )
        lane = lax.broadcasted_iota(jnp.int32, (rows, 128), 1)
        kept = jnp.zeros((rows, 128), F32)
        for head in range(heads):
            kept = jnp.where(lane == head, highest[head] + jnp.log(total[head]), kept)
        lse_out[position] = kept

        @pl.when(position == span_count // 2 - 1)
        def second_parts():
            for member in gate_up_gathers[1:-1]:
                member.forward()

        @pl.when(position == span_count - 2)
        def last_part():
            gate_up_gathers[-1].forward()

        return unused

    gate_up_gathers[0].forward()
    lax.fori_loop(0, span_count, attend, 0)
    down_gather.share()

    for index in range(span_count):
        attended_send[index] = raw_out[order[index]].astype(BF)
    attended_exchange = Exchange(
        place, attended_send, attended_all, attended_send_sem, attended_recv_sem
    )
    attended_exchange.start()
    keep(raw_out, raw_result)
    keep(lse_out, lse_result)
    gate_up_gathers[0].share()
    out_gather.end()
    attended_exchange.wait()
    attended[...] = jnp.concatenate([attended_all[i] for i in range(span_count)], axis=1)

    hidden_mid = tokens[...].astype(F32) + dot_nn(attended[...], out_whole[...])
    outward[...] = hidden_mid
    scaled, inverse = normalize_parts(hidden_mid)
    normed[...] = (scaled * gains_out[1:2, :]).astype(BF)
    normed_left[...] = jnp.transpose(normed[...])
    attended_left[...] = jnp.transpose(attended[...])
    normed_grad[...] = jnp.zeros_like(normed_grad)
    down_gather.end()
    block = 256

    per_part = parts[0][1] // block

    def step(index, unused):
        for number in range(len(parts)):

            @pl.when(index == number * per_part)
            def columns_here():
                if number + 1 < len(parts):
                    gate_up_gathers[number + 1].share()
                gate_up_gathers[number].end()

        start = index // per_part * per_part * block
        size = jnp.minimum(per_part * block, hidden - start)
        offset = lax.rem(index, per_part) * block
        gate_at = pl.ds(pl.multiple_of(2 * start + offset, block), block)
        up_at = pl.ds(pl.multiple_of(2 * start + size + offset, block), block)
        here = pl.ds(pl.multiple_of(index * block, block), block)
        there = pl.ds(pl.multiple_of(hidden + index * block, block), block)
        gate = dot_nn(normed[...], gate_up_whole[:, gate_at])
        upward = dot_nn(normed[...], gate_up_whole[:, up_at])
        activation_grad = dot_nt(out_grad[...], down_whole[here, :])
        sigmoid = jax.nn.sigmoid(gate)
        swish = gate * sigmoid
        activation = (swish * upward).astype(BF)
        activation_left[here, :] = jnp.transpose(activation)
        gate_grad = (
            activation_grad * upward * sigmoid * (1.0 + gate * (1.0 - sigmoid))
        ).astype(BF)
        up_grad = (activation_grad * swish).astype(BF)
        gate_up_grad[:, here] = gate_grad
        gate_up_grad[:, there] = up_grad
        outward[...] += dot_nn(activation, down_whole[here, :])
        normed_grad[...] += dot_nt(gate_grad, gate_up_whole[:, gate_at]) + dot_nt(
            up_grad, gate_up_whole[:, up_at]
        )
        return unused

    lax.fori_loop(0, hidden // block, step, 0)
    keep(gate_up_grad, gate_up_grad_result)
    keep(activation_left, activation_result)
    layer_low[...] = outward[...].astype(BF)
    hidden_mid = tokens[...].astype(F32) + dot_nn(attended[...], out_whole[...])
    scaled, inverse = normalize_parts(hidden_mid)
    grad = out_grad[...].astype(F32) + norm_backward(
        normed_grad[...], scaled, inverse, gains_out[1:2, :]
    )
    mid_grad[...] = grad
    mid_grad_low[...] = grad.astype(BF)
    attended_grad[...] = dot_nt(mid_grad_low[...], out_whole[...]).astype(BF)

    for copy in gains_copies:
        copy.wait_send()
    for exchange in (first_exchange, counts_exchange, attended_exchange):
        exchange.finish()
    for step in range(span_count):

        @pl.when((span - step >= 0) & (span < last))
        def sent_up():
            pass_on(jnp.maximum(span - step, 0), step, 0).wait_send()

        @pl.when((span + step <= last) & (span > 0))
        def sent_down():
            pass_on(jnp.minimum(span + step, last), step, 1).wait_send()

    for copy in results:
        copy.wait()


def hidden_parts(hidden):
    size = 256 * -(-hidden // 1024)
    return [(start, min(size, hidden - start)) for start in range(0, hidden, size)]


def forward_call(
    dp_count, span_count, order, tokens, first_values, segments, gains_mine, qkv_mine,
    out_mine, gate_up_mine, down_mine, cosine, sine, out_grad,
):
    rows, width = tokens.shape
    group = width // span_count
    heads = group // HEAD_DIM
    owned = qkv_mine.shape[0]
    doubled = gate_up_mine.shape[1]
    hidden = doubled // 2
    gathers = 3 + len(hidden_parts(hidden))
    slots = Gather.slots(dp_count // 4)
    dma = pltpu.SemaphoreType.DMA
    by_span = (span_count, rows, group)
    kept = (
        ((width, span_count * rows), BF),
        (by_span, BF),
        (by_span, BF),
        (by_span, BF),
        (by_span, F32),
        ((span_count, rows, 128), F32),
        ((rows, doubled), BF),
        ((hidden, rows), BF),
    )
    return pl.pallas_call(
        functools.partial(forward_kernel, dp_count, span_count),
        out_shape=(
            jax.ShapeDtypeStruct((8, 128), F32),
            jax.ShapeDtypeStruct((8, width), F32),
            jax.ShapeDtypeStruct((rows, width), BF),
            jax.ShapeDtypeStruct((rows, width), F32),
            jax.ShapeDtypeStruct((rows, width), BF),
            jax.ShapeDtypeStruct((width, rows), BF),
            jax.ShapeDtypeStruct((width, rows), BF),
            jax.ShapeDtypeStruct((rows, width), BF),
            jax.ShapeDtypeStruct((width, 3 * group), BF),
        )
        + tuple(jax.ShapeDtypeStruct(shape, kind) for shape, kind in kept),
        in_specs=[pl.BlockSpec(memory_space=pltpu.SMEM)]
        + [full_spec()] * 4
        + [any_spec()]
        + [full_spec()] * 6,
        out_specs=(full_spec(),) * 8 + (any_spec(),) * 9,
        scratch_shapes=[pltpu.VMEM(shape, kind) for shape, kind in kept]
        + [
            pltpu.VMEM((8, owned), F32),
            pltpu.VMEM((owned, 3 * group), F32),
            pltpu.VMEM((width, width), BF),
            pltpu.VMEM((width, doubled), BF),
            pltpu.VMEM((hidden, width), BF),
            pltpu.VMEM((width, 3 * group), BF),
            pltpu.VMEM((rows, width), BF),
            pltpu.VMEM((rows, width), BF),
            pltpu.VMEM((rows, width), F32),
            pltpu.VMEM((rows, width), F32),
            pltpu.VMEM((dp_count, 8, owned), F32),
            pltpu.VMEM((span_count, 8, 128), F32),
            pltpu.VMEM((span_count, 8, 128), F32),
            pltpu.VMEM(by_span, BF),
            pltpu.VMEM(by_span, BF),
            pltpu.VMEM((span_count, rows, width), BF),
            pltpu.VMEM((heads, span_count, rows, rows), F32),
            pltpu.VMEM(by_span, BF),
            pltpu.VMEM(by_span, BF),
            dma((gathers, slots)),
            dma((gathers, slots)),
            dma((dp_count,)),
            dma((dp_count,)),
            dma((span_count,)),
            dma((span_count,)),
            dma((span_count,)),
            dma((span_count,)),
            dma((2, span_count)),
            dma((2, span_count)),
            dma((span_count,)),
            dma((span_count,)),
            dma((3,)),
            dma((9,)),
        ],
        compiler_params=pltpu.CompilerParams(
            collective_id=0, has_side_effects=True, vmem_limit_bytes=61 << 20
        ),
    )(
        order, tokens, first_values, segments, gains_mine, qkv_mine, out_mine,
        gate_up_mine, down_mine, cosine, sine, out_grad,
    )


class Pair:
    def __init__(
        self,
        place,
        left_whole,
        left,
        left_other,
        right_whole,
        right,
        right_other,
        send_sems,
        recv_sems,
    ):
        self.place = place
        self.left = left
        self.left_other = left_other
        self.right = right
        self.right_other = right_other
        other = (place.at(place.outer, place.inner, 1 - place.core), place.span)
        self.left_copy = remote(
            left_whole.at[:, 1 - place.core], left_other, send_sems.at[0], recv_sems.at[0], other
        )
        self.own_copy = pltpu.make_async_copy(
            left_whole.at[:, place.core], left, send_sems.at[2]
        )
        self.right_copy = remote(
            right_whole, right_other, send_sems.at[1], recv_sems.at[1], other
        )
        self.own_right = None
        if right_whole is not right:
            self.own_right = pltpu.make_async_copy(right_whole, right, send_sems.at[3])

    def lend_left(self):
        self.left_copy.start()
        self.own_copy.start()

    def lend_right(self):
        self.right_copy.start()
        self.own_right.start()

    def wait(self):
        self.own_copy.wait()
        if self.own_right is not None:
            self.own_right.wait()
        self.left_copy.wait_recv()
        self.right_copy.wait_recv()

    def finish(self):
        self.left_copy.wait_send()
        self.right_copy.wait_send()

    def product(self, outer, inner, columns):
        chip = outer * self.place.inner_count + inner
        depth = self.right.shape[1]
        found = None
        for block in range(self.right.shape[0]):
            at = slice(block * depth, (block + 1) * depth)
            mine = dot_nn(self.left[chip, :, at], self.right[block, :, columns])
            theirs = dot_nn(self.left_other[chip, :, at], self.right_other[block, :, columns])
            found = mine + theirs if found is None else found + mine + theirs
        return found


class Piece:
    def __init__(self, pair, columns, kind, buffers, sems, result):
        self.pair = pair
        self.place = pair.place
        self.columns = columns
        self.kind = kind
        self.send1, self.recv1, self.send2, self.recv2 = buffers[:4]
        mine = self.recv1.at[0, pair.place.inner if kind == 0 else pair.place.outer]
        self.line = [mine] + list(buffers[4:])
        self.send_sems, self.recv_sems = sems
        self.result = result
        self.sent = []

    def send(self, source, target, slot, far_slot, dp, span=None):
        copy = remote(
            source,
            target,
            self.send_sems.at[slot],
            self.recv_sems.at[far_slot],
            (dp, self.place.span if span is None else span),
        )
        copy.start()
        self.sent.append(copy)

    def arrived(self, target, slot):
        remote(
            target, target, self.send_sems.at[slot], self.recv_sems.at[slot], (self.place.dp, self.place.span)
        ).wait_recv()

    def across(self):
        place = self.place
        return place.at(1 - place.outer, place.inner, place.core)

    def beside(self, offset):
        place = self.place
        return place.at(place.outer, place.inner_plus(offset), place.core)

    def product(self, outer, inner):
        return self.pair.product(outer, inner, self.columns)

    def first(self):
        place, count = self.place, self.place.inner_count
        if self.kind == 0:
            for inner in range(count):
                self.send1[0, inner] = self.product(1 - place.outer, inner).astype(BF)
            self.send(self.send1.at[0], self.recv1.at[0], 0, 0, self.across())
            return
        for offset in range(1, count):
            for outer in range(2):
                self.send1[offset - 1, outer] = self.product(
                    outer, place.inner_plus(offset)
                ).astype(BF)
            self.send(
                self.send1.at[offset - 1],
                self.recv1.at[count - offset - 1],
                offset - 1,
                count - offset - 1,
                self.beside(offset),
            )

    def second(self):
        place, count = self.place, self.place.inner_count
        base = count
        if self.kind == 0:
            self.arrived(self.recv1.at[0], 0)
            for offset in range(1, count):
                inner = place.inner_plus(offset)
                total = self.product(place.outer, inner) + self.recv1[0, inner].astype(F32)
                self.send2[offset - 1] = total.astype(BF)
                self.send(
                    self.send2.at[offset - 1],
                    self.recv2.at[count - offset - 1],
                    base + offset - 1,
                    base + count - offset - 1,
                    self.beside(offset),
                )
            return
        total = self.product(1 - place.outer, place.inner)
        for offset in range(1, count):
            self.arrived(self.recv1.at[offset - 1], offset - 1)
            total = total + self.recv1[offset - 1, 1 - place.outer].astype(F32)
        self.send2[0] = total.astype(BF)
        self.send(self.send2.at[0], self.recv2.at[0], base, base, self.across())

    def total(self):
        place, count = self.place, self.place.inner_count
        base = count
        total = self.product(place.outer, place.inner)
        if self.kind == 0:
            total = total + self.recv1[0, place.inner].astype(F32)
            for offset in range(1, count):
                self.arrived(self.recv2.at[offset - 1], base + offset - 1)
                total = total + self.recv2[offset - 1].astype(F32)
            return total
        for offset in range(1, count):
            total = total + self.recv1[offset - 1, place.outer].astype(F32)
        self.arrived(self.recv2.at[0], base)
        return total + self.recv2[0].astype(F32)


    def shape_of_line(self):
        place = self.place
        half = place.span_count // 2
        low = place.span < half
        depth = jnp.where(low, place.span, place.span_count - 1 - place.span)
        inward = jnp.where(low, place.span + 1, place.span - 1)
        outward = jnp.where(low, place.span - 1, place.span + 1)
        outward = jnp.clip(outward, 0, place.span_count - 1)
        return half, depth, inward, outward

    def line_copy(self, source, target, slot, span):
        base = 2 * self.place.inner_count
        return remote(
            source,
            target,
            self.send_sems.at[base + slot],
            self.recv_sems.at[base + slot],
            (self.place.dp, span),
        )

    def send_inward(self):
        half, depth, inward, outward = self.shape_of_line()
        sum_here, from_out, from_mid = self.line

        @pl.when(depth == half - 1)
        def cross():
            self.line_copy(sum_here, from_mid, 1, inward).start()

        @pl.when(depth < half - 1)
        def in_():
            self.line_copy(sum_here, from_out, 0, inward).start()

    def line_start(self):
        half, depth, inward, outward = self.shape_of_line()
        sum_here, from_out, from_mid = self.line
        sum_here[...] = self.total().astype(BF)

        @pl.when(depth == 0)
        def go():
            self.send_inward()

    def line_in(self):
        half, depth, inward, outward = self.shape_of_line()
        sum_here, from_out, from_mid = self.line

        @pl.when(depth > 0)
        def go():
            self.line_copy(from_out, from_out, 0, outward).wait_recv()
            sum_here[...] = (sum_here[...].astype(F32) + from_out[...].astype(F32)).astype(BF)
            self.send_inward()

    def line_mid(self):
        half, depth, inward, outward = self.shape_of_line()
        sum_here, from_out, from_mid = self.line

        @pl.when(depth == half - 1)
        def go():
            self.line_copy(from_mid, from_mid, 1, inward).wait_recv()
            self.result[...] = (
                sum_here[...].astype(F32) + from_mid[...].astype(F32)
            ).astype(BF)

            @pl.when(depth > 0)
            def out():
                self.line_copy(self.result, self.result, 2, outward).start()

    def line_out(self):
        half, depth, inward, outward = self.shape_of_line()

        @pl.when(depth < half - 1)
        def go():
            self.line_copy(self.result, self.result, 2, inward).wait_recv()

            @pl.when(depth > 0)
            def out():
                self.line_copy(self.result, self.result, 2, outward).start()

    def line_finish(self):
        half, depth, inward, outward = self.shape_of_line()
        sum_here, from_out, from_mid = self.line

        @pl.when(depth == half - 1)
        def cross():
            self.line_copy(sum_here, from_mid, 1, inward).wait_send()

        @pl.when(depth < half - 1)
        def in_():
            self.line_copy(sum_here, from_out, 0, inward).wait_send()

        @pl.when(depth > 0)
        def out():
            self.line_copy(self.result, self.result, 2, outward).wait_send()


    def spread_start(self, results):
        place = self.place
        base = 2 * place.inner_count
        self.results = results
        results[place.span, :, self.columns] = self.total().astype(BF)
        for offset in range(1, place.span_count):
            peer = lax.rem(place.span + offset, place.span_count)
            block = results.at[place.span, :, self.columns]
            self.send(
                block, block, base + offset, base + place.span_count - offset, place.dp, peer
            )

    def spread_wait(self):
        place = self.place
        base = 2 * place.inner_count
        for offset in range(1, place.span_count):
            peer = lax.rem(place.span + offset, place.span_count)
            self.arrived(self.results.at[peer, :, self.columns], base + offset)

    def finish(self):
        for copy in self.sent:
            copy.wait_send()


def cut_columns(width):
    if width > 4096:
        quarter = width // 4 // 128 * 128
        return [slice(i * quarter, (i + 1) * quarter if i < 3 else width) for i in range(4)]
    half = width // 2 // 128 * 128
    return [slice(0, half), slice(half, width)]


def piece_scratch(inner_count, rows, columns, kind, on_line):
    width = columns.stop - columns.start
    if kind == 0:
        shapes = [(1, inner_count, rows, width)] * 2 + [(inner_count - 1, rows, width)] * 2
    else:
        shapes = [(inner_count - 1, 2, rows, width)] * 2 + [(1, rows, width)] * 2
    if on_line:
        shapes += [(rows, width)] * 2
    return shapes


GATE_UP, DOWN, OUT, QKV = range(4)
WAIT_PAIR, ATTEND, CLOSE, WAIT_GRAD, LEND_MIXED, SEND_BLENDED, WAIT_BLENDED, CHAIN, CHAIN_END = range(9)
ORDER = (
    (WAIT_PAIR, DOWN, 0),
    (Piece.first, DOWN, 0),
    (Piece.first, DOWN, 1),
    (WAIT_PAIR, GATE_UP, 0),
    (Piece.first, GATE_UP, 2),
    (Piece.first, GATE_UP, 3),
    (WAIT_GRAD, None, 0),
    (WAIT_PAIR, OUT, 0),
    (Piece.first, GATE_UP, 0),
    (ATTEND, None, 0),
    (CLOSE, None, 0),
    (SEND_BLENDED, None, 0),
    (Piece.second, DOWN, 0),
    (Piece.second, GATE_UP, 2),
    (Piece.line_start, DOWN, 0),
    (LEND_MIXED, None, 0),
    (Piece.second, DOWN, 1),
    (Piece.second, GATE_UP, 0),
    (Piece.line_start, GATE_UP, 2),
    (Piece.first, OUT, 0),
    (Piece.first, OUT, 1),
    (Piece.line_in, DOWN, 0),
    (Piece.second, GATE_UP, 3),
    (Piece.line_in, GATE_UP, 2),
    (WAIT_PAIR, QKV, 0),
    (Piece.first, GATE_UP, 1),
    (Piece.line_start, GATE_UP, 0),
    (Piece.line_mid, DOWN, 0),
    (Piece.second, OUT, 1),
    (Piece.line_start, DOWN, 1),
    (Piece.second, OUT, 0),
    (Piece.line_in, GATE_UP, 0),
    (Piece.line_start, GATE_UP, 3),
    (Piece.first, QKV, 0),
    (Piece.line_start, OUT, 1),
    (WAIT_BLENDED, None, 0),
    (Piece.line_in, DOWN, 1),
    (Piece.line_mid, GATE_UP, 2),
    (Piece.second, GATE_UP, 1),
    (Piece.second, QKV, 0),
    (Piece.line_start, OUT, 0),
    (Piece.line_out, DOWN, 0),
    (Piece.first, QKV, 1),
    (Piece.line_in, GATE_UP, 3),
    (Piece.line_mid, GATE_UP, 0),
    (CHAIN, None, 0),
    (Piece.line_out, GATE_UP, 2),
    (Piece.spread_start, QKV, 0),
    (Piece.second, QKV, 1),
    (Piece.line_mid, DOWN, 1),
    (Piece.line_in, OUT, 0),
    (Piece.line_mid, GATE_UP, 3),
    (Piece.line_start, GATE_UP, 1),
    (CHAIN, None, 1),
    (Piece.line_in, OUT, 1),
    (Piece.spread_start, QKV, 1),
    (Piece.spread_wait, QKV, 0),
    (Piece.line_mid, OUT, 0),
    (Piece.line_mid, OUT, 1),
    (Piece.line_out, OUT, 1),
    (Piece.line_out, DOWN, 1),
    (Piece.line_in, GATE_UP, 1),
    (Piece.line_out, GATE_UP, 0),
    (Piece.line_out, GATE_UP, 3),
    (CHAIN, None, 2),
    (Piece.line_mid, GATE_UP, 1),
    (CHAIN_END, None, 0),
    (Piece.line_out, GATE_UP, 1),
    (Piece.line_out, OUT, 0),
    (Piece.spread_wait, QKV, 1),
)


def backward_kernel(
    dp_count,
    span_count,
    order,
    gate_up_left,
    gate_up_right,
    down_left,
    down_right,
    out_left,
    out_right,
    qkv_left,
    attended_grad_whole,
    query_whole,
    key_whole,
    value_whole,
    raw_whole,
    lse_whole,
    qkv_whole,
    counts,
    cosine,
    sine,
    gate_up_result,
    down_result,
    out_result,
    qkv_result,
    blended_result,
    normed_result,
    attended_grad,
    query,
    key,
    value,
    raw,
    lse,
    qkv_copy,
    load_sem,
    gate_up_own,
    gate_up_other,
    gate_up_right_own,
    gate_up_right_other,
    down_own,
    down_other,
    down_right_own,
    down_right_other,
    out_own,
    out_other,
    out_right_own,
    out_right_other,
    qkv_own,
    qkv_other,
    mixed_other,
    mixed,
    grad_send,
    grad_all,
    key_sum,
    value_sum,
    key_turned,
    query_sum,
    blended_all,
    chain,
    pair_send,
    pair_recv,
    piece_send,
    piece_recv,
    grad_send_sem,
    grad_recv_sem,
    blended_send_sem,
    blended_recv_sem,
    chain_send,
    chain_recv,
    *piece_buffers,
):
    place = Place(dp_count, span_count)
    span, last = place.span, span_count - 1
    rows, width = attended_grad.shape
    group = width // span_count
    heads = group // HEAD_DIM

    loads = []
    for source, target in (
        (attended_grad_whole, attended_grad),
        (key_whole, key),
        (query_whole, query),
        (value_whole, value),
        (raw_whole, raw),
        (lse_whole, lse),
        (qkv_whole, qkv_copy),
    ):
        loads.append(pltpu.make_async_copy(source, target, load_sem.at[len(loads)]))
        loads[-1].start()
    place.greet_all()
    loads[0].wait()
    for index in range(span_count):
        grad_send[index] = attended_grad[:, index * group : (index + 1) * group]
    grad_exchange = Exchange(place, grad_send, grad_all, grad_send_sem, grad_recv_sem)
    grad_exchange.start()
    pairs = [
        Pair(place, *members, pair_send.at[i], pair_recv.at[i])
        for i, members in enumerate(
            (
                (
                    gate_up_left, gate_up_own, gate_up_other,
                    gate_up_right, gate_up_right_own, gate_up_right_other,
                ),
                (down_left, down_own, down_other, down_right, down_right_own, down_right_other),
                (out_left, out_own, out_other, out_right, out_right_own, out_right_other),
                (qkv_left, qkv_own, qkv_other, mixed, mixed, mixed_other),
            )
        )
    ]
    for which in (OUT, DOWN, GATE_UP):
        pairs[which].lend_left()
        pairs[which].lend_right()
    pairs[QKV].lend_left()

    free = list(piece_buffers)
    pieces = []
    for pair, result, on_line in zip(
        pairs, (gate_up_result, down_result, out_result, qkv_result), (True, True, True, False)
    ):
        members = []
        for i, columns in enumerate(cut_columns(pair.right.shape[2])):
            number = 6 if on_line else 4
            buffers, free = free[:number], free[number:]
            at = len(pieces) * 4 + i
            members.append(
                Piece(
                    pair,
                    columns,
                    i % 2,
                    buffers,
                    (piece_send.at[at], piece_recv.at[at]),
                    result.at[:, columns] if on_line else None,
                )
            )
        pieces.append(members)
    def clear(index, unused):
        key_sum[index] = jnp.zeros((rows, group), F32)
        value_sum[index] = jnp.zeros((rows, group), F32)
        return unused

    lax.fori_loop(0, span_count, clear, 0)

    def clear_chain(index, unused):
        chain[index] = jnp.zeros(chain.shape[1:], BF)
        return unused

    @pl.when(span == 0)
    def nothing_from_below():
        lax.fori_loop(1, span_count + 1, clear_chain, 0)

    @pl.when(span == last)
    def nothing_from_above():
        lax.fori_loop(0, span_count, clear_chain, 0)

    cuts = counts[...]
    bounds = [cuts[i : i + 1, 0:1] for i in range(3)]

    def turned_back(rows_in, position):
        cos_here, sin_here = angles_of(cosine, sine, position, heads)
        low = rows_in.astype(BF).astype(F32)
        return (low * cos_here - swap_halves(low) * sin_here).astype(BF)

    for copy in loads[1:]:
        copy.wait()

    def turn_keys(position, unused):
        key_turned[position] = jnp.transpose(key[position])
        return unused

    lax.fori_loop(0, span_count, turn_keys, 0)

    def attend_back(position, unused):
        query_here = (query[position].astype(F32) * SCALE).astype(BF)
        grad_here = grad_all[slot_with(order, position)]
        query_parts = [head_part(query_here, head) for head in range(heads)]
        grad_parts = [head_part(grad_here, head) for head in range(heads)]
        query_stack = jnp.concatenate(query_parts, axis=0)
        grad_stack = jnp.concatenate(grad_parts, axis=0)
        agreed = jnp.transpose(grad_here.astype(F32) * raw[position])
        logs = jnp.transpose(lse[position])
        query_position = (
            lax.broadcasted_iota(jnp.int32, (1, rows), 1) + position * rows
        ).astype(F32)
        start = jnp.zeros((1, rows), F32)
        for cut in bounds:
            start = jnp.where(query_position >= cut, cut, start)
        query_sum[...] = jnp.zeros((group, rows), F32)

        def block(other, unused):
            key_here, value_here, key_back = key[other], value[other], key_turned[other]
            key_position = (
                lax.broadcasted_iota(jnp.int32, (rows, 1), 0) + other * rows
            ).astype(F32)
            allowed = (key_position <= query_position) & (key_position >= start)
            lows, grads = [], []
            for head in range(heads):
                at = slice(head * HEAD_DIM, (head + 1) * HEAD_DIM)
                scores = dot_nt(key_here, query_parts[head])
                weights = jnp.where(allowed, jnp.exp(scores - logs[head : head + 1]), 0.0)
                weights_grad = dot_nt(value_here, grad_parts[head])
                delta = jnp.sum(agreed[at], axis=0, keepdims=True)
                scores_grad = (weights * (weights_grad - delta)).astype(BF)
                lows.append(weights.astype(BF))
                grads.append(scores_grad)
                query_sum[at, :] += dot_nn(key_back[at], scores_grad)
            key_sum[other] += dot_nn(jnp.concatenate(grads, axis=1), query_stack)
            value_sum[other] += dot_nn(jnp.concatenate(lows, axis=1), grad_stack)
            return unused

        lax.fori_loop(0, position + 1, block, 0)
        mixed[position, :, :group] = turned_back(
            jnp.transpose(query_sum[...]) * SCALE, position
        )
        return unused

    def close(position, unused):
        mixed[position, :, group : 2 * group] = turned_back(key_sum[position], position)
        mixed[position, :, 2 * group :] = (
            BLEND_MIX * value_sum[position].astype(BF).astype(F32)
        ).astype(BF)
        return unused

    blended_send = grad_send
    blended_exchange = Exchange(
        place, blended_send, blended_all, blended_send_sem, blended_recv_sem
    )

    def normed_grad(block):
        return dot_nt(mixed[order[block]], qkv_copy[...])

    def pass_on(block, way):
        return remote(
            chain.at[block + 1 - way],
            chain.at[block + 1 - way],
            chain_send.at[way, block],
            chain_recv.at[way, block],
            (place.dp, jnp.minimum(span + 1, last) if way == 0 else jnp.maximum(span - 1, 0)),
        )

    def chain_step(step):
        up = last + span - step
        down = step - (last - span)

        @pl.when((span <= step) & (up > span))
        def going_up():
            block = jnp.clip(up, 0, last)

            @pl.when(span > 0)
            def more():
                pass_on(block, 0).wait_recv()

            chain[block + 1] = (normed_grad(block) + chain[block + 1].astype(F32)).astype(BF)
            pass_on(block, 0).start()

        @pl.when((down >= 0) & (down < span))
        def going_down():
            block = jnp.clip(down, 0, last)

            @pl.when(span < last)
            def more():
                pass_on(block, 1).wait_recv()

            chain[block] = (normed_grad(block) + chain[block].astype(F32)).astype(BF)
            pass_on(block, 1).start()

    def chain_end():
        @pl.when(span > 0)
        def from_below():
            pass_on(span, 0).wait_recv()

        @pl.when(span < last)
        def from_above():
            pass_on(span, 1).wait_recv()

        normed_result[...] = (
            normed_grad(span) + chain[span + 1].astype(F32) + chain[span].astype(F32)
        )

    def send_blended():
        grad_exchange.finish()
        for index in range(span_count):
            blended_send[index] = value_sum[order[index]].astype(BF)
        blended_exchange.start()

    def keep_blended():
        blended_exchange.wait()
        blended_result[...] = jnp.concatenate(
            [blended_all[i] for i in range(span_count)], axis=1
        )

    single = {
        WAIT_GRAD: grad_exchange.wait,
        CLOSE: lambda: lax.fori_loop(0, span_count, close, 0),
        LEND_MIXED: pairs[3].right_copy.start,
        SEND_BLENDED: send_blended,
        WAIT_BLENDED: keep_blended,
        CHAIN_END: chain_end,
    }
    for action, which, number in ORDER:
        if action in single:
            single[action]()
        elif action == WAIT_PAIR:
            pairs[which].wait()
        elif action == ATTEND:
            lax.fori_loop(0, span_count, attend_back, 0)
        elif action == CHAIN:
            for step in [number] if number < 2 else range(2, last):
                chain_step(step)
        elif action == Piece.spread_start:
            pieces[which][number].spread_start(qkv_result)
        else:
            action(pieces[which][number])

    for pair in pairs:
        pair.finish()
    blended_exchange.finish()
    for which, members in enumerate(pieces):
        for member in members:
            if which != QKV:
                member.line_finish()
            member.finish()
    for step in range(last):
        up = last + span - step
        down_block = step - (last - span)

        @pl.when((span <= step) & (up > span))
        def sent_up():
            pass_on(jnp.clip(up, 0, last), 0).wait_send()

        @pl.when((down_block >= 0) & (down_block < span))
        def sent_down():
            pass_on(jnp.clip(down_block, 0, last), 1).wait_send()


def backward_call(dp_count, span_count, order, factors, others, tables):
    (gate_up_left, gate_up_right, down_left, down_right, out_left, out_right, qkv_left) = factors
    rows, width = others[0].shape
    kept = [pltpu.VMEM(member.shape, member.dtype) for member in others]
    group = width // span_count
    inner_count = dp_count // 4
    dma = pltpu.SemaphoreType.DMA
    by_span = (span_count, rows, group)
    mixed_shape = (span_count, rows, 3 * group)

    def less(left):
        return (left.shape[0],) + left.shape[2:]

    scratch = []
    for left, columns_in, on_line in (
        (gate_up_left, gate_up_right.shape[2], True),
        (down_left, down_right.shape[2], True),
        (out_left, out_right.shape[2], True),
        (qkv_left, 3 * group, False),
    ):
        for i, columns in enumerate(cut_columns(columns_in)):
            scratch += [
                pltpu.VMEM(shape, BF)
                for shape in piece_scratch(inner_count, left.shape[2], columns, i % 2, on_line)
            ]
    slots = 2 * inner_count + max(3, span_count)
    return pl.pallas_call(
        functools.partial(backward_kernel, dp_count, span_count),
        out_shape=(
            jax.ShapeDtypeStruct((gate_up_left.shape[2], gate_up_right.shape[2]), BF),
            jax.ShapeDtypeStruct((down_left.shape[2], down_right.shape[2]), BF),
            jax.ShapeDtypeStruct((out_left.shape[2], out_right.shape[2]), BF),
            jax.ShapeDtypeStruct((span_count, qkv_left.shape[2], 3 * group), BF),
            jax.ShapeDtypeStruct((rows, width), BF),
            jax.ShapeDtypeStruct((rows, width), F32),
        ),
        in_specs=[pl.BlockSpec(memory_space=pltpu.SMEM)]
        + [any_spec()] * (len(factors) + len(others))
        + [full_spec()] * len(tables),
        out_specs=(full_spec(),) * 6,
        scratch_shapes=kept
        + [
            dma((len(others),)),
            pltpu.VMEM(less(gate_up_left), BF),
            pltpu.VMEM(less(gate_up_left), BF),
            pltpu.VMEM(gate_up_right.shape, BF),
            pltpu.VMEM(gate_up_right.shape, BF),
            pltpu.VMEM(less(down_left), BF),
            pltpu.VMEM(less(down_left), BF),
            pltpu.VMEM(down_right.shape, BF),
            pltpu.VMEM(down_right.shape, BF),
            pltpu.VMEM(less(out_left), BF),
            pltpu.VMEM(less(out_left), BF),
            pltpu.VMEM(out_right.shape, BF),
            pltpu.VMEM(out_right.shape, BF),
            pltpu.VMEM(less(qkv_left), BF),
            pltpu.VMEM(less(qkv_left), BF),
            pltpu.VMEM(mixed_shape, BF),
            pltpu.VMEM(mixed_shape, BF),
            pltpu.VMEM(by_span, BF),
            pltpu.VMEM(by_span, BF),
            pltpu.VMEM(by_span, F32),
            pltpu.VMEM(by_span, F32),
            pltpu.VMEM((span_count, group, rows), BF),
            pltpu.VMEM((group, rows), F32),
            pltpu.VMEM(by_span, BF),
            pltpu.VMEM((span_count + 1, rows, width), BF),
            dma((4, 4)),
            dma((4, 4)),
            dma((16, slots)),
            dma((16, slots)),
            dma((span_count,)),
            dma((span_count,)),
            dma((span_count,)),
            dma((span_count,)),
            dma((2, span_count)),
            dma((2, span_count)),
        ]
        + scratch,
        compiler_params=pltpu.CompilerParams(
            collective_id=1, has_side_effects=True, vmem_limit_bytes=61 << 20
        ),
    )(order, *factors, *others, *tables)


def update_rows(master, first_state, second_state, gradient, rate, decay):
    next_first = BETA_FIRST * first_state + (1.0 - BETA_FIRST) * gradient
    next_second = BETA_SECOND * second_state + (1.0 - BETA_SECOND) * gradient * gradient
    first_hat = next_first * (1.0 / (1.0 - BETA_FIRST**STEP))
    second_hat = next_second * (1.0 / (1.0 - BETA_SECOND**STEP))
    new_master = master - rate * (first_hat / (jnp.sqrt(second_hat) + ADAM_EPS) + decay * master)
    return (new_master, next_first, next_second)


def finish_kernel(
    qkv_total,
    out_total,
    gate_up_total,
    down_total,
    gains,
    gains_first,
    gains_second,
    tokens,
    mid_grad,
    normed_grad,
    gains_rows,
    blended_grad,
    layer_low,
    qkv,
    qkv_first,
    qkv_second,
    out,
    out_first,
    out_second,
    gate_up,
    gate_up_first,
    gate_up_second,
    down,
    down_first,
    down_second,
    layer_out,
    tokens_grad,
    values_grad,
    new_gains,
    new_gains_first,
    new_gains_second,
    *rest,
):
    results, held, sums, in_sem, out_sem = rest[:12], rest[12:24], rest[24], rest[25], rest[26]
    states = (
        (qkv, qkv_first, qkv_second),
        (out, out_first, out_second),
        (gate_up, gate_up_first, gate_up_second),
        (down, down_first, down_second),
    )
    width = tokens.shape[1]
    span_count = qkv_total.shape[0]
    group = width // span_count

    def qkv_rows(part):
        def rows(at):
            return jnp.concatenate(
                [
                    qkv_total[i, at, part * group : (part + 1) * group].astype(F32)
                    for i in range(span_count)
                ],
                axis=1,
            )

        return rows

    def rows_of(total, columns):
        return lambda at: total[at, columns].astype(F32)

    parts = []
    for columns in cut_columns(gate_up_total.shape[1]):
        parts.append((2, columns, rows_of(gate_up_total, columns)))
    for part in range(3):
        parts.append((0, slice(part * width, (part + 1) * width), qkv_rows(part)))
    for columns in cut_columns(width):
        parts.append((3, columns, rows_of(down_total, columns)))
    parts.append((1, slice(0, width), rows_of(out_total, slice(0, width))))

    def moves(number, source, target, sems):
        weight, columns, _ = parts[number]
        return [
            pltpu.make_async_copy(
                source[i].at[:, columns], target[i].at[:, columns], sems.at[number, i]
            )
            for i in range(3)
        ]

    loads, stores = [], []
    for number, (weight, _, _) in enumerate(parts):
        here = held[3 * weight : 3 * weight + 3]
        loads.append(moves(number, states[weight], here, in_sem))
        stores.append(moves(number, here, results[3 * weight : 3 * weight + 3], out_sem))
        for copy in loads[-1]:
            copy.start()

    residual = tokens[...].astype(F32)
    scaled, inverse = normalize_parts(residual)
    tokens_grad[...] = mid_grad[...] + norm_backward(
        normed_grad[...], scaled, inverse, gains_rows[0:1, :]
    )
    layer_out[...] = layer_low[...]
    sums[...] = jnp.zeros_like(sums)
    values_grad[...] = (1.0 - BLEND_MIX) * blended_grad[...].astype(F32)

    for number, (weight, columns, total) in enumerate(parts):
        here = held[3 * weight : 3 * weight + 3]
        for copy in loads[number]:
            copy.wait()
        owned = here[0].shape[0]
        wants_sum = weight in (0, 2)

        def step(index, unused):
            at = pl.ds(pl.multiple_of(index * 16, 16), 16)
            gradient = total(at)
            master = here[0][at, columns]
            if wants_sum:
                partial = jnp.sum(
                    gradient * master.astype(BF).astype(F32), axis=1, keepdims=True
                )
                lane = 0 if weight == 0 else 1
                slot = lax.broadcasted_iota(jnp.int32, (16, 128), 1) == lane
                sums[at, :] += jnp.where(slot, partial, 0.0)
            updated = update_rows(
                master,
                here[1][at, columns],
                here[2][at, columns],
                gradient,
                MATRIX_RATE,
                MATRIX_DECAY,
            )
            for i in range(3):
                here[i][at, columns] = updated[i]
            return unused

        lax.fori_loop(0, owned // 16, step, 0)
        for copy in stores[number]:
            copy.start()

    gain = gains[...]
    gains_total = jnp.transpose(sums[...])[:2, :] / gain.astype(BF).astype(F32)
    updated = update_rows(gain, gains_first[...], gains_second[...], gains_total, GAIN_RATE, 0.0)
    new_gains[...], new_gains_first[...], new_gains_second[...] = updated
    for group_of_copies in stores:
        for copy in group_of_copies:
            copy.wait()


def finish_call(totals, gains_states, token_parts, states):
    flat = [member for weight in states for member in weight]
    rows, width = token_parts[0].shape
    gains_shape = jax.ShapeDtypeStruct(gains_states[0].shape, F32)
    dma = pltpu.SemaphoreType.DMA
    count = len(cut_columns(totals[2].shape[1])) + 3 + 2 + 1
    return pl.pallas_call(
        finish_kernel,
        out_shape=(
            jax.ShapeDtypeStruct((rows, width), BF),
            jax.ShapeDtypeStruct((rows, width), F32),
            jax.ShapeDtypeStruct((rows, width), F32),
            gains_shape,
            gains_shape,
            gains_shape,
        )
        + tuple(jax.ShapeDtypeStruct(member.shape, F32) for member in flat),
        in_specs=[full_spec()] * 13 + [any_spec()] * 12,
        out_specs=(full_spec(),) * 6 + (any_spec(),) * 12,
        scratch_shapes=[pltpu.VMEM(member.shape, F32) for member in flat]
        + [
            pltpu.VMEM((gains_states[0].shape[1], 128), F32),
            dma((count, 3)),
            dma((count, 3)),
        ],
        compiler_params=pltpu.CompilerParams(vmem_limit_bytes=VMEM_BYTES),
    )(*totals, *gains_states, *token_parts, *flat)


def to_heads(rows, span_count):
    return lax.all_to_all(
        rows.reshape(rows.shape[0], span_count, rows.shape[1] // span_count),
        "seq",
        split_axis=1,
        concat_axis=0,
        tiled=True,
    ).reshape(rows.shape[0] * span_count, rows.shape[1] // span_count)


def to_spans(columns, span_count):
    rows_here = columns.shape[0] // span_count
    got = lax.all_to_all(
        columns.reshape(span_count, rows_here, columns.shape[1]),
        "seq",
        split_axis=0,
        concat_axis=0,
        tiled=True,
    )
    return jnp.transpose(got, (1, 0, 2)).reshape(rows_here, columns.shape[1] * span_count)


def on_device(
    tokens,
    first_values,
    out_grad,
    segments,
    span_order,
    qkv_weight,
    out_weight,
    gate_up_weight,
    down_weight,
    norm_gains,
    first_qkv,
    first_out,
    first_gate_up,
    first_down,
    first_gains,
    second_qkv,
    second_out,
    second_gate_up,
    second_down,
    second_gains,
):
    span_count = lax.axis_size("seq")
    mine = lax.axis_index("seq")
    owned_rows, triple = qkv_weight.shape
    model_width = triple // 3
    group = model_width // span_count
    group_heads = group // HEAD_DIM
    residual = tokens[0].astype(F32)
    rows_here = residual.shape[0]
    length = rows_here * span_count
    hidden_width = gate_up_weight.shape[1] // 2

    dp_count = lax.axis_size("dp")
    gains_owned = norm_gains.astype(BF).astype(F32)
    in_kernels = (
        length * model_width <= 1 << 20
        and dp_count % 4 == 0
        and dp_count >= 8
        and span_count % 2 == 0
        and group % 128 == 0
        and span_count * HEAD_DIM // 2 <= 128
        and hidden_width % 256 == 0
    )
    if in_kernels:
        half_width = HEAD_DIM // 2
        lane = lax.broadcasted_iota(jnp.int32, (rows_here, 128), 1)
        position = lax.broadcasted_iota(jnp.int32, (rows_here, 128), 0) + lane // half_width * rows_here
        frequency = jnp.exp(
            (jnp.arange(128, dtype=jnp.int32) % half_width).astype(F32)
            * (-math.log(ROPE_BASE) / half_width)
        )
        angles = lax.optimization_barrier(position).astype(F32) * frequency[None, :]
        cosine, sine = jnp.cos(angles), jnp.sin(angles)
        gains_states = tuple(
            jnp.transpose(member) for member in (norm_gains, first_gains, second_gains)
        )
        (
            counts, gains_rows, layer_low, hidden_mid_grad, mid_grad_low, normed_mid_left,
            attended_left, attended_grad, qkv_copy, normed_left, query_pos, key_pos, value_pos,
            raw_pos, lse_pos, gate_up_grad, activation_left,
        ) = forward_call(
            dp_count, span_count, span_order, tokens[0], first_values[0], segments,
            gains_states[0], qkv_weight, out_weight, gate_up_weight, down_weight, cosine, sine, out_grad[0],
        )
        def in_blocks(left):
            return left.reshape(dp_count // 2, 2, left.shape[0] // dp_count, left.shape[1])

        factors = (
            in_blocks(normed_mid_left),
            gate_up_grad[None],
            in_blocks(activation_left),
            out_grad,
            in_blocks(attended_left),
            mid_grad_low[None],
            in_blocks(normed_left),
        )
        others = (
            attended_grad,
            query_pos, key_pos, value_pos, raw_pos, lse_pos, qkv_copy,
        )
        gate_up_total, down_total, out_total, qkv_part, blended_grad, normed_in_grad = backward_call(
            dp_count, span_count, span_order, factors, others, (counts, cosine, sine)
        )
        finished = finish_call(
            (qkv_part, out_total, gate_up_total, down_total),
            gains_states,
            (tokens[0], hidden_mid_grad, normed_in_grad, gains_rows, blended_grad, layer_low),
            (
                (qkv_weight, first_qkv, second_qkv),
                (out_weight, first_out, second_out),
                (gate_up_weight, first_gate_up, second_gate_up),
                (down_weight, first_down, second_down),
            ),
        )
        new_gains = tuple(jnp.transpose(member) for member in finished[3:6])
        return (
            tuple(member[None] for member in finished[:3])
            + finished[6::3]
            + new_gains[:1]
            + finished[7::3]
            + new_gains[1:2]
            + finished[8::3]
            + new_gains[2:]
        )

    qkv_owned = qkv_weight.reshape(owned_rows, 3, model_width).astype(BF)
    qkv_mine = lax.dynamic_slice_in_dim(qkv_owned, mine * group, group, 2).reshape(
        owned_rows, 3 * group
    )
    gains_full = lax.all_gather(norm_gains.astype(BF), "dp", axis=0, tiled=True).astype(F32)
    qkv_copy = lax.all_gather(qkv_mine, "dp", axis=0, tiled=True)
    out_copy = lax.all_gather(out_weight.astype(BF), "dp", axis=0, tiled=True)
    gate_up_copy = lax.all_gather(gate_up_weight.astype(BF), "dp", axis=0, tiled=True)
    down_copy = lax.all_gather(down_weight.astype(BF), "dp", axis=0, tiled=True)

    row_index = jnp.arange(length, dtype=jnp.int32)
    owner_table = (row_index // rows_here)[:, None] == jnp.arange(span_count, dtype=jnp.int32)[
        None, :
    ]
    positions = (
        jnp.sum(jnp.where(owner_table, span_order[None, :], 0), axis=1) * rows_here
        + row_index % rows_here
    )
    all_segments = lax.all_gather(segments[0], "seq", axis=0, tiled=True)
    cosine, sine_table = rotary(positions)
    allowed = (all_segments[:, None] == all_segments[None, :]) & (
        positions[None, :] <= positions[:, None]
    )

    scaled_in, inverse_in = normalize_parts(residual)
    normed_in = (scaled_in * gains_full[:, 0]).astype(BF)
    normed_all = lax.all_gather(normed_in, "seq", axis=0, tiled=True)
    first_all = to_heads(first_values[0], span_count)
    mixed = dot_nn(normed_all, qkv_copy)
    queries = rotate(
        mixed[:, :group].reshape(length, group_heads, HEAD_DIM), cosine, sine_table
    ).astype(BF)
    keys = rotate(
        mixed[:, group : 2 * group].reshape(length, group_heads, HEAD_DIM), cosine, sine_table
    ).astype(BF)
    blended = (
        (BLEND_MIX * mixed[:, 2 * group :] + (1.0 - BLEND_MIX) * first_all.astype(F32))
        .astype(BF)
        .reshape(length, group_heads, HEAD_DIM)
    )
    scores = jnp.einsum("qhd,khd->hqk", queries, keys, preferred_element_type=F32) * SCALE
    masked = jnp.where(allowed[None], scores, MASK_FILL)
    highest = jnp.max(masked, axis=-1, keepdims=True)
    raised = jnp.where(allowed[None], jnp.exp(masked - highest), 0.0)
    weights = raised / jnp.sum(raised, axis=-1, keepdims=True)
    weights_low = weights.astype(BF)
    attended_raw = jnp.einsum("hqk,khd->qhd", weights_low, blended, preferred_element_type=F32)
    attended = to_spans(attended_raw.reshape(length, group).astype(BF), span_count)

    hidden_mid = residual + dot_nn(attended, out_copy)
    scaled_mid, inverse_mid = normalize_parts(hidden_mid)
    normed_mid = (scaled_mid * gains_full[:, 1]).astype(BF)
    gate_up = dot_nn(normed_mid, gate_up_copy)
    gate_part = gate_up[:, :hidden_width]
    upward = gate_up[:, hidden_width:]
    sigmoid_gate = jax.nn.sigmoid(gate_part)
    swish_gate = gate_part * sigmoid_gate
    activation = (swish_gate * upward).astype(BF)
    layer_out = (hidden_mid + dot_nn(activation, down_copy)).astype(BF)
    back_rows = out_grad[0]
    activation_grad = dot_nt(back_rows, down_copy)
    gate_up_grad = jnp.concatenate(
        [
            activation_grad * upward * sigmoid_gate * (1.0 + gate_part * (1.0 - sigmoid_gate)),
            activation_grad * swish_gate,
        ],
        axis=1,
    ).astype(BF)
    normed_mid_grad = dot_nt(gate_up_grad, gate_up_copy)
    hidden_mid_grad = back_rows.astype(F32) + norm_backward(
        normed_mid_grad, scaled_mid, inverse_mid, gains_full[:, 1]
    )
    mid_grad_low = hidden_mid_grad.astype(BF)
    attended_grad = to_heads(dot_nt(mid_grad_low, out_copy).astype(BF), span_count)

    heads_grad = attended_grad.reshape(length, group_heads, HEAD_DIM)
    delta = jnp.transpose(jnp.sum(heads_grad.astype(F32) * attended_raw, axis=-1))
    weights_grad = jnp.einsum("qhd,khd->hqk", heads_grad, blended, preferred_element_type=F32)
    scores_grad = (weights * (weights_grad - delta[..., None])).astype(BF)
    queries_grad = (
        jnp.einsum("hqk,khd->qhd", scores_grad, keys, preferred_element_type=F32) * SCALE
    ).astype(BF).astype(F32)
    keys_grad = (
        jnp.einsum("hqk,qhd->khd", scores_grad, queries, preferred_element_type=F32) * SCALE
    ).astype(BF).astype(F32)
    blended_grad = jnp.einsum(
        "hqk,qhd->khd", weights_low, heads_grad, preferred_element_type=F32
    ).astype(BF).reshape(length, group)
    values_grad = (1.0 - BLEND_MIX) * to_spans(blended_grad, span_count).astype(F32)
    mixed_grad = jnp.concatenate(
        [
            rotate(queries_grad, cosine, -sine_table).reshape(length, group),
            rotate(keys_grad, cosine, -sine_table).reshape(length, group),
            BLEND_MIX * blended_grad.astype(F32),
        ],
        axis=1,
    ).astype(BF)
    normed_in_grad = lax.psum_scatter(
        dot_nt(mixed_grad, qkv_copy).astype(BF), "seq", scatter_dimension=0, tiled=True
    ).astype(F32)
    tokens_grad = hidden_mid_grad + norm_backward(
        normed_in_grad, scaled_in, inverse_in, gains_full[:, 0]
    )

    def to_owner(terms):
        return lax.psum_scatter(terms.astype(BF), "dp", scatter_dimension=0, tiled=True)

    qkv_part = lax.all_gather(to_owner(dot_tn(normed_all, mixed_grad)), "seq", axis=0)
    qkv_total = (
        jnp.transpose(qkv_part.reshape(span_count, owned_rows, 3, group), (1, 2, 0, 3))
        .reshape(owned_rows, triple)
        .astype(F32)
    )
    out_total, gate_up_total, down_total = lax.psum(
        (
            to_owner(dot_tn(attended, mid_grad_low)),
            to_owner(dot_tn(normed_mid, gate_up_grad)),
            to_owner(dot_tn(activation, back_rows)),
        ),
        "seq",
    )
    out_total, gate_up_total, down_total = (
        out_total.astype(F32),
        gate_up_total.astype(F32),
        down_total.astype(F32),
    )

    gains_total = jnp.stack(
        [
            jnp.sum(qkv_total * qkv_weight.astype(BF).astype(F32), axis=1),
            jnp.sum(gate_up_total * gate_up_weight.astype(BF).astype(F32), axis=1),
        ],
        axis=1,
    ) / gains_owned
    masters = (qkv_weight, out_weight, gate_up_weight, down_weight, norm_gains)
    firsts = (first_qkv, first_out, first_gate_up, first_down, first_gains)
    seconds = (second_qkv, second_out, second_gate_up, second_down, second_gains)
    totals = (qkv_total, out_total, gate_up_total, down_total, gains_total)
    rate_list = (MATRIX_RATE, MATRIX_RATE, MATRIX_RATE, MATRIX_RATE, GAIN_RATE)
    decays = (MATRIX_DECAY, MATRIX_DECAY, MATRIX_DECAY, MATRIX_DECAY, 0.0)
    updated = [
        apply_adamw(masters[i], firsts[i], seconds[i], totals[i], rate_list[i], decays[i])
        for i in range(5)
    ]
    return (
        (layer_out[None], tokens_grad[None], values_grad[None])
        + tuple(member[0] for member in updated)
        + tuple(member[1] for member in updated)
        + tuple(member[2] for member in updated)
    )


def solution(mesh):
    rows = P("dp", "seq", None)
    owned = P("dp", None)
    return jax.shard_map(
        on_device,
        mesh=mesh,
        in_specs=(rows, rows, rows, P("dp", "seq"), P()) + (owned,) * 15,
        out_specs=(rows,) * 3 + (owned,) * 15,
        check_vma=False,
    )
```

```python
import functools
import math

import jax
import jax.numpy as jnp
from jax import lax
from jax.experimental import pallas as pl
from jax.experimental.pallas import tpu as pltpu
from jax.sharding import PartitionSpec as P

HEAD_DIM = 64
STEP = 10


NORM_EPS = 1e-06
ADAM_EPS = 1e-08
BLEND_MIX = 0.5
BETA_FIRST = 0.5
BETA_SECOND = 0.5
MATRIX_RATE = 0.06
MATRIX_DECAY = 0.1
GAIN_RATE = 0.5
ROPE_BASE = 10000.0
MASK_FILL = -1e30
SCALE = HEAD_DIM ** (-0.5)

BF = jnp.bfloat16
F32 = jnp.float32


def dot_nn(left, right):
    return lax.dot_general(left, right, (((1,), (0,)), ((), ())), preferred_element_type=F32)


def dot_nt(left, right):
    return lax.dot_general(left, right, (((1,), (1,)), ((), ())), preferred_element_type=F32)


def dot_tn(left, right):
    return lax.dot_general(left, right, (((0,), (0,)), ((), ())), preferred_element_type=F32)


def normalize_parts(matrix):
    inverse = lax.rsqrt(jnp.mean(matrix * matrix, axis=-1, keepdims=True) + NORM_EPS)
    return (matrix * inverse, inverse)


def norm_backward(grad_rows, scaled, inverse, gain_column):
    pushed = grad_rows * gain_column
    return inverse * (pushed - scaled * jnp.mean(pushed * scaled, axis=-1, keepdims=True))


def rotary(positions):
    half_width = HEAD_DIM // 2
    frequency = jnp.exp(
        jnp.arange(half_width, dtype=F32) * (-math.log(ROPE_BASE) / half_width)
    )
    angles = positions.astype(F32)[:, None] * frequency[None, :]
    return (jnp.cos(angles)[:, None, :], jnp.sin(angles)[:, None, :])


def rotate(head_rows, cosine, sine_table):
    half_width = head_rows.shape[-1] // 2
    lower_half = head_rows[..., :half_width]
    upper_half = head_rows[..., half_width:]
    return jnp.concatenate(
        [
            lower_half * cosine - upper_half * sine_table,
            upper_half * cosine + lower_half * sine_table,
        ],
        axis=-1,
    )


def apply_adamw(master, first_state, second_state, gradient, rate, decay):
    next_first = BETA_FIRST * first_state + (1.0 - BETA_FIRST) * gradient
    next_second = BETA_SECOND * second_state + (1.0 - BETA_SECOND) * gradient * gradient
    first_hat = next_first / (1.0 - BETA_FIRST**STEP)
    second_hat = next_second / (1.0 - BETA_SECOND**STEP)
    new_master = master - rate * (first_hat / (jnp.sqrt(second_hat) + ADAM_EPS) + decay * master)
    return (new_master, next_first, next_second)


MESH = pl.DeviceIdType.MESH
VMEM_BYTES = 58 << 20


def full_spec():
    return pl.BlockSpec(memory_space=pltpu.VMEM)


def any_spec():
    return pl.BlockSpec(memory_space=pl.ANY)


class Place:
    def __init__(self, dp_count, span_count):
        self.dp_count = dp_count
        self.span_count = span_count
        self.inner_count = dp_count // 4
        self.dp = lax.axis_index("dp")
        self.span = lax.axis_index("seq")
        self.core = lax.rem(self.dp, 2)
        self.inner = lax.rem(self.dp // 2, self.inner_count)
        self.outer = self.dp // (2 * self.inner_count)

    def at(self, outer, inner, core):
        return (outer * self.inner_count + inner) * 2 + core

    def inner_plus(self, offset):
        return lax.rem(self.inner + offset, self.inner_count)

    def greet_all(self):
        barrier = pltpu.get_barrier_semaphore()
        for offset in range(1, self.dp_count):
            pl.semaphore_signal(
                barrier,
                inc=1,
                device_id=(lax.rem(self.dp + offset, self.dp_count), self.span),
                device_id_type=MESH,
            )
        for offset in range(1, self.span_count):
            pl.semaphore_signal(
                barrier,
                inc=1,
                device_id=(self.dp, lax.rem(self.span + offset, self.span_count)),
                device_id_type=MESH,
            )
        pl.semaphore_wait(barrier, self.dp_count + self.span_count - 2)


def remote(source, target, send_sem, recv_sem, device):
    return pltpu.make_async_remote_copy(
        src_ref=source,
        dst_ref=target,
        send_sem=send_sem,
        recv_sem=recv_sem,
        device_id=device,
        device_id_type=MESH,
    )


def half_rows(rows):
    return rows // 2 // 16 * 16


class Gather:
    def __init__(self, place, whole, columns, send_sems, recv_sems):
        self.place = place
        self.whole = whole
        self.columns = columns
        self.rows = whole.shape[0] // place.dp_count
        self.send_sems = send_sems
        self.recv_sems = recv_sems
        count = place.inner_count
        self.near, self.lower, self.upper, self.pair = 0, count, 2 * count, 3 * count

    @staticmethod
    def slots(inner_count):
        return 6 * inner_count + 1

    def block(self, index, part=None):
        first = half_rows(self.rows)
        start, size = {None: (0, self.rows), 0: (0, first), 1: (first, self.rows - first)}[part]
        return self.whole.at[
            pl.ds(pl.multiple_of(index * self.rows + start, 16), size), self.columns
        ]

    def send(self, source, target, slot, far_slot, device):
        remote(
            source, target, self.send_sems.at[slot], self.recv_sems.at[far_slot], (device, self.place.span)
        ).start()

    def left(self, block, slot):
        remote(
            block, block, self.send_sems.at[slot], self.recv_sems.at[slot], (self.place.dp, self.place.span)
        ).wait_send()

    def arrived(self, block, slot):
        remote(
            block, block, self.send_sems.at[slot], self.recv_sems.at[slot], (self.place.dp, self.place.span)
        ).wait_recv()

    def sibling(self, block, slot):
        place = self.place
        self.send(block, block, slot, slot, place.at(place.outer, place.inner, 1 - place.core))

    def begin(self):
        place, count = self.place, self.place.inner_count
        mine = self.block(place.dp)
        self.send(mine, mine, 0, 0, place.at(1 - place.outer, place.inner, place.core))
        for offset in range(1, count):
            self.send(
                mine,
                mine,
                offset,
                count - offset,
                place.at(place.outer, place.inner_plus(offset), place.core),
            )
        self.sibling(mine, self.pair)

    def forward(self):
        place, count = self.place, self.place.inner_count
        across = place.at(1 - place.outer, place.inner, place.core)
        self.arrived(self.block(across), 0)
        for offset in range(1, count):
            self.send(
                self.block(across, 0),
                self.block(across, 0),
                self.lower + offset,
                self.lower + count - offset,
                place.at(place.outer, place.inner_plus(offset), place.core),
            )
        for offset in range(1, count):
            beside = place.at(place.outer, place.inner_plus(offset), place.core)
            self.arrived(self.block(beside), offset)
            self.send(
                self.block(beside, 1),
                self.block(beside, 1),
                self.upper + offset,
                self.upper + offset,
                across,
            )
        self.sibling(self.block(across), self.pair + count)
        for offset in range(1, count):
            beside = place.at(place.outer, place.inner_plus(offset), place.core)
            self.sibling(self.block(beside), self.pair + offset)

    def share(self):
        place, count = self.place, self.place.inner_count
        for offset in range(1, count):
            far = place.at(1 - place.outer, place.inner_plus(offset), place.core)
            self.arrived(self.block(far, 0), self.lower + offset)
            self.sibling(self.block(far, 0), self.pair + count + offset)
            self.arrived(self.block(far, 1), self.upper + offset)
            self.sibling(self.block(far, 1), self.pair + 2 * count + offset)

    def end(self):
        place, count = self.place, self.place.inner_count
        other = 1 - place.core
        self.arrived(self.block(place.at(place.outer, place.inner, other)), self.pair)
        self.arrived(self.block(place.at(1 - place.outer, place.inner, other)), self.pair + count)
        for offset in range(1, count):
            inner = place.inner_plus(offset)
            self.arrived(self.block(place.at(place.outer, inner, other)), self.pair + offset)
            far = place.at(1 - place.outer, inner, other)
            self.arrived(self.block(far, 0), self.pair + count + offset)
            self.arrived(self.block(far, 1), self.pair + 2 * count + offset)
        mine = self.block(place.dp)
        across = self.block(place.at(1 - place.outer, place.inner, place.core))
        self.left(mine, 0)
        self.left(mine, self.pair)
        self.left(across, self.pair + count)
        for offset in range(1, count):
            inner = place.inner_plus(offset)
            beside = place.at(place.outer, inner, place.core)
            far = place.at(1 - place.outer, inner, place.core)
            self.left(mine, offset)
            self.left(self.block(beside), self.pair + offset)
            self.left(
                self.block(place.at(1 - place.outer, place.inner, place.core), 0),
                self.lower + offset,
            )
            self.left(self.block(beside, 1), self.upper + offset)
            self.left(self.block(far, 0), self.pair + count + offset)
            self.left(self.block(far, 1), self.pair + 2 * count + offset)


class Exchange:
    def __init__(self, place, sources, targets, send_sems, recv_sems):
        self.place = place
        self.sources = sources
        self.targets = targets
        self.send_sems = send_sems
        self.recv_sems = recv_sems

    def copy(self, offset):
        place = self.place
        count = place.span_count
        peer = lax.rem(place.span + offset, count)
        return remote(
            self.sources.at[peer],
            self.targets.at[place.span],
            self.send_sems.at[offset],
            self.recv_sems.at[count - offset],
            (place.dp, peer),
        )

    def start(self):
        for offset in range(1, self.place.span_count):
            self.copy(offset).start()
        self.targets[self.place.span] = self.sources[self.place.span]

    def wait(self):
        place = self.place
        count = place.span_count
        for offset in range(1, count):
            peer = lax.rem(place.span + offset, count)
            remote(
                self.sources.at[peer],
                self.targets.at[peer],
                self.send_sems.at[offset],
                self.recv_sems.at[offset],
                (place.dp, peer),
            ).wait_recv()

    def finish(self):
        for offset in range(1, self.place.span_count):
            self.copy(offset).wait_send()


def cast_rows(source, target, first, moves=None):
    rows = source.shape[0]

    def step(index, unused):
        at = pl.ds(pl.multiple_of(index * 16, 16), 16)
        there = pl.ds(pl.multiple_of(first + index * 16, 16), 16)
        for from_columns, to_columns in moves or ((slice(None), slice(None)),):
            target[there, to_columns] = source[at, from_columns].astype(BF)
        return unused

    lax.fori_loop(0, rows // 16, step, 0)


def swap_halves(rows):
    width = rows.shape[1]
    half = HEAD_DIM // 2
    if width % 128:
        pieces = []
        for start in range(0, width, HEAD_DIM):
            pieces += [rows[:, start + half : start + HEAD_DIM], rows[:, start : start + half]]
        return jnp.concatenate(pieces, axis=1)
    lane = lax.broadcasted_iota(jnp.int32, rows.shape, 1)
    return jnp.where(
        lane % HEAD_DIM < half, pltpu.roll(rows, width - half, 1), pltpu.roll(rows, half, 1)
    )


def angles_of(cosine, sine, position, heads):
    half = HEAD_DIM // 2
    back = lax.rem(cosine.shape[1] - half * position, cosine.shape[1])
    cos_half = pltpu.roll(cosine[...], back, 1)[:, :half]
    sin_half = pltpu.roll(sine[...], back, 1)[:, :half]
    return (
        jnp.concatenate([cos_half] * (2 * heads), axis=1),
        jnp.concatenate([-sin_half, sin_half] * heads, axis=1),
    )


def slot_with(order, position):
    slot = 0
    for index in range(order.shape[0]):
        slot = jnp.where(order[index] == position, index, slot)
    return slot


def segment_starts(bounds, rows, first):
    position = lax.broadcasted_iota(jnp.int32, (rows, 1), 0) + first
    position = position.astype(F32)
    start = jnp.zeros((rows, 1), F32)
    for cut in bounds:
        start = jnp.where(position >= cut, cut, start)
    return position, start


def head_part(matrix, head):
    if matrix.shape[1] == HEAD_DIM:
        return matrix
    lane = lax.broadcasted_iota(jnp.int32, (1, matrix.shape[1]), 1)
    return jnp.where(lane // HEAD_DIM == head, matrix, jnp.zeros_like(matrix))


def forward_kernel(
    dp_count,
    span_count,
    order,
    tokens,
    first_values,
    segments,
    gains_mine,
    qkv_mine,
    out_mine,
    gate_up_mine,
    down_mine,
    cosine,
    sine,
    out_grad,
    counts_out,
    gains_out,
    layer_low,
    mid_grad,
    mid_grad_low,
    normed_left,
    attended_left,
    attended_grad,
    qkv_result,
    normed_result,
    query_result,
    key_result,
    value_result,
    raw_result,
    lse_result,
    gate_up_grad_result,
    activation_result,
    normed_out,
    query_out,
    key_out,
    value_out,
    raw_out,
    lse_out,
    gate_up_grad,
    activation_left,
    gains_send,
    qkv_held,
    out_whole,
    gate_up_whole,
    down_whole,
    qkv_whole,
    attended,
    normed,
    outward,
    normed_grad,
    gains_all,
    counts_send,
    counts_all,
    first_send,
    first_all,
    normed_all,
    scores_kept,
    attended_send,
    attended_all,
    gather_send,
    gather_recv,
    gains_send_sem,
    gains_recv_sem,
    counts_send_sem,
    counts_recv_sem,
    first_send_sem,
    first_recv_sem,
    ring_send,
    ring_recv,
    attended_send_sem,
    attended_recv_sem,
    local_sem,
    result_sem,
):
    place = Place(dp_count, span_count)
    rows, width = tokens.shape
    group = width // span_count
    hidden = down_whole.shape[0]
    owned = out_mine.shape[0]
    heads = group // HEAD_DIM
    last = span_count - 1
    span = place.span

    qkv_loads = []
    for part in range(3):
        first = pl.multiple_of(part * width + span * group, 128)
        copy = pltpu.make_async_copy(
            qkv_mine.at[:, pl.ds(first, group)],
            qkv_held.at[:, part * group : (part + 1) * group],
            local_sem.at[part],
        )
        copy.start()
        qkv_loads.append(copy)

    place.greet_all()
    gains_send[...] = jnp.zeros_like(gains_send)
    gains_send[0:2, :] = gains_mine[...].astype(BF).astype(F32)
    gains_all[place.dp] = gains_send[...]
    gains_copies = []
    for offset in range(1, dp_count):
        peer = lax.rem(place.dp + offset, dp_count)
        copy = remote(
            gains_send,
            gains_all.at[place.dp],
            gains_send_sem.at[offset],
            gains_recv_sem.at[dp_count - offset],
            (peer, span),
        )
        copy.start()
        gains_copies.append(copy)
    parts = hidden_parts(hidden)
    moves = []
    gate_up_columns = []
    for start, size in parts:
        moves.append((slice(start, start + size), slice(2 * start, 2 * start + size)))
        moves.append(
            (
                slice(hidden + start, hidden + start + size),
                slice(2 * start + size, 2 * start + 2 * size),
            )
        )
        gate_up_columns.append(slice(2 * start, 2 * (start + size)))
    every = slice(None)
    sources = [(qkv_whole, every), (out_whole, every), (down_whole, every)]
    sources += [(gate_up_whole, columns) for columns in gate_up_columns]
    gathers = [
        Gather(place, whole, columns, gather_send.at[i], gather_recv.at[i])
        for i, (whole, columns) in enumerate(sources)
    ]
    qkv_gather, out_gather, down_gather = gathers[:3]
    gate_up_gathers = gathers[3:]
    for copy in qkv_loads:
        copy.wait()
    cast_rows(qkv_held, qkv_whole, place.dp * owned)
    qkv_gather.begin()
    for index in range(span_count):
        first_send[index] = first_values[:, index * group : (index + 1) * group]
    first_exchange = Exchange(place, first_send, first_all, first_send_sem, first_recv_sem)
    ids = segments[...]
    row = lax.broadcasted_iota(jnp.int32, (8, 128), 0)
    counts = jnp.zeros((8, 128), F32)
    for cut in range(3):
        below = jnp.sum(jnp.where(ids <= cut, 1.0, 0.0), axis=1, keepdims=True)
        counts = jnp.where(row == cut, below, counts)
    for index in range(span_count):
        counts_send[index] = counts
    counts_exchange = Exchange(place, counts_send, counts_all, counts_send_sem, counts_recv_sem)
    counts_exchange.start()

    residual = tokens[...].astype(F32)
    scaled = residual * lax.rsqrt(jnp.mean(residual * residual, axis=1, keepdims=True) + NORM_EPS)
    for offset in range(1, dp_count):
        peer = lax.rem(place.dp + offset, dp_count)
        remote(
            gains_send,
            gains_all.at[peer],
            gains_send_sem.at[offset],
            gains_recv_sem.at[offset],
            (peer, span),
        ).wait_recv()
    gains_row = jnp.concatenate([gains_all[i] for i in range(dp_count)], axis=1)
    gains_out[...] = gains_row
    normed_all[span] = (scaled * gains_row[0:1, :]).astype(BF)

    def pass_on(block, step, way):
        return remote(
            normed_all.at[block],
            normed_all.at[block],
            ring_send.at[way, step],
            ring_recv.at[way, step],
            (place.dp, jnp.where(way == 0, jnp.minimum(span + 1, last), jnp.maximum(span - 1, 0))),
        )

    @pl.when(span < last)
    def up():
        pass_on(span, 0, 0).start()

    @pl.when(span > 0)
    def down():
        pass_on(span, 0, 1).start()

    cast_rows(out_mine, out_whole, place.dp * owned)
    out_gather.begin()
    cast_rows(down_mine, down_whole, place.dp * down_mine.shape[0])
    qkv_gather.forward()
    down_gather.begin()
    cast_rows(gate_up_mine, gate_up_whole, place.dp * owned, moves)
    for member in gate_up_gathers:
        member.begin()
    qkv_gather.share()
    out_gather.forward()

    for step in range(1, span_count):

        @pl.when(span - step >= 0)
        def from_below():
            block = jnp.maximum(span - step, 0)
            pass_on(block, step - 1, 0).wait_recv()

            @pl.when(span < last)
            def on():
                pass_on(block, step, 0).start()

        @pl.when(span + step <= last)
        def from_above():
            block = jnp.minimum(span + step, last)
            pass_on(block, step - 1, 1).wait_recv()

            @pl.when(span > 0)
            def on():
                pass_on(block, step, 1).start()

        if step == last - 1:
            first_exchange.start()

    qkv_gather.end()
    results = []

    def keep(source, target):
        copy = pltpu.make_async_copy(source, target, result_sem.at[len(results)])
        copy.start()
        results.append(copy)

    keep(qkv_whole, qkv_result)
    counts_exchange.wait()
    cuts = counts_all[0]
    for index in range(1, span_count):
        cuts = cuts + counts_all[index]
    counts_out[...] = cuts
    bounds = [cuts[i : i + 1, 0:1] for i in range(3)]

    def project(position, unused):
        slot = slot_with(order, position)
        normed_here = normed_all[slot]
        normed_out[:, pl.ds(pl.multiple_of(position * rows, rows), rows)] = jnp.transpose(normed_here)
        mixed = dot_nn(normed_here, qkv_whole[...])
        cos_here, sin_here = angles_of(cosine, sine, position, heads)
        query = mixed[:, :group]
        key = mixed[:, group : 2 * group]
        query_out[position] = (query * cos_here + swap_halves(query) * sin_here).astype(BF)
        key_out[position] = (key * cos_here + swap_halves(key) * sin_here).astype(BF)
        raw_out[position] = BLEND_MIX * mixed[:, 2 * group :]
        return unused

    def blend(position, unused):
        slot = slot_with(order, position)
        value_out[position] = (
            raw_out[position] + (1.0 - BLEND_MIX) * first_all[slot].astype(F32)
        ).astype(BF)
        return unused

    lax.fori_loop(0, span_count, project, 0)
    first_exchange.wait()
    lax.fori_loop(0, span_count, blend, 0)
    for source, target in (
        (normed_out, normed_result),
        (query_out, query_result),
        (key_out, key_result),
        (value_out, value_result),
    ):
        keep(source, target)
    out_gather.share()
    down_gather.forward()

    def attend(position, unused):
        query = query_out[position]
        parts = [head_part(query, head) for head in range(heads)]
        query_position, start = segment_starts(bounds, rows, position * rows)

        def score(other, highest):
            key = key_out[other]
            key_position = (
                lax.broadcasted_iota(jnp.int32, (1, rows), 1) + other * rows
            ).astype(F32)
            allowed = (key_position <= query_position) & (key_position >= start)
            found = []
            for head in range(heads):
                masked = jnp.where(allowed, dot_nt(parts[head], key) * SCALE, MASK_FILL)
                scores_kept[head, other] = masked
                found.append(jnp.maximum(highest[head], jnp.max(masked, axis=1, keepdims=True)))
            return tuple(found)

        highest = lax.fori_loop(
            0, position + 1, score, (jnp.full((rows, 1), MASK_FILL, F32),) * heads
        )

        def raise_scores(other, total):
            added = []
            for head in range(heads):
                raised = jnp.exp(scores_kept[head, other] - highest[head])
                scores_kept[head, other] = raised
                added.append(total[head] + jnp.sum(raised, axis=1, keepdims=True))
            return tuple(added)

        total = lax.fori_loop(
            0, position + 1, raise_scores, (jnp.zeros((rows, 1), F32),) * heads
        )
        inverse = [1.0 / member for member in total]

        def gather_values(other, attended):
            value = value_out[other]
            for head in range(heads):
                weights = (scores_kept[head, other] * inverse[head]).astype(BF)
                attended = attended + dot_nn(weights, head_part(value, head))
            return attended

        raw_out[position] = lax.fori_loop(
            0, position + 1, gather_values, jnp.zeros((rows, group), F32)
        )
        lane = lax.broadcasted_iota(jnp.int32, (rows, 128), 1)
        kept = jnp.zeros((rows, 128), F32)
        for head in range(heads):
            kept = jnp.where(lane == head, highest[head] + jnp.log(total[head]), kept)
        lse_out[position] = kept

        @pl.when(position == span_count // 2 - 1)
        def second_parts():
            for member in gate_up_gathers[1:-1]:
                member.forward()

        @pl.when(position == span_count - 2)
        def last_part():
            gate_up_gathers[-1].forward()

        return unused

    gate_up_gathers[0].forward()
    lax.fori_loop(0, span_count, attend, 0)
    down_gather.share()

    for index in range(span_count):
        attended_send[index] = raw_out[order[index]].astype(BF)
    attended_exchange = Exchange(
        place, attended_send, attended_all, attended_send_sem, attended_recv_sem
    )
    attended_exchange.start()
    keep(raw_out, raw_result)
    keep(lse_out, lse_result)
    gate_up_gathers[0].share()
    out_gather.end()
    attended_exchange.wait()
    attended[...] = jnp.concatenate([attended_all[i] for i in range(span_count)], axis=1)

    hidden_mid = tokens[...].astype(F32) + dot_nn(attended[...], out_whole[...])
    outward[...] = hidden_mid
    scaled, inverse = normalize_parts(hidden_mid)
    normed[...] = (scaled * gains_out[1:2, :]).astype(BF)
    normed_left[...] = jnp.transpose(normed[...])
    attended_left[...] = jnp.transpose(attended[...])
    normed_grad[...] = jnp.zeros_like(normed_grad)
    down_gather.end()
    block = 256

    per_part = parts[0][1] // block

    def step(index, unused):
        for number in range(len(parts)):

            @pl.when(index == number * per_part)
            def columns_here():
                if number + 1 < len(parts):
                    gate_up_gathers[number + 1].share()
                gate_up_gathers[number].end()

        start = index // per_part * per_part * block
        size = jnp.minimum(per_part * block, hidden - start)
        offset = lax.rem(index, per_part) * block
        gate_at = pl.ds(pl.multiple_of(2 * start + offset, block), block)
        up_at = pl.ds(pl.multiple_of(2 * start + size + offset, block), block)
        here = pl.ds(pl.multiple_of(index * block, block), block)
        there = pl.ds(pl.multiple_of(hidden + index * block, block), block)
        gate = dot_nn(normed[...], gate_up_whole[:, gate_at])
        upward = dot_nn(normed[...], gate_up_whole[:, up_at])
        activation_grad = dot_nt(out_grad[...], down_whole[here, :])
        sigmoid = jax.nn.sigmoid(gate)
        swish = gate * sigmoid
        activation = (swish * upward).astype(BF)
        activation_left[here, :] = jnp.transpose(activation)
        gate_grad = (
            activation_grad * upward * sigmoid * (1.0 + gate * (1.0 - sigmoid))
        ).astype(BF)
        up_grad = (activation_grad * swish).astype(BF)
        gate_up_grad[:, here] = gate_grad
        gate_up_grad[:, there] = up_grad
        outward[...] += dot_nn(activation, down_whole[here, :])
        normed_grad[...] += dot_nt(gate_grad, gate_up_whole[:, gate_at]) + dot_nt(
            up_grad, gate_up_whole[:, up_at]
        )
        return unused

    lax.fori_loop(0, hidden // block, step, 0)
    keep(gate_up_grad, gate_up_grad_result)
    keep(activation_left, activation_result)
    layer_low[...] = outward[...].astype(BF)
    hidden_mid = tokens[...].astype(F32) + dot_nn(attended[...], out_whole[...])
    scaled, inverse = normalize_parts(hidden_mid)
    grad = out_grad[...].astype(F32) + norm_backward(
        normed_grad[...], scaled, inverse, gains_out[1:2, :]
    )
    mid_grad[...] = grad
    mid_grad_low[...] = grad.astype(BF)
    attended_grad[...] = dot_nt(mid_grad_low[...], out_whole[...]).astype(BF)

    for copy in gains_copies:
        copy.wait_send()
    for exchange in (first_exchange, counts_exchange, attended_exchange):
        exchange.finish()
    for step in range(span_count):

        @pl.when((span - step >= 0) & (span < last))
        def sent_up():
            pass_on(jnp.maximum(span - step, 0), step, 0).wait_send()

        @pl.when((span + step <= last) & (span > 0))
        def sent_down():
            pass_on(jnp.minimum(span + step, last), step, 1).wait_send()

    for copy in results:
        copy.wait()


def hidden_parts(hidden):
    size = 256 * -(-hidden // 1024)
    return [(start, min(size, hidden - start)) for start in range(0, hidden, size)]


def forward_call(
    dp_count, span_count, order, tokens, first_values, segments, gains_mine, qkv_mine,
    out_mine, gate_up_mine, down_mine, cosine, sine, out_grad,
):
    rows, width = tokens.shape
    group = width // span_count
    heads = group // HEAD_DIM
    owned = qkv_mine.shape[0]
    doubled = gate_up_mine.shape[1]
    hidden = doubled // 2
    gathers = 3 + len(hidden_parts(hidden))
    slots = Gather.slots(dp_count // 4)
    dma = pltpu.SemaphoreType.DMA
    by_span = (span_count, rows, group)
    kept = (
        ((width, span_count * rows), BF),
        (by_span, BF),
        (by_span, BF),
        (by_span, BF),
        (by_span, F32),
        ((span_count, rows, 128), F32),
        ((rows, doubled), BF),
        ((hidden, rows), BF),
    )
    return pl.pallas_call(
        functools.partial(forward_kernel, dp_count, span_count),
        out_shape=(
            jax.ShapeDtypeStruct((8, 128), F32),
            jax.ShapeDtypeStruct((8, width), F32),
            jax.ShapeDtypeStruct((rows, width), BF),
            jax.ShapeDtypeStruct((rows, width), F32),
            jax.ShapeDtypeStruct((rows, width), BF),
            jax.ShapeDtypeStruct((width, rows), BF),
            jax.ShapeDtypeStruct((width, rows), BF),
            jax.ShapeDtypeStruct((rows, width), BF),
            jax.ShapeDtypeStruct((width, 3 * group), BF),
        )
        + tuple(jax.ShapeDtypeStruct(shape, kind) for shape, kind in kept),
        in_specs=[pl.BlockSpec(memory_space=pltpu.SMEM)]
        + [full_spec()] * 4
        + [any_spec()]
        + [full_spec()] * 6,
        out_specs=(full_spec(),) * 8 + (any_spec(),) * 9,
        scratch_shapes=[pltpu.VMEM(shape, kind) for shape, kind in kept]
        + [
            pltpu.VMEM((8, owned), F32),
            pltpu.VMEM((owned, 3 * group), F32),
            pltpu.VMEM((width, width), BF),
            pltpu.VMEM((width, doubled), BF),
            pltpu.VMEM((hidden, width), BF),
            pltpu.VMEM((width, 3 * group), BF),
            pltpu.VMEM((rows, width), BF),
            pltpu.VMEM((rows, width), BF),
            pltpu.VMEM((rows, width), F32),
            pltpu.VMEM((rows, width), F32),
            pltpu.VMEM((dp_count, 8, owned), F32),
            pltpu.VMEM((span_count, 8, 128), F32),
            pltpu.VMEM((span_count, 8, 128), F32),
            pltpu.VMEM(by_span, BF),
            pltpu.VMEM(by_span, BF),
            pltpu.VMEM((span_count, rows, width), BF),
            pltpu.VMEM((heads, span_count, rows, rows), F32),
            pltpu.VMEM(by_span, BF),
            pltpu.VMEM(by_span, BF),
            dma((gathers, slots)),
            dma((gathers, slots)),
            dma((dp_count,)),
            dma((dp_count,)),
            dma((span_count,)),
            dma((span_count,)),
            dma((span_count,)),
            dma((span_count,)),
            dma((2, span_count)),
            dma((2, span_count)),
            dma((span_count,)),
            dma((span_count,)),
            dma((3,)),
            dma((9,)),
        ],
        compiler_params=pltpu.CompilerParams(
            collective_id=0, has_side_effects=True, vmem_limit_bytes=61 << 20
        ),
    )(
        order, tokens, first_values, segments, gains_mine, qkv_mine, out_mine,
        gate_up_mine, down_mine, cosine, sine, out_grad,
    )


class Pair:
    def __init__(
        self,
        place,
        left_whole,
        left,
        left_other,
        right_whole,
        right,
        right_other,
        send_sems,
        recv_sems,
    ):
        self.place = place
        self.left = left
        self.left_other = left_other
        self.right = right
        self.right_other = right_other
        other = (place.at(place.outer, place.inner, 1 - place.core), place.span)
        self.left_copy = remote(
            left_whole.at[:, 1 - place.core], left_other, send_sems.at[0], recv_sems.at[0], other
        )
        self.own_copy = pltpu.make_async_copy(
            left_whole.at[:, place.core], left, send_sems.at[2]
        )
        self.right_copy = remote(
            right_whole, right_other, send_sems.at[1], recv_sems.at[1], other
        )
        self.own_right = None
        if right_whole is not right:
            self.own_right = pltpu.make_async_copy(right_whole, right, send_sems.at[3])

    def lend_left(self):
        self.left_copy.start()
        self.own_copy.start()

    def lend_right(self):
        self.right_copy.start()
        self.own_right.start()

    def wait(self):
        self.own_copy.wait()
        if self.own_right is not None:
            self.own_right.wait()
        self.left_copy.wait_recv()
        self.right_copy.wait_recv()

    def finish(self):
        self.left_copy.wait_send()
        self.right_copy.wait_send()

    def product(self, outer, inner, columns):
        chip = outer * self.place.inner_count + inner
        depth = self.right.shape[1]
        found = None
        for block in range(self.right.shape[0]):
            at = slice(block * depth, (block + 1) * depth)
            mine = dot_nn(self.left[chip, :, at], self.right[block, :, columns])
            theirs = dot_nn(self.left_other[chip, :, at], self.right_other[block, :, columns])
            found = mine + theirs if found is None else found + mine + theirs
        return found


class Piece:
    def __init__(self, pair, columns, kind, buffers, sems, result):
        self.pair = pair
        self.place = pair.place
        self.columns = columns
        self.kind = kind
        self.send1, self.recv1, self.send2, self.recv2 = buffers[:4]
        mine = self.recv1.at[0, pair.place.inner if kind == 0 else pair.place.outer]
        self.line = [mine] + list(buffers[4:])
        self.send_sems, self.recv_sems = sems
        self.result = result
        self.sent = []

    def send(self, source, target, slot, far_slot, dp, span=None):
        copy = remote(
            source,
            target,
            self.send_sems.at[slot],
            self.recv_sems.at[far_slot],
            (dp, self.place.span if span is None else span),
        )
        copy.start()
        self.sent.append(copy)

    def arrived(self, target, slot):
        remote(
            target, target, self.send_sems.at[slot], self.recv_sems.at[slot], (self.place.dp, self.place.span)
        ).wait_recv()

    def across(self):
        place = self.place
        return place.at(1 - place.outer, place.inner, place.core)

    def beside(self, offset):
        place = self.place
        return place.at(place.outer, place.inner_plus(offset), place.core)

    def product(self, outer, inner):
        return self.pair.product(outer, inner, self.columns)

    def first(self):
        place, count = self.place, self.place.inner_count
        if self.kind == 0:
            for inner in range(count):
                self.send1[0, inner] = self.product(1 - place.outer, inner).astype(BF)
            self.send(self.send1.at[0], self.recv1.at[0], 0, 0, self.across())
            return
        for offset in range(1, count):
            for outer in range(2):
                self.send1[offset - 1, outer] = self.product(
                    outer, place.inner_plus(offset)
                ).astype(BF)
            self.send(
                self.send1.at[offset - 1],
                self.recv1.at[count - offset - 1],
                offset - 1,
                count - offset - 1,
                self.beside(offset),
            )

    def second(self):
        place, count = self.place, self.place.inner_count
        base = count
        if self.kind == 0:
            self.arrived(self.recv1.at[0], 0)
            for offset in range(1, count):
                inner = place.inner_plus(offset)
                total = self.product(place.outer, inner) + self.recv1[0, inner].astype(F32)
                self.send2[offset - 1] = total.astype(BF)
                self.send(
                    self.send2.at[offset - 1],
                    self.recv2.at[count - offset - 1],
                    base + offset - 1,
                    base + count - offset - 1,
                    self.beside(offset),
                )
            return
        total = self.product(1 - place.outer, place.inner)
        for offset in range(1, count):
            self.arrived(self.recv1.at[offset - 1], offset - 1)
            total = total + self.recv1[offset - 1, 1 - place.outer].astype(F32)
        self.send2[0] = total.astype(BF)
        self.send(self.send2.at[0], self.recv2.at[0], base, base, self.across())

    def total(self):
        place, count = self.place, self.place.inner_count
        base = count
        total = self.product(place.outer, place.inner)
        if self.kind == 0:
            total = total + self.recv1[0, place.inner].astype(F32)
            for offset in range(1, count):
                self.arrived(self.recv2.at[offset - 1], base + offset - 1)
                total = total + self.recv2[offset - 1].astype(F32)
            return total
        for offset in range(1, count):
            total = total + self.recv1[offset - 1, place.outer].astype(F32)
        self.arrived(self.recv2.at[0], base)
        return total + self.recv2[0].astype(F32)


    def shape_of_line(self):
        place = self.place
        half = place.span_count // 2
        low = place.span < half
        depth = jnp.where(low, place.span, place.span_count - 1 - place.span)
        inward = jnp.where(low, place.span + 1, place.span - 1)
        outward = jnp.where(low, place.span - 1, place.span + 1)
        outward = jnp.clip(outward, 0, place.span_count - 1)
        return half, depth, inward, outward

    def line_copy(self, source, target, slot, span):
        base = 2 * self.place.inner_count
        return remote(
            source,
            target,
            self.send_sems.at[base + slot],
            self.recv_sems.at[base + slot],
            (self.place.dp, span),
        )

    def send_inward(self):
        half, depth, inward, outward = self.shape_of_line()
        sum_here, from_out, from_mid = self.line

        @pl.when(depth == half - 1)
        def cross():
            self.line_copy(sum_here, from_mid, 1, inward).start()

        @pl.when(depth < half - 1)
        def in_():
            self.line_copy(sum_here, from_out, 0, inward).start()

    def line_start(self):
        half, depth, inward, outward = self.shape_of_line()
        sum_here, from_out, from_mid = self.line
        sum_here[...] = self.total().astype(BF)

        @pl.when(depth == 0)
        def go():
            self.send_inward()

    def line_in(self):
        half, depth, inward, outward = self.shape_of_line()
        sum_here, from_out, from_mid = self.line

        @pl.when(depth > 0)
        def go():
            self.line_copy(from_out, from_out, 0, outward).wait_recv()
            sum_here[...] = (sum_here[...].astype(F32) + from_out[...].astype(F32)).astype(BF)
            self.send_inward()

    def line_mid(self):
        half, depth, inward, outward = self.shape_of_line()
        sum_here, from_out, from_mid = self.line

        @pl.when(depth == half - 1)
        def go():
            self.line_copy(from_mid, from_mid, 1, inward).wait_recv()
            self.result[...] = (
                sum_here[...].astype(F32) + from_mid[...].astype(F32)
            ).astype(BF)

            @pl.when(depth > 0)
            def out():
                self.line_copy(self.result, self.result, 2, outward).start()

    def line_out(self):
        half, depth, inward, outward = self.shape_of_line()

        @pl.when(depth < half - 1)
        def go():
            self.line_copy(self.result, self.result, 2, inward).wait_recv()

            @pl.when(depth > 0)
            def out():
                self.line_copy(self.result, self.result, 2, outward).start()

    def line_finish(self):
        half, depth, inward, outward = self.shape_of_line()
        sum_here, from_out, from_mid = self.line

        @pl.when(depth == half - 1)
        def cross():
            self.line_copy(sum_here, from_mid, 1, inward).wait_send()

        @pl.when(depth < half - 1)
        def in_():
            self.line_copy(sum_here, from_out, 0, inward).wait_send()

        @pl.when(depth > 0)
        def out():
            self.line_copy(self.result, self.result, 2, outward).wait_send()


    def spread_start(self, results):
        place = self.place
        base = 2 * place.inner_count
        self.results = results
        results[place.span, :, self.columns] = self.total().astype(BF)
        for offset in range(1, place.span_count):
            peer = lax.rem(place.span + offset, place.span_count)
            block = results.at[place.span, :, self.columns]
            self.send(
                block, block, base + offset, base + place.span_count - offset, place.dp, peer
            )

    def spread_wait(self):
        place = self.place
        base = 2 * place.inner_count
        for offset in range(1, place.span_count):
            peer = lax.rem(place.span + offset, place.span_count)
            self.arrived(self.results.at[peer, :, self.columns], base + offset)

    def finish(self):
        for copy in self.sent:
            copy.wait_send()


def cut_columns(width):
    if width > 4096:
        quarter = width // 4 // 128 * 128
        return [slice(i * quarter, (i + 1) * quarter if i < 3 else width) for i in range(4)]
    half = width // 2 // 128 * 128
    return [slice(0, half), slice(half, width)]


def piece_scratch(inner_count, rows, columns, kind, on_line):
    width = columns.stop - columns.start
    if kind == 0:
        shapes = [(1, inner_count, rows, width)] * 2 + [(inner_count - 1, rows, width)] * 2
    else:
        shapes = [(inner_count - 1, 2, rows, width)] * 2 + [(1, rows, width)] * 2
    if on_line:
        shapes += [(rows, width)] * 2
    return shapes


GATE_UP, DOWN, OUT, QKV = range(4)
WAIT_PAIR, ATTEND, CLOSE, WAIT_GRAD, LEND_MIXED, SEND_BLENDED, WAIT_BLENDED, CHAIN, CHAIN_END = range(9)
ORDER = (
    (WAIT_PAIR, DOWN, 0),
    (Piece.first, DOWN, 0),
    (Piece.first, DOWN, 1),
    (WAIT_PAIR, GATE_UP, 0),
    (Piece.first, GATE_UP, 2),
    (Piece.first, GATE_UP, 3),
    (WAIT_GRAD, None, 0),
    (WAIT_PAIR, OUT, 0),
    (Piece.first, GATE_UP, 0),
    (ATTEND, None, 0),
    (CLOSE, None, 0),
    (SEND_BLENDED, None, 0),
    (Piece.second, DOWN, 0),
    (Piece.second, GATE_UP, 2),
    (Piece.line_start, DOWN, 0),
    (LEND_MIXED, None, 0),
    (Piece.second, DOWN, 1),
    (Piece.second, GATE_UP, 0),
    (Piece.line_start, GATE_UP, 2),
    (Piece.first, OUT, 0),
    (Piece.first, OUT, 1),
    (Piece.line_in, DOWN, 0),
    (Piece.second, GATE_UP, 3),
    (Piece.line_in, GATE_UP, 2),
    (WAIT_PAIR, QKV, 0),
    (Piece.first, GATE_UP, 1),
    (Piece.line_start, GATE_UP, 0),
    (Piece.line_mid, DOWN, 0),
    (Piece.second, OUT, 1),
    (Piece.line_start, DOWN, 1),
    (Piece.second, OUT, 0),
    (Piece.line_in, GATE_UP, 0),
    (Piece.line_start, GATE_UP, 3),
    (Piece.first, QKV, 0),
    (Piece.line_start, OUT, 1),
    (WAIT_BLENDED, None, 0),
    (Piece.line_in, DOWN, 1),
    (Piece.line_mid, GATE_UP, 2),
    (Piece.second, GATE_UP, 1),
    (Piece.second, QKV, 0),
    (Piece.line_start, OUT, 0),
    (Piece.line_out, DOWN, 0),
    (Piece.first, QKV, 1),
    (Piece.line_in, GATE_UP, 3),
    (Piece.line_mid, GATE_UP, 0),
    (CHAIN, None, 0),
    (Piece.line_out, GATE_UP, 2),
    (Piece.spread_start, QKV, 0),
    (Piece.second, QKV, 1),
    (Piece.line_mid, DOWN, 1),
    (Piece.line_in, OUT, 0),
    (Piece.line_mid, GATE_UP, 3),
    (Piece.line_start, GATE_UP, 1),
    (CHAIN, None, 1),
    (Piece.line_in, OUT, 1),
    (Piece.spread_start, QKV, 1),
    (Piece.spread_wait, QKV, 0),
    (Piece.line_mid, OUT, 0),
    (Piece.line_mid, OUT, 1),
    (Piece.line_out, OUT, 1),
    (Piece.line_out, DOWN, 1),
    (Piece.line_in, GATE_UP, 1),
    (Piece.line_out, GATE_UP, 0),
    (Piece.line_out, GATE_UP, 3),
    (CHAIN, None, 2),
    (Piece.line_mid, GATE_UP, 1),
    (CHAIN_END, None, 0),
    (Piece.line_out, GATE_UP, 1),
    (Piece.line_out, OUT, 0),
    (Piece.spread_wait, QKV, 1),
)


def backward_kernel(
    dp_count,
    span_count,
    order,
    gate_up_left,
    gate_up_right,
    down_left,
    down_right,
    out_left,
    out_right,
    qkv_left,
    attended_grad_whole,
    query_whole,
    key_whole,
    value_whole,
    raw_whole,
    lse_whole,
    qkv_whole,
    counts,
    cosine,
    sine,
    gate_up_result,
    down_result,
    out_result,
    qkv_result,
    blended_result,
    normed_result,
    attended_grad,
    query,
    key,
    value,
    raw,
    lse,
    qkv_copy,
    load_sem,
    gate_up_own,
    gate_up_other,
    gate_up_right_own,
    gate_up_right_other,
    down_own,
    down_other,
    down_right_own,
    down_right_other,
    out_own,
    out_other,
    out_right_own,
    out_right_other,
    qkv_own,
    qkv_other,
    mixed_other,
    mixed,
    grad_send,
    grad_all,
    key_sum,
    value_sum,
    key_turned,
    query_sum,
    blended_all,
    chain,
    pair_send,
    pair_recv,
    piece_send,
    piece_recv,
    grad_send_sem,
    grad_recv_sem,
    blended_send_sem,
    blended_recv_sem,
    chain_send,
    chain_recv,
    *piece_buffers,
):
    place = Place(dp_count, span_count)
    span, last = place.span, span_count - 1
    rows, width = attended_grad.shape
    group = width // span_count
    heads = group // HEAD_DIM

    loads = []
    for source, target in (
        (attended_grad_whole, attended_grad),
        (key_whole, key),
        (query_whole, query),
        (value_whole, value),
        (raw_whole, raw),
        (lse_whole, lse),
        (qkv_whole, qkv_copy),
    ):
        loads.append(pltpu.make_async_copy(source, target, load_sem.at[len(loads)]))
        loads[-1].start()
    place.greet_all()
    loads[0].wait()
    for index in range(span_count):
        grad_send[index] = attended_grad[:, index * group : (index + 1) * group]
    grad_exchange = Exchange(place, grad_send, grad_all, grad_send_sem, grad_recv_sem)
    grad_exchange.start()
    pairs = [
        Pair(place, *members, pair_send.at[i], pair_recv.at[i])
        for i, members in enumerate(
            (
                (
                    gate_up_left, gate_up_own, gate_up_other,
                    gate_up_right, gate_up_right_own, gate_up_right_other,
                ),
                (down_left, down_own, down_other, down_right, down_right_own, down_right_other),
                (out_left, out_own, out_other, out_right, out_right_own, out_right_other),
                (qkv_left, qkv_own, qkv_other, mixed, mixed, mixed_other),
            )
        )
    ]
    for which in (OUT, DOWN, GATE_UP):
        pairs[which].lend_left()
        pairs[which].lend_right()
    pairs[QKV].lend_left()

    free = list(piece_buffers)
    pieces = []
    for pair, result, on_line in zip(
        pairs, (gate_up_result, down_result, out_result, qkv_result), (True, True, True, False)
    ):
        members = []
        for i, columns in enumerate(cut_columns(pair.right.shape[2])):
            number = 6 if on_line else 4
            buffers, free = free[:number], free[number:]
            at = len(pieces) * 4 + i
            members.append(
                Piece(
                    pair,
                    columns,
                    i % 2,
                    buffers,
                    (piece_send.at[at], piece_recv.at[at]),
                    result.at[:, columns] if on_line else None,
                )
            )
        pieces.append(members)
    def clear(index, unused):
        key_sum[index] = jnp.zeros((rows, group), F32)
        value_sum[index] = jnp.zeros((rows, group), F32)
        return unused

    lax.fori_loop(0, span_count, clear, 0)

    def clear_chain(index, unused):
        chain[index] = jnp.zeros(chain.shape[1:], BF)
        return unused

    @pl.when(span == 0)
    def nothing_from_below():
        lax.fori_loop(1, span_count + 1, clear_chain, 0)

    @pl.when(span == last)
    def nothing_from_above():
        lax.fori_loop(0, span_count, clear_chain, 0)

    cuts = counts[...]
    bounds = [cuts[i : i + 1, 0:1] for i in range(3)]

    def turned_back(rows_in, position):
        cos_here, sin_here = angles_of(cosine, sine, position, heads)
        low = rows_in.astype(BF).astype(F32)
        return (low * cos_here - swap_halves(low) * sin_here).astype(BF)

    for copy in loads[1:]:
        copy.wait()

    def turn_keys(position, unused):
        key_turned[position] = jnp.transpose(key[position])
        return unused

    lax.fori_loop(0, span_count, turn_keys, 0)

    def attend_back(position, unused):
        query_here = (query[position].astype(F32) * SCALE).astype(BF)
        grad_here = grad_all[slot_with(order, position)]
        query_parts = [head_part(query_here, head) for head in range(heads)]
        grad_parts = [head_part(grad_here, head) for head in range(heads)]
        query_stack = jnp.concatenate(query_parts, axis=0)
        grad_stack = jnp.concatenate(grad_parts, axis=0)
        agreed = jnp.transpose(grad_here.astype(F32) * raw[position])
        logs = jnp.transpose(lse[position])
        query_position = (
            lax.broadcasted_iota(jnp.int32, (1, rows), 1) + position * rows
        ).astype(F32)
        start = jnp.zeros((1, rows), F32)
        for cut in bounds:
            start = jnp.where(query_position >= cut, cut, start)
        query_sum[...] = jnp.zeros((group, rows), F32)

        def block(other, unused):
            key_here, value_here, key_back = key[other], value[other], key_turned[other]
            key_position = (
                lax.broadcasted_iota(jnp.int32, (rows, 1), 0) + other * rows
            ).astype(F32)
            allowed = (key_position <= query_position) & (key_position >= start)
            lows, grads = [], []
            for head in range(heads):
                at = slice(head * HEAD_DIM, (head + 1) * HEAD_DIM)
                scores = dot_nt(key_here, query_parts[head])
                weights = jnp.where(allowed, jnp.exp(scores - logs[head : head + 1]), 0.0)
                weights_grad = dot_nt(value_here, grad_parts[head])
                delta = jnp.sum(agreed[at], axis=0, keepdims=True)
                scores_grad = (weights * (weights_grad - delta)).astype(BF)
                lows.append(weights.astype(BF))
                grads.append(scores_grad)
                query_sum[at, :] += dot_nn(key_back[at], scores_grad)
            key_sum[other] += dot_nn(jnp.concatenate(grads, axis=1), query_stack)
            value_sum[other] += dot_nn(jnp.concatenate(lows, axis=1), grad_stack)
            return unused

        lax.fori_loop(0, position + 1, block, 0)
        mixed[position, :, :group] = turned_back(
            jnp.transpose(query_sum[...]) * SCALE, position
        )
        return unused

    def close(position, unused):
        mixed[position, :, group : 2 * group] = turned_back(key_sum[position], position)
        mixed[position, :, 2 * group :] = (
            BLEND_MIX * value_sum[position].astype(BF).astype(F32)
        ).astype(BF)
        return unused

    blended_send = grad_send
    blended_exchange = Exchange(
        place, blended_send, blended_all, blended_send_sem, blended_recv_sem
    )

    def normed_grad(block):
        return dot_nt(mixed[order[block]], qkv_copy[...])

    def add_normed(block, at):
        def step(index, unused):
            here = pl.ds(pl.multiple_of(index * 256, 256), 256)
            more = dot_nt(mixed[order[block]], qkv_copy[here, :])
            chain[at, :, here] = (more + chain[at, :, here].astype(F32)).astype(BF)
            return unused

        lax.fori_loop(0, width // 256, step, 0)

    def pass_on(block, way):
        return remote(
            chain.at[block + 1 - way],
            chain.at[block + 1 - way],
            chain_send.at[way, block],
            chain_recv.at[way, block],
            (place.dp, jnp.minimum(span + 1, last) if way == 0 else jnp.maximum(span - 1, 0)),
        )

    def chain_step(step):
        up = last + span - step
        down = step - (last - span)

        @pl.when((span <= step) & (up > span))
        def going_up():
            block = jnp.clip(up, 0, last)

            @pl.when(span > 0)
            def more():
                pass_on(block, 0).wait_recv()

            add_normed(block, block + 1)
            pass_on(block, 0).start()

        @pl.when((down >= 0) & (down < span))
        def going_down():
            block = jnp.clip(down, 0, last)

            @pl.when(span < last)
            def more():
                pass_on(block, 1).wait_recv()

            add_normed(block, block)
            pass_on(block, 1).start()

    def chain_end():
        @pl.when(span > 0)
        def from_below():
            pass_on(span, 0).wait_recv()

        @pl.when(span < last)
        def from_above():
            pass_on(span, 1).wait_recv()

        normed_result[...] = (
            normed_grad(span) + chain[span + 1].astype(F32) + chain[span].astype(F32)
        )

    def send_blended():
        grad_exchange.finish()
        for index in range(span_count):
            blended_send[index] = value_sum[order[index]].astype(BF)
        blended_exchange.start()

    def keep_blended():
        blended_exchange.wait()
        blended_result[...] = jnp.concatenate(
            [blended_all[i] for i in range(span_count)], axis=1
        )

    single = {
        WAIT_GRAD: grad_exchange.wait,
        CLOSE: lambda: lax.fori_loop(0, span_count, close, 0),
        LEND_MIXED: pairs[3].right_copy.start,
        SEND_BLENDED: send_blended,
        WAIT_BLENDED: keep_blended,
        CHAIN_END: chain_end,
    }
    for action, which, number in ORDER:
        if action in single:
            single[action]()
        elif action == WAIT_PAIR:
            pairs[which].wait()
        elif action == ATTEND:
            lax.fori_loop(0, span_count, attend_back, 0)
        elif action == CHAIN:
            for step in [number] if number < 2 else range(2, last):
                chain_step(step)
        elif action == Piece.spread_start:
            pieces[which][number].spread_start(qkv_result)
        else:
            action(pieces[which][number])

    for pair in pairs:
        pair.finish()
    blended_exchange.finish()
    for which, members in enumerate(pieces):
        for member in members:
            if which != QKV:
                member.line_finish()
            member.finish()
    for step in range(last):
        up = last + span - step
        down_block = step - (last - span)

        @pl.when((span <= step) & (up > span))
        def sent_up():
            pass_on(jnp.clip(up, 0, last), 0).wait_send()

        @pl.when((down_block >= 0) & (down_block < span))
        def sent_down():
            pass_on(jnp.clip(down_block, 0, last), 1).wait_send()


def backward_call(dp_count, span_count, order, factors, others, tables):
    (gate_up_left, gate_up_right, down_left, down_right, out_left, out_right, qkv_left) = factors
    rows, width = others[0].shape
    kept = [pltpu.VMEM(member.shape, member.dtype) for member in others]
    group = width // span_count
    inner_count = dp_count // 4
    dma = pltpu.SemaphoreType.DMA
    by_span = (span_count, rows, group)
    mixed_shape = (span_count, rows, 3 * group)

    def less(left):
        return (left.shape[0],) + left.shape[2:]

    scratch = []
    for left, columns_in, on_line in (
        (gate_up_left, gate_up_right.shape[2], True),
        (down_left, down_right.shape[2], True),
        (out_left, out_right.shape[2], True),
        (qkv_left, 3 * group, False),
    ):
        for i, columns in enumerate(cut_columns(columns_in)):
            scratch += [
                pltpu.VMEM(shape, BF)
                for shape in piece_scratch(inner_count, left.shape[2], columns, i % 2, on_line)
            ]
    slots = 2 * inner_count + max(3, span_count)
    return pl.pallas_call(
        functools.partial(backward_kernel, dp_count, span_count),
        out_shape=(
            jax.ShapeDtypeStruct((gate_up_left.shape[2], gate_up_right.shape[2]), BF),
            jax.ShapeDtypeStruct((down_left.shape[2], down_right.shape[2]), BF),
            jax.ShapeDtypeStruct((out_left.shape[2], out_right.shape[2]), BF),
            jax.ShapeDtypeStruct((span_count, qkv_left.shape[2], 3 * group), BF),
            jax.ShapeDtypeStruct((rows, width), BF),
            jax.ShapeDtypeStruct((rows, width), F32),
        ),
        in_specs=[pl.BlockSpec(memory_space=pltpu.SMEM)]
        + [any_spec()] * (len(factors) + len(others))
        + [full_spec()] * len(tables),
        out_specs=(full_spec(),) * 6,
        scratch_shapes=kept
        + [
            dma((len(others),)),
            pltpu.VMEM(less(gate_up_left), BF),
            pltpu.VMEM(less(gate_up_left), BF),
            pltpu.VMEM(gate_up_right.shape, BF),
            pltpu.VMEM(gate_up_right.shape, BF),
            pltpu.VMEM(less(down_left), BF),
            pltpu.VMEM(less(down_left), BF),
            pltpu.VMEM(down_right.shape, BF),
            pltpu.VMEM(down_right.shape, BF),
            pltpu.VMEM(less(out_left), BF),
            pltpu.VMEM(less(out_left), BF),
            pltpu.VMEM(out_right.shape, BF),
            pltpu.VMEM(out_right.shape, BF),
            pltpu.VMEM(less(qkv_left), BF),
            pltpu.VMEM(less(qkv_left), BF),
            pltpu.VMEM(mixed_shape, BF),
            pltpu.VMEM(mixed_shape, BF),
            pltpu.VMEM(by_span, BF),
            pltpu.VMEM(by_span, BF),
            pltpu.VMEM(by_span, F32),
            pltpu.VMEM(by_span, F32),
            pltpu.VMEM((span_count, group, rows), BF),
            pltpu.VMEM((group, rows), F32),
            pltpu.VMEM(by_span, BF),
            pltpu.VMEM((span_count + 1, rows, width), BF),
            dma((4, 4)),
            dma((4, 4)),
            dma((16, slots)),
            dma((16, slots)),
            dma((span_count,)),
            dma((span_count,)),
            dma((span_count,)),
            dma((span_count,)),
            dma((2, span_count)),
            dma((2, span_count)),
        ]
        + scratch,
        compiler_params=pltpu.CompilerParams(
            collective_id=1, has_side_effects=True, vmem_limit_bytes=61 << 20
        ),
    )(order, *factors, *others, *tables)


def update_rows(master, first_state, second_state, gradient, rate, decay):
    next_first = BETA_FIRST * first_state + (1.0 - BETA_FIRST) * gradient
    next_second = BETA_SECOND * second_state + (1.0 - BETA_SECOND) * gradient * gradient
    first_hat = next_first * (1.0 / (1.0 - BETA_FIRST**STEP))
    second_hat = next_second * (1.0 / (1.0 - BETA_SECOND**STEP))
    new_master = master - rate * (first_hat / (jnp.sqrt(second_hat) + ADAM_EPS) + decay * master)
    return (new_master, next_first, next_second)


def finish_kernel(
    qkv_total,
    out_total,
    gate_up_total,
    down_total,
    gains,
    gains_first,
    gains_second,
    tokens,
    mid_grad,
    normed_grad,
    gains_rows,
    blended_grad,
    layer_low,
    qkv,
    qkv_first,
    qkv_second,
    out,
    out_first,
    out_second,
    gate_up,
    gate_up_first,
    gate_up_second,
    down,
    down_first,
    down_second,
    layer_out,
    tokens_grad,
    values_grad,
    new_gains,
    new_gains_first,
    new_gains_second,
    *rest,
):
    results, held, sums, in_sem, out_sem = rest[:12], rest[12:24], rest[24], rest[25], rest[26]
    states = (
        (qkv, qkv_first, qkv_second),
        (out, out_first, out_second),
        (gate_up, gate_up_first, gate_up_second),
        (down, down_first, down_second),
    )
    width = tokens.shape[1]
    span_count = qkv_total.shape[0]
    group = width // span_count

    def qkv_rows(part):
        def rows(at):
            return jnp.concatenate(
                [
                    qkv_total[i, at, part * group : (part + 1) * group].astype(F32)
                    for i in range(span_count)
                ],
                axis=1,
            )

        return rows

    def rows_of(total, columns):
        return lambda at: total[at, columns].astype(F32)

    parts = []
    for columns in cut_columns(gate_up_total.shape[1]):
        parts.append((2, columns, rows_of(gate_up_total, columns)))
    for part in range(3):
        parts.append((0, slice(part * width, (part + 1) * width), qkv_rows(part)))
    for columns in cut_columns(width):
        parts.append((3, columns, rows_of(down_total, columns)))
    parts.append((1, slice(0, width), rows_of(out_total, slice(0, width))))

    def moves(number, source, target, sems):
        weight, columns, _ = parts[number]
        return [
            pltpu.make_async_copy(
                source[i].at[:, columns], target[i].at[:, columns], sems.at[number, i]
            )
            for i in range(3)
        ]

    loads, stores = [], []
    for number, (weight, _, _) in enumerate(parts):
        here = held[3 * weight : 3 * weight + 3]
        loads.append(moves(number, states[weight], here, in_sem))
        stores.append(moves(number, here, results[3 * weight : 3 * weight + 3], out_sem))
        for copy in loads[-1]:
            copy.start()

    residual = tokens[...].astype(F32)
    scaled, inverse = normalize_parts(residual)
    tokens_grad[...] = mid_grad[...] + norm_backward(
        normed_grad[...], scaled, inverse, gains_rows[0:1, :]
    )
    layer_out[...] = layer_low[...]
    sums[...] = jnp.zeros_like(sums)
    values_grad[...] = (1.0 - BLEND_MIX) * blended_grad[...].astype(F32)

    for number, (weight, columns, total) in enumerate(parts):
        here = held[3 * weight : 3 * weight + 3]
        for copy in loads[number]:
            copy.wait()
        owned = here[0].shape[0]
        wants_sum = weight in (0, 2)

        def step(index, unused):
            at = pl.ds(pl.multiple_of(index * 16, 16), 16)
            gradient = total(at)
            master = here[0][at, columns]
            if wants_sum:
                partial = jnp.sum(
                    gradient * master.astype(BF).astype(F32), axis=1, keepdims=True
                )
                lane = 0 if weight == 0 else 1
                slot = lax.broadcasted_iota(jnp.int32, (16, 128), 1) == lane
                sums[at, :] += jnp.where(slot, partial, 0.0)
            updated = update_rows(
                master,
                here[1][at, columns],
                here[2][at, columns],
                gradient,
                MATRIX_RATE,
                MATRIX_DECAY,
            )
            for i in range(3):
                here[i][at, columns] = updated[i]
            return unused

        lax.fori_loop(0, owned // 16, step, 0)
        for copy in stores[number]:
            copy.start()

    gain = gains[...]
    gains_total = jnp.transpose(sums[...])[:2, :] / gain.astype(BF).astype(F32)
    updated = update_rows(gain, gains_first[...], gains_second[...], gains_total, GAIN_RATE, 0.0)
    new_gains[...], new_gains_first[...], new_gains_second[...] = updated
    for group_of_copies in stores:
        for copy in group_of_copies:
            copy.wait()


def finish_call(totals, gains_states, token_parts, states):
    flat = [member for weight in states for member in weight]
    rows, width = token_parts[0].shape
    gains_shape = jax.ShapeDtypeStruct(gains_states[0].shape, F32)
    dma = pltpu.SemaphoreType.DMA
    count = len(cut_columns(totals[2].shape[1])) + 3 + 2 + 1
    return pl.pallas_call(
        finish_kernel,
        out_shape=(
            jax.ShapeDtypeStruct((rows, width), BF),
            jax.ShapeDtypeStruct((rows, width), F32),
            jax.ShapeDtypeStruct((rows, width), F32),
            gains_shape,
            gains_shape,
            gains_shape,
        )
        + tuple(jax.ShapeDtypeStruct(member.shape, F32) for member in flat),
        in_specs=[full_spec()] * 13 + [any_spec()] * 12,
        out_specs=(full_spec(),) * 6 + (any_spec(),) * 12,
        scratch_shapes=[pltpu.VMEM(member.shape, F32) for member in flat]
        + [
            pltpu.VMEM((gains_states[0].shape[1], 128), F32),
            dma((count, 3)),
            dma((count, 3)),
        ],
        compiler_params=pltpu.CompilerParams(vmem_limit_bytes=VMEM_BYTES),
    )(*totals, *gains_states, *token_parts, *flat)


def to_heads(rows, span_count):
    return lax.all_to_all(
        rows.reshape(rows.shape[0], span_count, rows.shape[1] // span_count),
        "seq",
        split_axis=1,
        concat_axis=0,
        tiled=True,
    ).reshape(rows.shape[0] * span_count, rows.shape[1] // span_count)


def to_spans(columns, span_count):
    rows_here = columns.shape[0] // span_count
    got = lax.all_to_all(
        columns.reshape(span_count, rows_here, columns.shape[1]),
        "seq",
        split_axis=0,
        concat_axis=0,
        tiled=True,
    )
    return jnp.transpose(got, (1, 0, 2)).reshape(rows_here, columns.shape[1] * span_count)


def on_device(
    tokens,
    first_values,
    out_grad,
    segments,
    span_order,
    qkv_weight,
    out_weight,
    gate_up_weight,
    down_weight,
    norm_gains,
    first_qkv,
    first_out,
    first_gate_up,
    first_down,
    first_gains,
    second_qkv,
    second_out,
    second_gate_up,
    second_down,
    second_gains,
):
    span_count = lax.axis_size("seq")
    mine = lax.axis_index("seq")
    owned_rows, triple = qkv_weight.shape
    model_width = triple // 3
    group = model_width // span_count
    group_heads = group // HEAD_DIM
    residual = tokens[0].astype(F32)
    rows_here = residual.shape[0]
    length = rows_here * span_count
    hidden_width = gate_up_weight.shape[1] // 2

    dp_count = lax.axis_size("dp")
    gains_owned = norm_gains.astype(BF).astype(F32)
    in_kernels = (
        length * model_width <= 1 << 20
        and dp_count % 4 == 0
        and dp_count >= 8
        and span_count % 2 == 0
        and group % 128 == 0
        and span_count * HEAD_DIM // 2 <= 128
        and hidden_width % 256 == 0
    )
    if in_kernels:
        half_width = HEAD_DIM // 2
        lane = lax.broadcasted_iota(jnp.int32, (rows_here, 128), 1)
        position = lax.broadcasted_iota(jnp.int32, (rows_here, 128), 0) + lane // half_width * rows_here
        frequency = jnp.exp(
            (jnp.arange(128, dtype=jnp.int32) % half_width).astype(F32)
            * (-math.log(ROPE_BASE) / half_width)
        )
        angles = lax.optimization_barrier(position).astype(F32) * frequency[None, :]
        cosine, sine = jnp.cos(angles), jnp.sin(angles)
        gains_states = tuple(
            jnp.transpose(member) for member in (norm_gains, first_gains, second_gains)
        )
        (
            counts, gains_rows, layer_low, hidden_mid_grad, mid_grad_low, normed_mid_left,
            attended_left, attended_grad, qkv_copy, normed_left, query_pos, key_pos, value_pos,
            raw_pos, lse_pos, gate_up_grad, activation_left,
        ) = forward_call(
            dp_count, span_count, span_order, tokens[0], first_values[0], segments,
            gains_states[0], qkv_weight, out_weight, gate_up_weight, down_weight, cosine, sine, out_grad[0],
        )
        def in_blocks(left):
            return left.reshape(dp_count // 2, 2, left.shape[0] // dp_count, left.shape[1])

        factors = (
            in_blocks(normed_mid_left),
            gate_up_grad[None],
            in_blocks(activation_left),
            out_grad,
            in_blocks(attended_left),
            mid_grad_low[None],
            in_blocks(normed_left),
        )
        others = (
            attended_grad,
            query_pos, key_pos, value_pos, raw_pos, lse_pos, qkv_copy,
        )
        gate_up_total, down_total, out_total, qkv_part, blended_grad, normed_in_grad = backward_call(
            dp_count, span_count, span_order, factors, others, (counts, cosine, sine)
        )
        finished = finish_call(
            (qkv_part, out_total, gate_up_total, down_total),
            gains_states,
            (tokens[0], hidden_mid_grad, normed_in_grad, gains_rows, blended_grad, layer_low),
            (
                (qkv_weight, first_qkv, second_qkv),
                (out_weight, first_out, second_out),
                (gate_up_weight, first_gate_up, second_gate_up),
                (down_weight, first_down, second_down),
            ),
        )
        new_gains = tuple(jnp.transpose(member) for member in finished[3:6])
        return (
            tuple(member[None] for member in finished[:3])
            + finished[6::3]
            + new_gains[:1]
            + finished[7::3]
            + new_gains[1:2]
            + finished[8::3]
            + new_gains[2:]
        )

    qkv_owned = qkv_weight.reshape(owned_rows, 3, model_width).astype(BF)
    qkv_mine = lax.dynamic_slice_in_dim(qkv_owned, mine * group, group, 2).reshape(
        owned_rows, 3 * group
    )
    gains_full = lax.all_gather(norm_gains.astype(BF), "dp", axis=0, tiled=True).astype(F32)
    qkv_copy = lax.all_gather(qkv_mine, "dp", axis=0, tiled=True)
    out_copy = lax.all_gather(out_weight.astype(BF), "dp", axis=0, tiled=True)
    gate_up_copy = lax.all_gather(gate_up_weight.astype(BF), "dp", axis=0, tiled=True)
    down_copy = lax.all_gather(down_weight.astype(BF), "dp", axis=0, tiled=True)

    row_index = jnp.arange(length, dtype=jnp.int32)
    owner_table = (row_index // rows_here)[:, None] == jnp.arange(span_count, dtype=jnp.int32)[
        None, :
    ]
    positions = (
        jnp.sum(jnp.where(owner_table, span_order[None, :], 0), axis=1) * rows_here
        + row_index % rows_here
    )
    all_segments = lax.all_gather(segments[0], "seq", axis=0, tiled=True)
    cosine, sine_table = rotary(positions)
    allowed = (all_segments[:, None] == all_segments[None, :]) & (
        positions[None, :] <= positions[:, None]
    )

    scaled_in, inverse_in = normalize_parts(residual)
    normed_in = (scaled_in * gains_full[:, 0]).astype(BF)
    normed_all = lax.all_gather(normed_in, "seq", axis=0, tiled=True)
    first_all = to_heads(first_values[0], span_count)
    mixed = dot_nn(normed_all, qkv_copy)
    queries = rotate(
        mixed[:, :group].reshape(length, group_heads, HEAD_DIM), cosine, sine_table
    ).astype(BF)
    keys = rotate(
        mixed[:, group : 2 * group].reshape(length, group_heads, HEAD_DIM), cosine, sine_table
    ).astype(BF)
    blended = (
        (BLEND_MIX * mixed[:, 2 * group :] + (1.0 - BLEND_MIX) * first_all.astype(F32))
        .astype(BF)
        .reshape(length, group_heads, HEAD_DIM)
    )
    scores = jnp.einsum("qhd,khd->hqk", queries, keys, preferred_element_type=F32) * SCALE
    masked = jnp.where(allowed[None], scores, MASK_FILL)
    highest = jnp.max(masked, axis=-1, keepdims=True)
    raised = jnp.where(allowed[None], jnp.exp(masked - highest), 0.0)
    weights = raised / jnp.sum(raised, axis=-1, keepdims=True)
    weights_low = weights.astype(BF)
    attended_raw = jnp.einsum("hqk,khd->qhd", weights_low, blended, preferred_element_type=F32)
    attended = to_spans(attended_raw.reshape(length, group).astype(BF), span_count)

    hidden_mid = residual + dot_nn(attended, out_copy)
    scaled_mid, inverse_mid = normalize_parts(hidden_mid)
    normed_mid = (scaled_mid * gains_full[:, 1]).astype(BF)
    gate_up = dot_nn(normed_mid, gate_up_copy)
    gate_part = gate_up[:, :hidden_width]
    upward = gate_up[:, hidden_width:]
    sigmoid_gate = jax.nn.sigmoid(gate_part)
    swish_gate = gate_part * sigmoid_gate
    activation = (swish_gate * upward).astype(BF)
    layer_out = (hidden_mid + dot_nn(activation, down_copy)).astype(BF)
    back_rows = out_grad[0]
    activation_grad = dot_nt(back_rows, down_copy)
    gate_up_grad = jnp.concatenate(
        [
            activation_grad * upward * sigmoid_gate * (1.0 + gate_part * (1.0 - sigmoid_gate)),
            activation_grad * swish_gate,
        ],
        axis=1,
    ).astype(BF)
    normed_mid_grad = dot_nt(gate_up_grad, gate_up_copy)
    hidden_mid_grad = back_rows.astype(F32) + norm_backward(
        normed_mid_grad, scaled_mid, inverse_mid, gains_full[:, 1]
    )
    mid_grad_low = hidden_mid_grad.astype(BF)
    attended_grad = to_heads(dot_nt(mid_grad_low, out_copy).astype(BF), span_count)

    heads_grad = attended_grad.reshape(length, group_heads, HEAD_DIM)
    delta = jnp.transpose(jnp.sum(heads_grad.astype(F32) * attended_raw, axis=-1))
    weights_grad = jnp.einsum("qhd,khd->hqk", heads_grad, blended, preferred_element_type=F32)
    scores_grad = (weights * (weights_grad - delta[..., None])).astype(BF)
    queries_grad = (
        jnp.einsum("hqk,khd->qhd", scores_grad, keys, preferred_element_type=F32) * SCALE
    ).astype(BF).astype(F32)
    keys_grad = (
        jnp.einsum("hqk,qhd->khd", scores_grad, queries, preferred_element_type=F32) * SCALE
    ).astype(BF).astype(F32)
    blended_grad = jnp.einsum(
        "hqk,qhd->khd", weights_low, heads_grad, preferred_element_type=F32
    ).astype(BF).reshape(length, group)
    values_grad = (1.0 - BLEND_MIX) * to_spans(blended_grad, span_count).astype(F32)
    mixed_grad = jnp.concatenate(
        [
            rotate(queries_grad, cosine, -sine_table).reshape(length, group),
            rotate(keys_grad, cosine, -sine_table).reshape(length, group),
            BLEND_MIX * blended_grad.astype(F32),
        ],
        axis=1,
    ).astype(BF)
    normed_in_grad = lax.psum_scatter(
        dot_nt(mixed_grad, qkv_copy).astype(BF), "seq", scatter_dimension=0, tiled=True
    ).astype(F32)
    tokens_grad = hidden_mid_grad + norm_backward(
        normed_in_grad, scaled_in, inverse_in, gains_full[:, 0]
    )

    def to_owner(terms):
        return lax.psum_scatter(terms.astype(BF), "dp", scatter_dimension=0, tiled=True)

    qkv_part = lax.all_gather(to_owner(dot_tn(normed_all, mixed_grad)), "seq", axis=0)
    qkv_total = (
        jnp.transpose(qkv_part.reshape(span_count, owned_rows, 3, group), (1, 2, 0, 3))
        .reshape(owned_rows, triple)
        .astype(F32)
    )
    out_total, gate_up_total, down_total = lax.psum(
        (
            to_owner(dot_tn(attended, mid_grad_low)),
            to_owner(dot_tn(normed_mid, gate_up_grad)),
            to_owner(dot_tn(activation, back_rows)),
        ),
        "seq",
    )
    out_total, gate_up_total, down_total = (
        out_total.astype(F32),
        gate_up_total.astype(F32),
        down_total.astype(F32),
    )

    gains_total = jnp.stack(
        [
            jnp.sum(qkv_total * qkv_weight.astype(BF).astype(F32), axis=1),
            jnp.sum(gate_up_total * gate_up_weight.astype(BF).astype(F32), axis=1),
        ],
        axis=1,
    ) / gains_owned
    masters = (qkv_weight, out_weight, gate_up_weight, down_weight, norm_gains)
    firsts = (first_qkv, first_out, first_gate_up, first_down, first_gains)
    seconds = (second_qkv, second_out, second_gate_up, second_down, second_gains)
    totals = (qkv_total, out_total, gate_up_total, down_total, gains_total)
    rate_list = (MATRIX_RATE, MATRIX_RATE, MATRIX_RATE, MATRIX_RATE, GAIN_RATE)
    decays = (MATRIX_DECAY, MATRIX_DECAY, MATRIX_DECAY, MATRIX_DECAY, 0.0)
    updated = [
        apply_adamw(masters[i], firsts[i], seconds[i], totals[i], rate_list[i], decays[i])
        for i in range(5)
    ]
    return (
        (layer_out[None], tokens_grad[None], values_grad[None])
        + tuple(member[0] for member in updated)
        + tuple(member[1] for member in updated)
        + tuple(member[2] for member in updated)
    )


def solution(mesh):
    rows = P("dp", "seq", None)
    owned = P("dp", None)
    return jax.shard_map(
        on_device,
        mesh=mesh,
        in_specs=(rows, rows, rows, P("dp", "seq"), P()) + (owned,) * 15,
        out_specs=(rows,) * 3 + (owned,) * 15,
        check_vma=False,
    )
```
